128 devices in a mesh: dp: 32 (over x, z, y_hi), tensor: 4 (over y_lo, core).
Axes of the slice: x: 4, y: 4 (y_hi: 2, y_lo: 2; y = y_hi * 2 + y_lo), z: 4, core: 2. Of those that a mesh axis runs over, the one named last changes fastest.
Arguments:
- hidden_in: bfloat16 [32768, 1536], P(('dp', 'tensor')), may hold values from -6 to 6
- seg_ids: int32 [32768], P('dp'), may hold values from 0 to 4, as said below
- pre_gain: float32 [1536], replicated, may hold values from 0.1 to 1.9
- proj_gate: bfloat16 [1536, 3072], P('dp', 'tensor'), may hold values from -0.15625 to 0.15625
- proj_x: bfloat16 [1536, 3072], P('dp', 'tensor'), may hold values from -0.15625 to 0.15625
- proj_bc: bfloat16 [1536, 256], P('dp'), may hold values from -0.15625 to 0.15625
- proj_dt: bfloat16 [1536, 48], P('dp', 'tensor'), may hold values from -0.15625 to 0.15625
- conv_x: float32 [4, 3072], replicated, may hold values from -0.5 to 0.5
- conv_bias_x: float32 [3072], replicated, may hold values from -0.5 to 0.5
- conv_bc: float32 [4, 256], replicated, may hold values from -0.5 to 0.5
- conv_bias_bc: float32 [256], replicated, may hold values from -0.5 to 0.5
- dt_bias: float32 [48], replicated, may hold values from -9 to -3
- a_log: float32 [48], replicated, may hold values from -1 to 2.77
- skip_d: float32 [48], replicated, may hold values from 0.5 to 1.5
- gate_gain: float32 [3072], replicated, may hold values from 0.1 to 1.9
- proj_out: bfloat16 [3072, 1536], P('tensor', 'dp'), may hold values from -0.109375 to 0.109375
- cotangent: bfloat16 [32768, 1536], P(('dp', 'tensor')), may hold values from -6 to 6
Outputs:
- out: bfloat16 [32768, 1536], P(('dp', 'tensor'))
- d_hidden: float32 [32768, 1536], P(('dp', 'tensor'))
- d_pre_gain: float32 [1536], replicated
- d_proj_gate: float32 [1536, 3072], P('dp', 'tensor')
- d_proj_x: float32 [1536, 3072], P('dp', 'tensor')
- d_proj_bc: float32 [1536, 256], P('dp')
- d_proj_dt: float32 [1536, 48], P('dp', 'tensor')
- d_conv_x: float32 [4, 3072], replicated
- d_conv_bias_x: float32 [3072], replicated
- d_conv_bc: float32 [4, 256], replicated
- d_conv_bias_bc: float32 [256], replicated
- d_dt_bias: float32 [48], replicated
- d_a_log: float32 [48], replicated
- d_skip_d: float32 [48], replicated
- d_gate_gain: float32 [3072], replicated
- d_proj_out: float32 [3072, 1536], P('tensor', 'dp')
The draws below stay inside these ranges and needn't reach their ends.
Inputs may be any that keep to these rules, and one draw needn't show every extreme that they name: `seg_ids`: within each sequence of 1024 tokens (those of one index of dp) the numbers start at 0, never fall and rise by one at each of exactly four document starts; one document's first token has an index of at most 128 within its sequence (counting from 0), and its last token an index of at least 895.
All inputs are finite; a program needn't handle non-finite values.
Results may differ from the reference program's by a relative error of at most 0.0082.
Values may be sent and summed in bfloat16 or wider, within the bound.
A program may use at most 128 MiB of HBM per device.

```python
import jax
import jax.numpy as jnp
from jax import lax

D = 1536
HEADS = 48
STATE = 128
CONV_WIDTH = 4
GROUP = 256
TOK_DEV = 256
INNER = 3072
SEQ_LEN = 1024
TOKENS = 32768
N_DP = 32


def draw_seg_ids(key, part):
    key = jax.random.fold_in(key, 7)

    def one_sequence(seq_key):
        sub_keys = jax.random.split(seq_key, 4)
        start_long = jax.random.randint(sub_keys[0], (), 2, TOK_DEV // 2 + 1)
        first_cut = jax.random.randint(sub_keys[1], (), 1, start_long)
        end_long = jax.random.randint(sub_keys[2], (), SEQ_LEN - TOK_DEV // 2, SEQ_LEN - 1)
        last_cut = jax.random.randint(sub_keys[3], (), end_long + 1, SEQ_LEN)
        positions = jnp.arange(SEQ_LEN, dtype=jnp.int32)
        counted = (positions >= first_cut).astype(jnp.int32) + (positions >= start_long).astype(jnp.int32)
        counted = counted + (positions >= end_long).astype(jnp.int32) + (positions >= last_cut).astype(jnp.int32)
        return counted
    return jax.vmap(one_sequence)(jax.random.split(key, N_DP)).reshape(-1)


def level_of(rng, dims, cuts, low, largest):
    gain, own = 1.0, jax.random.fold_in(rng, 6)
    for axis_at, parts in cuts:
        draws = jnp.exp(jax.random.uniform(jax.random.fold_in(own, axis_at), (parts,), jnp.float32, low / len(cuts), largest / len(cuts)))
        gain = gain * jnp.repeat(draws, dims[axis_at] // parts).reshape([-1 if axis == axis_at else 1 for axis in range(len(dims))])
    return gain


def noise(stream_key, extent, width, bound, cuts=(), held_as=jnp.bfloat16):
    gain = level_of(stream_key, extent, cuts, -0.22, 0.18) if cuts else 1.0
    drawn = jax.random.normal(stream_key, extent, jnp.float32) * width * gain
    return jnp.minimum(jnp.maximum(drawn, -bound), bound).astype(held_as)


def setup_inputs(seed: int = 0) -> dict:
    arg_keys = jax.random.split(jax.random.key(seed), 18)
    return {
        "hidden_in": noise(arg_keys[0], (TOKENS, D), 1.0, 6.0, ((0, 128),)),
        "seg_ids": draw_seg_ids(jax.random.fold_in(arg_keys[17], 71), 0),
        "pre_gain": jnp.clip(1.0 + 0.18 * jax.random.normal(arg_keys[2], (D,), jnp.float32), 0.1, 1.9),
        "proj_gate": noise(arg_keys[3], (D, INNER), D ** -0.5, 0.15625, ((0, 32), (1, 4))),
        "proj_x": noise(arg_keys[4], (D, INNER), D ** -0.5, 0.15625, ((0, 32), (1, 4))),
        "proj_bc": noise(arg_keys[5], (D, 2 * STATE), D ** -0.5, 0.15625, ((0, 32),)),
        "proj_dt": noise(arg_keys[6], (D, HEADS), D ** -0.5, 0.15625, ((0, 32), (1, 4))),
        "conv_x": jnp.clip(jax.random.uniform(arg_keys[7], (CONV_WIDTH, INNER), jnp.float32, -0.5, 0.5), -0.5, 0.5),
        "conv_bias_x": jnp.clip(jax.random.uniform(arg_keys[8], (INNER,), jnp.float32, -0.5, 0.5), -0.5, 0.5),
        "conv_bc": jnp.clip(jax.random.uniform(arg_keys[9], (CONV_WIDTH, 2 * STATE), jnp.float32, -0.5, 0.5), -0.5, 0.5),
        "conv_bias_bc": jnp.clip(jax.random.uniform(arg_keys[10], (2 * STATE,), jnp.float32, -0.5, 0.5), -0.5, 0.5),
        "dt_bias": jnp.clip(jax.random.uniform(arg_keys[11], (HEADS,), jnp.float32, -9.0, -3.0), -9.0, -3.0),
        "a_log": jnp.clip(jax.random.uniform(arg_keys[12], (HEADS,), jnp.float32, -1.0, 2.77), -1.0, 2.77),
        "skip_d": jnp.clip(jax.random.uniform(arg_keys[13], (HEADS,), jnp.float32, 0.5, 1.5), 0.5, 1.5),
        "gate_gain": jnp.clip(1.0 + 0.18 * jax.random.normal(arg_keys[14], (INNER,), jnp.float32), 0.1, 1.9),
        "proj_out": noise(arg_keys[15], (INNER, D), INNER ** -0.5, 0.109375, ((0, 4), (1, 32))),
        "cotangent": noise(arg_keys[16], (TOKENS, D), 1.0, 6.0, ((0, 128),)),
    }


EPS = 1e-05

@jax.custom_vjp
def low(v):
    return lax.optimization_barrier(v.astype(jnp.bfloat16)).astype(jnp.float32)

@jax.custom_vjp
def low_back(v):
    return v

def low_keep(v):
    return (low(v), None)

def low_pass(kept, grad):
    return (grad,)

def back_keep(v):
    return (v, None)

def back_low(kept, grad):
    return (low(grad),)
low.defvjp(low_keep, low_pass)
low_back.defvjp(back_keep, back_low)

def matmul(left, right):
    return jnp.dot(left, right, precision=lax.Precision.HIGHEST, preferred_element_type=jnp.float32)

def pre_norm(hidden, gain_vec):
    inv_rms = lax.rsqrt(lax.optimization_barrier(jnp.mean(hidden * hidden, axis=1)) + EPS)
    return hidden * inv_rms[:, None] * gain_vec[None, :]

def causal_conv(values, kernel, offset_bias, segment):
    kernel_len = kernel.shape[0]
    seq_len = values.shape[0]
    padded = jnp.pad(values, ((kernel_len - 1, 0), (0, 0)))
    seg_pad = jnp.pad(segment, (kernel_len - 1, 0), constant_values=-1)
    result = jnp.zeros_like(values) + offset_bias[None, :]
    for shift_at in range(kernel_len):
        matches = (seg_pad[shift_at:shift_at + seq_len] == segment).astype(jnp.float32)
        result = result + kernel[shift_at][None, :] * padded[shift_at:shift_at + seq_len] * matches[:, None]
    return result

def block_step(decay_rates, carried, block_in):
    x_block, dt_block, b_block, c_block, seg_block, seg_before = block_in
    block_rows = seg_block.shape[0]
    log_decay = jnp.cumsum(dt_block * decay_rates[None, :], axis=0)
    cum_heads = log_decay.T
    position = lax.iota(jnp.int32, block_rows)
    allowed = (position[:, None] >= position[None, :]) & (seg_block[:, None] == seg_block[None, :])
    log_gaps = jnp.where(allowed[None], cum_heads[:, :, None] - cum_heads[:, None, :], 0.0)
    decay_mat = jnp.where(allowed[None], jnp.exp(log_gaps), 0.0)
    query_key = jnp.dot(c_block, b_block.T, precision=lax.Precision.HIGHEST, preferred_element_type=jnp.float32)
    mixing = decay_mat * query_key[None] * dt_block.T[:, None, :]
    within = jnp.einsum('hts,shp->thp', mixing, x_block, precision=lax.Precision.HIGHEST)
    carry_on = (seg_block == seg_before).astype(jnp.float32)
    from_state = jnp.einsum('tn,hpn->thp', c_block, carried, precision=lax.Precision.HIGHEST)
    from_past = from_state * (jnp.exp(log_decay) * carry_on[:, None])[:, :, None]
    last_seg = seg_block[block_rows - 1]
    tail_weight = jnp.exp(log_decay[block_rows - 1][None, :] - log_decay) * (seg_block == last_seg).astype(jnp.float32)[:, None] * dt_block
    keep_state = jnp.exp(log_decay[block_rows - 1]) * (last_seg == seg_before).astype(jnp.float32)
    new_state = carried * keep_state[:, None, None] + jnp.einsum('sh,sn,shp->hpn', tail_weight, b_block, x_block, precision=lax.Precision.HIGHEST)
    return (new_state, within + from_past)

def scan_ssd(x_heads, step_sizes, decay_rates, b_all, c_all, segment):
    seq_len, head_count, head_size = x_heads.shape
    blocks = seq_len // GROUP
    state_size = b_all.shape[1]
    seg_blocks = segment.reshape(blocks, GROUP).astype(jnp.int32)
    seg_before = jnp.concatenate([jnp.full((1,), -1, dtype=jnp.int32), seg_blocks[:-1, GROUP - 1]])
    initial = jnp.zeros((head_count, head_size, state_size), jnp.float32)
    stepper = jax.checkpoint(block_step)

    def scan_body(carried, block_in):
        return stepper(decay_rates, carried, block_in)
    final_state, outputs = lax.scan(scan_body, initial, (x_heads.reshape(blocks, GROUP, head_count, head_size), step_sizes.reshape(blocks, GROUP, head_count), b_all.reshape(blocks, GROUP, state_size), c_all.reshape(blocks, GROUP, state_size), seg_blocks, seg_before))
    return outputs.reshape(seq_len, head_count, head_size)

def ssm_mixer(x_proj, bc_proj, dt_proj, gate_proj, conv_x, conv_bias_x, conv_bc, conv_bias_bc, dt_bias, a_log, skip_d, segment):
    x_conv = jax.nn.silu(causal_conv(x_proj, conv_x, conv_bias_x, segment))
    bc_conv = jax.nn.silu(causal_conv(bc_proj, conv_bc, conv_bias_bc, segment))
    state_size = bc_conv.shape[1] // 2
    step_sizes = jax.nn.softplus(dt_proj + dt_bias[None, :])
    decay_rates = -jnp.exp(a_log)
    seq_len = x_proj.shape[0]
    head_count = dt_proj.shape[1]
    x_heads = x_conv.reshape(seq_len, head_count, -1)
    scanned = scan_ssd(x_heads, step_sizes, decay_rates, bc_conv[:, :state_size], bc_conv[:, state_size:], segment)
    scanned = scanned + skip_d[None, :, None] * x_heads
    return scanned.reshape(seq_len, -1) * jax.nn.silu(gate_proj)

def block_forward(hidden, segment, pre_gain, proj_gate, proj_x, proj_bc, proj_dt, conv_x, conv_bias_x, conv_bc, conv_bias_bc, dt_bias, a_log, skip_d, gate_gain, proj_out):
    normed = low(pre_norm(hidden, pre_gain))
    gate_val = low_back(matmul(normed, proj_gate))
    x_val = low_back(matmul(normed, proj_x))
    bc_val = low_back(matmul(normed, proj_bc))
    dt_val = low_back(matmul(normed, proj_dt))
    gated_out = ssm_mixer(x_val, bc_val, dt_val, gate_val, conv_x, conv_bias_x, conv_bc, conv_bias_bc, dt_bias, a_log, skip_d, segment)
    inv_scale = lax.rsqrt(lax.optimization_barrier(jnp.mean(gated_out * gated_out, axis=1)) + EPS)
    normed_out = low(gated_out * inv_scale[:, None] * gate_gain[None, :])
    return hidden + matmul(normed_out, proj_out)

def reference(hidden_in, seg_ids, pre_gain, proj_gate, proj_x, proj_bc, proj_dt, conv_x, conv_bias_x, conv_bc, conv_bias_bc, dt_bias, a_log, skip_d, gate_gain, proj_out, cotangent):
    params = tuple((weight_arr.astype(jnp.float32) for weight_arr in (pre_gain, proj_gate, proj_x, proj_bc, proj_dt, conv_x, conv_bias_x, conv_bc, conv_bias_bc, dt_bias, a_log, skip_d, gate_gain, proj_out)))
    hidden_seq = hidden_in.astype(jnp.float32).reshape(N_DP, SEQ_LEN, D)
    cot_seq = cotangent.astype(jnp.float32).reshape(N_DP, SEQ_LEN, D)
    seg_seq = seg_ids.astype(jnp.int32).reshape(N_DP, SEQ_LEN)

    def one_sequence(totals, seq_item):
        hidden, cot_rows, segment = seq_item

        def forward(hidden_arg, *weights):
            return block_forward(hidden_arg, segment, *weights)
        result, backward = jax.vjp(forward, hidden, *params)
        gradients = backward(cot_rows)
        summed = tuple((total_one + grad_one for total_one, grad_one in zip(totals, gradients[1:])))
        return (summed, (result, gradients[0]))
    initial = tuple((jnp.zeros_like(weight_arr) for weight_arr in params))
    totals, outputs = lax.scan(one_sequence, initial, (hidden_seq, cot_seq, seg_seq))
    results, d_hidden = outputs
    return (results.reshape(TOKENS, D).astype(jnp.bfloat16), d_hidden.reshape(TOKENS, D), totals[0], totals[1], totals[2], totals[3], totals[4], totals[5], totals[6], totals[7], totals[8], totals[9], totals[10], totals[11], totals[12], totals[13])
```

```python
import functools

import jax
import jax.numpy as jnp
from jax import lax
from jax.experimental import pallas as pl
from jax.experimental.pallas import tpu as pltpu
from jax.sharding import PartitionSpec as P

MESH = pl.DeviceIdType.MESH
F32 = jnp.float32
BF = jnp.bfloat16


def place():
    dp = lax.axis_index("dp")
    t = lax.axis_index("tensor")
    return dp // 8, (dp // 2) % 4, dp % 2, t


def dev(x, z, yh, t):
    return ((x * 4 + z) * 2 + yh, t)


def ag_kernel(ten, wa, wb, h, c, oa, ob, oh, oc, lsem, wsend, wrecv, tsend, trecv):
    x, z, yh, t = place()
    yl = t // 2; co = t % 2
    m4 = lambda v: (v + 8) % 4
    def nb(axis, d):
        if axis == "x": return dev(m4(x + d), z, yh, t)
        return dev(x, m4(z + d), yh, t)
    ypeer = dev(x, z, 1 - yh, t)
    tc_ = dev(x, z, yh, yl * 2 + (1 - co))
    ty = dev(x, z, yh, (1 - yl) * 2 + co)
    bar = pltpu.get_barrier_semaphore()
    peers = [ypeer, nb("x", 1), nb("x", -1), nb("z", 1), nb("z", -1), tc_, ty]
    for p in peers:
        pl.semaphore_signal(bar, inc=1, device_id=p, device_id_type=MESH)
    pl.semaphore_wait(bar, len(peers))
    sends = []
    def rc(src, dst, ss, rs, to):
        cp = pltpu.make_async_remote_copy(src_ref=src, dst_ref=dst, send_sem=ss, recv_sem=rs, device_id=to, device_id_type=MESH)
        cp.start(); sends.append(cp); return cp
    halves = ((wa, oa, "x", "z"), (wb, ob, "z", "x"))
    def blk(o, r1, d1, d2, y=None, yn=None):
        ix, iz = (m4(x + d1), m4(z + d2)) if r1 == "x" else (m4(x + d2), m4(z + d1))
        return o.at[ix, iz] if y is None else o.at[ix, iz, y]
    sem = [0, 0]
    def wc(i, src, dst, to):
        k = sem[i]; sem[i] += 1
        return rc(src, dst, wsend.at[i, k], wrecv.at[i, k], to)
    loc = []
    for i, (w, o, *_) in enumerate(halves):
        cp = pltpu.make_async_copy(w, o.at[x, z, yh], lsem.at[i]); cp.start(); loc.append(cp)
    for i, (s, o) in enumerate(((h, oh), (c, oc))):
        cp = pltpu.make_async_copy(s, o.at[t], lsem.at[2 + i]); cp.start(); loc.append(cp)
    yc = []; a0 = []; b0 = []
    for i, (w, o, r1, r2) in enumerate(halves):
        yc.append(wc(i, w, o.at[x, z, yh], ypeer))
    for i, (w, o, r1, r2) in enumerate(halves):
        me = o.at[x, z, yh]
        a0.append([wc(i, w, me, nb(r1, d)) for d in (1, -1)])
    for i, (w, o, r1, r2) in enumerate(halves):
        me = o.at[x, z, yh]
        b0.append([wc(i, w, me, nb(r2, d)) for d in (1, -1)])
    a1 = []; b1 = []
    for i, (w, o, r1, r2) in enumerate(halves):
        yc[i].wait_recv()
        pe = o.at[x, z, 1 - yh]
        a1.append([wc(i, pe, pe, nb(r1, d)) for d in (1, -1)])
    if ten:
        tc1 = []
        for i, (s, o) in enumerate(((h, oh), (c, oc))):
            a = rc(s, o.at[t], tsend.at[i, 0], trecv.at[i, 0], ty)
            b = rc(s, o.at[t], tsend.at[i, 1], trecv.at[i, 1], tc_)
            tc1.append((a, b))
    for i, (w, o, r1, r2) in enumerate(halves):
        pe = o.at[x, z, 1 - yh]
        b1.append([wc(i, pe, pe, nb(r2, d)) for d in (1, -1)])
    a2 = []; b2 = []
    for i, (w, o, r1, r2) in enumerate(halves):
        for k in (0, 1):
            a0[i][k].wait_recv(); a1[i][k].wait_recv()
        l_ = blk(o, r1, -1, 0, 0); r_ = blk(o, r1, 1, 0, 1)
        a2.append((wc(i, l_, l_, nb(r1, 1)), wc(i, r_, r_, nb(r1, -1))))
    for i, (w, o, r1, r2) in enumerate(halves):
        bb = []
        for d1 in (-1, 1):
            bl = blk(o, r1, d1, 0)
            bb.append([wc(i, bl, bl, nb(r2, d)) for d in (1, -1)])
        b2.append(bb)
    b3 = []
    for i, (w, o, r1, r2) in enumerate(halves):
        a2[i][0].wait_recv(); a2[i][1].wait_recv()
        bl = blk(o, r1, 2, 0)
        b3.append([wc(i, bl, bl, nb(r2, d)) for d in (1, -1)])
    if ten:
        tc2 = []
        for i, (s, o) in enumerate(((h, oh), (c, oc))):
            tc1[i][0].wait_recv()
            bk = o.at[(1 - yl) * 2 + co]
            tc2.append(rc(bk, bk, tsend.at[i, 2], trecv.at[i, 2], tc_))
    last = []
    def fw(i, o, r1, d1):
        l_ = blk(o, r1, d1, -1, 0); r_ = blk(o, r1, d1, 1, 1); n = halves[i][3]
        last.append(wc(i, l_, l_, nb(n, 1))); last.append(wc(i, r_, r_, nb(n, -1)))
    for i, (w, o, r1, r2) in enumerate(halves):
        for k in (0, 1):
            b0[i][k].wait_recv(); b1[i][k].wait_recv()
        fw(i, o, r1, 0)
    for i, (w, o, r1, r2) in enumerate(halves):
        for j, d1 in enumerate((-1, 1)):
            for k in (0, 1): b2[i][j][k].wait_recv()
            fw(i, o, r1, d1)
    for i, (w, o, r1, r2) in enumerate(halves):
        for k in (0, 1): b3[i][k].wait_recv()
        fw(i, o, r1, 2)
    for l in loc: l.wait()
    if ten:
        for i in range(2):
            tc1[i][1].wait_recv(); tc2[i].wait_recv()
    for cp in last: cp.wait_recv()
    for cp in sends: cp.wait_send()

def gather(wa, wb, h, c, ten=True, vm=False):
    anyspec = pl.BlockSpec(memory_space=pl.ANY)
    ospec = pl.BlockSpec(memory_space=pltpu.VMEM) if vm else anyspec
    ca, cb = wa.shape[1], wb.shape[1]
    outs = (jax.ShapeDtypeStruct((4, 4, 2, 48, ca), jnp.bfloat16), jax.ShapeDtypeStruct((4, 4, 2, 48, cb), jnp.bfloat16),
            jax.ShapeDtypeStruct((4, 256, 1536), jnp.bfloat16), jax.ShapeDtypeStruct((4, 256, 1536), jnp.bfloat16))
    return pl.pallas_call(functools.partial(ag_kernel, ten), out_shape=outs, in_specs=[anyspec] * 4, out_specs=[ospec] * 4,
        scratch_shapes=[pltpu.SemaphoreType.DMA((4,)), pltpu.SemaphoreType.DMA((2, 25)), pltpu.SemaphoreType.DMA((2, 25)),
                        pltpu.SemaphoreType.DMA((2, 3)), pltpu.SemaphoreType.DMA((2, 3))],
        compiler_params=pltpu.CompilerParams(collective_id=0, has_side_effects=True, vmem_limit_bytes=60*2**20), name="gather_all")(wa, wb, h, c)


def rs_kernel(ga, gb, po, pn, sv, oa, ob, oo, on, osv,
              va, vb, vo, vn, r1a, r1b, r2a, r2b, ha, hb, q1a, q1b, q2a, q2b, ka, kb, ya, yb,
              co_buf, cy_buf, cs_buf, sacc, sx, sz, sy, st, bct,
              lsem, wsend, wrecv, tsend, trecv, ssend, srecv):
    x, z, yh, t = place()
    yl = t // 2; co = t % 2
    m4 = lambda v: (v + 8) % 4
    def nb(axis, d):
        if axis == "x": return dev(m4(x + d), z, yh, t)
        return dev(x, m4(z + d), yh, t)
    ypeer = dev(x, z, 1 - yh, t)
    tcore = dev(x, z, yh, yl * 2 + (1 - co))
    tyl = dev(x, z, yh, (1 - yl) * 2 + co)
    tdiag = dev(x, z, yh, (1 - yl) * 2 + 1 - co)
    bar = pltpu.get_barrier_semaphore()
    peers = [ypeer, tcore, tyl, tdiag] + [nb(a, d) for a in "xz" for d in (1, 2, 3)]
    for p in peers:
        pl.semaphore_signal(bar, inc=1, device_id=p, device_id_type=MESH)
    loads = []
    for i, (s, d) in enumerate(((ga, va), (gb, vb), (po, vo), (pn, vn))):
        cp = pltpu.make_async_copy(s, d, lsem.at[i]); cp.start(); loads.append(cp)
    pl.semaphore_wait(bar, len(peers))
    sends = []
    def rc(src, dst, ss, rs, to):
        cp = pltpu.make_async_remote_copy(src_ref=src, dst_ref=dst, send_sem=ss, recv_sem=rs, device_id=to, device_id_type=MESH)
        cp.start(); sends.append(cp); return cp
    def acc(dst, idx, terms):
        pass
    pos = {"x": x, "z": z}
    halves = ((va, "z", "x", r1a, r2a, ha, q1a, q2a, ka, ya, oa), (vb, "x", "z", r1b, r2b, hb, q1b, q2b, kb, yb, ob))
    def b1(v, a1, d, k=None):
        p = m4(pos[a1] + d)
        if a1 == "z": return v.at[:, p] if k is None else v.at[pl.ds(2 * k, 2), p]
        return v.at[p] if k is None else v.at[p, pl.ds(2 * k, 2)]
    small = []
    for d in (1, 2, 3):
        small.append(rc(sv, sx.at[d - 1], ssend.at[d - 1], srecv.at[d - 1], nb("x", d)))
    for l in loads[:2]: l.wait()
    s1 = []
    for i, (v, a1, a2, r1, r2, *_) in enumerate(halves):
        s1.append((rc(b1(v, a1, 2, 0), r1.at[0], wsend.at[i, 0], wrecv.at[i, 0], nb(a1, 1)),
                   rc(b1(v, a1, 2, 1), r1.at[1], wsend.at[i, 1], wrecv.at[i, 1], nb(a1, -1))))
    s1b = []
    for i, (v, a1, a2, r1, r2, *_) in enumerate(halves):
        s1b.append((rc(b1(v, a1, 1, 1), r2.at[0, pl.ds(2, 2)], wsend.at[i, 2], wrecv.at[i, 2], nb(a1, 1)),
                    rc(b1(v, a1, -1, 0), r2.at[1, pl.ds(0, 2)], wsend.at[i, 3], wrecv.at[i, 3], nb(a1, -1))))
    tr = []
    for l in loads[2:]: l.wait()
    for i, v in enumerate((vo, vn)):
        a = rc(v.at[(1 - yl) * 2 + 1 - co], co_buf.at[i, 0], tsend.at[i, 0], trecv.at[i, 0], tcore)
        b = rc(v.at[yl * 2 + 1 - co], co_buf.at[i, 1], tsend.at[i, 1], trecv.at[i, 1], tcore)
        tr.append((a, b))
    for i, v in enumerate((vo, vn)):
        tr[i][0].wait_recv()
        def addc(j, _, i=i, v=v):
            rows = pl.ds(pl.multiple_of(j * 32, 32), 32)
            cs_buf[i, rows] = (v[(1 - yl) * 2 + co, rows].astype(F32) + co_buf[i, 0, rows].astype(F32)).astype(BF)
            return 0
        lax.fori_loop(0, 8, addc, 0)
        tr[i] = tr[i] + (rc(cs_buf.at[i], cy_buf.at[i], tsend.at[i, 2], trecv.at[i, 2], tyl),)
    for s in small: s.wait_recv()
    sacc[0] = sv[...] + sx[0] + sx[1] + sx[2]
    small = [rc(sacc.at[0], sz.at[d - 1], ssend.at[2 + d], srecv.at[2 + d], nb("z", d)) for d in (1, 2, 3)]
    s1c = []
    for i, (v, a1, a2, r1, r2, *_) in enumerate(halves):
        for side, dd, k in ((0, 1, 0), (1, -1, 1)):
            s1[i][side].wait_recv()
            p = m4(pos[a1] + dd)
            def add1(j, _, v=v, a1=a1, r1=r1, side=side, p=p, k=k):
                e = j // 2 ; y = j % 2
                if a1 == "z":
                    v[2 * k + e, p, y] = (v[2 * k + e, p, y].astype(F32) + r1[side, e, y].astype(F32)).astype(BF)
                else:
                    v[p, 2 * k + e, y] = (v[p, 2 * k + e, y].astype(F32) + r1[side, e, y].astype(F32)).astype(BF)
                return 0
            lax.fori_loop(0, 4, add1, 0)
            s1c.append(rc(b1(v, a1, dd, k), r2.at[side, pl.ds(2 * k, 2)], wsend.at[i, 4 + side], wrecv.at[i, 4 + side], nb(a1, dd)))
    for s in small: s.wait_recv()
    sacc[1] = sacc[0] + sz[0] + sz[1] + sz[2]
    small = [rc(sacc.at[1], sy, ssend.at[6], srecv.at[6], ypeer)]
    s2 = []
    for i, (v, a1, a2, r1, r2, h, q1, q2, kk, yy, oo_) in enumerate(halves):
        s1b[i][0].wait_recv(); s1b[i][1].wait_recv()
        s1c[2 * i].wait_recv(); s1c[2 * i + 1].wait_recv()
        p = pos[a1]
        def add2(j, _, v=v, a1=a1, r2=r2, h=h, p=p):
            e = j // 2; y = j % 2
            own = v[e, p, y] if a1 == "z" else v[p, e, y]
            h[e, y] = (own.astype(F32) + r2[0, e, y].astype(F32) + r2[1, e, y].astype(F32)).astype(BF)
            return 0
        lax.fori_loop(0, 8, add2, 0)
        q = pos[a2]
        s2.append((rc(h.at[m4(q + 2), 0], q1.at[0], wsend.at[i, 6], wrecv.at[i, 6], nb(a2, 1)),
                   rc(h.at[m4(q + 2), 1], q1.at[1], wsend.at[i, 7], wrecv.at[i, 7], nb(a2, -1)),
                   rc(h.at[m4(q + 1), 1], q2.at[0, 1], wsend.at[i, 8], wrecv.at[i, 8], nb(a2, 1)),
                   rc(h.at[m4(q - 1), 0], q2.at[1, 0], wsend.at[i, 9], wrecv.at[i, 9], nb(a2, -1))))
    for s in small: s.wait_recv()
    sacc[2] = sacc[1] + sy[...]
    small = [rc(sacc.at[2], st.at[j], ssend.at[7 + j], srecv.at[7 + j], d_) for j, d_ in enumerate((tcore, tyl, tdiag))]
    s2c = []
    for i, (v, a1, a2, r1, r2, h, q1, q2, kk, yy, oo_) in enumerate(halves):
        q = pos[a2]
        for side, dd in ((0, 1), (1, -1)):
            s2[i][side].wait_recv()
            pp = m4(q + dd)
            h[pp, side] = (h[pp, side].astype(F32) + q1[side].astype(F32)).astype(BF)
            s2c.append(rc(h.at[pp, side], q2.at[side, side], wsend.at[i, 10 + side], wrecv.at[i, 10 + side], nb(a2, dd)))
    s3 = []
    for i, (v, a1, a2, r1, r2, h, q1, q2, kk, yy, oo_) in enumerate(halves):
        q = pos[a2]
        s2[i][2].wait_recv(); s2[i][3].wait_recv()
        s2c[2 * i].wait_recv(); s2c[2 * i + 1].wait_recv()
        kk[...] = (h[q, 1 - yh].astype(F32) + q2[0, 1 - yh].astype(F32) + q2[1, 1 - yh].astype(F32)).astype(BF)
        s3.append(rc(kk, yy, wsend.at[i, 12], wrecv.at[i, 12], ypeer))
    for i, (v, o) in enumerate(((vo, oo), (vn, on))):
        tr[i][1].wait_recv(); tr[i][2].wait_recv()
        def addf(j, _, i=i, v=v, o=o):
            rows = pl.ds(pl.multiple_of(j * 32, 32), 32)
            o[rows] = v[t, rows].astype(F32) + co_buf[i, 1, rows].astype(F32) + cy_buf[i, rows].astype(F32)
            return 0
        lax.fori_loop(0, 8, addf, 0)
    for i, (v, a1, a2, r1, r2, h, q1, q2, kk, yy, o) in enumerate(halves):
        q = pos[a2]
        s3[i].wait_recv()
        o[...] = h[q, yh].astype(F32) + q2[0, yh].astype(F32) + q2[1, yh].astype(F32) + yy[...].astype(F32)
    for s in small: s.wait_recv()
    osv[t] = sacc[2]
    osv[yl * 2 + 1 - co] = st[0]
    osv[(1 - yl) * 2 + co] = st[1]
    osv[(1 - yl) * 2 + 1 - co] = st[2]
    for cp in sends: cp.wait_send()

def reduce_all(ga, gb, po, pn, sv):
    anys = pl.BlockSpec(memory_space=pl.ANY); vm = pl.BlockSpec(memory_space=pltpu.VMEM)
    ca, cb = ga.shape[-1], gb.shape[-1]; R = sv.shape[0]
    outs = (jax.ShapeDtypeStruct((48, ca), F32), jax.ShapeDtypeStruct((48, cb), F32), jax.ShapeDtypeStruct((256, 1536), F32),
            jax.ShapeDtypeStruct((256, 1536), F32), jax.ShapeDtypeStruct((4, R, 128), F32))
    D = pltpu.SemaphoreType.DMA
    V = lambda *s, d=BF: pltpu.VMEM(s, d)
    scratch = [V(4, 4, 2, 48, ca), V(4, 4, 2, 48, cb), V(4, 256, 1536), V(4, 256, 1536),
               V(2, 2, 2, 48, ca), V(2, 2, 2, 48, cb), V(2, 4, 2, 48, ca), V(2, 4, 2, 48, cb),
               V(4, 2, 48, ca), V(4, 2, 48, cb), V(2, 48, ca), V(2, 48, cb), V(2, 2, 48, ca), V(2, 2, 48, cb),
               V(48, ca), V(48, cb), V(48, ca), V(48, cb),
               V(2, 2, 256, 1536), V(2, 256, 1536), V(2, 256, 1536),
               V(3, R, 128, d=F32), V(3, R, 128, d=F32), V(3, R, 128, d=F32), V(R, 128, d=F32), V(3, R, 128, d=F32), V(8, 128, d=F32),
               D((4,)), D((2, 13)), D((2, 13)), D((2, 3)), D((2, 3)), D((10,)), D((10,))]
    return pl.pallas_call(rs_kernel, out_shape=outs, in_specs=[anys] * 4 + [vm], out_specs=[vm] * 5, scratch_shapes=scratch,
        compiler_params=pltpu.CompilerParams(collective_id=1, has_side_effects=True, vmem_limit_bytes=60 * 2**20), name="reduce_all")(ga, gb, po, pn, sv)


GROUP = 256
INNER = 3072
EPS = 1e-05


def causal_conv(values, kernel, offset_bias, segment):
    kernel_len = kernel.shape[0]
    seq_len = values.shape[0]
    padded = jnp.pad(values, ((kernel_len - 1, 0), (0, 0)))
    seg_pad = jnp.pad(segment, (kernel_len - 1, 0), constant_values=-1)
    result = jnp.zeros_like(values) + offset_bias[None, :]
    for shift_at in range(kernel_len):
        matches = (seg_pad[shift_at : shift_at + seq_len] == segment).astype(F32)
        result = result + kernel[shift_at][None, :] * padded[shift_at : shift_at + seq_len] * matches[:, None]
    return result


def block_step(decay_rates, carried, block_in):
    x_block, dt_block, b_block, c_block, seg_block, seg_before = block_in
    block_rows = seg_block.shape[0]
    log_decay = jnp.cumsum(dt_block * decay_rates[None, :], axis=0)
    cum_heads = log_decay.T
    position = lax.iota(jnp.int32, block_rows)
    allowed = (position[:, None] >= position[None, :]) & (seg_block[:, None] == seg_block[None, :])
    log_gaps = jnp.where(allowed[None], cum_heads[:, :, None] - cum_heads[:, None, :], 0.0)
    decay_mat = jnp.where(allowed[None], jnp.exp(log_gaps), 0.0)
    query_key = jnp.dot(c_block, b_block.T, precision=lax.Precision.HIGHEST, preferred_element_type=F32)
    mixing = decay_mat * query_key[None] * dt_block.T[:, None, :]
    within = jnp.einsum("hts,shp->thp", mixing, x_block, precision=lax.Precision.HIGHEST)
    carry_on = (seg_block == seg_before).astype(F32)
    from_state = jnp.einsum("tn,hpn->thp", c_block, carried, precision=lax.Precision.HIGHEST)
    from_past = from_state * (jnp.exp(log_decay) * carry_on[:, None])[:, :, None]
    last_seg = seg_block[block_rows - 1]
    tail_weight = (
        jnp.exp(log_decay[block_rows - 1][None, :] - log_decay)
        * (seg_block == last_seg).astype(F32)[:, None]
        * dt_block
    )
    keep_state = jnp.exp(log_decay[block_rows - 1]) * (last_seg == seg_before).astype(F32)
    new_state = carried * keep_state[:, None, None] + jnp.einsum(
        "sh,sn,shp->hpn", tail_weight, b_block, x_block, precision=lax.Precision.HIGHEST
    )
    return (new_state, within + from_past)


def scan_ssd(x_heads, step_sizes, decay_rates, b_all, c_all, segment):
    seq_len, head_count, head_size = x_heads.shape
    blocks = seq_len // GROUP
    state_size = b_all.shape[1]
    seg_blocks = segment.reshape(blocks, GROUP)
    seg_before = jnp.concatenate([jnp.full((1,), -1, dtype=jnp.int32), seg_blocks[:-1, GROUP - 1]])
    initial = jnp.zeros((head_count, head_size, state_size), F32)
    stepper = jax.checkpoint(block_step)

    def scan_body(carried, block_in):
        return stepper(decay_rates, carried, block_in)

    _, outputs = lax.scan(
        scan_body,
        initial,
        (
            x_heads.reshape(blocks, GROUP, head_count, head_size),
            step_sizes.reshape(blocks, GROUP, head_count),
            b_all.reshape(blocks, GROUP, state_size),
            c_all.reshape(blocks, GROUP, state_size),
            seg_blocks,
            seg_before,
        ),
    )
    return outputs.reshape(seq_len, head_count, head_size)


def ssm_mixer(segment, x_proj, bc_proj, dt_proj, gate_proj, conv_x, conv_bias_x, conv_bc, conv_bias_bc, dt_bias, a_log, skip_d):
    x_conv = jax.nn.silu(causal_conv(x_proj, conv_x, conv_bias_x, segment))
    bc_conv = jax.nn.silu(causal_conv(bc_proj, conv_bc, conv_bias_bc, segment))
    state_size = bc_conv.shape[1] // 2
    step_sizes = jax.nn.softplus(dt_proj + dt_bias[None, :])
    decay_rates = -jnp.exp(a_log)
    seq_len = x_proj.shape[0]
    head_count = dt_proj.shape[1]
    x_heads = x_conv.reshape(seq_len, head_count, -1)
    scanned = scan_ssd(
        x_heads, step_sizes, decay_rates, bc_conv[:, :state_size], bc_conv[:, state_size:], segment
    )
    scanned = scanned + skip_d[None, :, None] * x_heads
    return scanned.reshape(seq_len, -1) * jax.nn.silu(gate_proj)


def dot_nt(left, right):
    return lax.dot_general(left, right, (((1,), (1,)), ((), ())), preferred_element_type=F32)


def dot_tn(left, right):
    return lax.dot_general(left, right, (((0,), (0,)), ((), ())), preferred_element_type=F32)


def per_device(
    hidden_in, seg_ids, pre_gain, proj_gate, proj_x, proj_bc, proj_dt, conv_x, conv_bias_x, conv_bc, conv_bias_bc,
    dt_bias, a_log, skip_d, gate_gain, proj_out, cotangent,
):
    t = lax.axis_index("tensor")
    inner = proj_gate.shape[1]
    heads = proj_dt.shape[1]
    own = lambda v, n: lax.dynamic_slice_in_dim(v, t * n, n, v.ndim - 1)
    gain_dev = own(gate_gain, inner)
    hidden = hidden_in.astype(F32)
    inv_rms = lax.rsqrt(jnp.mean(hidden * hidden, axis=1) + EPS)
    normed_own = (hidden * inv_rms[:, None] * pre_gain[None, :]).astype(BF)
    rows = proj_x.shape[0]
    wa = jnp.concatenate([proj_x, proj_bc, proj_dt, jnp.zeros((rows, 128 - heads), BF)], axis=1)
    wb = jnp.concatenate([proj_gate, proj_out.T], axis=1)
    wa, wb, normed_all, cot_all = gather(wa, wb, normed_own, cotangent)
    wa = wa.reshape(-1, wa.shape[-1])
    wb = wb.reshape(-1, wb.shape[-1])
    normed_all = normed_all.reshape(-1, normed_all.shape[-1])
    cot_all = cot_all.reshape(-1, cot_all.shape[-1])
    w_gate, w_out = wb[:, :inner], wb[:, inner:]
    vals = jnp.dot(normed_all, wa, preferred_element_type=F32)
    x_val, bc_val, dt_val = vals[:, :inner], vals[:, inner : inner + 256], vals[:, inner + 256 : inner + 256 + heads]
    gate_val = jnp.dot(normed_all, w_gate, preferred_element_type=F32)
    gated, mixer_back = jax.vjp(
        functools.partial(ssm_mixer, seg_ids), x_val, bc_val, dt_val, gate_val,
        own(conv_x, inner), own(conv_bias_x, inner), conv_bc, conv_bias_bc, own(dt_bias, heads), own(a_log, heads), own(skip_d, heads),
    )
    grad_normed_out = jnp.dot(cot_all, w_out, preferred_element_type=F32)
    scaled_grad = grad_normed_out * gain_dev[None, :]
    sums = lax.psum(jnp.stack([jnp.sum(gated * gated, axis=1), jnp.sum(scaled_grad * gated, axis=1)]), "tensor")
    inv_scale = lax.rsqrt(sums[0] / INNER + EPS)
    normed_out = (gated * inv_scale[:, None] * gain_dev[None, :]).astype(BF)
    partial_out = dot_nt(normed_out, w_out).astype(BF)
    term_out = dot_tn(cot_all, normed_out)
    grad_gain_dev = jnp.sum(grad_normed_out * gated * inv_scale[:, None], axis=0)
    grad_gated = scaled_grad * inv_scale[:, None] - gated * (inv_scale * inv_scale * inv_scale * sums[1] / INNER)[:, None]
    (grad_x, grad_bc, grad_dt, grad_gate, g_conv_x, g_bias_x, g_conv_bc, g_bias_bc, g_dt_bias, g_a_log, g_skip) = mixer_back(grad_gated)
    low_a = jnp.concatenate([grad_x, grad_bc, grad_dt, jnp.zeros((grad_dt.shape[0], 128 - heads), F32)], axis=1).astype(BF)
    low_gate = grad_gate.astype(BF)
    grad_normed = (dot_nt(low_gate, w_gate) + dot_nt(low_a, wa)).astype(BF)
    term_a = dot_tn(normed_all, low_a).astype(BF)
    term_b = jnp.concatenate([dot_tn(normed_all, low_gate), term_out], axis=1).astype(BF)
    small = jnp.concatenate(
        [g_conv_x.reshape(-1), g_bias_x, grad_gain_dev, g_conv_bc.reshape(-1), g_bias_bc]
        + [jnp.pad(v, (0, 128 - heads)) for v in (g_dt_bias, g_a_log, g_skip)]
    )
    n_small = small.shape[0]
    small = jnp.pad(small, (0, 8192 - n_small)).reshape(64, 128)
    blocks = (4, 4, 2, rows)
    ra, rb, own_out, grad_own, smalls = reduce_all(
        term_a.reshape(blocks + term_a.shape[1:]), term_b.reshape(blocks + term_b.shape[1:]),
        partial_out.reshape(4, 256, -1), grad_normed.reshape(4, 256, -1), small,
    )
    output = (hidden + own_out).astype(BF)
    scaled = grad_own * pre_gain[None, :]
    proj = jnp.mean(scaled * hidden, axis=1)
    grad_hidden = cotangent.astype(F32) + scaled * inv_rms[:, None] - hidden * (inv_rms * inv_rms * inv_rms * proj)[:, None]
    part_pre = jnp.sum(grad_own * hidden * inv_rms[:, None], axis=0)
    d_pre = lax.psum(part_pre, ("dp", "tensor"))
    smalls = smalls.reshape(4, 8192)
    d_bc = lax.psum(ra[:, inner : inner + 256], "tensor")
    spread = lambda lo, n, k: smalls[:, lo : lo + n * k].reshape(4, k, n).transpose(1, 0, 2).reshape(k, 4 * n)
    d_conv_x = spread(0, inner, 4)
    at = 4 * inner
    d_bias_x = spread(at, inner, 1)[0]
    d_gain = spread(at + inner, inner, 1)[0]
    at = at + 2 * inner
    bc_sums = jnp.sum(smalls[:, at : at + 5 * 256], axis=0)
    at = at + 5 * 256
    d_dt_bias, d_a_log, d_skip = (spread(at + 128 * i, heads, 1)[0] for i in range(3))
    return (
        output, grad_hidden, d_pre, rb[:, :inner], ra[:, :inner], d_bc, ra[:, inner + 256 : inner + 256 + heads],
        d_conv_x, d_bias_x, bc_sums[:1024].reshape(4, 256), bc_sums[1024:], d_dt_bias, d_a_log, d_skip, d_gain,
        rb[:, inner:].T,
    )


def solution(mesh):
    tok = P(("dp", "tensor"), None)
    mat = P("dp", "tensor")
    in_specs = (tok, P("dp"), P(), mat, mat, P("dp", None), mat) + (P(),) * 8 + (P("tensor", "dp"), tok)
    out_specs = (tok, tok, P(), mat, mat, P("dp", None), mat) + (P(),) * 8 + (P("tensor", "dp"),)
    return jax.shard_map(per_device, mesh=mesh, in_specs=in_specs, out_specs=out_specs, check_vma=False)
```

```python
import functools

import jax
import jax.numpy as jnp
from jax import lax
from jax.experimental import pallas as pl
from jax.experimental.pallas import tpu as pltpu
from jax.sharding import PartitionSpec as P

MESH = pl.DeviceIdType.MESH
F32 = jnp.float32
BF = jnp.bfloat16


def place():
    dp = lax.axis_index("dp")
    t = lax.axis_index("tensor")
    return dp // 8, (dp // 2) % 4, dp % 2, t


def dev(x, z, yh, t):
    return ((x * 4 + z) * 2 + yh, t)


def ag_kernel(ten, wa, wb, h, c, oa, ob, oh, oc, lsem, wsend, wrecv, tsend, trecv):
    x, z, yh, t = place()
    yl = t // 2; co = t % 2
    m4 = lambda v: (v + 8) % 4
    def nb(axis, d):
        if axis == "x": return dev(m4(x + d), z, yh, t)
        return dev(x, m4(z + d), yh, t)
    ypeer = dev(x, z, 1 - yh, t)
    tc_ = dev(x, z, yh, yl * 2 + (1 - co))
    ty = dev(x, z, yh, (1 - yl) * 2 + co)
    bar = pltpu.get_barrier_semaphore()
    peers = [ypeer, nb("x", 1), nb("x", -1), nb("z", 1), nb("z", -1), tc_, ty]
    for p in peers:
        pl.semaphore_signal(bar, inc=1, device_id=p, device_id_type=MESH)
    pl.semaphore_wait(bar, len(peers))
    sends = []
    def rc(src, dst, ss, rs, to):
        cp = pltpu.make_async_remote_copy(src_ref=src, dst_ref=dst, send_sem=ss, recv_sem=rs, device_id=to, device_id_type=MESH)
        cp.start(); sends.append(cp); return cp
    halves = ((wa, oa, "x", "z"), (wb, ob, "z", "x"))
    def blk(o, r1, d1, d2, y=None, yn=None):
        ix, iz = (m4(x + d1), m4(z + d2)) if r1 == "x" else (m4(x + d2), m4(z + d1))
        return o.at[ix, iz] if y is None else o.at[ix, iz, y]
    sem = [0, 0]
    def wc(i, src, dst, to):
        k = sem[i]; sem[i] += 1
        return rc(src, dst, wsend.at[i, k], wrecv.at[i, k], to)
    loc = []
    for i, (w, o, *_) in enumerate(halves):
        cp = pltpu.make_async_copy(w, o.at[x, z, yh], lsem.at[i]); cp.start(); loc.append(cp)
    for i, (s, o) in enumerate(((h, oh), (c, oc))):
        cp = pltpu.make_async_copy(s, o.at[t], lsem.at[2 + i]); cp.start(); loc.append(cp)
    yc = []; a0 = []; b0 = []
    for i, (w, o, r1, r2) in enumerate(halves):
        yc.append(wc(i, w, o.at[x, z, yh], ypeer))
    for i, (w, o, r1, r2) in enumerate(halves):
        me = o.at[x, z, yh]
        a0.append([wc(i, w, me, nb(r1, d)) for d in (1, -1)])
    for i, (w, o, r1, r2) in enumerate(halves):
        me = o.at[x, z, yh]
        b0.append([wc(i, w, me, nb(r2, d)) for d in (1, -1)])
    a1 = []; b1 = []
    for i, (w, o, r1, r2) in enumerate(halves):
        yc[i].wait_recv()
        pe = o.at[x, z, 1 - yh]
        a1.append([wc(i, pe, pe, nb(r1, d)) for d in (1, -1)])
    if ten:
        tc1 = []
        for i, (s, o) in enumerate(((h, oh), (c, oc))):
            a = rc(s, o.at[t], tsend.at[i, 0], trecv.at[i, 0], ty)
            b = rc(s, o.at[t], tsend.at[i, 1], trecv.at[i, 1], tc_)
            tc1.append((a, b))
    for i, (w, o, r1, r2) in enumerate(halves):
        pe = o.at[x, z, 1 - yh]
        b1.append([wc(i, pe, pe, nb(r2, d)) for d in (1, -1)])
    a2 = []; b2 = []
    for i, (w, o, r1, r2) in enumerate(halves):
        for k in (0, 1):
            a0[i][k].wait_recv(); a1[i][k].wait_recv()
        l_ = blk(o, r1, -1, 0, 0); r_ = blk(o, r1, 1, 0, 1)
        a2.append((wc(i, l_, l_, nb(r1, 1)), wc(i, r_, r_, nb(r1, -1))))
    for i, (w, o, r1, r2) in enumerate(halves):
        bb = []
        for d1 in (-1, 1):
            bl = blk(o, r1, d1, 0)
            bb.append([wc(i, bl, bl, nb(r2, d)) for d in (1, -1)])
        b2.append(bb)
    b3 = []
    for i, (w, o, r1, r2) in enumerate(halves):
        a2[i][0].wait_recv(); a2[i][1].wait_recv()
        bl = blk(o, r1, 2, 0)
        b3.append([wc(i, bl, bl, nb(r2, d)) for d in (1, -1)])
    if ten:
        tc2 = []
        for i, (s, o) in enumerate(((h, oh), (c, oc))):
            tc1[i][0].wait_recv()
            bk = o.at[(1 - yl) * 2 + co]
            tc2.append(rc(bk, bk, tsend.at[i, 2], trecv.at[i, 2], tc_))
    last = []
    def fw(i, o, r1, d1):
        l_ = blk(o, r1, d1, -1, 0); r_ = blk(o, r1, d1, 1, 1); n = halves[i][3]
        last.append(wc(i, l_, l_, nb(n, 1))); last.append(wc(i, r_, r_, nb(n, -1)))
    for i, (w, o, r1, r2) in enumerate(halves):
        for k in (0, 1):
            b0[i][k].wait_recv(); b1[i][k].wait_recv()
        fw(i, o, r1, 0)
    for i, (w, o, r1, r2) in enumerate(halves):
        for j, d1 in enumerate((-1, 1)):
            for k in (0, 1): b2[i][j][k].wait_recv()
            fw(i, o, r1, d1)
    for i, (w, o, r1, r2) in enumerate(halves):
        for k in (0, 1): b3[i][k].wait_recv()
        fw(i, o, r1, 2)
    for l in loc: l.wait()
    if ten:
        for i in range(2):
            tc1[i][1].wait_recv(); tc2[i].wait_recv()
    for cp in last: cp.wait_recv()
    for cp in sends: cp.wait_send()

def gather(wa, wb, h, c, ten=True, vm=False):
    anyspec = pl.BlockSpec(memory_space=pl.ANY)
    ospec = pl.BlockSpec(memory_space=pltpu.VMEM) if vm else anyspec
    ca, cb = wa.shape[1], wb.shape[1]
    outs = (jax.ShapeDtypeStruct((4, 4, 2, 48, ca), jnp.bfloat16), jax.ShapeDtypeStruct((4, 4, 2, 48, cb), jnp.bfloat16),
            jax.ShapeDtypeStruct((4, 256, 1536), jnp.bfloat16), jax.ShapeDtypeStruct((4, 256, 1536), jnp.bfloat16))
    return pl.pallas_call(functools.partial(ag_kernel, ten), out_shape=outs, in_specs=[anyspec] * 4, out_specs=[ospec] * 4,
        scratch_shapes=[pltpu.SemaphoreType.DMA((4,)), pltpu.SemaphoreType.DMA((2, 25)), pltpu.SemaphoreType.DMA((2, 25)),
                        pltpu.SemaphoreType.DMA((2, 3)), pltpu.SemaphoreType.DMA((2, 3))],
        compiler_params=pltpu.CompilerParams(collective_id=0, has_side_effects=True, vmem_limit_bytes=60*2**20), name="gather_all")(wa, wb, h, c)


def rs_kernel(bc0, ga, gb, po, pn, sv, oa, ob, oo, on, osv,
              va, vb, vo, vn, r1a, r1b, r2a, r2b, ha, hb, q1a, q1b, q2a, q2b, ka, kb, ya, yb,
              co_buf, cy_buf, cs_buf, sacc, sx, sz, sy, st, bct,
              lsem, wsend, wrecv, tsend, trecv, ssend, srecv, bsend, brecv):
    x, z, yh, t = place()
    yl = t // 2; co = t % 2
    m4 = lambda v: (v + 8) % 4
    def nb(axis, d):
        if axis == "x": return dev(m4(x + d), z, yh, t)
        return dev(x, m4(z + d), yh, t)
    ypeer = dev(x, z, 1 - yh, t)
    tcore = dev(x, z, yh, yl * 2 + (1 - co))
    tyl = dev(x, z, yh, (1 - yl) * 2 + co)
    tdiag = dev(x, z, yh, (1 - yl) * 2 + 1 - co)
    bar = pltpu.get_barrier_semaphore()
    peers = [ypeer, tcore, tyl, tdiag] + [nb(a, d) for a in "xz" for d in (1, 2, 3)]
    for p in peers:
        pl.semaphore_signal(bar, inc=1, device_id=p, device_id_type=MESH)
    loads = []
    for i, (s, d) in enumerate(((ga, va), (gb, vb), (po, vo), (pn, vn))):
        cp = pltpu.make_async_copy(s, d, lsem.at[i]); cp.start(); loads.append(cp)
    pl.semaphore_wait(bar, len(peers))
    sends = []
    def rc(src, dst, ss, rs, to):
        cp = pltpu.make_async_remote_copy(src_ref=src, dst_ref=dst, send_sem=ss, recv_sem=rs, device_id=to, device_id_type=MESH)
        cp.start(); sends.append(cp); return cp
    pos = {"x": x, "z": z}
    halves = ((va, "z", "x", r1a, r2a, ha, q1a, q2a, ka, ya, oa), (vb, "x", "z", r1b, r2b, hb, q1b, q2b, kb, yb, ob))
    def b1(v, a1, d, k=None):
        p = m4(pos[a1] + d)
        if a1 == "z": return v.at[:, p] if k is None else v.at[pl.ds(2 * k, 2), p]
        return v.at[p] if k is None else v.at[p, pl.ds(2 * k, 2)]
    small = []
    for d in (1, 2, 3):
        small.append(rc(sv, sx.at[d - 1], ssend.at[d - 1], srecv.at[d - 1], nb("x", d)))
    for l in loads[:2]: l.wait()
    s1 = []
    for i, (v, a1, a2, r1, r2, *_) in enumerate(halves):
        s1.append((rc(b1(v, a1, 2, 0), r1.at[0], wsend.at[i, 0], wrecv.at[i, 0], nb(a1, 1)),
                   rc(b1(v, a1, 2, 1), r1.at[1], wsend.at[i, 1], wrecv.at[i, 1], nb(a1, -1))))
    s1b = []
    for i, (v, a1, a2, r1, r2, *_) in enumerate(halves):
        s1b.append((rc(b1(v, a1, 1, 1), r2.at[0, pl.ds(2, 2)], wsend.at[i, 2], wrecv.at[i, 2], nb(a1, 1)),
                    rc(b1(v, a1, -1, 0), r2.at[1, pl.ds(0, 2)], wsend.at[i, 3], wrecv.at[i, 3], nb(a1, -1))))
    tr = []
    for l in loads[2:]: l.wait()
    for i, v in enumerate((vo, vn)):
        a = rc(v.at[(1 - yl) * 2 + 1 - co], co_buf.at[i, 0], tsend.at[i, 0], trecv.at[i, 0], tcore)
        b = rc(v.at[yl * 2 + 1 - co], co_buf.at[i, 1], tsend.at[i, 1], trecv.at[i, 1], tcore)
        tr.append((a, b))
    for i, v in enumerate((vo, vn)):
        tr[i][0].wait_recv()
        def addc(j, _, i=i, v=v):
            rows = pl.ds(pl.multiple_of(j * 32, 32), 32)
            cs_buf[i, rows] = (v[(1 - yl) * 2 + co, rows].astype(F32) + co_buf[i, 0, rows].astype(F32)).astype(BF)
            return 0
        lax.fori_loop(0, 8, addc, 0)
        tr[i] = tr[i] + (rc(cs_buf.at[i], cy_buf.at[i], tsend.at[i, 2], trecv.at[i, 2], tyl),)
    for s in small: s.wait_recv()
    sacc[0] = sv[...] + sx[0] + sx[1] + sx[2]
    small = [rc(sacc.at[0], sz.at[d - 1], ssend.at[2 + d], srecv.at[2 + d], nb("z", d)) for d in (1, 2, 3)]
    s1c = []
    for i, (v, a1, a2, r1, r2, *_) in enumerate(halves):
        for side, dd, k in ((0, 1, 0), (1, -1, 1)):
            s1[i][side].wait_recv()
            p = m4(pos[a1] + dd)
            def add1(j, _, v=v, a1=a1, r1=r1, side=side, p=p, k=k):
                e = j // 2 ; y = j % 2
                if a1 == "z":
                    v[2 * k + e, p, y] = (v[2 * k + e, p, y].astype(F32) + r1[side, e, y].astype(F32)).astype(BF)
                else:
                    v[p, 2 * k + e, y] = (v[p, 2 * k + e, y].astype(F32) + r1[side, e, y].astype(F32)).astype(BF)
                return 0
            lax.fori_loop(0, 4, add1, 0)
            s1c.append(rc(b1(v, a1, dd, k), r2.at[side, pl.ds(2 * k, 2)], wsend.at[i, 4 + side], wrecv.at[i, 4 + side], nb(a1, dd)))
    for s in small: s.wait_recv()
    sacc[1] = sacc[0] + sz[0] + sz[1] + sz[2]
    small = [rc(sacc.at[1], sy, ssend.at[6], srecv.at[6], ypeer)]
    s2 = []
    for i, (v, a1, a2, r1, r2, h, q1, q2, kk, yy, oo_) in enumerate(halves):
        s1b[i][0].wait_recv(); s1b[i][1].wait_recv()
        s1c[2 * i].wait_recv(); s1c[2 * i + 1].wait_recv()
        p = pos[a1]
        def add2(j, _, v=v, a1=a1, r2=r2, h=h, p=p):
            e = j // 2; y = j % 2
            own = v[e, p, y] if a1 == "z" else v[p, e, y]
            h[e, y] = (own.astype(F32) + r2[0, e, y].astype(F32) + r2[1, e, y].astype(F32)).astype(BF)
            return 0
        lax.fori_loop(0, 8, add2, 0)
        q = pos[a2]
        s2.append((rc(h.at[m4(q + 2), 0], q1.at[0], wsend.at[i, 6], wrecv.at[i, 6], nb(a2, 1)),
                   rc(h.at[m4(q + 2), 1], q1.at[1], wsend.at[i, 7], wrecv.at[i, 7], nb(a2, -1)),
                   rc(h.at[m4(q + 1), 1], q2.at[0, 1], wsend.at[i, 8], wrecv.at[i, 8], nb(a2, 1)),
                   rc(h.at[m4(q - 1), 0], q2.at[1, 0], wsend.at[i, 9], wrecv.at[i, 9], nb(a2, -1))))
    for s in small: s.wait_recv()
    sacc[2] = sacc[1] + sy[...]
    small = [rc(sacc.at[2], st.at[j], ssend.at[7 + j], srecv.at[7 + j], d_) for j, d_ in enumerate((tcore, tyl, tdiag))]
    s2c = []
    for i, (v, a1, a2, r1, r2, h, q1, q2, kk, yy, oo_) in enumerate(halves):
        q = pos[a2]
        for side, dd in ((0, 1), (1, -1)):
            s2[i][side].wait_recv()
            pp = m4(q + dd)
            h[pp, side] = (h[pp, side].astype(F32) + q1[side].astype(F32)).astype(BF)
            s2c.append(rc(h.at[pp, side], q2.at[side, side], wsend.at[i, 10 + side], wrecv.at[i, 10 + side], nb(a2, dd)))
    s3 = []
    for i, (v, a1, a2, r1, r2, h, q1, q2, kk, yy, oo_) in enumerate(halves):
        q = pos[a2]
        s2[i][2].wait_recv(); s2[i][3].wait_recv()
        s2c[2 * i].wait_recv(); s2c[2 * i + 1].wait_recv()
        kk[...] = (h[q, 1 - yh].astype(F32) + q2[0, 1 - yh].astype(F32) + q2[1, 1 - yh].astype(F32)).astype(BF)
        s3.append(rc(kk, yy, wsend.at[i, 12], wrecv.at[i, 12], ypeer))
    for i, (v, o) in enumerate(((vo, oo), (vn, on))):
        tr[i][1].wait_recv(); tr[i][2].wait_recv()
        def addf(j, _, i=i, v=v, o=o):
            rows = pl.ds(pl.multiple_of(j * 32, 32), 32)
            o[rows] = v[t, rows].astype(F32) + co_buf[i, 1, rows].astype(F32) + cy_buf[i, rows].astype(F32)
            return 0
        lax.fori_loop(0, 8, addf, 0)
    tens = []
    for i, (v, a1, a2, r1, r2, h, q1, q2, kk, yy, o) in enumerate(halves):
        q = pos[a2]
        s3[i].wait_recv()
        o[...] = h[q, yh].astype(F32) + q2[0, yh].astype(F32) + q2[1, yh].astype(F32) + yy[...].astype(F32)
        if i == 0:
            bct[3] = o[:, bc0 : bc0 + 256]
            tens = [rc(bct.at[3], bct.at[j], bsend.at[j], brecv.at[j], d_) for j, d_ in enumerate((tcore, tyl, tdiag))]
    for cp in tens: cp.wait_recv()
    oa[:, bc0 : bc0 + 256] = bct[3] + bct[0] + bct[1] + bct[2]
    for s in small: s.wait_recv()
    osv[t] = sacc[2]
    osv[yl * 2 + 1 - co] = st[0]
    osv[(1 - yl) * 2 + co] = st[1]
    osv[(1 - yl) * 2 + 1 - co] = st[2]
    for cp in sends: cp.wait_send()

def reduce_all(bc0, ga, gb, po, pn, sv):
    anys = pl.BlockSpec(memory_space=pl.ANY); vm = pl.BlockSpec(memory_space=pltpu.VMEM)
    ca, cb = ga.shape[-1], gb.shape[-1]; R = sv.shape[0]
    outs = (jax.ShapeDtypeStruct((48, ca), F32), jax.ShapeDtypeStruct((48, cb), F32), jax.ShapeDtypeStruct((256, 1536), F32),
            jax.ShapeDtypeStruct((256, 1536), F32), jax.ShapeDtypeStruct((4, R, 128), F32))
    D = pltpu.SemaphoreType.DMA
    V = lambda *s, d=BF: pltpu.VMEM(s, d)
    scratch = [V(4, 4, 2, 48, ca), V(4, 4, 2, 48, cb), V(4, 256, 1536), V(4, 256, 1536),
               V(2, 2, 2, 48, ca), V(2, 2, 2, 48, cb), V(2, 4, 2, 48, ca), V(2, 4, 2, 48, cb),
               V(4, 2, 48, ca), V(4, 2, 48, cb), V(2, 48, ca), V(2, 48, cb), V(2, 2, 48, ca), V(2, 2, 48, cb),
               V(48, ca), V(48, cb), V(48, ca), V(48, cb),
               V(2, 2, 256, 1536), V(2, 256, 1536), V(2, 256, 1536),
               V(3, R, 128, d=F32), V(3, R, 128, d=F32), V(3, R, 128, d=F32), V(R, 128, d=F32), V(3, R, 128, d=F32), V(4, 48, 256, d=F32),
               D((4,)), D((2, 13)), D((2, 13)), D((2, 3)), D((2, 3)), D((10,)), D((10,)), D((3,)), D((3,))]
    return pl.pallas_call(functools.partial(rs_kernel, bc0), out_shape=outs, in_specs=[anys] * 4 + [vm], out_specs=[vm] * 5, scratch_shapes=scratch,
        compiler_params=pltpu.CompilerParams(collective_id=1, has_side_effects=True, vmem_limit_bytes=60 * 2**20), name="reduce_all")(ga, gb, po, pn, sv)


Q = 256
LOG2E = 1.4426950408889634
NEG = -1e30


def dnn(a, b):
    return jnp.dot(a, b, preferred_element_type=F32)


def dnt(a, b):
    return lax.dot_general(a, b, (((1,), (1,)), ((), ())), preferred_element_type=F32)


def split3(v):
    hi = v.astype(BF)
    r = v - hi.astype(F32)
    mid = r.astype(BF)
    lo = (r - mid.astype(F32)).astype(BF)
    return hi, mid, lo


def spread3(v, mat):
    hi, mid, lo = split3(v)
    return dnn(jnp.concatenate([hi, mid, lo], axis=1), jnp.concatenate([mat, mat, mat], axis=0))


def tri_times(mat, v):
    hi, mid, lo = split3(v)
    out = dnn(mat, jnp.concatenate([hi, mid, lo], axis=1))
    w = v.shape[1]
    return out[:, :w] + out[:, w : 2 * w] + out[:, 2 * w :]


def ii(shape, dim):
    return lax.broadcasted_iota(jnp.int32, shape, dim)


def sigmoid(v):
    return 1.0 / (1.0 + jnp.exp2(v * -LOG2E))


def softplus(v):
    e = jnp.exp2(jnp.abs(v) * -LOG2E)
    u = 1.0 + e
    log1p = jnp.where(u == 1.0, e, jnp.log(u) * (e / jnp.where(u == 1.0, 1.0, u - 1.0)))
    return jnp.maximum(v, 0.0) + log1p


def conv_terms(ext, match, taps):
    n = ext.shape[0] - 8
    shifted = [ext[8:]] + [jnp.where(match[k], ext[8 - k : 8 + n - k], 0.0) for k in (1, 2, 3)]
    pre = taps[4:5] + sum(taps[3 - k : 4 - k] * shifted[k] for k in range(4))
    return pre, shifted


def with_earlier(ref, r0, lanes):
    prev = ref[pl.ds(pl.multiple_of(jnp.maximum(r0 - 8, 0), 8), 8), lanes]
    return jnp.concatenate([prev, ref[pl.ds(r0, Q), lanes]], axis=0)


def match_rows(segc, r0):
    prev = segc[pl.ds(pl.multiple_of(jnp.maximum(r0 - 8, 0), 8), 8), :]
    prev = jnp.where(r0 > 0, prev, -1.0)
    cur = segc[pl.ds(r0, Q), :]
    ext = jnp.concatenate([prev, cur], axis=0)
    return [None] + [ext[8 - k : 8 + Q - k] == cur for k in (1, 2, 3)]


def block_setup(c, nv, vals, segc, segr, cbc, hp, bt_ref, b_ref, c_ref, ct_ref, qk_ref, bias_ref, cum_ref, cumt_ref, step_ref, tail_ref, keep_ref, ex_ref, keep_out):
    r0 = pl.multiple_of(c * Q, Q)
    match = match_rows(segc, r0)
    m2 = [None] + [jnp.concatenate([m, m], axis=1) for m in match[1:]]
    ext = with_earlier(vals, r0, pl.ds(nv, 256))
    pre, shifted = conv_terms(ext, m2, cbc[...])
    bc = pre * sigmoid(pre)
    bb = bc[:, :128].astype(BF)
    cc = bc[:, 128:].astype(BF)
    b_ref[...] = bb
    c_ref[...] = cc
    bt_ref[...] = bc[:, :128].T.astype(BF)
    if ct_ref is not None:
        ct_ref[...] = bc[:, 128:].T.astype(BF)
    qk_ref[...] = dnt(cc, bb)
    seg = segc[pl.ds(r0, Q), :]
    segs = segr[0:1, pl.ds(r0, Q)]
    tt, ss = ii((Q, Q), 0), ii((Q, Q), 1)
    allowed = (tt >= ss) & (jnp.concatenate([seg, seg], axis=1) == segs)
    bias_ref[...] = jnp.where(allowed, 0.0, NEG)
    raw = vals[pl.ds(r0, Q), pl.ds(nv + 256, 128)] + hp[0:1]
    step = softplus(raw)
    tri = (tt >= ss).astype(BF)
    cum = tri_times(tri, step * (hp[1:2] * LOG2E))
    cumt = cum.T
    for h in range(nv // 64):
        cumt_ref[h] = jnp.broadcast_to(cumt[h : h + 1], (8, Q))
    exm = ex_ref[...]
    cum_ref[...] = spread3(cum, exm)
    e64 = (ii((128, nv), 0) == ii((128, nv), 1) // 64).astype(BF)
    step_ref[...] = spread3(step, e64)
    prev_seg = jnp.where(c > 0, segc[pl.ds(pl.multiple_of(jnp.maximum(r0 - 8, 0), 8), 8), :][7:8], -1.0)
    last_seg = seg[Q - 1 :]
    cum_last = cum[Q - 1 :]
    carry = (seg == prev_seg).astype(F32)
    tailm = (seg == last_seg).astype(F32)
    tail = jnp.exp2(cum_last - cum) * tailm
    tail_ref[...] = spread3(tail, e64)
    keep = jnp.exp2(cum_last) * (last_seg == prev_seg).astype(F32)
    keep_ref[...] = spread3(jnp.broadcast_to(keep, (8, 128)), e64)
    keep_out[...] = spread3(jnp.exp2(cum) * carry, e64)
    return match, pre, shifted, raw, step


def decay(cum_ref, cumt_ref, bias_ref, h, rows, cols):
    col = cum_ref[rows, pl.ds(pl.multiple_of(h * 128, 128), 128)]
    row = cumt_ref[h, 0:1, cols]
    return jnp.exp2(col - row + bias_ref[rows, cols])


def fwd_scratch(nv):
    V = lambda s, d=F32: pltpu.VMEM(s, d)
    nh = nv // 64
    return dict(
        bt=V((128, Q), BF), b=V((Q, 128), BF), c=V((Q, 128), BF), qk=V((Q, Q)), bias=V((Q, Q)), cum=V((Q, nh * 128)), cumt=V((nh, 8, Q)),
        step=V((Q, nv)), tail=V((Q, nv)), keep=V((8, nv)), ecum=V((Q, nv)), ex=V((128, nh * 128), BF), state=V((128, nv)), m=V((2, Q, Q), BF),
    )


def ssd_forward(nv, vals, segc, segr, cx, cbc, hp, ssd, states, s):
    nh = nv // 64
    s["ex"][...] = (ii((128, nh * 128), 0) == ii((128, nh * 128), 1) // 128).astype(BF)
    s["state"][...] = jnp.zeros_like(s["state"])
    s["m"][...] = jnp.zeros_like(s["m"])

    def block(c, _):
        r0 = pl.multiple_of(c * Q, Q)
        match, *_r = block_setup(c, nv, vals, segc, segr, cbc, hp, s["bt"], s["b"], s["c"], None, s["qk"], s["bias"], s["cum"], s["cumt"], s["step"], s["tail"], s["keep"], s["ex"], s["ecum"])
        states[c] = s["state"][...]

        def pair(j, _):
            lanes = pl.ds(pl.multiple_of(j * 128, 128), 128)
            pre, _sh = conv_terms(with_earlier(vals, r0, lanes), match, cx[:, lanes])
            x = pre * sigmoid(pre)
            u = x * s["step"][:, lanes]
            ub = u.astype(BF)
            st = s["state"][:, lanes]
            y = dnn(s["c"][...], st.astype(BF)) * s["ecum"][:, lanes]
            y = y + cx[5:6, lanes] * x
            for e in range(2):
                for r in range(4):
                    rows = slice(r * 64, r * 64 + 64)
                    for k in range(1 if r < 2 else 2):
                        cols = slice(k * 128, k * 128 + 128)
                        s["m"][e, rows, cols] = (decay(s["cum"], s["cumt"], s["bias"], 2 * j + e, rows, cols) * s["qk"][rows, cols]).astype(BF)
            y0 = dnn(s["m"][0], ub)
            y1 = dnn(s["m"][1], ub)
            ssd[pl.ds(r0, Q), lanes] = y + jnp.where(ii((Q, 128), 1) < 64, y0, y1)
            s["state"][:, lanes] = st * s["keep"][0:1, lanes] + dnn(s["bt"][...], (u * s["tail"][:, lanes]).astype(BF))
            return 0

        lax.fori_loop(0, nv // 128, pair, 0)
        return 0

    lax.fori_loop(0, vals.shape[0] // Q, block, 0)


def bwd_scratch(nv):
    V = lambda s, d=F32: pltpu.VMEM(s, d)
    d = fwd_scratch(nv)
    d.update(ct=V((128, Q), BF), dqk=V((Q, Q)), dstate=V((128, nv)), dcs=V((Q, 128)), dbs=V((Q, 128)), rowg=V((Q, 128)), colg=V((nv // 64, 8, Q)), rs=V((Q, 128)),
             gs=V((Q, 128)), ds=V((Q, 128)), krow=V((8, nv)), halo=V((8, nv)), halobc=V((8, 256)), dm=V((Q, Q)))
    return d


def to_head(v, j):
    red = (ii((128, 128), 1) == 2 * j + ii((128, 128), 0) // 64).astype(BF)
    hi = v.astype(BF)
    lo = (v - hi.astype(F32)).astype(BF)
    return dnn(jnp.concatenate([hi, lo], axis=1), jnp.concatenate([red, red], axis=0))


def later_sum(dpre, halo, match_ext, taps):
    ext = jnp.concatenate([dpre, halo], axis=0)
    n = dpre.shape[0]
    out = taps[3:4] * dpre
    for k in (1, 2, 3):
        out = out + taps[3 - k : 4 - k] * jnp.where(match_ext[k], ext[k : n + k], 0.0)
    return out


def ssd_backward(nv, vals, segc, segr, cx, cbc, hp, dy_ref, states, low, gx, gbc, gh, s):
    nh = nv // 64
    nb = vals.shape[0] // Q
    s["ex"][...] = (ii((128, nh * 128), 0) == ii((128, nh * 128), 1) // 128).astype(BF)
    for n in ("dstate", "halo", "halobc", "colg", "m"):
        s[n][...] = jnp.zeros_like(s[n])
    gx[...] = jnp.zeros_like(gx)
    gbc[...] = jnp.zeros_like(gbc)
    gh[...] = jnp.zeros_like(gh)

    def block(i, _):
        c = nb - 1 - i
        r0 = pl.multiple_of(c * Q, Q)
        match, bc_pre, bc_shifted, raw, step = block_setup(c, nv, vals, segc, segr, cbc, hp, s["bt"], s["b"], s["c"], s["ct"], s["qk"], s["bias"], s["cum"], s["cumt"], s["step"], s["tail"], s["keep"], s["ex"], s["ecum"])
        nxt = segc[pl.ds(pl.multiple_of(jnp.minimum(r0 + Q, segc.shape[0] - 8), 8), 8), :]
        seg = segc[pl.ds(r0, Q), :]
        ext = jnp.concatenate([seg, nxt], axis=0)
        after = [None] + [ext[k : Q + k] == seg for k in (1, 2, 3)]
        for n in ("dqk", "dcs", "dbs", "rowg", "rs", "gs", "ds"):
            s[n][...] = jnp.zeros_like(s[n])

        def pair(j, _):
            lanes = pl.ds(pl.multiple_of(j * 128, 128), 128)
            taps = cx[:, lanes]
            pre, shifted = conv_terms(with_earlier(vals, r0, lanes), match, taps)
            sig = sigmoid(pre)
            x = pre * sig
            stepe = s["step"][:, lanes]
            taile = s["tail"][:, lanes]
            u = x * stepe
            ub = u.astype(BF)
            dy = dy_ref[pl.ds(r0, Q), lanes].astype(F32)
            dyb = dy.astype(BF)
            dyt = dy.T.astype(BF)
            st = states[c, :, lanes]
            stb = st.astype(BF)
            dst = s["dstate"][:, lanes]
            dstb = dst.astype(BF)
            edy = s["ecum"][:, lanes] * dy
            edyb = edy.astype(BF)
            s["rs"][...] += to_head(edy * dnn(s["c"][...], stb), j)
            s["dcs"][...] += dnt(edyb, stb)
            tu = taile * u
            v = dnn(s["b"][...], dstb)
            s["dbs"][...] += dnt(tu.astype(BF), dstb)
            s["gs"][...] += to_head(tu * v, j)
            keep = s["keep"][0:1, lanes]
            s["krow"][:, lanes] = jnp.broadcast_to(keep * jnp.sum(st * dst, axis=0, keepdims=True), (8, 128))
            s["dstate"][:, lanes] = keep * dst + dnn(s["ct"][...], edyb)
            lane = ii((Q, 128), 1)
            parts = []
            for e in range(2):
                h = 2 * j + e
                mine = (lane < 64) if e == 0 else (lane >= 64)
                s["dm"][...] = dnt(jnp.where(mine, dy, 0.0).astype(BF), ub)
                colsum = [jnp.zeros((1, 128), F32), jnp.zeros((1, 128), F32)]
                for r in range(4):
                    rows = slice(r * 64, r * 64 + 64)
                    rowsum = jnp.zeros((64, 128), F32)
                    for k in range(1 if r < 2 else 2):
                        cols = slice(k * 128, k * 128 + 128)
                        dec = decay(s["cum"], s["cumt"], s["bias"], h, rows, cols)
                        qk = s["qk"][rows, cols]
                        p = s["dm"][rows, cols] * dec
                        s["dqk"][rows, cols] += p
                        g = p * qk
                        rowsum = rowsum + g
                        colsum[k] = colsum[k] + jnp.sum(g, axis=0, keepdims=True)
                        s["m"][e, rows, cols] = (dec * qk).astype(BF)
                    tot = jnp.sum(rowsum, axis=1, keepdims=True)
                    s["rowg"][rows] += jnp.where(ii((64, 128), 1) == h, tot, 0.0)
                s["colg"][h] = jnp.broadcast_to(jnp.concatenate(colsum, axis=1), (8, Q))
                parts.append(dnn(dyt[e * 64 : e * 64 + 64], s["m"][e]))
            du = jnp.concatenate(parts, axis=0).T + taile * v
            s["ds"][...] += to_head(du * x, j)
            skip = taps[5:6]
            dx = du * stepe + skip * dy
            dpre = dx * (sig + x * (1.0 - sig))
            low[pl.ds(r0, Q), lanes] = later_sum(dpre, s["halo"][:, lanes], after, taps).astype(BF)
            s["halo"][:, lanes] = dpre[:8]
            gx[:, lanes] += jnp.concatenate(
                [jnp.sum(dpre * shifted[3 - k], axis=0, keepdims=True) for k in range(4)]
                + [jnp.sum(dpre, axis=0, keepdims=True), jnp.sum(dy * x, axis=0, keepdims=True), jnp.zeros((2, 128), F32)], axis=0)
            return 0

        lax.fori_loop(0, nv // 128, pair, 0)
        tt, ss = ii((Q, Q), 0), ii((Q, Q), 1)
        e64t = (ii((nv, 128), 0) // 64 == ii((nv, 128), 1)).astype(BF)
        kh, km, kl = split3(s["krow"][...])
        kterm = dnn(kh, e64t) + dnn(km, e64t) + dnn(kl, e64t)
        colg = jnp.concatenate([s["colg"][h, 0:1] for h in range(nh)] + [jnp.zeros((128 - nh, Q), F32)], axis=0)
        dcum = s["rowg"][...] - colg.T + s["rs"][...]
        da = tri_times((ss >= tt).astype(BF), dcum) + tri_times((ss < tt).astype(BF), s["gs"][...]) + kterm[0:1]
        rate = hp[1:2]
        dstep = s["ds"][...] + rate * da
        draw = dstep * sigmoid(raw)
        draw = jnp.where(ii((Q, 128), 1) < nh, draw, 0.0)
        low[pl.ds(r0, Q), pl.ds(nv + 256, 128)] = draw.astype(BF)
        gh[...] += jnp.concatenate([jnp.sum(draw, axis=0, keepdims=True), jnp.sum(da * step, axis=0, keepdims=True) * rate, jnp.zeros((6, 128), F32)], axis=0)
        dqk = s["dqk"][...]
        dc = dnn(dqk.astype(BF), s["b"][...]) + s["dcs"][...]
        db = dnn(dqk.T.astype(BF), s["c"][...]) + s["dbs"][...]
        sig = sigmoid(bc_pre)
        dpre = jnp.concatenate([db, dc], axis=1) * (sig + bc_pre * sig * (1.0 - sig))
        after2 = [None] + [jnp.concatenate([m, m], axis=1) for m in after[1:]]
        low[pl.ds(r0, Q), pl.ds(nv, 256)] = later_sum(dpre, s["halobc"][...], after2, cbc[...]).astype(BF)
        s["halobc"][...] = dpre[:8]
        gbc[...] += jnp.concatenate(
            [jnp.sum(dpre * bc_shifted[3 - k], axis=0, keepdims=True) for k in range(4)] + [jnp.sum(dpre, axis=0, keepdims=True), jnp.zeros((3, 256), F32)], axis=0)
        return 0

    lax.fori_loop(0, nb, block, 0)


def run_forward(nv, vals, segc, segr, cx, cbc, hp):
    sc = fwd_scratch(nv)
    names = list(sc)
    rows = vals.shape[0]

    def kernel(vals, segc, segr, cx, cbc, hp, ssd, states, *scr):
        ssd_forward(nv, vals, segc, segr, cx, cbc, hp, ssd, states, dict(zip(names, scr)))

    vm = pl.BlockSpec(memory_space=pltpu.VMEM)
    return pl.pallas_call(
        kernel, out_shape=(jax.ShapeDtypeStruct((rows, nv), F32), jax.ShapeDtypeStruct((rows // Q, 128, nv), F32)),
        in_specs=[vm] * 6, out_specs=[vm] * 2, scratch_shapes=[sc[n] for n in names],
        compiler_params=pltpu.CompilerParams(vmem_limit_bytes=60 * 2**20), name="scan_forward",
    )(vals, segc, segr, cx, cbc, hp)


def run_backward(nv, vals, segc, segr, cx, cbc, hp, dy, states):
    sc = bwd_scratch(nv)
    names = list(sc)
    rows = vals.shape[0]

    def kernel(vals, segc, segr, cx, cbc, hp, dy, states, low, gx, gbc, gh, *scr):
        ssd_backward(nv, vals, segc, segr, cx, cbc, hp, dy, states, low, gx, gbc, gh, dict(zip(names, scr)))

    vm = pl.BlockSpec(memory_space=pltpu.VMEM)
    outs = (jax.ShapeDtypeStruct((rows, nv + 384), BF), jax.ShapeDtypeStruct((8, nv), F32), jax.ShapeDtypeStruct((8, 256), F32), jax.ShapeDtypeStruct((8, 128), F32))
    return pl.pallas_call(
        kernel, out_shape=outs, in_specs=[vm] * 8, out_specs=[vm] * 4, scratch_shapes=[sc[n] for n in names],
        compiler_params=pltpu.CompilerParams(vmem_limit_bytes=60 * 2**20), name="scan_backward",
    )(vals, segc, segr, cx, cbc, hp, dy, states)


INNER = 3072
EPS = 1e-05


def dot_nt(left, right):
    return lax.dot_general(left, right, (((1,), (1,)), ((), ())), preferred_element_type=F32)


def dot_tn(left, right):
    return lax.dot_general(left, right, (((0,), (0,)), ((), ())), preferred_element_type=F32)


def per_device(
    hidden_in, seg_ids, pre_gain, proj_gate, proj_x, proj_bc, proj_dt, conv_x, conv_bias_x, conv_bc, conv_bias_bc,
    dt_bias, a_log, skip_d, gate_gain, proj_out, cotangent,
):
    t = lax.axis_index("tensor")
    inner = proj_gate.shape[1]
    heads = proj_dt.shape[1]
    own = lambda v, n: lax.dynamic_slice_in_dim(v, t * n, n, v.ndim - 1)
    gain_dev = own(gate_gain, inner)
    hidden = hidden_in.astype(F32)
    inv_rms = lax.rsqrt(jnp.mean(hidden * hidden, axis=1) + EPS)
    normed_own = (hidden * inv_rms[:, None] * pre_gain[None, :]).astype(BF)
    rows = proj_x.shape[0]
    wa = jnp.concatenate([proj_x, proj_bc, proj_dt, jnp.zeros((rows, 128 - heads), BF)], axis=1)
    wb = jnp.concatenate([proj_gate, proj_out.T], axis=1)
    wa, wb, normed_all, cot_all = gather(wa, wb, normed_own, cotangent)
    wa = wa.reshape(-1, wa.shape[-1])
    wb = wb.reshape(-1, wb.shape[-1])
    normed_all = normed_all.reshape(-1, normed_all.shape[-1])
    cot_all = cot_all.reshape(-1, cot_all.shape[-1])
    w_gate, w_out = wb[:, :inner], wb[:, inner:]
    vals = jnp.dot(normed_all, wa, preferred_element_type=F32)
    gate_val = jnp.dot(normed_all, w_gate, preferred_element_type=F32)
    seg = seg_ids.astype(F32)
    segc = jnp.broadcast_to(seg[:, None], (seg.shape[0], 128))
    segr = jnp.broadcast_to(seg[None, :], (8, seg.shape[0]))
    heads_row = lambda v: jnp.pad(own(v, heads), (0, 128 - heads))[None]
    skip_row = jnp.broadcast_to(own(skip_d, heads)[:, None], (heads, 64)).reshape(1, inner)
    cx = jnp.concatenate([own(conv_x, inner), own(conv_bias_x, inner)[None], skip_row, jnp.zeros((2, inner), F32)])
    cbc = jnp.concatenate([conv_bc, conv_bias_bc[None], jnp.zeros((3, 256), F32)])
    hp = jnp.concatenate([heads_row(dt_bias), -jnp.exp(heads_row(a_log)), jnp.zeros((6, 128), F32)])
    ssd, states = run_forward(inner, vals, segc, segr, cx, cbc, hp)
    gate_sig = sigmoid(gate_val)
    silu_gate = gate_val * gate_sig
    gated = ssd * silu_gate
    grad_normed_out = jnp.dot(cot_all, w_out, preferred_element_type=F32)
    scaled_grad = grad_normed_out * gain_dev[None, :]
    sums = lax.psum(jnp.stack([jnp.sum(gated * gated, axis=1), jnp.sum(scaled_grad * gated, axis=1)]), "tensor")
    inv_scale = lax.rsqrt(sums[0] / INNER + EPS)
    normed_out = (gated * inv_scale[:, None] * gain_dev[None, :]).astype(BF)
    partial_out = dot_nt(normed_out, w_out).astype(BF)
    term_out = dot_tn(cot_all, normed_out)
    grad_gain_dev = jnp.sum(grad_normed_out * gated * inv_scale[:, None], axis=0)
    grad_gated = scaled_grad * inv_scale[:, None] - gated * (inv_scale * inv_scale * inv_scale * sums[1] / INNER)[:, None]
    low_a, gx, gbc, gh = run_backward(inner, vals, segc, segr, cx, cbc, hp, grad_gated * silu_gate, states)
    grad_gate = grad_gated * ssd * (gate_sig + silu_gate * (1.0 - gate_sig))
    low_gate = grad_gate.astype(BF)
    grad_normed = dot_nt(low_gate, w_gate) + dot_nt(low_a, wa)
    part_pre = jnp.sum(grad_normed * normed_all.astype(F32), axis=0) / pre_gain
    grad_normed = grad_normed.astype(BF)
    term_a = dot_tn(normed_all, low_a).astype(BF)
    term_b = jnp.concatenate([dot_tn(normed_all, low_gate), term_out], axis=1).astype(BF)
    small = jnp.concatenate([gx[:5].reshape(-1), grad_gain_dev, gx[5], part_pre, gbc[:5].reshape(-1), gh[:2].reshape(-1)])
    small = jnp.pad(small, (0, 9216 - small.shape[0])).reshape(72, 128)
    blocks = (4, 4, 2, rows)
    ra, rb, own_out, grad_own, smalls = reduce_all(
        inner, term_a.reshape(blocks + term_a.shape[1:]), term_b.reshape(blocks + term_b.shape[1:]),
        partial_out.reshape(4, 256, -1), grad_normed.reshape(4, 256, -1), small,
    )
    output = (hidden + own_out).astype(BF)
    scaled = grad_own * pre_gain[None, :]
    proj = jnp.mean(scaled * hidden, axis=1)
    grad_hidden = cotangent.astype(F32) + scaled * inv_rms[:, None] - hidden * (inv_rms * inv_rms * inv_rms * proj)[:, None]
    smalls = smalls.reshape(4, 9216)
    spread = lambda lo, n, k: smalls[:, lo : lo + n * k].reshape(4, k, n).transpose(1, 0, 2).reshape(k, 4 * n)
    x_sums = spread(0, inner, 7)
    at = 7 * inner
    width = pre_gain.shape[0]
    d_skip = x_sums[6].reshape(-1, 64).sum(axis=1)
    both = jnp.sum(smalls[:, at : at + width + 5 * 256], axis=0)
    d_pre = both[:width]
    bc_sums = both[width:]
    at = at + width + 5 * 256
    d_dt_bias, d_a_log = (spread(at + 128 * i, 128, 1)[0].reshape(4, 128)[:, :heads].reshape(-1) for i in range(2))
    return (
        output, grad_hidden, d_pre, rb[:, :inner], ra[:, :inner], ra[:, inner : inner + 256], ra[:, inner + 256 : inner + 256 + heads],
        x_sums[:4], x_sums[4], bc_sums[:1024].reshape(4, 256), bc_sums[1024:], d_dt_bias, d_a_log, d_skip, x_sums[5],
        rb[:, inner:].T,
    )


def solution(mesh):
    tok = P(("dp", "tensor"), None)
    mat = P("dp", "tensor")
    in_specs = (tok, P("dp"), P(), mat, mat, P("dp", None), mat) + (P(),) * 8 + (P("tensor", "dp"), tok)
    out_specs = (tok, tok, P(), mat, mat, P("dp", None), mat) + (P(),) * 8 + (P("tensor", "dp"),)
    return jax.shard_map(per_device, mesh=mesh, in_specs=in_specs, out_specs=out_specs, check_vma=False)
```

```python
import functools

import jax
import jax.numpy as jnp
from jax import lax
from jax.experimental import pallas as pl
from jax.experimental.pallas import tpu as pltpu
from jax.sharding import PartitionSpec as P

MESH = pl.DeviceIdType.MESH
F32 = jnp.float32
BF = jnp.bfloat16


def place():
    dp = lax.axis_index("dp")
    t = lax.axis_index("tensor")
    return dp // 8, (dp // 2) % 4, dp % 2, t


def dev(x, z, yh, t):
    return ((x * 4 + z) * 2 + yh, t)


def m4(v):
    return (v + 8) % 4


def neighbour(axis, d):
    x, z, yh, t = place()
    return dev(m4(x + d), z, yh, t) if axis == "x" else dev(x, m4(z + d), yh, t)


def tensor_peers():
    x, z, yh, t = place()
    yl, co = t // 2, t % 2
    slots = (yl * 2 + 1 - co, (1 - yl) * 2 + co, (1 - yl) * 2 + 1 - co)
    return [dev(x, z, yh, s) for s in slots], slots


def greet(peers):
    bar = pltpu.get_barrier_semaphore()
    for p in peers:
        pl.semaphore_signal(bar, inc=1, device_id=p, device_id_type=MESH)
    pl.semaphore_wait(bar, len(peers))


def send(src, dst, send_sem, recv_sem, to):
    return pltpu.make_async_remote_copy(
        src_ref=src, dst_ref=dst, send_sem=send_sem, recv_sem=recv_sem, device_id=to, device_id_type=MESH
    )


class Gather:
    N = 25

    def __init__(self, own, dst, r1, send_sem, recv_sem):
        x, z, yh, _ = place()
        r2 = "z" if r1 == "x" else "x"
        n = own.shape[0]

        def rows(d1, d2, y=None):
            ix, iz = (m4(x + d1), m4(z + d2)) if r1 == "x" else (m4(x + d2), m4(z + d1))
            first = (ix * 4 + iz) * 2
            if y is None:
                return dst.at[pl.ds(pl.multiple_of(first * n, n), 2 * n)]
            return dst.at[pl.ds(pl.multiple_of((first + y) * n, n), n)]

        self.mine = rows(0, 0, yh)
        self.own = own
        near1, near2 = [neighbour(r1, 1), neighbour(r1, -1)], [neighbour(r2, 1), neighbour(r2, -1)]
        other = rows(0, 0, 1 - yh)
        plan = [(own, self.mine, dev(x, z, 1 - yh, place()[3]))]
        plan += [(own, self.mine, p) for p in near1 + near2]
        plan += [(other, other, p) for p in near1 + near2]
        plan += [(rows(-1, 0, 0),) * 2 + (near1[0],), (rows(1, 0, 1),) * 2 + (near1[1],)]
        for d1 in (-1, 1, 2):
            plan += [(rows(d1, 0),) * 2 + (p,) for p in near2]
        for d1 in (0, -1, 1, 2):
            plan += [(rows(d1, -1, 0),) * 2 + (near2[0],), (rows(d1, 1, 1),) * 2 + (near2[1],)]
        self.plan, self.send_sem, self.recv_sem = plan, send_sem, recv_sem

    def copy(self, k):
        src, dst, to = self.plan[k]
        return send(src, dst, self.send_sem.at[k], self.recv_sem.at[k], to)

    STEPS = (
        ((), (0, 1, 2, 3, 4)),
        ((0,), (5, 6, 7, 8)),
        ((1, 2, 5, 6), (9, 10, 11, 12, 13, 14)),
        ((9, 10), (15, 16)),
        ((3, 4, 7, 8), (17, 18)),
        ((11, 12, 13, 14), (19, 20, 21, 22)),
        ((15, 16), (23, 24)),
        ((17, 18, 19, 20, 21, 22, 23, 24), ()),
    )

    def step(self, k):
        arrive, go = self.STEPS[k]
        for i in arrive:
            self.copy(i).wait_recv()
        for i in go:
            self.copy(i).start()

    def finish(self):
        for k in range(self.N):
            self.copy(k).wait_send()


Q = 256
LOG2E = 1.4426950408889634
NEG = -1e30


def dnn(a, b):
    return jnp.dot(a, b, preferred_element_type=F32)


def dnt(a, b):
    return lax.dot_general(a, b, (((1,), (1,)), ((), ())), preferred_element_type=F32)


def split3(v):
    hi = v.astype(BF)
    r = v - hi.astype(F32)
    mid = r.astype(BF)
    lo = (r - mid.astype(F32)).astype(BF)
    return hi, mid, lo


def spread3(v, mat):
    hi, mid, lo = split3(v)
    return dnn(jnp.concatenate([hi, mid, lo], axis=1), jnp.concatenate([mat, mat, mat], axis=0))


def tri_times(mat, v):
    hi, mid, lo = split3(v)
    out = dnn(mat, jnp.concatenate([hi, mid, lo], axis=1))
    w = v.shape[1]
    return out[:, :w] + out[:, w : 2 * w] + out[:, 2 * w :]


def ii(shape, dim):
    return lax.broadcasted_iota(jnp.int32, shape, dim)


def sigmoid(v):
    return 1.0 / (1.0 + jnp.exp2(v * -LOG2E))


def softplus(v):
    e = jnp.exp2(jnp.abs(v) * -LOG2E)
    u = 1.0 + e
    log1p = jnp.where(u == 1.0, e, jnp.log(u) * (e / jnp.where(u == 1.0, 1.0, u - 1.0)))
    return jnp.maximum(v, 0.0) + log1p


def conv_terms(ext, match, taps):
    n = ext.shape[0] - 8
    shifted = [ext[8:]] + [jnp.where(match[k], ext[8 - k : 8 + n - k], 0.0) for k in (1, 2, 3)]
    pre = taps[4:5] + sum(taps[3 - k : 4 - k] * shifted[k] for k in range(4))
    return pre, shifted


def with_earlier(ref, r0, lanes):
    prev = ref[pl.ds(pl.multiple_of(jnp.maximum(r0 - 8, 0), 8), 8), lanes]
    return jnp.concatenate([prev, ref[pl.ds(r0, Q), lanes]], axis=0)


def match_rows(segc, r0):
    prev = segc[pl.ds(pl.multiple_of(jnp.maximum(r0 - 8, 0), 8), 8), :]
    prev = jnp.where(r0 > 0, prev, -1.0)
    cur = segc[pl.ds(r0, Q), :]
    ext = jnp.concatenate([prev, cur], axis=0)
    return [None] + [ext[8 - k : 8 + Q - k] == cur for k in (1, 2, 3)]


def block_setup(c, nv, vals, segc, segr, cbc, hp, bt_ref, b_ref, c_ref, ct_ref, qk_ref, bias_ref, cum_ref, cumt_ref, step_ref, tail_ref, keep_ref, ex_ref, keep_out):
    r0 = pl.multiple_of(c * Q, Q)
    match = match_rows(segc, r0)
    m2 = [None] + [jnp.concatenate([m, m], axis=1) for m in match[1:]]
    ext = with_earlier(vals, r0, pl.ds(nv, 256))
    pre, shifted = conv_terms(ext, m2, cbc[...])
    bc = pre * sigmoid(pre)
    bb = bc[:, :128].astype(BF)
    cc = bc[:, 128:].astype(BF)
    b_ref[...] = bb
    c_ref[...] = cc
    bt_ref[...] = bc[:, :128].T.astype(BF)
    if ct_ref is not None:
        ct_ref[...] = bc[:, 128:].T.astype(BF)
    qk_ref[...] = dnt(cc, bb)
    seg = segc[pl.ds(r0, Q), :]
    segs = segr[0:1, pl.ds(r0, Q)]
    tt, ss = ii((Q, Q), 0), ii((Q, Q), 1)
    allowed = (tt >= ss) & (jnp.concatenate([seg, seg], axis=1) == segs)
    bias_ref[...] = jnp.where(allowed, 0.0, NEG)
    raw = vals[pl.ds(r0, Q), pl.ds(nv + 256, 128)] + hp[0:1]
    step = softplus(raw)
    tri = (tt >= ss).astype(BF)
    cum = tri_times(tri, step * (hp[1:2] * LOG2E))
    cumt = cum.T
    for h in range(nv // 64):
        cumt_ref[h] = jnp.broadcast_to(cumt[h : h + 1], (8, Q))
    exm = ex_ref[...]
    cum_ref[...] = spread3(cum, exm)
    e64 = (ii((128, nv), 0) == ii((128, nv), 1) // 64).astype(BF)
    step_ref[...] = spread3(step, e64)
    prev_seg = jnp.where(c > 0, segc[pl.ds(pl.multiple_of(jnp.maximum(r0 - 8, 0), 8), 8), :][7:8], -1.0)
    last_seg = seg[Q - 1 :]
    cum_last = cum[Q - 1 :]
    carry = (seg == prev_seg).astype(F32)
    tailm = (seg == last_seg).astype(F32)
    tail = jnp.exp2(cum_last - cum) * tailm
    tail_ref[...] = spread3(tail, e64)
    keep = jnp.exp2(cum_last) * (last_seg == prev_seg).astype(F32)
    keep_ref[...] = spread3(jnp.broadcast_to(keep, (8, 128)), e64)
    keep_out[...] = spread3(jnp.exp2(cum) * carry, e64)
    return match, pre, shifted, raw, step


def decay(cum_ref, cumt_ref, bias_ref, h, rows, cols):
    col = cum_ref[rows, pl.ds(pl.multiple_of(h * 128, 128), 128)]
    row = cumt_ref[h, 0:1, cols]
    return jnp.exp2(col - row + bias_ref[rows, cols])


def fwd_scratch(nv):
    V = lambda s, d=F32: pltpu.VMEM(s, d)
    nh = nv // 64
    return dict(
        bt=V((128, Q), BF), b=V((Q, 128), BF), c=V((Q, 128), BF), qk=V((Q, Q)), bias=V((Q, Q)), cum=V((Q, nh * 128)), cumt=V((nh, 8, Q)),
        step=V((Q, nv)), tail=V((Q, nv)), keep=V((8, nv)), ecum=V((Q, nv)), ex=V((128, nh * 128), BF), state=V((128, nv)), m=V((2, Q, Q), BF),
    )


def ssd_forward(nv, vals, segc, segr, cx, cbc, hp, ssd, states, s, hook=lambda at: None):
    nh = nv // 64
    s["ex"][...] = (ii((128, nh * 128), 0) == ii((128, nh * 128), 1) // 128).astype(BF)
    s["state"][...] = jnp.zeros_like(s["state"])
    s["m"][...] = jnp.zeros_like(s["m"])

    def block(c, _):
        r0 = pl.multiple_of(c * Q, Q)
        match, *_r = block_setup(c, nv, vals, segc, segr, cbc, hp, s["bt"], s["b"], s["c"], None, s["qk"], s["bias"], s["cum"], s["cumt"], s["step"], s["tail"], s["keep"], s["ex"], s["ecum"])
        states[c] = s["state"][...]

        def pair(j, _):
            hook(c * (nv // 128) + j)
            lanes = pl.ds(pl.multiple_of(j * 128, 128), 128)
            pre, _sh = conv_terms(with_earlier(vals, r0, lanes), match, cx[:, lanes])
            x = pre * sigmoid(pre)
            u = x * s["step"][:, lanes]
            ub = u.astype(BF)
            st = s["state"][:, lanes]
            y = dnn(s["c"][...], st.astype(BF)) * s["ecum"][:, lanes]
            y = y + cx[5:6, lanes] * x
            for e in range(2):
                for r in range(4):
                    rows = slice(r * 64, r * 64 + 64)
                    for k in range(1 if r < 2 else 2):
                        cols = slice(k * 128, k * 128 + 128)
                        s["m"][e, rows, cols] = (decay(s["cum"], s["cumt"], s["bias"], 2 * j + e, rows, cols) * s["qk"][rows, cols]).astype(BF)
            y0 = dnn(s["m"][0], ub)
            y1 = dnn(s["m"][1], ub)
            ssd[pl.ds(r0, Q), lanes] = y + jnp.where(ii((Q, 128), 1) < 64, y0, y1)
            s["state"][:, lanes] = st * s["keep"][0:1, lanes] + dnn(s["bt"][...], (u * s["tail"][:, lanes]).astype(BF))
            return 0

        lax.fori_loop(0, nv // 128, pair, 0)
        return 0

    lax.fori_loop(0, vals.shape[0] // Q, block, 0)


def bwd_scratch(nv):
    V = lambda s, d=F32: pltpu.VMEM(s, d)
    d = fwd_scratch(nv)
    d.update(ct=V((128, Q), BF), dqk=V((Q, Q)), dstate=V((128, nv)), dcs=V((Q, 128)), dbs=V((Q, 128)), rowg=V((Q, 128)), colg=V((nv // 64, 8, Q)), rs=V((Q, 128)),
             gs=V((Q, 128)), ds=V((Q, 128)), krow=V((8, nv)), halo=V((8, nv)), halobc=V((8, 256)), dm=V((Q, Q)))
    return d


def to_head(v, j):
    red = (ii((128, 128), 1) == 2 * j + ii((128, 128), 0) // 64).astype(BF)
    hi = v.astype(BF)
    lo = (v - hi.astype(F32)).astype(BF)
    return dnn(jnp.concatenate([hi, lo], axis=1), jnp.concatenate([red, red], axis=0))


def later_sum(dpre, halo, match_ext, taps):
    ext = jnp.concatenate([dpre, halo], axis=0)
    n = dpre.shape[0]
    out = taps[3:4] * dpre
    for k in (1, 2, 3):
        out = out + taps[3 - k : 4 - k] * jnp.where(match_ext[k], ext[k : n + k], 0.0)
    return out


def ssd_backward(nv, vals, segc, segr, cx, cbc, hp, dy_ref, states, low, gx, gbc, gh, s, hook=lambda at: None):
    nh = nv // 64
    nb = vals.shape[0] // Q
    s["ex"][...] = (ii((128, nh * 128), 0) == ii((128, nh * 128), 1) // 128).astype(BF)
    for n in ("dstate", "halo", "halobc", "colg", "m"):
        s[n][...] = jnp.zeros_like(s[n])
    gx[...] = jnp.zeros_like(gx)
    gbc[...] = jnp.zeros_like(gbc)
    gh[...] = jnp.zeros_like(gh)

    def block(i, _):
        c = nb - 1 - i
        r0 = pl.multiple_of(c * Q, Q)
        match, bc_pre, bc_shifted, raw, step = block_setup(c, nv, vals, segc, segr, cbc, hp, s["bt"], s["b"], s["c"], s["ct"], s["qk"], s["bias"], s["cum"], s["cumt"], s["step"], s["tail"], s["keep"], s["ex"], s["ecum"])
        nxt = segc[pl.ds(pl.multiple_of(jnp.minimum(r0 + Q, segc.shape[0] - 8), 8), 8), :]
        seg = segc[pl.ds(r0, Q), :]
        ext = jnp.concatenate([seg, nxt], axis=0)
        after = [None] + [ext[k : Q + k] == seg for k in (1, 2, 3)]
        for n in ("dqk", "dcs", "dbs", "rowg", "rs", "gs", "ds"):
            s[n][...] = jnp.zeros_like(s[n])

        def pair(j, _):
            hook(i * (nv // 128) + j)
            lanes = pl.ds(pl.multiple_of(j * 128, 128), 128)
            taps = cx[:, lanes]
            pre, shifted = conv_terms(with_earlier(vals, r0, lanes), match, taps)
            sig = sigmoid(pre)
            x = pre * sig
            stepe = s["step"][:, lanes]
            taile = s["tail"][:, lanes]
            u = x * stepe
            ub = u.astype(BF)
            dy = dy_ref[pl.ds(r0, Q), lanes].astype(F32)
            dyb = dy.astype(BF)
            dyt = dy.T.astype(BF)
            st = states[c, :, lanes]
            stb = st.astype(BF)
            dst = s["dstate"][:, lanes]
            dstb = dst.astype(BF)
            edy = s["ecum"][:, lanes] * dy
            edyb = edy.astype(BF)
            s["rs"][...] += to_head(edy * dnn(s["c"][...], stb), j)
            s["dcs"][...] += dnt(edyb, stb)
            tu = taile * u
            v = dnn(s["b"][...], dstb)
            s["dbs"][...] += dnt(tu.astype(BF), dstb)
            s["gs"][...] += to_head(tu * v, j)
            keep = s["keep"][0:1, lanes]
            s["krow"][:, lanes] = jnp.broadcast_to(keep * jnp.sum(st * dst, axis=0, keepdims=True), (8, 128))
            s["dstate"][:, lanes] = keep * dst + dnn(s["ct"][...], edyb)
            lane = ii((Q, 128), 1)
            parts = []
            for e in range(2):
                h = 2 * j + e
                mine = (lane < 64) if e == 0 else (lane >= 64)
                s["dm"][...] = dnt(jnp.where(mine, dy, 0.0).astype(BF), ub)
                colsum = [jnp.zeros((1, 128), F32), jnp.zeros((1, 128), F32)]
                for r in range(4):
                    rows = slice(r * 64, r * 64 + 64)
                    rowsum = jnp.zeros((64, 128), F32)
                    for k in range(1 if r < 2 else 2):
                        cols = slice(k * 128, k * 128 + 128)
                        dec = decay(s["cum"], s["cumt"], s["bias"], h, rows, cols)
                        qk = s["qk"][rows, cols]
                        p = s["dm"][rows, cols] * dec
                        s["dqk"][rows, cols] += p
                        g = p * qk
                        rowsum = rowsum + g
                        colsum[k] = colsum[k] + jnp.sum(g, axis=0, keepdims=True)
                        s["m"][e, rows, cols] = (dec * qk).astype(BF)
                    tot = jnp.sum(rowsum, axis=1, keepdims=True)
                    s["rowg"][rows] += jnp.where(ii((64, 128), 1) == h, tot, 0.0)
                s["colg"][h] = jnp.broadcast_to(jnp.concatenate(colsum, axis=1), (8, Q))
                parts.append(dnn(dyt[e * 64 : e * 64 + 64], s["m"][e]))
            du = jnp.concatenate(parts, axis=0).T + taile * v
            s["ds"][...] += to_head(du * x, j)
            skip = taps[5:6]
            dx = du * stepe + skip * dy
            dpre = dx * (sig + x * (1.0 - sig))
            low[pl.ds(r0, Q), lanes] = later_sum(dpre, s["halo"][:, lanes], after, taps).astype(BF)
            s["halo"][:, lanes] = dpre[:8]
            gx[:, lanes] += jnp.concatenate(
                [jnp.sum(dpre * shifted[3 - k], axis=0, keepdims=True) for k in range(4)]
                + [jnp.sum(dpre, axis=0, keepdims=True), jnp.sum(dy * x, axis=0, keepdims=True), jnp.zeros((2, 128), F32)], axis=0)
            return 0

        lax.fori_loop(0, nv // 128, pair, 0)
        tt, ss = ii((Q, Q), 0), ii((Q, Q), 1)
        e64t = (ii((nv, 128), 0) // 64 == ii((nv, 128), 1)).astype(BF)
        kh, km, kl = split3(s["krow"][...])
        kterm = dnn(kh, e64t) + dnn(km, e64t) + dnn(kl, e64t)
        colg = jnp.concatenate([s["colg"][h, 0:1] for h in range(nh)] + [jnp.zeros((128 - nh, Q), F32)], axis=0)
        dcum = s["rowg"][...] - colg.T + s["rs"][...]
        da = tri_times((ss >= tt).astype(BF), dcum) + tri_times((ss < tt).astype(BF), s["gs"][...]) + kterm[0:1]
        rate = hp[1:2]
        dstep = s["ds"][...] + rate * da
        draw = dstep * sigmoid(raw)
        draw = jnp.where(ii((Q, 128), 1) < nh, draw, 0.0)
        low[pl.ds(r0, Q), pl.ds(nv + 256, 128)] = draw.astype(BF)
        gh[...] += jnp.concatenate([jnp.sum(draw, axis=0, keepdims=True), jnp.sum(da * step, axis=0, keepdims=True) * rate, jnp.zeros((6, 128), F32)], axis=0)
        dqk = s["dqk"][...]
        dc = dnn(dqk.astype(BF), s["b"][...]) + s["dcs"][...]
        db = dnn(dqk.T.astype(BF), s["c"][...]) + s["dbs"][...]
        sig = sigmoid(bc_pre)
        dpre = jnp.concatenate([db, dc], axis=1) * (sig + bc_pre * sig * (1.0 - sig))
        after2 = [None] + [jnp.concatenate([m, m], axis=1) for m in after[1:]]
        low[pl.ds(r0, Q), pl.ds(nv, 256)] = later_sum(dpre, s["halobc"][...], after2, cbc[...]).astype(BF)
        s["halobc"][...] = dpre[:8]
        gbc[...] += jnp.concatenate(
            [jnp.sum(dpre * bc_shifted[3 - k], axis=0, keepdims=True) for k in range(4)] + [jnp.sum(dpre, axis=0, keepdims=True), jnp.zeros((3, 256), F32)], axis=0)
        return 0

    lax.fori_loop(0, nb, block, 0)


def run_forward(nv, vals, segc, segr, cx, cbc, hp):
    sc = fwd_scratch(nv)
    names = list(sc)
    rows = vals.shape[0]

    def kernel(vals, segc, segr, cx, cbc, hp, ssd, states, *scr):
        ssd_forward(nv, vals, segc, segr, cx, cbc, hp, ssd, states, dict(zip(names, scr)))

    vm = pl.BlockSpec(memory_space=pltpu.VMEM)
    return pl.pallas_call(
        kernel, out_shape=(jax.ShapeDtypeStruct((rows, nv), F32), jax.ShapeDtypeStruct((rows // Q, 128, nv), F32)),
        in_specs=[vm] * 6, out_specs=[vm] * 2, scratch_shapes=[sc[n] for n in names],
        compiler_params=pltpu.CompilerParams(vmem_limit_bytes=60 * 2**20), name="scan_forward",
    )(vals, segc, segr, cx, cbc, hp)


def run_backward(nv, vals, segc, segr, cx, cbc, hp, dy, states):
    sc = bwd_scratch(nv)
    names = list(sc)
    rows = vals.shape[0]

    def kernel(vals, segc, segr, cx, cbc, hp, dy, states, low, gx, gbc, gh, *scr):
        ssd_backward(nv, vals, segc, segr, cx, cbc, hp, dy, states, low, gx, gbc, gh, dict(zip(names, scr)))

    vm = pl.BlockSpec(memory_space=pltpu.VMEM)
    outs = (jax.ShapeDtypeStruct((rows, nv + 384), BF), jax.ShapeDtypeStruct((8, nv), F32), jax.ShapeDtypeStruct((8, 256), F32), jax.ShapeDtypeStruct((8, 128), F32))
    return pl.pallas_call(
        kernel, out_shape=outs, in_specs=[vm] * 8, out_specs=[vm] * 4, scratch_shapes=[sc[n] for n in names],
        compiler_params=pltpu.CompilerParams(vmem_limit_bytes=60 * 2**20), name="scan_backward",
    )(vals, segc, segr, cx, cbc, hp, dy, states)


INNER = 3072
EPS = 1e-05


def at_step(step, events):
    for k, fn in events:
        pl.when(step == k)(fn)


def forward_kernel(
    names, nv,
    hid, cot_own, w_own0, w_own1, w_own2, w_own3, pgain, segc, segr, cx, cbc, hp, ggain,
    o_w0, o_w1, o_w2, o_w3, o_nrm, o_cot, o_vals, o_states, o_no, o_lg, o_dy, o_gg,
    w0, w1, w2, w3, nrm, cot, vals, states, ssd, gate, gno, no, lg, dy, sums_own, sums_in,
    wsend, wrecv, tsend, trecv, ssend, srecv, lsem, *scan_scratch,
):
    s = dict(zip(names, scan_scratch))
    x, z, yh, t = place()
    yl, co = t // 2, t % 2
    tp, slots = tensor_peers()
    width = hid.shape[1]
    greet([dev(x, z, 1 - yh, t)] + [neighbour(a, d) for a in "xz" for d in (1, -1)] + tp)
    owns, dsts, outs = (w_own0, w_own1, w_own2, w_own3), (w0, w1, w2, w3), (o_w0, o_w1, o_w2, o_w3)
    groups = lambda ks: [Gather(owns[k], dsts[k], "xz"[k % 2], wsend.at[k], wrecv.at[k]) for k in ks]
    first, second = (0, 1), (2, 3)

    def step(ks, n):
        for g in groups(ks):
            g.step(n)

    def saved(i, src, dst):
        return pltpu.make_async_copy(src, dst, lsem.at[i])

    mine = pl.ds(pl.multiple_of(t * 256, 256), 256)
    theirs = pl.ds(pl.multiple_of(slots[1] * 256, 256), 256)

    def tensor_copies(i, own, dst):
        return (
            send(own, dst.at[mine], tsend.at[i, 0], trecv.at[i, 0], tp[1]),
            send(own, dst.at[mine], tsend.at[i, 1], trecv.at[i, 1], tp[0]),
            send(dst.at[theirs], dst.at[theirs], tsend.at[i, 2], trecv.at[i, 2], tp[0]),
        )

    step(first, 0)

    def norm_rows(i, _):
        rows = pl.ds(pl.multiple_of(i * 64, 64), 64)
        h = hid[rows].astype(F32)
        inv = lax.rsqrt(jnp.mean(h * h, axis=1, keepdims=True) + EPS)
        nrm[pl.ds(pl.multiple_of(t * 256 + i * 64, 64), 64)] = (h * inv * pgain[0:1]).astype(BF)
        return 0

    lax.fori_loop(0, 4, norm_rows, 0)
    for k in range(4):
        g = groups((k,))[0]
        g.mine[...] = g.own[...]
    cot[mine] = cot_own[...]
    nrm_copies = tensor_copies(0, nrm.at[mine], nrm)
    cot_copies = tensor_copies(1, cot_own, cot)
    nrm_copies[0].start()
    nrm_copies[1].start()
    for n in (1, 2, 3):
        step(first, n)
    nrm_copies[0].wait_recv()
    nrm_copies[2].start()
    cot_copies[0].start()
    cot_copies[1].start()
    step(second, 0)
    for n in (4, 5, 6):
        step(first, n)
    step(second, 1)
    step(first, 7)
    nrm_copies[1].wait_recv()
    nrm_copies[2].wait_recv()

    def project(i, _):
        rows = pl.ds(pl.multiple_of(i * 256, 256), 256)
        n = nrm[rows]
        at = 0
        for w in (w0, w1):
            c = w.shape[1]
            vals[rows, at : at + c] = jnp.dot(n, w[...], preferred_element_type=F32)
            at += c
        return 0

    lax.fori_loop(0, 4, project, 0)
    early = [(0, w0, o_w0), (1, w1, o_w1), (2, nrm, o_nrm), (3, vals, o_vals)]
    for e in early:
        saved(*e).start()

    def cot_forward():
        cot_copies[0].wait_recv()
        cot_copies[2].start()

    events = [(0, lambda: step(second, 2)), (4, lambda: step(second, 3)), (8, lambda: step(second, 4)), (14, cot_forward), (16, lambda: step(second, 5)), (20, lambda: step(second, 6))]
    ssd_forward(nv, vals, segc, segr, cx, cbc, hp, ssd, states, s, lambda at: at_step(at, events))
    step(second, 7)
    cot_copies[1].wait_recv()
    cot_copies[2].wait_recv()
    late = [(4, w2, o_w2), (5, w3, o_w3), (6, cot, o_cot), (7, states, o_states)]
    for e in late:
        saved(*e).start()

    def inner(i, _):
        rows = pl.ds(pl.multiple_of(i * 256, 256), 256)
        g = jnp.dot(nrm[rows], w2[...], preferred_element_type=F32)
        gate[rows] = g
        o = jnp.dot(cot[rows], w3[...], preferred_element_type=F32)
        gno[rows] = o
        gated = ssd[rows] * (g * sigmoid(g))
        sq = jnp.sum(gated * gated, axis=1, keepdims=True)
        cr = jnp.sum(o * ggain[0:1] * gated, axis=1, keepdims=True)
        lane = ii((256, 128), 1)
        both = jnp.where(lane == 0, sq, jnp.where(lane == 1, cr, 0.0))
        sums_own[:, rows] = both.T[:8]
        return 0

    lax.fori_loop(0, 4, inner, 0)
    small = [send(sums_own, sums_in.at[k], ssend.at[k], srecv.at[k], p) for k, p in enumerate(tp)]
    for c in small:
        c.start()
    for c in small:
        c.wait_recv()
    o_gg[...] = jnp.zeros_like(o_gg)

    def outer(i, _):
        rows = pl.ds(pl.multiple_of(i * 256, 256), 256)
        tot = sums_own[:, rows] + sums_in[0, :, rows] + sums_in[1, :, rows] + sums_in[2, :, rows]
        cols = jnp.concatenate([tot, jnp.zeros((120, 256), F32)], axis=0).T
        inv = lax.rsqrt(cols[:, 0:1] / INNER + EPS)
        cross = inv * inv * inv * cols[:, 1:2] / INNER
        for k in range(nv // 128):
            lanes = pl.ds(k * 128, 128)
            g, y, o, gain = gate[rows, lanes], ssd[rows, lanes], gno[rows, lanes], ggain[0:1, lanes]
            sig = sigmoid(g)
            silu = g * sig
            gated = y * silu
            scaled = gated * inv
            no[rows, lanes] = (scaled * gain).astype(BF)
            o_gg[0:1, lanes] += jnp.sum(o * scaled, axis=0, keepdims=True)
            grad = o * gain * inv - gated * cross
            dy[rows, lanes] = (grad * silu).astype(BF)
            lg[rows, lanes] = (grad * y * (sig + silu * (1.0 - sig))).astype(BF)
        return 0

    lax.fori_loop(0, 4, outer, 0)
    last = [(8, no, o_no), (9, lg, o_lg), (10, dy, o_dy)]
    for e in last:
        saved(*e).start()
    for g in groups((0, 1, 2, 3)):
        g.finish()
    for c in nrm_copies + cot_copies + tuple(small):
        c.wait_send()
    for e in early + late + last:
        saved(*e).wait()


def run_k1(hid, cot_own, w_owns, pgain, segc, segr, cx, cbc, hp, ggain):
    anys, vm = pl.BlockSpec(memory_space=pl.ANY), pl.BlockSpec(memory_space=pltpu.VMEM)
    nv = cx.shape[1]
    rows = segc.shape[0]
    d = hid.shape[1]
    sh = jax.ShapeDtypeStruct
    cols = [w.shape[1] for w in w_owns]
    nvals = cols[0] + cols[1]
    outs = [sh((d, c), BF) for c in cols] + [sh((rows, d), BF)] * 2 + [sh((rows, nvals), F32), sh((rows // Q, 128, nv), F32)] + [sh((rows, nv), BF)] * 3 + [sh((8, nv), F32)]
    V = lambda shape, dt: pltpu.VMEM(shape, dt)
    D = pltpu.SemaphoreType.DMA
    scan = fwd_scratch(nv)
    scratch = [V((d, c), BF) for c in cols] + [V((rows, d), BF)] * 2 + [V((rows, nvals), F32), V((rows // Q, 128, nv), F32)] + [V((rows, nv), F32)] * 3 + [V((rows, nv), BF)] * 3
    scratch += [V((8, rows), F32), V((3, 8, rows), F32), D((4, Gather.N)), D((4, Gather.N)), D((2, 3)), D((2, 3)), D((3,)), D((3,)), D((11,))]
    scratch += list(scan.values())
    return pl.pallas_call(
        functools.partial(forward_kernel, list(scan), nv), out_shape=outs, in_specs=[vm] * 13, out_specs=[anys] * 11 + [vm], scratch_shapes=scratch,
        compiler_params=pltpu.CompilerParams(collective_id=0, has_side_effects=True, vmem_limit_bytes=62 * 2**20), name="forward_all",
    )(hid, cot_own, *w_owns, pgain, segc, segr, cx, cbc, hp, ggain)


def rs_kernel(bc0, ga, gb, po, pn, sv, oa, ob, oo, on, osv,
              va, vb, vo, vn, r1a, r1b, r2a, r2b, ha, hb, q1a, q1b, q2a, q2b, ka, kb, ya, yb,
              co_buf, cy_buf, cs_buf, sacc, sx, sz, sy, st, bct,
              lsem, wsend, wrecv, tsend, trecv, ssend, srecv, bsend, brecv):
    x, z, yh, t = place()
    yl = t // 2; co = t % 2
    m4 = lambda v: (v + 8) % 4
    def nb(axis, d):
        if axis == "x": return dev(m4(x + d), z, yh, t)
        return dev(x, m4(z + d), yh, t)
    ypeer = dev(x, z, 1 - yh, t)
    tcore = dev(x, z, yh, yl * 2 + (1 - co))
    tyl = dev(x, z, yh, (1 - yl) * 2 + co)
    tdiag = dev(x, z, yh, (1 - yl) * 2 + 1 - co)
    bar = pltpu.get_barrier_semaphore()
    peers = [ypeer, tcore, tyl, tdiag] + [nb(a, d) for a in "xz" for d in (1, 2, 3)]
    for p in peers:
        pl.semaphore_signal(bar, inc=1, device_id=p, device_id_type=MESH)
    loads = []
    for i, (s, d) in enumerate(((ga, va), (gb, vb), (po, vo), (pn, vn))):
        cp = pltpu.make_async_copy(s, d, lsem.at[i]); cp.start(); loads.append(cp)
    pl.semaphore_wait(bar, len(peers))
    sends = []
    def rc(src, dst, ss, rs, to):
        cp = pltpu.make_async_remote_copy(src_ref=src, dst_ref=dst, send_sem=ss, recv_sem=rs, device_id=to, device_id_type=MESH)
        cp.start(); sends.append(cp); return cp
    pos = {"x": x, "z": z}
    halves = ((va, "z", "x", r1a, r2a, ha, q1a, q2a, ka, ya, oa), (vb, "x", "z", r1b, r2b, hb, q1b, q2b, kb, yb, ob))
    def b1(v, a1, d, k=None):
        p = m4(pos[a1] + d)
        if a1 == "z": return v.at[:, p] if k is None else v.at[pl.ds(2 * k, 2), p]
        return v.at[p] if k is None else v.at[p, pl.ds(2 * k, 2)]
    small = []
    for d in (1, 2, 3):
        small.append(rc(sv, sx.at[d - 1], ssend.at[d - 1], srecv.at[d - 1], nb("x", d)))
    for l in loads[:2]: l.wait()
    s1 = []
    for i, (v, a1, a2, r1, r2, *_) in enumerate(halves):
        s1.append((rc(b1(v, a1, 2, 0), r1.at[0], wsend.at[i, 0], wrecv.at[i, 0], nb(a1, 1)),
                   rc(b1(v, a1, 2, 1), r1.at[1], wsend.at[i, 1], wrecv.at[i, 1], nb(a1, -1))))
    s1b = []
    for i, (v, a1, a2, r1, r2, *_) in enumerate(halves):
        s1b.append((rc(b1(v, a1, 1, 1), r2.at[0, pl.ds(2, 2)], wsend.at[i, 2], wrecv.at[i, 2], nb(a1, 1)),
                    rc(b1(v, a1, -1, 0), r2.at[1, pl.ds(0, 2)], wsend.at[i, 3], wrecv.at[i, 3], nb(a1, -1))))
    tr = []
    for l in loads[2:]: l.wait()
    for i, v in enumerate((vo, vn)):
        a = rc(v.at[(1 - yl) * 2 + 1 - co], co_buf.at[i, 0], tsend.at[i, 0], trecv.at[i, 0], tcore)
        b = rc(v.at[yl * 2 + 1 - co], co_buf.at[i, 1], tsend.at[i, 1], trecv.at[i, 1], tcore)
        tr.append((a, b))
    for i, v in enumerate((vo, vn)):
        tr[i][0].wait_recv()
        def addc(j, _, i=i, v=v):
            rows = pl.ds(pl.multiple_of(j * 32, 32), 32)
            cs_buf[i, rows] = (v[(1 - yl) * 2 + co, rows].astype(F32) + co_buf[i, 0, rows].astype(F32)).astype(BF)
            return 0
        lax.fori_loop(0, 8, addc, 0)
        tr[i] = tr[i] + (rc(cs_buf.at[i], cy_buf.at[i], tsend.at[i, 2], trecv.at[i, 2], tyl),)
    for s in small: s.wait_recv()
    sacc[0] = sv[...] + sx[0] + sx[1] + sx[2]
    small = [rc(sacc.at[0], sz.at[d - 1], ssend.at[2 + d], srecv.at[2 + d], nb("z", d)) for d in (1, 2, 3)]
    s1c = []
    for i, (v, a1, a2, r1, r2, *_) in enumerate(halves):
        for side, dd, k in ((0, 1, 0), (1, -1, 1)):
            s1[i][side].wait_recv()
            p = m4(pos[a1] + dd)
            def add1(j, _, v=v, a1=a1, r1=r1, side=side, p=p, k=k):
                e = j // 2 ; y = j % 2
                if a1 == "z":
                    v[2 * k + e, p, y] = (v[2 * k + e, p, y].astype(F32) + r1[side, e, y].astype(F32)).astype(BF)
                else:
                    v[p, 2 * k + e, y] = (v[p, 2 * k + e, y].astype(F32) + r1[side, e, y].astype(F32)).astype(BF)
                return 0
            lax.fori_loop(0, 4, add1, 0)
            s1c.append(rc(b1(v, a1, dd, k), r2.at[side, pl.ds(2 * k, 2)], wsend.at[i, 4 + side], wrecv.at[i, 4 + side], nb(a1, dd)))
    for s in small: s.wait_recv()
    sacc[1] = sacc[0] + sz[0] + sz[1] + sz[2]
    small = [rc(sacc.at[1], sy, ssend.at[6], srecv.at[6], ypeer)]
    s2 = []
    for i, (v, a1, a2, r1, r2, h, q1, q2, kk, yy, oo_) in enumerate(halves):
        s1b[i][0].wait_recv(); s1b[i][1].wait_recv()
        s1c[2 * i].wait_recv(); s1c[2 * i + 1].wait_recv()
        p = pos[a1]
        def add2(j, _, v=v, a1=a1, r2=r2, h=h, p=p):
            e = j // 2; y = j % 2
            own = v[e, p, y] if a1 == "z" else v[p, e, y]
            h[e, y] = (own.astype(F32) + r2[0, e, y].astype(F32) + r2[1, e, y].astype(F32)).astype(BF)
            return 0
        lax.fori_loop(0, 8, add2, 0)
        q = pos[a2]
        s2.append((rc(h.at[m4(q + 2), 0], q1.at[0], wsend.at[i, 6], wrecv.at[i, 6], nb(a2, 1)),
                   rc(h.at[m4(q + 2), 1], q1.at[1], wsend.at[i, 7], wrecv.at[i, 7], nb(a2, -1)),
                   rc(h.at[m4(q + 1), 1], q2.at[0, 1], wsend.at[i, 8], wrecv.at[i, 8], nb(a2, 1)),
                   rc(h.at[m4(q - 1), 0], q2.at[1, 0], wsend.at[i, 9], wrecv.at[i, 9], nb(a2, -1))))
    for s in small: s.wait_recv()
    sacc[2] = sacc[1] + sy[...]
    small = [rc(sacc.at[2], st.at[j], ssend.at[7 + j], srecv.at[7 + j], d_) for j, d_ in enumerate((tcore, tyl, tdiag))]
    s2c = []
    for i, (v, a1, a2, r1, r2, h, q1, q2, kk, yy, oo_) in enumerate(halves):
        q = pos[a2]
        for side, dd in ((0, 1), (1, -1)):
            s2[i][side].wait_recv()
            pp = m4(q + dd)
            h[pp, side] = (h[pp, side].astype(F32) + q1[side].astype(F32)).astype(BF)
            s2c.append(rc(h.at[pp, side], q2.at[side, side], wsend.at[i, 10 + side], wrecv.at[i, 10 + side], nb(a2, dd)))
    s3 = []
    for i, (v, a1, a2, r1, r2, h, q1, q2, kk, yy, oo_) in enumerate(halves):
        q = pos[a2]
        s2[i][2].wait_recv(); s2[i][3].wait_recv()
        s2c[2 * i].wait_recv(); s2c[2 * i + 1].wait_recv()
        kk[...] = (h[q, 1 - yh].astype(F32) + q2[0, 1 - yh].astype(F32) + q2[1, 1 - yh].astype(F32)).astype(BF)
        s3.append(rc(kk, yy, wsend.at[i, 12], wrecv.at[i, 12], ypeer))
    for i, (v, o) in enumerate(((vo, oo), (vn, on))):
        tr[i][1].wait_recv(); tr[i][2].wait_recv()
        def addf(j, _, i=i, v=v, o=o):
            rows = pl.ds(pl.multiple_of(j * 32, 32), 32)
            o[rows] = v[t, rows].astype(F32) + co_buf[i, 1, rows].astype(F32) + cy_buf[i, rows].astype(F32)
            return 0
        lax.fori_loop(0, 8, addf, 0)
    tens = []
    for i, (v, a1, a2, r1, r2, h, q1, q2, kk, yy, o) in enumerate(halves):
        q = pos[a2]
        s3[i].wait_recv()
        o[...] = h[q, yh].astype(F32) + q2[0, yh].astype(F32) + q2[1, yh].astype(F32) + yy[...].astype(F32)
        if i == 0:
            bct[3] = o[:, bc0 : bc0 + 256]
            tens = [rc(bct.at[3], bct.at[j], bsend.at[j], brecv.at[j], d_) for j, d_ in enumerate((tcore, tyl, tdiag))]
    for cp in tens: cp.wait_recv()
    oa[:, bc0 : bc0 + 256] = bct[3] + bct[0] + bct[1] + bct[2]
    for s in small: s.wait_recv()
    osv[t] = sacc[2]
    osv[yl * 2 + 1 - co] = st[0]
    osv[(1 - yl) * 2 + co] = st[1]
    osv[(1 - yl) * 2 + 1 - co] = st[2]
    for cp in sends: cp.wait_send()

def reduce_all(bc0, ga, gb, po, pn, sv):
    anys = pl.BlockSpec(memory_space=pl.ANY); vm = pl.BlockSpec(memory_space=pltpu.VMEM)
    ca, cb = ga.shape[-1], gb.shape[-1]; R = sv.shape[0]
    outs = (jax.ShapeDtypeStruct((48, ca), F32), jax.ShapeDtypeStruct((48, cb), F32), jax.ShapeDtypeStruct((256, 1536), F32),
            jax.ShapeDtypeStruct((256, 1536), F32), jax.ShapeDtypeStruct((4, R, 128), F32))
    D = pltpu.SemaphoreType.DMA
    V = lambda *s, d=BF: pltpu.VMEM(s, d)
    scratch = [V(4, 4, 2, 48, ca), V(4, 4, 2, 48, cb), V(4, 256, 1536), V(4, 256, 1536),
               V(2, 2, 2, 48, ca), V(2, 2, 2, 48, cb), V(2, 4, 2, 48, ca), V(2, 4, 2, 48, cb),
               V(4, 2, 48, ca), V(4, 2, 48, cb), V(2, 48, ca), V(2, 48, cb), V(2, 2, 48, ca), V(2, 2, 48, cb),
               V(48, ca), V(48, cb), V(48, ca), V(48, cb),
               V(2, 2, 256, 1536), V(2, 256, 1536), V(2, 256, 1536),
               V(3, R, 128, d=F32), V(3, R, 128, d=F32), V(3, R, 128, d=F32), V(R, 128, d=F32), V(3, R, 128, d=F32), V(4, 48, 256, d=F32),
               D((4,)), D((2, 13)), D((2, 13)), D((2, 3)), D((2, 3)), D((10,)), D((10,)), D((3,)), D((3,))]
    return pl.pallas_call(functools.partial(rs_kernel, bc0), out_shape=outs, in_specs=[anys] * 4 + [vm], out_specs=[vm] * 5, scratch_shapes=scratch,
        compiler_params=pltpu.CompilerParams(collective_id=1, has_side_effects=True, vmem_limit_bytes=60 * 2**20), name="reduce_all")(ga, gb, po, pn, sv)


def dot_nt(left, right):
    return lax.dot_general(left, right, (((1,), (1,)), ((), ())), preferred_element_type=F32)


def dot_tn(left, right):
    return lax.dot_general(left, right, (((0,), (0,)), ((), ())), preferred_element_type=F32)


def per_device(
    hidden_in, seg_ids, pre_gain, proj_gate, proj_x, proj_bc, proj_dt, conv_x, conv_bias_x, conv_bc, conv_bias_bc,
    dt_bias, a_log, skip_d, gate_gain, proj_out, cotangent,
):
    t = lax.axis_index("tensor")
    inner = proj_gate.shape[1]
    heads = proj_dt.shape[1]
    own = lambda v, n: lax.dynamic_slice_in_dim(v, t * n, n, v.ndim - 1)
    gain_dev = own(gate_gain, inner)
    hidden = hidden_in.astype(F32)
    inv_rms = lax.rsqrt(jnp.mean(hidden * hidden, axis=1) + EPS)
    rows = proj_x.shape[0]
    cut = inner - 128
    w_owns = (
        proj_x[:, :cut],
        jnp.concatenate([proj_x[:, cut:], proj_bc, proj_dt, jnp.zeros((rows, 128 - heads), BF)], axis=1),
        proj_gate,
        proj_out.T,
    )
    seg = seg_ids.astype(F32)
    segc = jnp.broadcast_to(seg[:, None], (seg.shape[0], 128))
    segr = jnp.broadcast_to(seg[None, :], (8, seg.shape[0]))
    heads_row = lambda v: jnp.pad(own(v, heads), (0, 128 - heads))[None]
    skip_row = jnp.broadcast_to(own(skip_d, heads)[:, None], (heads, 64)).reshape(1, inner)
    cx = jnp.concatenate([own(conv_x, inner), own(conv_bias_x, inner)[None], skip_row, jnp.zeros((2, inner), F32)])
    cbc = jnp.concatenate([conv_bc, conv_bias_bc[None], jnp.zeros((3, 256), F32)])
    hp = jnp.concatenate([heads_row(dt_bias), -jnp.exp(heads_row(a_log)), jnp.zeros((6, 128), F32)])
    spread8 = lambda v: jnp.broadcast_to(v[None, :], (8, v.shape[0]))
    w0, w1, w_gate, w_out, normed_all, cot_all, vals, states, normed_out, low_gate, dy, gg = run_k1(
        hidden_in, cotangent, w_owns, spread8(pre_gain), segc, segr, cx, cbc, hp, spread8(gain_dev)
    )
    partial_out = dot_nt(normed_out, w_out).astype(BF)
    term_out = dot_tn(cot_all, normed_out)
    low_a, gx, gbc, gh = run_backward(inner, vals, segc, segr, cx, cbc, hp, dy, states)
    grad_normed = dot_nt(low_gate, w_gate) + dot_nt(low_a[:, :cut], w0) + dot_nt(low_a[:, cut:], w1)
    part_pre = jnp.sum(grad_normed * normed_all.astype(F32), axis=0) / pre_gain
    grad_normed = grad_normed.astype(BF)
    term_a = dot_tn(normed_all, low_a).astype(BF)
    term_b = jnp.concatenate([dot_tn(normed_all, low_gate), term_out], axis=1).astype(BF)
    small = jnp.concatenate([gx[:5].reshape(-1), gg[0], gx[5], part_pre, gbc[:5].reshape(-1), gh[:2].reshape(-1)])
    small = jnp.pad(small, (0, 9216 - small.shape[0])).reshape(72, 128)
    blocks = (4, 4, 2, rows)
    ra, rb, own_out, grad_own, smalls = reduce_all(
        inner, term_a.reshape(blocks + term_a.shape[1:]), term_b.reshape(blocks + term_b.shape[1:]),
        partial_out.reshape(4, 256, -1), grad_normed.reshape(4, 256, -1), small,
    )
    output = (hidden + own_out).astype(BF)
    scaled = grad_own * pre_gain[None, :]
    proj = jnp.mean(scaled * hidden, axis=1)
    grad_hidden = cotangent.astype(F32) + scaled * inv_rms[:, None] - hidden * (inv_rms * inv_rms * inv_rms * proj)[:, None]
    smalls = smalls.reshape(4, 9216)
    spread = lambda lo, n, k: smalls[:, lo : lo + n * k].reshape(4, k, n).transpose(1, 0, 2).reshape(k, 4 * n)
    x_sums = spread(0, inner, 7)
    at = 7 * inner
    width = pre_gain.shape[0]
    d_skip = x_sums[6].reshape(-1, 64).sum(axis=1)
    both = jnp.sum(smalls[:, at : at + width + 5 * 256], axis=0)
    d_pre = both[:width]
    bc_sums = both[width:]
    at = at + width + 5 * 256
    d_dt_bias, d_a_log = (spread(at + 128 * i, 128, 1)[0].reshape(4, 128)[:, :heads].reshape(-1) for i in range(2))
    return (
        output, grad_hidden, d_pre, rb[:, :inner], ra[:, :inner], ra[:, inner : inner + 256], ra[:, inner + 256 : inner + 256 + heads],
        x_sums[:4], x_sums[4], bc_sums[:1024].reshape(4, 256), bc_sums[1024:], d_dt_bias, d_a_log, d_skip, x_sums[5],
        rb[:, inner:].T,
    )


def solution(mesh):
    tok = P(("dp", "tensor"), None)
    mat = P("dp", "tensor")
    in_specs = (tok, P("dp"), P(), mat, mat, P("dp", None), mat) + (P(),) * 8 + (P("tensor", "dp"), tok)
    out_specs = (tok, tok, P(), mat, mat, P("dp", None), mat) + (P(),) * 8 + (P("tensor", "dp"),)
    return jax.shard_map(per_device, mesh=mesh, in_specs=in_specs, out_specs=out_specs, check_vma=False)
```

```python
import functools

import jax
import jax.numpy as jnp
from jax import lax
from jax.experimental import pallas as pl
from jax.experimental.pallas import tpu as pltpu
from jax.sharding import PartitionSpec as P

MESH = pl.DeviceIdType.MESH
F32 = jnp.float32
BF = jnp.bfloat16


def place():
    dp = lax.axis_index("dp")
    t = lax.axis_index("tensor")
    return dp // 8, (dp // 2) % 4, dp % 2, t


def dev(x, z, yh, t):
    return ((x * 4 + z) * 2 + yh, t)


def m4(v):
    return (v + 8) % 4


def neighbour(axis, d):
    x, z, yh, t = place()
    return dev(m4(x + d), z, yh, t) if axis == "x" else dev(x, m4(z + d), yh, t)


def tensor_peers():
    x, z, yh, t = place()
    yl, co = t // 2, t % 2
    slots = (yl * 2 + 1 - co, (1 - yl) * 2 + co, (1 - yl) * 2 + 1 - co)
    return [dev(x, z, yh, s) for s in slots], slots


def greet(peers):
    bar = pltpu.get_barrier_semaphore()
    for p in peers:
        pl.semaphore_signal(bar, inc=1, device_id=p, device_id_type=MESH)
    pl.semaphore_wait(bar, len(peers))


def send(src, dst, send_sem, recv_sem, to):
    return pltpu.make_async_remote_copy(
        src_ref=src, dst_ref=dst, send_sem=send_sem, recv_sem=recv_sem, device_id=to, device_id_type=MESH
    )


class Gather:
    N = 25

    def __init__(self, own, dst, r1, send_sem, recv_sem):
        x, z, yh, _ = place()
        r2 = "z" if r1 == "x" else "x"
        n = own.shape[0]

        def rows(d1, d2, y=None):
            ix, iz = (m4(x + d1), m4(z + d2)) if r1 == "x" else (m4(x + d2), m4(z + d1))
            first = (ix * 4 + iz) * 2
            if y is None:
                return dst.at[pl.ds(pl.multiple_of(first * n, n), 2 * n)]
            return dst.at[pl.ds(pl.multiple_of((first + y) * n, n), n)]

        self.mine = rows(0, 0, yh)
        self.own = own
        near1, near2 = [neighbour(r1, 1), neighbour(r1, -1)], [neighbour(r2, 1), neighbour(r2, -1)]
        other = rows(0, 0, 1 - yh)
        plan = [(own, self.mine, dev(x, z, 1 - yh, place()[3]))]
        plan += [(own, self.mine, p) for p in near1 + near2]
        plan += [(other, other, p) for p in near1 + near2]
        plan += [(rows(-1, 0, 0),) * 2 + (near1[0],), (rows(1, 0, 1),) * 2 + (near1[1],)]
        for d1 in (-1, 1, 2):
            plan += [(rows(d1, 0),) * 2 + (p,) for p in near2]
        for d1 in (0, -1, 1, 2):
            plan += [(rows(d1, -1, 0),) * 2 + (near2[0],), (rows(d1, 1, 1),) * 2 + (near2[1],)]
        self.plan, self.send_sem, self.recv_sem = plan, send_sem, recv_sem

    def copy(self, k):
        src, dst, to = self.plan[k]
        return send(src, dst, self.send_sem.at[k], self.recv_sem.at[k], to)

    STEPS = (
        ((), (1, 2, 3, 4)),
        ((0,), (5, 6, 7, 8)),
        ((1, 2, 5, 6), (9, 10, 11, 12, 13, 14)),
        ((9, 10), (15, 16)),
        ((3, 4, 7, 8), (17, 18)),
        ((11, 12, 13, 14), (19, 20, 21, 22)),
        ((15, 16), (23, 24)),
        ((17, 18, 19, 20, 21, 22, 23, 24), ()),
    )

    def begin(self):
        self.copy(0).start()

    def step(self, k):
        arrive, go = self.STEPS[k]
        for i in arrive:
            self.copy(i).wait_recv()
        for i in go:
            self.copy(i).start()

    def finish(self):
        for k in range(self.N):
            self.copy(k).wait_send()


Q = 256
LOG2E = 1.4426950408889634
NEG = -1e30


def dnn(a, b):
    return jnp.dot(a, b, preferred_element_type=F32)


def dnt(a, b):
    return lax.dot_general(a, b, (((1,), (1,)), ((), ())), preferred_element_type=F32)


def split3(v):
    hi = v.astype(BF)
    r = v - hi.astype(F32)
    mid = r.astype(BF)
    lo = (r - mid.astype(F32)).astype(BF)
    return hi, mid, lo


def spread3(v, mat):
    hi, mid, lo = split3(v)
    return dnn(jnp.concatenate([hi, mid, lo], axis=1), jnp.concatenate([mat, mat, mat], axis=0))


def tri_times(mat, v):
    hi, mid, lo = split3(v)
    out = dnn(mat, jnp.concatenate([hi, mid, lo], axis=1))
    w = v.shape[1]
    return out[:, :w] + out[:, w : 2 * w] + out[:, 2 * w :]


def ii(shape, dim):
    return lax.broadcasted_iota(jnp.int32, shape, dim)


def sigmoid(v):
    return 1.0 / (1.0 + jnp.exp2(v * -LOG2E))


def softplus(v):
    e = jnp.exp2(jnp.abs(v) * -LOG2E)
    u = 1.0 + e
    log1p = jnp.where(u == 1.0, e, jnp.log(u) * (e / jnp.where(u == 1.0, 1.0, u - 1.0)))
    return jnp.maximum(v, 0.0) + log1p


def conv_terms(ext, match, taps):
    n = ext.shape[0] - 8
    shifted = [ext[8:]] + [jnp.where(match[k], ext[8 - k : 8 + n - k], 0.0) for k in (1, 2, 3)]
    pre = taps[4:5] + sum(taps[3 - k : 4 - k] * shifted[k] for k in range(4))
    return pre, shifted


def with_earlier(ref, r0, lanes):
    prev = ref[pl.ds(pl.multiple_of(jnp.maximum(r0 - 8, 0), 8), 8), lanes]
    return jnp.concatenate([prev, ref[pl.ds(r0, Q), lanes]], axis=0)


def match_rows(segc, r0):
    prev = segc[pl.ds(pl.multiple_of(jnp.maximum(r0 - 8, 0), 8), 8), :]
    prev = jnp.where(r0 > 0, prev, -1.0)
    cur = segc[pl.ds(r0, Q), :]
    ext = jnp.concatenate([prev, cur], axis=0)
    return [None] + [ext[8 - k : 8 + Q - k] == cur for k in (1, 2, 3)]


def block_setup(c, nv, vals, segc, segr, cbc, hp, bt_ref, b_ref, c_ref, ct_ref, qk_ref, bias_ref, cum_ref, cumt_ref, step_ref, tail_ref, keep_ref, ex_ref, keep_out):
    r0 = pl.multiple_of(c * Q, Q)
    match = match_rows(segc, r0)
    m2 = [None] + [jnp.concatenate([m, m], axis=1) for m in match[1:]]
    ext = with_earlier(vals, r0, pl.ds(nv, 256))
    pre, shifted = conv_terms(ext, m2, cbc[...])
    bc = pre * sigmoid(pre)
    bb = bc[:, :128].astype(BF)
    cc = bc[:, 128:].astype(BF)
    b_ref[...] = bb
    c_ref[...] = cc
    bt_ref[...] = bc[:, :128].T.astype(BF)
    if ct_ref is not None:
        ct_ref[...] = bc[:, 128:].T.astype(BF)
    qk_ref[...] = dnt(cc, bb)
    seg = segc[pl.ds(r0, Q), :]
    segs = segr[0:1, pl.ds(r0, Q)]
    tt, ss = ii((Q, Q), 0), ii((Q, Q), 1)
    allowed = (tt >= ss) & (jnp.concatenate([seg, seg], axis=1) == segs)
    bias_ref[...] = jnp.where(allowed, 0.0, NEG)
    raw = vals[pl.ds(r0, Q), pl.ds(nv + 256, 128)] + hp[0:1]
    step = softplus(raw)
    tri = (tt >= ss).astype(BF)
    cum = tri_times(tri, step * (hp[1:2] * LOG2E))
    cumt = cum.T
    for h in range(nv // 64):
        cumt_ref[h] = jnp.broadcast_to(cumt[h : h + 1], (8, Q))
    exm = ex_ref[...]
    cum_ref[...] = spread3(cum, exm)
    e64 = (ii((128, nv), 0) == ii((128, nv), 1) // 64).astype(BF)
    step_ref[...] = spread3(step, e64)
    prev_seg = jnp.where(c > 0, segc[pl.ds(pl.multiple_of(jnp.maximum(r0 - 8, 0), 8), 8), :][7:8], -1.0)
    last_seg = seg[Q - 1 :]
    cum_last = cum[Q - 1 :]
    carry = (seg == prev_seg).astype(F32)
    tailm = (seg == last_seg).astype(F32)
    tail = jnp.exp2(cum_last - cum) * tailm
    tail_ref[...] = spread3(tail, e64)
    keep = jnp.exp2(cum_last) * (last_seg == prev_seg).astype(F32)
    keep_ref[...] = spread3(jnp.broadcast_to(keep, (8, 128)), e64)
    keep_out[...] = spread3(jnp.exp2(cum) * carry, e64)
    return match, pre, shifted, raw, step


def decay(cum_ref, cumt_ref, bias_ref, h, rows, cols):
    col = cum_ref[rows, pl.ds(pl.multiple_of(h * 128, 128), 128)]
    row = cumt_ref[h, 0:1, cols]
    return jnp.exp2(col - row + bias_ref[rows, cols])


def fwd_scratch(nv):
    V = lambda s, d=F32: pltpu.VMEM(s, d)
    nh = nv // 64
    return dict(
        bt=V((128, Q), BF), b=V((Q, 128), BF), c=V((Q, 128), BF), qk=V((Q, Q)), bias=V((Q, Q)), cum=V((Q, nh * 128)), cumt=V((nh, 8, Q)),
        step=V((Q, nv)), tail=V((Q, nv)), keep=V((8, nv)), ecum=V((Q, nv)), ex=V((128, nh * 128), BF), state=V((128, nv)), m=V((2, Q, Q), BF),
    )


def ssd_forward(nv, vals, segc, segr, cx, cbc, hp, ssd, states, s, hook=lambda at: None):
    nh = nv // 64
    s["ex"][...] = (ii((128, nh * 128), 0) == ii((128, nh * 128), 1) // 128).astype(BF)
    s["state"][...] = jnp.zeros_like(s["state"])
    s["m"][...] = jnp.zeros_like(s["m"])

    def block(c, _):
        r0 = pl.multiple_of(c * Q, Q)
        match, *_r = block_setup(c, nv, vals, segc, segr, cbc, hp, s["bt"], s["b"], s["c"], None, s["qk"], s["bias"], s["cum"], s["cumt"], s["step"], s["tail"], s["keep"], s["ex"], s["ecum"])
        states[c] = s["state"][...].astype(BF)

        def pair(j, _):
            hook(c * (nv // 128) + j)
            lanes = pl.ds(pl.multiple_of(j * 128, 128), 128)
            pre, _sh = conv_terms(with_earlier(vals, r0, lanes), match, cx[:, lanes])
            x = pre * sigmoid(pre)
            u = x * s["step"][:, lanes]
            ub = u.astype(BF)
            st = s["state"][:, lanes]
            y = dnn(s["c"][...], st.astype(BF)) * s["ecum"][:, lanes]
            y = y + cx[5:6, lanes] * x
            for e in range(2):
                for r in range(4):
                    rows = slice(r * 64, r * 64 + 64)
                    for k in range(1 if r < 2 else 2):
                        cols = slice(k * 128, k * 128 + 128)
                        s["m"][e, rows, cols] = (decay(s["cum"], s["cumt"], s["bias"], 2 * j + e, rows, cols) * s["qk"][rows, cols]).astype(BF)
            y0 = dnn(s["m"][0], ub)
            y1 = dnn(s["m"][1], ub)
            ssd[pl.ds(r0, Q), lanes] = y + jnp.where(ii((Q, 128), 1) < 64, y0, y1)
            s["state"][:, lanes] = st * s["keep"][0:1, lanes] + dnn(s["bt"][...], (u * s["tail"][:, lanes]).astype(BF))
            return 0

        lax.fori_loop(0, nv // 128, pair, 0)
        return 0

    lax.fori_loop(0, vals.shape[0] // Q, block, 0)


def bwd_scratch(nv):
    V = lambda s, d=F32: pltpu.VMEM(s, d)
    d = fwd_scratch(nv)
    d.update(ct=V((128, Q), BF), dqk=V((Q, Q)), dstate=V((128, nv)), dcs=V((Q, 128)), dbs=V((Q, 128)), rowg=V((Q, 128)), colg=V((nv // 64, 8, Q)), rs=V((Q, 128)),
             gs=V((Q, 128)), ds=V((Q, 128)), krow=V((8, nv)), halo=V((8, nv)), halobc=V((8, 256)), dm=V((Q, Q)))
    return d


def to_head(v, j):
    red = (ii((128, 128), 1) == 2 * j + ii((128, 128), 0) // 64).astype(BF)
    hi = v.astype(BF)
    lo = (v - hi.astype(F32)).astype(BF)
    return dnn(jnp.concatenate([hi, lo], axis=1), jnp.concatenate([red, red], axis=0))


def later_sum(dpre, halo, match_ext, taps):
    ext = jnp.concatenate([dpre, halo], axis=0)
    n = dpre.shape[0]
    out = taps[3:4] * dpre
    for k in (1, 2, 3):
        out = out + taps[3 - k : 4 - k] * jnp.where(match_ext[k], ext[k : n + k], 0.0)
    return out


def ssd_backward(nv, vals, segc, segr, cx, cbc, hp, dy_ref, states, low, gx, gbc, gh, s, hook=lambda at: None):
    nh = nv // 64
    nb = vals.shape[0] // Q
    s["ex"][...] = (ii((128, nh * 128), 0) == ii((128, nh * 128), 1) // 128).astype(BF)
    for n in ("dstate", "halo", "halobc", "colg", "m"):
        s[n][...] = jnp.zeros_like(s[n])
    gx[...] = jnp.zeros_like(gx)
    gbc[...] = jnp.zeros_like(gbc)
    gh[...] = jnp.zeros_like(gh)

    def block(i, _):
        c = nb - 1 - i
        r0 = pl.multiple_of(c * Q, Q)
        match, bc_pre, bc_shifted, raw, step = block_setup(c, nv, vals, segc, segr, cbc, hp, s["bt"], s["b"], s["c"], s["ct"], s["qk"], s["bias"], s["cum"], s["cumt"], s["step"], s["tail"], s["keep"], s["ex"], s["ecum"])
        nxt = segc[pl.ds(pl.multiple_of(jnp.minimum(r0 + Q, segc.shape[0] - 8), 8), 8), :]
        seg = segc[pl.ds(r0, Q), :]
        ext = jnp.concatenate([seg, nxt], axis=0)
        after = [None] + [ext[k : Q + k] == seg for k in (1, 2, 3)]
        for n in ("dqk", "dcs", "dbs", "rowg", "rs", "gs", "ds"):
            s[n][...] = jnp.zeros_like(s[n])

        def pair(j, _):
            hook(i * (nv // 128) + j)
            lanes = pl.ds(pl.multiple_of(j * 128, 128), 128)
            taps = cx[:, lanes]
            pre, shifted = conv_terms(with_earlier(vals, r0, lanes), match, taps)
            sig = sigmoid(pre)
            x = pre * sig
            stepe = s["step"][:, lanes]
            taile = s["tail"][:, lanes]
            u = x * stepe
            ub = u.astype(BF)
            dy = dy_ref[pl.ds(r0, Q), lanes].astype(F32)
            dyb = dy.astype(BF)
            dyt = dy.T.astype(BF)
            stb = states[c, :, lanes]
            dst = s["dstate"][:, lanes]
            dstb = dst.astype(BF)
            edy = s["ecum"][:, lanes] * dy
            edyb = edy.astype(BF)
            s["rs"][...] += to_head(edy * dnn(s["c"][...], stb), j)
            s["dcs"][...] += dnt(edyb, stb)
            tu = taile * u
            v = dnn(s["b"][...], dstb)
            s["dbs"][...] += dnt(tu.astype(BF), dstb)
            s["gs"][...] += to_head(tu * v, j)
            keep = s["keep"][0:1, lanes]
            s["krow"][:, lanes] = jnp.broadcast_to(keep * jnp.sum(stb.astype(F32) * dst, axis=0, keepdims=True), (8, 128))
            s["dstate"][:, lanes] = keep * dst + dnn(s["ct"][...], edyb)
            lane = ii((Q, 128), 1)
            parts = []
            for e in range(2):
                h = 2 * j + e
                mine = (lane < 64) if e == 0 else (lane >= 64)
                s["dm"][...] = dnt(jnp.where(mine, dy, 0.0).astype(BF), ub)
                colsum = [jnp.zeros((1, 128), F32), jnp.zeros((1, 128), F32)]
                for r in range(4):
                    rows = slice(r * 64, r * 64 + 64)
                    rowsum = jnp.zeros((64, 128), F32)
                    for k in range(1 if r < 2 else 2):
                        cols = slice(k * 128, k * 128 + 128)
                        dec = decay(s["cum"], s["cumt"], s["bias"], h, rows, cols)
                        qk = s["qk"][rows, cols]
                        p = s["dm"][rows, cols] * dec
                        s["dqk"][rows, cols] += p
                        g = p * qk
                        rowsum = rowsum + g
                        colsum[k] = colsum[k] + jnp.sum(g, axis=0, keepdims=True)
                        s["m"][e, rows, cols] = (dec * qk).astype(BF)
                    tot = jnp.sum(rowsum, axis=1, keepdims=True)
                    s["rowg"][rows] += jnp.where(ii((64, 128), 1) == h, tot, 0.0)
                s["colg"][h] = jnp.broadcast_to(jnp.concatenate(colsum, axis=1), (8, Q))
                parts.append(dnn(dyt[e * 64 : e * 64 + 64], s["m"][e]))
            du = jnp.concatenate(parts, axis=0).T + taile * v
            s["ds"][...] += to_head(du * x, j)
            skip = taps[5:6]
            dx = du * stepe + skip * dy
            dpre = dx * (sig + x * (1.0 - sig))
            low[pl.ds(r0, Q), lanes] = later_sum(dpre, s["halo"][:, lanes], after, taps).astype(BF)
            s["halo"][:, lanes] = dpre[:8]
            gx[:, lanes] += jnp.concatenate(
                [jnp.sum(dpre * shifted[3 - k], axis=0, keepdims=True) for k in range(4)]
                + [jnp.sum(dpre, axis=0, keepdims=True), jnp.sum(dy * x, axis=0, keepdims=True), jnp.zeros((2, 128), F32)], axis=0)
            return 0

        lax.fori_loop(0, nv // 128, pair, 0)
        tt, ss = ii((Q, Q), 0), ii((Q, Q), 1)
        e64t = (ii((nv, 128), 0) // 64 == ii((nv, 128), 1)).astype(BF)
        kh, km, kl = split3(s["krow"][...])
        kterm = dnn(kh, e64t) + dnn(km, e64t) + dnn(kl, e64t)
        colg = jnp.concatenate([s["colg"][h, 0:1] for h in range(nh)] + [jnp.zeros((128 - nh, Q), F32)], axis=0)
        dcum = s["rowg"][...] - colg.T + s["rs"][...]
        da = tri_times((ss >= tt).astype(BF), dcum) + tri_times((ss < tt).astype(BF), s["gs"][...]) + kterm[0:1]
        rate = hp[1:2]
        dstep = s["ds"][...] + rate * da
        draw = dstep * sigmoid(raw)
        draw = jnp.where(ii((Q, 128), 1) < nh, draw, 0.0)
        low[pl.ds(r0, Q), pl.ds(nv + 256, 128)] = draw.astype(BF)
        gh[...] += jnp.concatenate([jnp.sum(draw, axis=0, keepdims=True), jnp.sum(da * step, axis=0, keepdims=True) * rate, jnp.zeros((6, 128), F32)], axis=0)
        dqk = s["dqk"][...]
        dc = dnn(dqk.astype(BF), s["b"][...]) + s["dcs"][...]
        db = dnn(dqk.T.astype(BF), s["c"][...]) + s["dbs"][...]
        sig = sigmoid(bc_pre)
        dpre = jnp.concatenate([db, dc], axis=1) * (sig + bc_pre * sig * (1.0 - sig))
        after2 = [None] + [jnp.concatenate([m, m], axis=1) for m in after[1:]]
        low[pl.ds(r0, Q), pl.ds(nv, 256)] = later_sum(dpre, s["halobc"][...], after2, cbc[...]).astype(BF)
        s["halobc"][...] = dpre[:8]
        gbc[...] += jnp.concatenate(
            [jnp.sum(dpre * bc_shifted[3 - k], axis=0, keepdims=True) for k in range(4)] + [jnp.sum(dpre, axis=0, keepdims=True), jnp.zeros((3, 256), F32)], axis=0)
        return 0

    lax.fori_loop(0, nb, block, 0)


def run_forward(nv, vals, segc, segr, cx, cbc, hp):
    sc = fwd_scratch(nv)
    names = list(sc)
    rows = vals.shape[0]

    def kernel(vals, segc, segr, cx, cbc, hp, ssd, states, *scr):
        ssd_forward(nv, vals, segc, segr, cx, cbc, hp, ssd, states, dict(zip(names, scr)))

    vm = pl.BlockSpec(memory_space=pltpu.VMEM)
    return pl.pallas_call(
        kernel, out_shape=(jax.ShapeDtypeStruct((rows, nv), F32), jax.ShapeDtypeStruct((rows // Q, 128, nv), F32)),
        in_specs=[vm] * 6, out_specs=[vm] * 2, scratch_shapes=[sc[n] for n in names],
        compiler_params=pltpu.CompilerParams(vmem_limit_bytes=60 * 2**20), name="scan_forward",
    )(vals, segc, segr, cx, cbc, hp)


def run_backward(nv, vals, segc, segr, cx, cbc, hp, dy, states):
    sc = bwd_scratch(nv)
    names = list(sc)
    rows = vals.shape[0]

    def kernel(vals, segc, segr, cx, cbc, hp, dy, states, low, gx, gbc, gh, *scr):
        ssd_backward(nv, vals, segc, segr, cx, cbc, hp, dy, states, low, gx, gbc, gh, dict(zip(names, scr)))

    vm = pl.BlockSpec(memory_space=pltpu.VMEM)
    outs = (jax.ShapeDtypeStruct((rows, nv + 384), BF), jax.ShapeDtypeStruct((8, nv), F32), jax.ShapeDtypeStruct((8, 256), F32), jax.ShapeDtypeStruct((8, 128), F32))
    return pl.pallas_call(
        kernel, out_shape=outs, in_specs=[vm] * 8, out_specs=[vm] * 4, scratch_shapes=[sc[n] for n in names],
        compiler_params=pltpu.CompilerParams(vmem_limit_bytes=60 * 2**20), name="scan_backward",
    )(vals, segc, segr, cx, cbc, hp, dy, states)


INNER = 3072
EPS = 1e-05


def at_step(step, events):
    for k, fn in events:

        @pl.when(step == k)
        def _(fn=fn):
            fn()


def forward_kernel(
    names, nv,
    hid, cot_own, w_own0, w_own1, w_own2, w_own3, pgain, segc, segr, cx, cbc, hp, ggain,
    o_w0, o_w1, o_w2, o_w3, o_nrm, o_cot, o_vals, o_states, o_no, o_lg, o_dy, o_gg,
    w0, w1, w2, w3, nrm, cot, vals, states, ssd, gate, gno, no, lg, dy, sums_own, sums_in,
    wsend, wrecv, tsend, trecv, ssend, srecv, lsem, *scan_scratch,
):
    s = dict(zip(names, scan_scratch))
    x, z, yh, t = place()
    yl, co = t // 2, t % 2
    tp, slots = tensor_peers()
    width = hid.shape[1]
    greet([dev(x, z, 1 - yh, t)] + [neighbour(a, d) for a in "xz" for d in (1, -1)] + tp)
    owns, dsts, outs = (w_own0, w_own1, w_own2, w_own3), (w0, w1, w2, w3), (o_w0, o_w1, o_w2, o_w3)
    groups = lambda ks: [Gather(owns[k], dsts[k], "xz"[k % 2], wsend.at[k], wrecv.at[k]) for k in ks]
    first, second = (0, 1), (2, 3)

    def step(ks, n):
        for g in groups(ks):
            g.step(n)

    def saved(i, src, dst):
        return pltpu.make_async_copy(src, dst, lsem.at[i])

    mine = pl.ds(pl.multiple_of(t * 256, 256), 256)
    theirs = pl.ds(pl.multiple_of(slots[1] * 256, 256), 256)

    def tensor_copies(i, own, dst):
        return (
            send(own, dst.at[mine], tsend.at[i, 0], trecv.at[i, 0], tp[1]),
            send(own, dst.at[mine], tsend.at[i, 1], trecv.at[i, 1], tp[0]),
            send(dst.at[theirs], dst.at[theirs], tsend.at[i, 2], trecv.at[i, 2], tp[0]),
        )

    for g in groups((0, 1, 2, 3)):
        g.begin()
    step(first, 0)

    def norm_rows(i, _):
        rows = pl.ds(pl.multiple_of(i * 64, 64), 64)
        h = hid[rows].astype(F32)
        inv = lax.rsqrt(jnp.mean(h * h, axis=1, keepdims=True) + EPS)
        nrm[pl.ds(pl.multiple_of(t * 256 + i * 64, 64), 64)] = (h * inv * pgain[0:1]).astype(BF)
        return 0

    lax.fori_loop(0, 4, norm_rows, 0)
    for k in range(4):
        g = groups((k,))[0]
        g.mine[...] = g.own[...]
    cot[mine] = cot_own[...]
    nrm_copies = tensor_copies(0, nrm.at[mine], nrm)
    cot_copies = tensor_copies(1, cot_own, cot)
    nrm_copies[0].start()
    nrm_copies[1].start()
    for n in (1, 4, 2, 3):
        step(first, n)
    cot_copies[0].start()
    cot_copies[1].start()
    step(second, 0)
    step(second, 1)
    step(first, 5)
    step(first, 6)
    nrm_copies[0].wait_recv()
    nrm_copies[2].start()
    step(second, 4)
    step(first, 7)
    nrm_copies[1].wait_recv()
    nrm_copies[2].wait_recv()

    def project(i, _):
        pl.when(i == 2)(lambda: step(second, 2))
        rows = pl.ds(pl.multiple_of(i * 256, 256), 256)
        n = nrm[rows]
        at = 0
        for w in (w0, w1):
            c = w.shape[1]
            vals[rows, at : at + c] = jnp.dot(n, w[...], preferred_element_type=F32)
            at += c
        return 0

    lax.fori_loop(0, 4, project, 0)
    early = [(0, w0, o_w0), (1, w1, o_w1), (2, nrm, o_nrm), (3, vals, o_vals)]
    for e in early:
        saved(*e).start()

    def cot_forward():
        cot_copies[0].wait_recv()
        cot_copies[2].start()

    events = [(1, lambda: step(second, 3)), (6, lambda: step(second, 5)), (10, lambda: step(second, 6)), (14, cot_forward)]
    ssd_forward(nv, vals, segc, segr, cx, cbc, hp, ssd, states, s, lambda at: at_step(at, events))
    step(second, 7)
    cot_copies[1].wait_recv()
    cot_copies[2].wait_recv()
    late = [(4, w2, o_w2), (5, w3, o_w3), (6, cot, o_cot), (7, states, o_states)]
    for e in late:
        saved(*e).start()

    def inner(i, _):
        rows = pl.ds(pl.multiple_of(i * 256, 256), 256)
        g = jnp.dot(nrm[rows], w2[...], preferred_element_type=F32)
        gate[rows] = g
        o = jnp.dot(cot[rows], w3[...], preferred_element_type=F32)
        gno[rows] = o
        gated = ssd[rows] * (g * sigmoid(g))
        sq = jnp.sum(gated * gated, axis=1, keepdims=True)
        cr = jnp.sum(o * ggain[0:1] * gated, axis=1, keepdims=True)
        lane = ii((256, 128), 1)
        both = jnp.where(lane == 0, sq, jnp.where(lane == 1, cr, 0.0))
        sums_own[:, rows] = both.T[:8]
        return 0

    lax.fori_loop(0, 4, inner, 0)
    small = [send(sums_own, sums_in.at[k], ssend.at[k], srecv.at[k], p) for k, p in enumerate(tp)]
    for c in small:
        c.start()
    for c in small:
        c.wait_recv()
    o_gg[...] = jnp.zeros_like(o_gg)

    def outer(i, _):
        rows = pl.ds(pl.multiple_of(i * 256, 256), 256)
        tot = sums_own[:, rows] + sums_in[0, :, rows] + sums_in[1, :, rows] + sums_in[2, :, rows]
        cols = jnp.concatenate([tot, jnp.zeros((120, 256), F32)], axis=0).T
        inv = lax.rsqrt(cols[:, 0:1] / INNER + EPS)
        cross = inv * inv * inv * cols[:, 1:2] / INNER
        for k in range(nv // 128):
            lanes = pl.ds(k * 128, 128)
            g, y, o, gain = gate[rows, lanes], ssd[rows, lanes], gno[rows, lanes], ggain[0:1, lanes]
            sig = sigmoid(g)
            silu = g * sig
            gated = y * silu
            scaled = gated * inv
            no[rows, lanes] = (scaled * gain).astype(BF)
            o_gg[0:1, lanes] += jnp.sum(o * scaled, axis=0, keepdims=True)
            grad = o * gain * inv - gated * cross
            dy[rows, lanes] = (grad * silu).astype(BF)
            lg[rows, lanes] = (grad * y * (sig + silu * (1.0 - sig))).astype(BF)
        return 0

    lax.fori_loop(0, 4, outer, 0)
    last = [(8, no, o_no), (9, lg, o_lg), (10, dy, o_dy)]
    for e in last:
        saved(*e).start()
    for g in groups((0, 1, 2, 3)):
        g.finish()
    for c in nrm_copies + cot_copies + tuple(small):
        c.wait_send()
    for e in early + late + last:
        saved(*e).wait()


def run_k1(hid, cot_own, w_owns, pgain, segc, segr, cx, cbc, hp, ggain):
    anys, vm = pl.BlockSpec(memory_space=pl.ANY), pl.BlockSpec(memory_space=pltpu.VMEM)
    nv = cx.shape[1]
    rows = segc.shape[0]
    d = hid.shape[1]
    sh = jax.ShapeDtypeStruct
    cols = [w.shape[1] for w in w_owns]
    nvals = cols[0] + cols[1]
    outs = [sh((d, c), BF) for c in cols] + [sh((rows, d), BF)] * 2 + [sh((rows, nvals), F32), sh((rows // Q, 128, nv), BF)] + [sh((rows, nv), BF)] * 3 + [sh((8, nv), F32)]
    V = lambda shape, dt: pltpu.VMEM(shape, dt)
    D = pltpu.SemaphoreType.DMA
    scan = fwd_scratch(nv)
    scratch = [V((d, c), BF) for c in cols] + [V((rows, d), BF)] * 2 + [V((rows, nvals), F32), V((rows // Q, 128, nv), BF)] + [V((rows, nv), F32)] * 3 + [V((rows, nv), BF)] * 3
    scratch += [V((8, rows), F32), V((3, 8, rows), F32), D((4, Gather.N)), D((4, Gather.N)), D((2, 3)), D((2, 3)), D((3,)), D((3,)), D((11,))]
    scratch += list(scan.values())
    return pl.pallas_call(
        functools.partial(forward_kernel, list(scan), nv), out_shape=outs, in_specs=[vm] * 13, out_specs=[anys] * 11 + [vm], scratch_shapes=scratch,
        compiler_params=pltpu.CompilerParams(collective_id=0, has_side_effects=True, vmem_limit_bytes=62 * 2**20), name="forward_all",
    )(hid, cot_own, *w_owns, pgain, segc, segr, cx, cbc, hp, ggain)


class Scatter:
    N = 13

    def __init__(self, v, bufs, out, a1, send_sem, recv_sem):
        x, z, yh, t = place()
        self.v, self.out, self.a1, self.yh = v, out, a1, yh
        self.r1, self.r2, self.q1, self.q2, self.kk, self.yy = bufs
        self.h = self.r2.at[0]
        a2 = "z" if a1 == "x" else "x"
        self.p, self.q = (x, z) if a1 == "x" else (z, x)
        self.send_sem, self.recv_sem = send_sem, recv_sem
        right1, left1, right2, left2 = neighbour(a1, 1), neighbour(a1, -1), neighbour(a2, 1), neighbour(a2, -1)
        r1, r2, h, q1, q2, q = self.r1, self.r2, self.h, self.q1, self.q2, self.q
        self.plan = [
            (self.half(2, 0), r1.at[0], right1), (self.half(2, 1), r1.at[1], left1),
            (self.half(1, 1), r2.at[0, pl.ds(2, 2)], right1), (self.half(-1, 0), r2.at[1, pl.ds(0, 2)], left1),
            (self.half(1, 0), r2.at[0, pl.ds(0, 2)], right1), (self.half(-1, 1), r2.at[1, pl.ds(2, 2)], left1),
            (h.at[m4(q + 2), 0], q1.at[0], right2), (h.at[m4(q + 2), 1], q1.at[1], left2),
            (h.at[m4(q + 1), 1], q2.at[0, 1], right2), (h.at[m4(q - 1), 0], q2.at[1, 0], left2),
            (h.at[m4(q + 1), 0], q2.at[0, 0], right2), (h.at[m4(q - 1), 1], q2.at[1, 1], left2),
            (self.kk, self.yy, dev(x, z, 1 - yh, t)),
        ]

    def half(self, d, k):
        at = m4(self.p + d)
        return self.v.at[pl.ds(2 * k, 2), at] if self.a1 == "z" else self.v.at[at, pl.ds(2 * k, 2)]

    def copy(self, k):
        src, dst, to = self.plan[k]
        return send(src, dst, self.send_sem.at[k], self.recv_sem.at[k], to)

    def start(self, *ks):
        for k in ks:
            self.copy(k).start()

    def arrive(self, *ks):
        for k in ks:
            self.copy(k).wait_recv()

    def step(self, n):
        v, r1, r2, h, q1, q2, p, q, yh = self.v, self.r1, self.r2, self.h, self.q1, self.q2, self.p, self.q, self.yh
        if n == 0:
            self.start(0, 1, 2, 3)
        elif n == 1:
            for side, d in ((0, 1), (1, -1)):
                self.arrive(side)
                at = m4(p + d)

                def add(j, _, side=side, at=at):
                    e, y = j // 2, j % 2
                    ix = (2 * side + e, at, y) if self.a1 == "z" else (at, 2 * side + e, y)
                    v[ix] = (v[ix].astype(F32) + r1[side, e, y].astype(F32)).astype(BF)
                    return 0

                lax.fori_loop(0, 4, add, 0)
                self.start(4 + side)
        elif n == 2:
            self.arrive(2, 3, 4, 5)

            def add(j, _):
                e, y = j // 2, j % 2
                own = v[e, p, y] if self.a1 == "z" else v[p, e, y]
                h[e, y] = (own.astype(F32) + r2[0, e, y].astype(F32) + r2[1, e, y].astype(F32)).astype(BF)
                return 0

            lax.fori_loop(0, 8, add, 0)
            self.start(6, 7, 8, 9)
        elif n == 3:
            for side, d in ((0, 1), (1, -1)):
                self.arrive(6 + side)
                at = m4(q + d)
                h[at, side] = (h[at, side].astype(F32) + q1[side].astype(F32)).astype(BF)
                self.start(10 + side)
        elif n == 4:
            self.arrive(8, 9, 10, 11)
            self.kk[...] = (h[q, 1 - yh].astype(F32) + q2[0, 1 - yh].astype(F32) + q2[1, 1 - yh].astype(F32)).astype(BF)
            self.start(12)
        else:
            self.arrive(12)
            self.out[...] = h[q, yh].astype(F32) + q2[0, yh].astype(F32) + q2[1, yh].astype(F32) + self.yy[...].astype(F32)

    def finish(self):
        for k in range(self.N):
            self.copy(k).wait_send()


class TokenScatter:
    def __init__(self, v, from_core, from_chip, out, send_sem, recv_sem):
        t = place()[3]
        tp, slots = tensor_peers()
        self.t, self.v, self.from_core, self.from_chip, self.out = t, v, from_core, from_chip, out
        rows = lambda s: pl.ds(pl.multiple_of(s * 256, 256), 256)
        self.pass_on, self.mine = slots[1], rows(t)
        self.copies = lambda k: (
            lambda: send(v.at[rows(slots[2])], from_core.at[0], send_sem.at[0], recv_sem.at[0], tp[0]),
            lambda: send(v.at[rows(slots[0])], from_core.at[1], send_sem.at[1], recv_sem.at[1], tp[0]),
            lambda: send(v.at[rows(slots[1])], from_chip, send_sem.at[2], recv_sem.at[2], tp[1]),
        )[k]()

    def step(self, n):
        if n == 0:
            self.copies(0).start()
            self.copies(1).start()
        elif n == 1:
            self.copies(0).wait_recv()

            def add(j, _):
                rows = pl.ds(pl.multiple_of(j * 32, 32), 32)
                own = pl.ds(pl.multiple_of(self.pass_on * 256 + j * 32, 32), 32)
                self.v[own] = (self.v[own].astype(F32) + self.from_core[0, rows].astype(F32)).astype(BF)
                return 0

            lax.fori_loop(0, 8, add, 0)
            self.copies(2).start()
        else:
            self.copies(1).wait_recv()
            self.copies(2).wait_recv()

            def add(j, _):
                rows = pl.ds(pl.multiple_of(j * 32, 32), 32)
                own = self.v[pl.ds(pl.multiple_of(self.t * 256 + j * 32, 32), 32)]
                self.out[rows] = own.astype(F32) + self.from_core[1, rows].astype(F32) + self.from_chip[rows].astype(F32)
                return 0

            lax.fori_loop(0, 8, add, 0)

    def finish(self):
        for k in range(3):
            self.copies(k).wait_send()


def backward_kernel(
    names, nv,
    h_w0, h_w1, h_w2, h_w3, h_nrm, h_cot, h_vals, h_states, h_no, h_lg, h_dy, pgain, segc, segr, cx, cbc, hp, gg,
    o_gate, o_out, o_x0, o_x1, o_bc, o_own, o_grad, o_small,
    w0, w1, w23, nrm, cot, vals, states, nody, lg, low, po, t_gate, t_out, t_x0, t_x1,
    own_v, sx, sz, sy, st, sacc, bct, fc0, ch0, fc1, ch1, gx, gbc, gh, pre,
    wsend, wrecv, tsend, trecv, ssend, srecv, bsend, brecv, lsem, *rest,
):
    bufs, s = [rest[6 * k : 6 * k + 6] for k in range(4)], dict(zip(names, rest[24:]))
    x, z, yh, t = place()
    tp, slots = tensor_peers()
    loads = [
        pltpu.make_async_copy(a, b, lsem.at[k])
        for k, (a, b) in enumerate(((h_no, nody), (h_w3, w23), (h_cot, cot), (h_nrm, nrm), (h_lg, lg), (h_vals, vals), (h_states, states), (h_w0, w0), (h_w1, w1)))
    ]
    for c in loads:
        c.start()
    load_dy, load_w2 = pltpu.make_async_copy(h_dy, nody, lsem.at[9]), pltpu.make_async_copy(h_w2, w23, lsem.at[10])
    greet([dev(x, z, 1 - yh, t)] + [neighbour(a, d) for a in "xz" for d in (1, 2, 3)] + tp)
    scat = [
        Scatter(v, bufs[k], o, a1, wsend.at[k], wrecv.at[k])
        for k, (v, o, a1) in enumerate(((t_out, o_out, "x"), (t_gate, o_gate, "z"), (t_x0, o_x0, "x"), (t_x1, o_x1, "z")))
    ]
    s_out, s_gate, s_x0, s_x1 = scat
    k_out = TokenScatter(po, fc0, ch0, o_own, tsend.at[0], trecv.at[0])
    k_nrm = TokenScatter(cot, fc1, ch1, o_grad, tsend.at[1], trecv.at[1])

    def by_rows(fn):
        def body(i, _):
            fn(pl.ds(pl.multiple_of(i * 256, 256), 256))
            return 0

        lax.fori_loop(0, 4, body, 0)

    def outer_product(dst, left, right):
        def body(i, _):
            cols = pl.ds(pl.multiple_of(i * 384, 384), 384)
            r = lax.dot_general(left[:, cols], right[...], (((0,), (0,)), ((), ())), preferred_element_type=F32)
            dst[i] = r.astype(BF).reshape(dst.shape[1:])
            return 0

        lax.fori_loop(0, 4, body, 0)

    for k in (0, 1):
        loads[k].wait()

    def out_rows(rows):
        left = nody[rows]
        for k in range(0, po.shape[1], 512):
            po[rows, k : k + 512] = dnt(left, w23[k : k + 512]).astype(BF)

    by_rows(out_rows)
    load_w2.start()
    k_out.step(0)
    loads[2].wait()
    outer_product(t_out, cot, nody)
    load_dy.start()
    s_out.step(0)
    k_out.step(1)
    loads[3].wait()
    loads[4].wait()
    outer_product(t_gate, nrm, lg)
    s_gate.step(0)
    for k in (5, 6, 7, 8):
        loads[k].wait()
    load_dy.wait()
    both = lambda n: lambda: (s_out.step(n), s_gate.step(n))
    events = [(6, both(1)), (12, both(2)), (16, both(3)), (18, both(4)), (20, both(5)), (22, lambda: k_out.step(2))]
    ssd_backward(nv, vals, segc, segr, cx, cbc, hp, nody, states, low, gx, gbc, gh, s, lambda at: at_step(at, events))
    load_w2.wait()
    pre[...] = jnp.zeros_like(pre)
    c0 = w0.shape[1]

    def grad_rows(rows):
        for k in range(0, cot.shape[1], 512):
            cols = slice(k, k + 512)
            g = dnt(lg[rows], w23[cols]) + dnt(low[rows, :c0], w0[cols]) + dnt(low[rows, c0:], w1[cols])
            pre[0:1, cols] += jnp.sum(g * nrm[rows, cols].astype(F32), axis=0, keepdims=True)
            cot[rows, cols] = g.astype(BF)

    by_rows(grad_rows)
    k_nrm.step(0)
    outer_product(t_x0, nrm, low.at[:, :c0])
    s_x0.step(0)
    k_nrm.step(1)
    own_v[...] = jnp.zeros_like(own_v)
    own_v[0:6] = gx[0:6]
    own_v[6:7] = gg[0:1]
    pv = pre[0:1] / pgain[0:1]
    own_v[7:8], own_v[8:9] = pv[:, :nv], pv[:, nv:]
    for k in range(3):
        own_v[9:10, k * 256 : k * 256 + 256] = gbc[k : k + 1]
    for k in range(2):
        own_v[10:11, k * 256 : k * 256 + 256] = gbc[3 + k : 4 + k]
        own_v[11:12, k * 128 : k * 128 + 128] = gh[k : k + 1]
    small = [send(own_v, sx.at[d - 1], ssend.at[d - 1], srecv.at[d - 1], neighbour("x", d)) for d in (1, 2, 3)]
    for c in small:
        c.start()
    outer_product(t_x1, nrm, low.at[:, c0:])
    s_x1.step(0)
    last = lambda n: (s_x0.step(n), s_x1.step(n))

    def next_small(have, total, copies):
        for c in have:
            c.wait_recv()
        total()
        for c in copies:
            c.start()
        return copies

    def total_x():
        sacc[0] = own_v[...] + sx[0] + sx[1] + sx[2]

    def total_z():
        sacc[1] = sacc[0] + sz[0] + sz[1] + sz[2]

    def total_y():
        sacc[2] = sacc[1] + sy[...]

    small_z = next_small(small, total_x, [send(sacc.at[0], sz.at[d - 1], ssend.at[2 + d], srecv.at[2 + d], neighbour("z", d)) for d in (1, 2, 3)])
    last(1)
    small_y = next_small(small_z, total_z, [send(sacc.at[1], sy, ssend.at[6], srecv.at[6], dev(x, z, 1 - yh, t))])
    last(2)
    small_t = next_small(small_y, total_y, [send(sacc.at[2], st.at[k], ssend.at[7 + k], srecv.at[7 + k], p) for k, p in enumerate(tp)])
    k_nrm.step(2)
    last(3)
    last(4)
    s_x1.step(5)
    bc0 = o_x1.shape[1] - 384
    bct[3] = o_x1[:, bc0 : bc0 + 256]
    bcs = [send(bct.at[3], bct.at[k], bsend.at[k], brecv.at[k], p) for k, p in enumerate(tp)]
    for c in bcs:
        c.start()
    s_x0.step(5)
    for c in small_t:
        c.wait_recv()
    o_small[t] = sacc[2]
    for k in range(3):
        o_small[slots[k]] = st[k]
    for c in bcs:
        c.wait_recv()
    o_bc[...] = bct[3] + bct[0] + bct[1] + bct[2]
    for c in small + small_z + small_y + small_t + bcs:
        c.wait_send()
    for g in scat + [k_out, k_nrm]:
        g.finish()


def run_k2(ws, nrm, cot, vals, states, no, lg, dy, pgain, segc, segr, cx, cbc, hp, gg):
    anys, vm = pl.BlockSpec(memory_space=pl.ANY), pl.BlockSpec(memory_space=pltpu.VMEM)
    nv = cx.shape[1]
    rows, d = nrm.shape
    sh = lambda *s: jax.ShapeDtypeStruct(s, F32)
    cols = [w.shape[1] for w in ws]
    n = d // 32
    V = lambda *s, dt=BF: pltpu.VMEM(s, dt)
    D = pltpu.SemaphoreType.DMA
    outs = [sh(n, cols[2]), sh(n, cols[3]), sh(n, cols[0]), sh(n, cols[1]), sh(n, 256), sh(256, d), sh(256, d), sh(4, 16, nv)]
    term = lambda c: V(4, 4, 2, n, c)
    scratch = [V(d, cols[0]), V(d, cols[1]), V(d, cols[2]), V(rows, d), V(rows, d), V(*vals.shape, dt=F32), V(*states.shape), V(rows, nv), V(rows, nv), V(*vals.shape), V(rows, d)]
    scratch += [term(cols[2]), term(cols[3]), term(cols[0]), term(cols[1])]
    sv = (16, nv)
    scratch += [V(*sv, dt=F32), V(3, *sv, dt=F32), V(3, *sv, dt=F32), V(*sv, dt=F32), V(3, *sv, dt=F32), V(3, *sv, dt=F32), V(4, n, 256, dt=F32)]
    scratch += [V(2, 256, d), V(256, d)] * 2
    scratch += [V(8, nv, dt=F32), V(8, 256, dt=F32), V(8, 128, dt=F32), V(8, d, dt=F32)]
    scratch += [D((4, Scatter.N))] * 2 + [D((2, 3))] * 2 + [D((10,))] * 2 + [D((3,))] * 2 + [D((11,))]
    for c in (cols[3], cols[2], cols[0], cols[1]):
        scratch += [V(2, 2, 2, n, c), V(2, 4, 2, n, c), V(2, n, c), V(2, 2, n, c), V(n, c), V(n, c)]
    scan = bwd_scratch(nv)
    scratch += list(scan.values())
    return pl.pallas_call(
        functools.partial(backward_kernel, list(scan), nv), out_shape=outs, in_specs=[anys] * 11 + [vm] * 7, out_specs=[vm] * 8, scratch_shapes=scratch,
        compiler_params=pltpu.CompilerParams(collective_id=1, has_side_effects=True, vmem_limit_bytes=64 * 2**20), name="backward_all",
    )(*ws, nrm, cot, vals, states, no, lg, dy, pgain, segc, segr, cx, cbc, hp, gg)


def dot_nt(left, right):
    return lax.dot_general(left, right, (((1,), (1,)), ((), ())), preferred_element_type=F32)


def dot_tn(left, right):
    return lax.dot_general(left, right, (((0,), (0,)), ((), ())), preferred_element_type=F32)


def per_device(
    hidden_in, seg_ids, pre_gain, proj_gate, proj_x, proj_bc, proj_dt, conv_x, conv_bias_x, conv_bc, conv_bias_bc,
    dt_bias, a_log, skip_d, gate_gain, proj_out, cotangent,
):
    t = lax.axis_index("tensor")
    inner = proj_gate.shape[1]
    heads = proj_dt.shape[1]
    own = lambda v, n: lax.dynamic_slice_in_dim(v, t * n, n, v.ndim - 1)
    gain_dev = own(gate_gain, inner)
    hidden = hidden_in.astype(F32)
    inv_rms = lax.rsqrt(jnp.mean(hidden * hidden, axis=1) + EPS)
    rows = proj_x.shape[0]
    cut = inner - 128
    w_owns = (
        proj_x[:, :cut],
        jnp.concatenate([proj_x[:, cut:], proj_bc, proj_dt, jnp.zeros((rows, 128 - heads), BF)], axis=1),
        proj_gate,
        proj_out.T,
    )
    seg = seg_ids.astype(F32)
    segc = jnp.broadcast_to(seg[:, None], (seg.shape[0], 128))
    segr = jnp.broadcast_to(seg[None, :], (8, seg.shape[0]))
    heads_row = lambda v: jnp.pad(own(v, heads), (0, 128 - heads))[None]
    skip_row = jnp.broadcast_to(own(skip_d, heads)[:, None], (heads, 64)).reshape(1, inner)
    cx = jnp.concatenate([own(conv_x, inner), own(conv_bias_x, inner)[None], skip_row, jnp.zeros((2, inner), F32)])
    cbc = jnp.concatenate([conv_bc, conv_bias_bc[None], jnp.zeros((3, 256), F32)])
    hp = jnp.concatenate([heads_row(dt_bias), -jnp.exp(heads_row(a_log)), jnp.zeros((6, 128), F32)])
    spread8 = lambda v: jnp.broadcast_to(v[None, :], (8, v.shape[0]))
    w0, w1, w_gate, w_out, normed_all, cot_all, vals, states, normed_out, low_gate, dy, gg = run_k1(
        hidden_in, cotangent, w_owns, spread8(pre_gain), segc, segr, cx, cbc, hp, spread8(gain_dev)
    )
    r_gate, r_out, r_x0, r_x1, d_bc, own_out, grad_own, smalls = run_k2(
        (w0, w1, w_gate, w_out), normed_all, cot_all, vals, states, normed_out, low_gate, dy, spread8(pre_gain), segc, segr, cx, cbc, hp, gg
    )
    output = (hidden + own_out).astype(BF)
    scaled = grad_own * pre_gain[None, :]
    proj = jnp.mean(scaled * hidden, axis=1)
    grad_hidden = cotangent.astype(F32) + scaled * inv_rms[:, None] - hidden * (inv_rms * inv_rms * inv_rms * proj)[:, None]
    across = lambda i, k=1: smalls[:, i : i + k].transpose(1, 0, 2).reshape(k, -1)
    d_skip = across(5).reshape(-1, 64).sum(axis=1)
    both = jnp.sum(smalls[:, 7:11], axis=0)
    taps = both[2:4].reshape(2, 3, 256)
    d_conv_bc = jnp.concatenate([taps[0], taps[1, :1]])
    per_head = lambda i: smalls[:, 11, 128 * i : 128 * i + heads].reshape(-1)
    return (
        output, grad_hidden, both[:2].reshape(-1), r_gate, jnp.concatenate([r_x0, r_x1[:, : inner - cut]], axis=1), d_bc,
        r_x1[:, inner - cut + 256 : inner - cut + 256 + heads],
        across(0, 4), across(4)[0], d_conv_bc, taps[1, 1], per_head(0), per_head(1), d_skip, across(6)[0],
        r_out.T,
    )


def solution(mesh):
    tok = P(("dp", "tensor"), None)
    mat = P("dp", "tensor")
    in_specs = (tok, P("dp"), P(), mat, mat, P("dp", None), mat) + (P(),) * 8 + (P("tensor", "dp"), tok)
    out_specs = (tok, tok, P(), mat, mat, P("dp", None), mat) + (P(),) * 8 + (P("tensor", "dp"),)
    return jax.shard_map(per_device, mesh=mesh, in_specs=in_specs, out_specs=out_specs, check_vma=False)
```

```python
import functools

import jax
import jax.numpy as jnp
from jax import lax
from jax.experimental import pallas as pl
from jax.experimental.pallas import tpu as pltpu
from jax.sharding import PartitionSpec as P

MESH = pl.DeviceIdType.MESH
F32 = jnp.float32
BF = jnp.bfloat16


def place():
    dp = lax.axis_index("dp")
    t = lax.axis_index("tensor")
    return dp // 8, (dp // 2) % 4, dp % 2, t


def dev(x, z, yh, t):
    return ((x * 4 + z) * 2 + yh, t)


def m4(v):
    return (v + 8) % 4


def neighbour(axis, d):
    x, z, yh, t = place()
    return dev(m4(x + d), z, yh, t) if axis == "x" else dev(x, m4(z + d), yh, t)


def tensor_peers():
    x, z, yh, t = place()
    yl, co = t // 2, t % 2
    slots = (yl * 2 + 1 - co, (1 - yl) * 2 + co, (1 - yl) * 2 + 1 - co)
    return [dev(x, z, yh, s) for s in slots], slots


def greet(peers):
    bar = pltpu.get_barrier_semaphore()
    for p in peers:
        pl.semaphore_signal(bar, inc=1, device_id=p, device_id_type=MESH)
    pl.semaphore_wait(bar, len(peers))


def send(src, dst, send_sem, recv_sem, to):
    return pltpu.make_async_remote_copy(
        src_ref=src, dst_ref=dst, send_sem=send_sem, recv_sem=recv_sem, device_id=to, device_id_type=MESH
    )


class Gather:
    N = 25

    def __init__(self, own, dst, r1, send_sem, recv_sem):
        x, z, yh, _ = place()
        r2 = "z" if r1 == "x" else "x"
        n = own.shape[0]

        def rows(d1, d2, y=None):
            ix, iz = (m4(x + d1), m4(z + d2)) if r1 == "x" else (m4(x + d2), m4(z + d1))
            first = (ix * 4 + iz) * 2
            if y is None:
                return dst.at[pl.ds(pl.multiple_of(first * n, n), 2 * n)]
            return dst.at[pl.ds(pl.multiple_of((first + y) * n, n), n)]

        self.mine = rows(0, 0, yh)
        self.own = own
        near1, near2 = [neighbour(r1, 1), neighbour(r1, -1)], [neighbour(r2, 1), neighbour(r2, -1)]
        other = rows(0, 0, 1 - yh)
        plan = [(own, self.mine, dev(x, z, 1 - yh, place()[3]))]
        plan += [(own, self.mine, p) for p in near1 + near2]
        plan += [(other, other, p) for p in near1 + near2]
        plan += [(rows(-1, 0, 0),) * 2 + (near1[0],), (rows(1, 0, 1),) * 2 + (near1[1],)]
        for d1 in (-1, 1, 2):
            plan += [(rows(d1, 0),) * 2 + (p,) for p in near2]
        for d1 in (0, -1, 1, 2):
            plan += [(rows(d1, -1, 0),) * 2 + (near2[0],), (rows(d1, 1, 1),) * 2 + (near2[1],)]
        self.plan, self.send_sem, self.recv_sem = plan, send_sem, recv_sem

    def copy(self, k):
        src, dst, to = self.plan[k]
        return send(src, dst, self.send_sem.at[k], self.recv_sem.at[k], to)

    STEPS = (
        ((), (1, 2, 3, 4)),
        ((0,), (5, 6, 7, 8)),
        ((1, 2, 5, 6), (9, 10, 11, 12, 13, 14)),
        ((9, 10), (15, 16)),
        ((3, 4, 7, 8), (17, 18)),
        ((11, 12, 13, 14), (19, 20, 21, 22)),
        ((15, 16), (23, 24)),
        ((17, 18, 19, 20, 21, 22, 23, 24), ()),
    )

    def begin(self):
        self.copy(0).start()

    def step(self, k):
        arrive, go = self.STEPS[k]
        for i in arrive:
            self.copy(i).wait_recv()
        for i in go:
            self.copy(i).start()

    def finish(self):
        for k in range(self.N):
            self.copy(k).wait_send()


Q = 256
LOG2E = 1.4426950408889634
NEG = -1e30


def dnn(a, b):
    return jnp.dot(a, b, preferred_element_type=F32)


def dnt(a, b):
    return lax.dot_general(a, b, (((1,), (1,)), ((), ())), preferred_element_type=F32)


def split3(v):
    hi = v.astype(BF)
    r = v - hi.astype(F32)
    mid = r.astype(BF)
    lo = (r - mid.astype(F32)).astype(BF)
    return hi, mid, lo


def spread3(v, mat):
    hi, mid, lo = split3(v)
    return dnn(jnp.concatenate([hi, mid, lo], axis=1), jnp.concatenate([mat, mat, mat], axis=0))


def tri_times(mat, v):
    hi, mid, lo = split3(v)
    out = dnn(mat, jnp.concatenate([hi, mid, lo], axis=1))
    w = v.shape[1]
    return out[:, :w] + out[:, w : 2 * w] + out[:, 2 * w :]


def ii(shape, dim):
    return lax.broadcasted_iota(jnp.int32, shape, dim)


def sigmoid(v):
    return 1.0 / (1.0 + jnp.exp2(v * -LOG2E))


def softplus(v):
    e = jnp.exp2(jnp.abs(v) * -LOG2E)
    u = 1.0 + e
    log1p = jnp.where(u == 1.0, e, jnp.log(u) * (e / jnp.where(u == 1.0, 1.0, u - 1.0)))
    return jnp.maximum(v, 0.0) + log1p


def conv_terms(ext, match, taps):
    n = ext.shape[0] - 8
    shifted = [ext[8:]] + [jnp.where(match[k], ext[8 - k : 8 + n - k], 0.0) for k in (1, 2, 3)]
    pre = taps[4:5] + sum(taps[3 - k : 4 - k] * shifted[k] for k in range(4))
    return pre, shifted


def with_earlier(ref, r0, lanes):
    prev = ref[pl.ds(pl.multiple_of(jnp.maximum(r0 - 8, 0), 8), 8), lanes]
    return jnp.concatenate([prev, ref[pl.ds(r0, Q), lanes]], axis=0)


def match_rows(segc, r0):
    prev = segc[pl.ds(pl.multiple_of(jnp.maximum(r0 - 8, 0), 8), 8), :]
    prev = jnp.where(r0 > 0, prev, -1.0)
    cur = segc[pl.ds(r0, Q), :]
    ext = jnp.concatenate([prev, cur], axis=0)
    return [None] + [ext[8 - k : 8 + Q - k] == cur for k in (1, 2, 3)]


def block_setup(c, nv, vals, segc, segr, cbc, hp, bt_ref, b_ref, c_ref, ct_ref, qk_ref, bias_ref, cum_ref, cumt_ref, step_ref, tail_ref, keep_ref, ex_ref, keep_out):
    r0 = pl.multiple_of(c * Q, Q)
    match = match_rows(segc, r0)
    m2 = [None] + [jnp.concatenate([m, m], axis=1) for m in match[1:]]
    ext = with_earlier(vals, r0, pl.ds(nv, 256))
    pre, shifted = conv_terms(ext, m2, cbc[...])
    bc = pre * sigmoid(pre)
    bb = bc[:, :128].astype(BF)
    cc = bc[:, 128:].astype(BF)
    b_ref[...] = bb
    c_ref[...] = cc
    bt_ref[...] = bc[:, :128].T.astype(BF)
    if ct_ref is not None:
        ct_ref[...] = bc[:, 128:].T.astype(BF)
    qk_ref[...] = dnt(cc, bb)
    seg = segc[pl.ds(r0, Q), :]
    segs = segr[0:1, pl.ds(r0, Q)]
    tt, ss = ii((Q, Q), 0), ii((Q, Q), 1)
    allowed = (tt >= ss) & (jnp.concatenate([seg, seg], axis=1) == segs)
    bias_ref[...] = jnp.where(allowed, 0.0, NEG)
    raw = vals[pl.ds(r0, Q), pl.ds(nv + 256, 128)] + hp[0:1]
    step = softplus(raw)
    tri = (tt >= ss).astype(BF)
    cum = tri_times(tri, step * (hp[1:2] * LOG2E))
    cumt = cum.T
    for h in range(nv // 64):
        cumt_ref[h] = jnp.broadcast_to(cumt[h : h + 1], (8, Q))
    exm = ex_ref[...]
    cum_ref[...] = spread3(cum, exm)
    e64 = (ii((128, nv), 0) == ii((128, nv), 1) // 64).astype(BF)
    step_ref[...] = spread3(step, e64)
    prev_seg = jnp.where(c > 0, segc[pl.ds(pl.multiple_of(jnp.maximum(r0 - 8, 0), 8), 8), :][7:8], -1.0)
    last_seg = seg[Q - 1 :]
    cum_last = cum[Q - 1 :]
    carry = (seg == prev_seg).astype(F32)
    tailm = (seg == last_seg).astype(F32)
    tail = jnp.exp2(cum_last - cum) * tailm
    tail_ref[...] = spread3(tail, e64)
    keep = jnp.exp2(cum_last) * (last_seg == prev_seg).astype(F32)
    keep_ref[...] = spread3(jnp.broadcast_to(keep, (8, 128)), e64)
    keep_out[...] = spread3(jnp.exp2(cum) * carry, e64)
    return match, pre, shifted, raw, step


def decay(cum_ref, cumt_ref, bias_ref, h, rows, cols):
    col = cum_ref[rows, pl.ds(pl.multiple_of(h * 128, 128), 128)]
    row = cumt_ref[h, 0:1, cols]
    return jnp.exp2(col - row + bias_ref[rows, cols])


def fwd_scratch(nv):
    V = lambda s, d=F32: pltpu.VMEM(s, d)
    nh = nv // 64
    return dict(
        bt=V((128, Q), BF), b=V((Q, 128), BF), c=V((Q, 128), BF), qk=V((Q, Q)), bias=V((Q, Q)), cum=V((Q, nh * 128)), cumt=V((nh, 8, Q)),
        step=V((Q, nv)), tail=V((Q, nv)), keep=V((8, nv)), ecum=V((Q, nv)), ex=V((128, nh * 128), BF), state=V((128, nv)), m=V((2, Q, Q), BF),
    )


def ssd_forward(nv, vals, segc, segr, cx, cbc, hp, ssd, states, s, hook=lambda at: None):
    nh = nv // 64
    s["ex"][...] = (ii((128, nh * 128), 0) == ii((128, nh * 128), 1) // 128).astype(BF)
    s["state"][...] = jnp.zeros_like(s["state"])
    s["m"][...] = jnp.zeros_like(s["m"])

    def block(c, _):
        r0 = pl.multiple_of(c * Q, Q)
        match, *_r = block_setup(c, nv, vals, segc, segr, cbc, hp, s["bt"], s["b"], s["c"], None, s["qk"], s["bias"], s["cum"], s["cumt"], s["step"], s["tail"], s["keep"], s["ex"], s["ecum"])
        states[c] = s["state"][...].astype(BF)

        def pair(j, _):
            hook(c * (nv // 128) + j)
            lanes = pl.ds(pl.multiple_of(j * 128, 128), 128)
            pre, _sh = conv_terms(with_earlier(vals, r0, lanes), match, cx[:, lanes])
            x = pre * sigmoid(pre)
            u = x * s["step"][:, lanes]
            ub = u.astype(BF)
            st = s["state"][:, lanes]
            y = dnn(s["c"][...], st.astype(BF)) * s["ecum"][:, lanes]
            y = y + cx[5:6, lanes] * x
            for e in range(2):
                for r in range(4):
                    rows = slice(r * 64, r * 64 + 64)
                    for k in range(1 if r < 2 else 2):
                        cols = slice(k * 128, k * 128 + 128)
                        s["m"][e, rows, cols] = (decay(s["cum"], s["cumt"], s["bias"], 2 * j + e, rows, cols) * s["qk"][rows, cols]).astype(BF)
            y0 = dnn(s["m"][0], ub)
            y1 = dnn(s["m"][1], ub)
            ssd[pl.ds(r0, Q), lanes] = y + jnp.where(ii((Q, 128), 1) < 64, y0, y1)
            s["state"][:, lanes] = st * s["keep"][0:1, lanes] + dnn(s["bt"][...], (u * s["tail"][:, lanes]).astype(BF))
            return 0

        lax.fori_loop(0, nv // 128, pair, 0)
        return 0

    lax.fori_loop(0, vals.shape[0] // Q, block, 0)


def bwd_scratch(nv):
    V = lambda s, d=F32: pltpu.VMEM(s, d)
    d = fwd_scratch(nv)
    d.update(ct=V((128, Q), BF), dqk=V((Q, Q)), dstate=V((128, nv)), dcs=V((Q, 128)), dbs=V((Q, 128)), rowg=V((Q, 128)), colg=V((nv // 64, 8, Q)), rs=V((Q, 128)),
             gs=V((Q, 128)), ds=V((Q, 128)), krow=V((8, nv)), halo=V((8, nv)), halobc=V((8, 256)), dm=V((Q, Q)))
    return d


def to_head(v, j):
    red = (ii((128, 128), 1) == 2 * j + ii((128, 128), 0) // 64).astype(BF)
    hi = v.astype(BF)
    lo = (v - hi.astype(F32)).astype(BF)
    return dnn(jnp.concatenate([hi, lo], axis=1), jnp.concatenate([red, red], axis=0))


def later_sum(dpre, halo, match_ext, taps):
    ext = jnp.concatenate([dpre, halo], axis=0)
    n = dpre.shape[0]
    out = taps[3:4] * dpre
    for k in (1, 2, 3):
        out = out + taps[3 - k : 4 - k] * jnp.where(match_ext[k], ext[k : n + k], 0.0)
    return out


def ssd_backward(nv, vals, segc, segr, cx, cbc, hp, dy_ref, states, low, gx, gbc, gh, s, hook=lambda at: None):
    nh = nv // 64
    nb = vals.shape[0] // Q
    s["ex"][...] = (ii((128, nh * 128), 0) == ii((128, nh * 128), 1) // 128).astype(BF)
    for n in ("dstate", "halo", "halobc", "colg", "m"):
        s[n][...] = jnp.zeros_like(s[n])
    gx[...] = jnp.zeros_like(gx)
    gbc[...] = jnp.zeros_like(gbc)
    gh[...] = jnp.zeros_like(gh)

    def block(i, _):
        c = nb - 1 - i
        r0 = pl.multiple_of(c * Q, Q)
        match, bc_pre, bc_shifted, raw, step = block_setup(c, nv, vals, segc, segr, cbc, hp, s["bt"], s["b"], s["c"], s["ct"], s["qk"], s["bias"], s["cum"], s["cumt"], s["step"], s["tail"], s["keep"], s["ex"], s["ecum"])
        nxt = segc[pl.ds(pl.multiple_of(jnp.minimum(r0 + Q, segc.shape[0] - 8), 8), 8), :]
        seg = segc[pl.ds(r0, Q), :]
        ext = jnp.concatenate([seg, nxt], axis=0)
        after = [None] + [ext[k : Q + k] == seg for k in (1, 2, 3)]
        for n in ("dqk", "dcs", "dbs", "rowg", "rs", "gs", "ds"):
            s[n][...] = jnp.zeros_like(s[n])

        def pair(j, _):
            hook(i * (nv // 128) + j)
            lanes = pl.ds(pl.multiple_of(j * 128, 128), 128)
            taps = cx[:, lanes]
            pre, shifted = conv_terms(with_earlier(vals, r0, lanes), match, taps)
            sig = sigmoid(pre)
            x = pre * sig
            stepe = s["step"][:, lanes]
            taile = s["tail"][:, lanes]
            u = x * stepe
            ub = u.astype(BF)
            dy = dy_ref[pl.ds(r0, Q), lanes].astype(F32)
            dyb = dy.astype(BF)
            dyt = dy.T.astype(BF)
            stb = states[c, :, lanes]
            dst = s["dstate"][:, lanes]
            dstb = dst.astype(BF)
            edy = s["ecum"][:, lanes] * dy
            edyb = edy.astype(BF)
            s["rs"][...] += to_head(edy * dnn(s["c"][...], stb), j)
            s["dcs"][...] += dnt(edyb, stb)
            tu = taile * u
            v = dnn(s["b"][...], dstb)
            s["dbs"][...] += dnt(tu.astype(BF), dstb)
            s["gs"][...] += to_head(tu * v, j)
            keep = s["keep"][0:1, lanes]
            s["krow"][:, lanes] = jnp.broadcast_to(keep * jnp.sum(stb.astype(F32) * dst, axis=0, keepdims=True), (8, 128))
            s["dstate"][:, lanes] = keep * dst + dnn(s["ct"][...], edyb)
            lane = ii((Q, 128), 1)
            parts = []
            for e in range(2):
                h = 2 * j + e
                mine = (lane < 64) if e == 0 else (lane >= 64)
                s["dm"][...] = dnt(jnp.where(mine, dy, 0.0).astype(BF), ub)
                colsum = [jnp.zeros((1, 128), F32), jnp.zeros((1, 128), F32)]
                for r in range(4):
                    rows = slice(r * 64, r * 64 + 64)
                    rowsum = jnp.zeros((64, 128), F32)
                    for k in range(1 if r < 2 else 2):
                        cols = slice(k * 128, k * 128 + 128)
                        dec = decay(s["cum"], s["cumt"], s["bias"], h, rows, cols)
                        qk = s["qk"][rows, cols]
                        p = s["dm"][rows, cols] * dec
                        s["dqk"][rows, cols] += p
                        g = p * qk
                        rowsum = rowsum + g
                        colsum[k] = colsum[k] + jnp.sum(g, axis=0, keepdims=True)
                        s["m"][e, rows, cols] = (dec * qk).astype(BF)
                    tot = jnp.sum(rowsum, axis=1, keepdims=True)
                    s["rowg"][rows] += jnp.where(ii((64, 128), 1) == h, tot, 0.0)
                s["colg"][h] = jnp.broadcast_to(jnp.concatenate(colsum, axis=1), (8, Q))
                parts.append(dnn(dyt[e * 64 : e * 64 + 64], s["m"][e]))
            du = jnp.concatenate(parts, axis=0).T + taile * v
            s["ds"][...] += to_head(du * x, j)
            skip = taps[5:6]
            dx = du * stepe + skip * dy
            dpre = dx * (sig + x * (1.0 - sig))
            low[pl.ds(r0, Q), lanes] = later_sum(dpre, s["halo"][:, lanes], after, taps).astype(BF)
            s["halo"][:, lanes] = dpre[:8]
            gx[:, lanes] += jnp.concatenate(
                [jnp.sum(dpre * shifted[3 - k], axis=0, keepdims=True) for k in range(4)]
                + [jnp.sum(dpre, axis=0, keepdims=True), jnp.sum(dy * x, axis=0, keepdims=True), jnp.zeros((2, 128), F32)], axis=0)
            return 0

        lax.fori_loop(0, nv // 128, pair, 0)
        tt, ss = ii((Q, Q), 0), ii((Q, Q), 1)
        e64t = (ii((nv, 128), 0) // 64 == ii((nv, 128), 1)).astype(BF)
        kh, km, kl = split3(s["krow"][...])
        kterm = dnn(kh, e64t) + dnn(km, e64t) + dnn(kl, e64t)
        colg = jnp.concatenate([s["colg"][h, 0:1] for h in range(nh)] + [jnp.zeros((128 - nh, Q), F32)], axis=0)
        dcum = s["rowg"][...] - colg.T + s["rs"][...]
        da = tri_times((ss >= tt).astype(BF), dcum) + tri_times((ss < tt).astype(BF), s["gs"][...]) + kterm[0:1]
        rate = hp[1:2]
        dstep = s["ds"][...] + rate * da
        draw = dstep * sigmoid(raw)
        draw = jnp.where(ii((Q, 128), 1) < nh, draw, 0.0)
        low[pl.ds(r0, Q), pl.ds(nv + 256, 128)] = draw.astype(BF)
        gh[...] += jnp.concatenate([jnp.sum(draw, axis=0, keepdims=True), jnp.sum(da * step, axis=0, keepdims=True) * rate, jnp.zeros((6, 128), F32)], axis=0)
        dqk = s["dqk"][...]
        dc = dnn(dqk.astype(BF), s["b"][...]) + s["dcs"][...]
        db = dnn(dqk.T.astype(BF), s["c"][...]) + s["dbs"][...]
        sig = sigmoid(bc_pre)
        dpre = jnp.concatenate([db, dc], axis=1) * (sig + bc_pre * sig * (1.0 - sig))
        after2 = [None] + [jnp.concatenate([m, m], axis=1) for m in after[1:]]
        low[pl.ds(r0, Q), pl.ds(nv, 256)] = later_sum(dpre, s["halobc"][...], after2, cbc[...]).astype(BF)
        s["halobc"][...] = dpre[:8]
        gbc[...] += jnp.concatenate(
            [jnp.sum(dpre * bc_shifted[3 - k], axis=0, keepdims=True) for k in range(4)] + [jnp.sum(dpre, axis=0, keepdims=True), jnp.zeros((3, 256), F32)], axis=0)
        return 0

    lax.fori_loop(0, nb, block, 0)


def run_forward(nv, vals, segc, segr, cx, cbc, hp):
    sc = fwd_scratch(nv)
    names = list(sc)
    rows = vals.shape[0]

    def kernel(vals, segc, segr, cx, cbc, hp, ssd, states, *scr):
        ssd_forward(nv, vals, segc, segr, cx, cbc, hp, ssd, states, dict(zip(names, scr)))

    vm = pl.BlockSpec(memory_space=pltpu.VMEM)
    return pl.pallas_call(
        kernel, out_shape=(jax.ShapeDtypeStruct((rows, nv), F32), jax.ShapeDtypeStruct((rows // Q, 128, nv), F32)),
        in_specs=[vm] * 6, out_specs=[vm] * 2, scratch_shapes=[sc[n] for n in names],
        compiler_params=pltpu.CompilerParams(vmem_limit_bytes=60 * 2**20), name="scan_forward",
    )(vals, segc, segr, cx, cbc, hp)


def run_backward(nv, vals, segc, segr, cx, cbc, hp, dy, states):
    sc = bwd_scratch(nv)
    names = list(sc)
    rows = vals.shape[0]

    def kernel(vals, segc, segr, cx, cbc, hp, dy, states, low, gx, gbc, gh, *scr):
        ssd_backward(nv, vals, segc, segr, cx, cbc, hp, dy, states, low, gx, gbc, gh, dict(zip(names, scr)))

    vm = pl.BlockSpec(memory_space=pltpu.VMEM)
    outs = (jax.ShapeDtypeStruct((rows, nv + 384), BF), jax.ShapeDtypeStruct((8, nv), F32), jax.ShapeDtypeStruct((8, 256), F32), jax.ShapeDtypeStruct((8, 128), F32))
    return pl.pallas_call(
        kernel, out_shape=outs, in_specs=[vm] * 8, out_specs=[vm] * 4, scratch_shapes=[sc[n] for n in names],
        compiler_params=pltpu.CompilerParams(vmem_limit_bytes=60 * 2**20), name="scan_backward",
    )(vals, segc, segr, cx, cbc, hp, dy, states)


INNER = 3072
EPS = 1e-05


def at_step(step, events):
    for k, fn in events:

        @pl.when(step == k)
        def _(fn=fn):
            fn()


def forward_kernel(
    names, nv,
    hid, cot_own, p_x, p_bc, p_dt, p_gate, p_out, pgain, seg, conv_x, bias_x, conv_bc, bias_bc, dt_bias, a_log, skip_d, gate_gain,
    o_w0, o_w1, o_w2, o_w3, o_nrm, o_cot, o_vals, o_states, o_no, o_lg, o_dy, o_gg, cx, cbc, hp, segc, segr,
    square, w_own1, w0, w1, w2, w3, nrm, cot, vals, states, ssd, gate, gno, no, lg, dy, sums_own, sums_in,
    wsend, wrecv, tsend, trecv, ssend, srecv, lsem, *scan_scratch,
):
    s = dict(zip(names, scan_scratch))
    x, z, yh, t = place()
    yl, co = t // 2, t % 2
    tp, slots = tensor_peers()
    width = hid.shape[1]
    cut = w0.shape[1]
    w_own0, w_own2, w_own3 = p_x.at[:, :cut], p_gate, p_out
    w_own1[...] = jnp.zeros_like(w_own1)
    w_own1[:, : nv - cut] = p_x[:, cut:]
    w_own1[:, nv - cut : nv - cut + 256] = p_bc[...]
    square[...] = jnp.zeros_like(square)
    square[: p_dt.shape[0], : p_dt.shape[1]] = p_dt[...].astype(F32)
    w_own1[:, nv - cut + 256 :] = square[...].T[: p_dt.shape[1]].astype(BF)
    greet([dev(x, z, 1 - yh, t)] + [neighbour(a, d) for a in "xz" for d in (1, -1)] + tp)
    owns, dsts, outs = (w_own0, w_own1, w_own2, w_own3), (w0, w1, w2, w3), (o_w0, o_w1, o_w2, o_w3)
    groups = lambda ks: [Gather(owns[k], dsts[k], "xz"[k % 2], wsend.at[k], wrecv.at[k]) for k in ks]
    first, second = (0, 1), (2, 3)

    def step(ks, n):
        for g in groups(ks):
            g.step(n)

    def saved(i, src, dst):
        return pltpu.make_async_copy(src, dst, lsem.at[i])

    mine = pl.ds(pl.multiple_of(t * 256, 256), 256)
    theirs = pl.ds(pl.multiple_of(slots[1] * 256, 256), 256)

    def tensor_copies(i, own, dst):
        return (
            send(own, dst.at[mine], tsend.at[i, 0], trecv.at[i, 0], tp[1]),
            send(own, dst.at[mine], tsend.at[i, 1], trecv.at[i, 1], tp[0]),
            send(dst.at[theirs], dst.at[theirs], tsend.at[i, 2], trecv.at[i, 2], tp[0]),
        )

    for g in groups((0, 1, 2, 3)):
        g.begin()
    step(first, 0)

    def norm_rows(i, _):
        rows = pl.ds(pl.multiple_of(i * 64, 64), 64)
        h = hid[rows].astype(F32)
        inv = lax.rsqrt(jnp.mean(h * h, axis=1, keepdims=True) + EPS)
        nrm[pl.ds(pl.multiple_of(t * 256 + i * 64, 64), 64)] = (h * inv * pgain[0:1]).astype(BF)
        return 0

    lax.fori_loop(0, 4, norm_rows, 0)
    own_lanes = pl.ds(pl.multiple_of(t * nv, 128), nv)
    heads = p_dt.shape[0]

    def own_heads(v, lanes, per):
        i, j = ii((v.shape[1], lanes), 0), ii((v.shape[1], lanes), 1)
        pick = ((i == t * heads + j // per) & (j < heads * per)).astype(BF)
        return sum(dnn(part, pick) for part in split3(jnp.broadcast_to(v[...], (8, v.shape[1]))))

    cx[0:4] = conv_x[:, own_lanes]
    cx[4:5] = bias_x[:, own_lanes]
    cx[5:8] = own_heads(skip_d, nv, 64)[5:8]
    cbc[0:4] = conv_bc[...]
    cbc[4:8] = jnp.broadcast_to(bias_bc[...], (4, 256))
    hp[0:1] = own_heads(dt_bias, 128, 1)[0:1]
    hp[1:2] = jnp.where(ii((1, 128), 1) < heads, -jnp.exp(own_heads(a_log, 128, 1)[0:1]), 0.0)
    hp[2:8] = jnp.zeros((6, 128), F32)
    gains = gate_gain[:, own_lanes]
    sf = seg[...].astype(F32)
    for k in range(seg.shape[0]):
        segr[:, k * 128 : k * 128 + 128] = jnp.broadcast_to(sf[k : k + 1], (8, 128))
        segc[k * 128 : k * 128 + 128] = jnp.broadcast_to(sf[k : k + 1], (128, 128)).T
    for k in range(4):
        g = groups((k,))[0]
        g.mine[...] = g.own[...]
    cot[mine] = cot_own[...]
    nrm_copies = tensor_copies(0, nrm.at[mine], nrm)
    cot_copies = tensor_copies(1, cot_own, cot)
    nrm_copies[0].start()
    nrm_copies[1].start()
    for n in (1, 4, 2, 3):
        step(first, n)
    cot_copies[0].start()
    cot_copies[1].start()
    step(second, 0)
    step(second, 1)
    step(first, 5)
    step(first, 6)
    nrm_copies[0].wait_recv()
    nrm_copies[2].start()
    step(second, 4)
    step(first, 7)
    nrm_copies[1].wait_recv()
    nrm_copies[2].wait_recv()

    def project(i, _):
        pl.when(i == 2)(lambda: step(second, 2))
        rows = pl.ds(pl.multiple_of(i * 256, 256), 256)
        n = nrm[rows]
        at = 0
        for w in (w0, w1):
            c = w.shape[1]
            vals[rows, at : at + c] = jnp.dot(n, w[...], preferred_element_type=F32)
            at += c
        return 0

    lax.fori_loop(0, 4, project, 0)
    early = [(0, w0, o_w0), (1, w1, o_w1), (2, nrm, o_nrm), (3, vals, o_vals)]
    for e in early:
        saved(*e).start()

    def cot_forward():
        cot_copies[0].wait_recv()
        cot_copies[2].start()

    events = [(1, lambda: step(second, 3)), (6, lambda: step(second, 5)), (10, lambda: step(second, 6)), (14, cot_forward)]
    ssd_forward(nv, vals, segc, segr, cx, cbc, hp, ssd, states, s, lambda at: at_step(at, events))
    step(second, 7)
    cot_copies[1].wait_recv()
    cot_copies[2].wait_recv()
    late = [(4, w2, o_w2), (5, w3, o_w3), (6, cot, o_cot), (7, states, o_states)]
    for e in late:
        saved(*e).start()

    def inner(i, _):
        rows = pl.ds(pl.multiple_of(i * 256, 256), 256)
        g = jnp.dot(nrm[rows], w2[...], preferred_element_type=F32)
        gate[rows] = g
        o = jnp.dot(cot[rows], w3[...], preferred_element_type=F32)
        gno[rows] = o
        gated = ssd[rows] * (g * sigmoid(g))
        sq = jnp.sum(gated * gated, axis=1, keepdims=True)
        cr = jnp.sum(o * gains * gated, axis=1, keepdims=True)
        lane = ii((256, 128), 1)
        both = jnp.where(lane == 0, sq, jnp.where(lane == 1, cr, 0.0))
        sums_own[:, rows] = both.T[:8]
        return 0

    lax.fori_loop(0, 4, inner, 0)
    small = [send(sums_own, sums_in.at[k], ssend.at[k], srecv.at[k], p) for k, p in enumerate(tp)]
    for c in small:
        c.start()
    for c in small:
        c.wait_recv()
    o_gg[...] = jnp.zeros_like(o_gg)

    def outer(i, _):
        rows = pl.ds(pl.multiple_of(i * 256, 256), 256)
        tot = sums_own[:, rows] + sums_in[0, :, rows] + sums_in[1, :, rows] + sums_in[2, :, rows]
        cols = jnp.concatenate([tot, jnp.zeros((120, 256), F32)], axis=0).T
        inv = lax.rsqrt(cols[:, 0:1] / INNER + EPS)
        cross = inv * inv * inv * cols[:, 1:2] / INNER
        for k in range(nv // 128):
            lanes = pl.ds(k * 128, 128)
            g, y, o, gain = gate[rows, lanes], ssd[rows, lanes], gno[rows, lanes], gains[:, k * 128 : k * 128 + 128]
            sig = sigmoid(g)
            silu = g * sig
            gated = y * silu
            scaled = gated * inv
            no[rows, lanes] = (scaled * gain).astype(BF)
            o_gg[0:1, lanes] += jnp.sum(o * scaled, axis=0, keepdims=True)
            grad = o * gain * inv - gated * cross
            dy[rows, lanes] = (grad * silu).astype(BF)
            lg[rows, lanes] = (grad * y * (sig + silu * (1.0 - sig))).astype(BF)
        return 0

    lax.fori_loop(0, 4, outer, 0)
    last = [(8, no, o_no), (9, lg, o_lg), (10, dy, o_dy)]
    for e in last:
        saved(*e).start()
    for g in groups((0, 1, 2, 3)):
        g.finish()
    for c in nrm_copies + cot_copies + tuple(small):
        c.wait_send()
    for e in early + late + last:
        saved(*e).wait()


def run_k1(hid, cot_own, projs, pgain, seg, params):
    anys, vm = pl.BlockSpec(memory_space=pl.ANY), pl.BlockSpec(memory_space=pltpu.VMEM)
    nv = projs[0].shape[1]
    rows = seg.shape[0] * seg.shape[1]
    n, d = projs[0].shape[0], hid.shape[1]
    sh = jax.ShapeDtypeStruct
    cols = [nv - 128, 512, nv, nv]
    nvals = cols[0] + cols[1]
    outs = [sh((d, c), BF) for c in cols] + [sh((rows, d), BF)] * 2 + [sh((rows, nvals), F32), sh((rows // Q, 128, nv), BF)] + [sh((rows, nv), BF)] * 3
    outs += [sh((8, nv), F32), sh((8, nv), F32), sh((8, 256), F32), sh((8, 128), F32), sh((rows, 128), F32), sh((8, rows), F32)]
    V = lambda shape, dt: pltpu.VMEM(shape, dt)
    D = pltpu.SemaphoreType.DMA
    scan = fwd_scratch(nv)
    scratch = [V((128, 128), F32), V((n, cols[1]), BF)] + [V((d, c), BF) for c in cols] + [V((rows, d), BF)] * 2
    scratch += [V((rows, nvals), F32), V((rows // Q, 128, nv), BF)] + [V((rows, nv), F32)] * 3 + [V((rows, nv), BF)] * 3
    scratch += [V((8, rows), F32), V((3, 8, rows), F32), D((4, Gather.N)), D((4, Gather.N)), D((2, 3)), D((2, 3)), D((3,)), D((3,)), D((11,))]
    scratch += list(scan.values())
    return pl.pallas_call(
        functools.partial(forward_kernel, list(scan), nv), out_shape=outs, in_specs=[vm] * 17, out_specs=[anys] * 11 + [vm] * 6, scratch_shapes=scratch,
        compiler_params=pltpu.CompilerParams(collective_id=0, has_side_effects=True, vmem_limit_bytes=62 * 2**20), name="forward_all",
    )(hid, cot_own, *projs, pgain, seg, *params)


class Scatter:
    N = 13

    def __init__(self, v, bufs, out, a1, send_sem, recv_sem):
        x, z, yh, t = place()
        self.v, self.out, self.a1, self.yh = v, out, a1, yh
        self.r1, self.r2, self.q1, self.q2, self.kk, self.yy = bufs
        self.h = self.r2.at[0]
        a2 = "z" if a1 == "x" else "x"
        self.p, self.q = (x, z) if a1 == "x" else (z, x)
        self.send_sem, self.recv_sem = send_sem, recv_sem
        right1, left1, right2, left2 = neighbour(a1, 1), neighbour(a1, -1), neighbour(a2, 1), neighbour(a2, -1)
        r1, r2, h, q1, q2, q = self.r1, self.r2, self.h, self.q1, self.q2, self.q
        self.plan = [
            (self.half(2, 0), r1.at[0], right1), (self.half(2, 1), r1.at[1], left1),
            (self.half(1, 1), r2.at[0, pl.ds(2, 2)], right1), (self.half(-1, 0), r2.at[1, pl.ds(0, 2)], left1),
            (self.half(1, 0), r2.at[0, pl.ds(0, 2)], right1), (self.half(-1, 1), r2.at[1, pl.ds(2, 2)], left1),
            (h.at[m4(q + 2), 0], q1.at[0], right2), (h.at[m4(q + 2), 1], q1.at[1], left2),
            (h.at[m4(q + 1), 1], q2.at[0, 1], right2), (h.at[m4(q - 1), 0], q2.at[1, 0], left2),
            (h.at[m4(q + 1), 0], q2.at[0, 0], right2), (h.at[m4(q - 1), 1], q2.at[1, 1], left2),
            (self.kk, self.yy, dev(x, z, 1 - yh, t)),
        ]

    def half(self, d, k):
        at = m4(self.p + d)
        return self.v.at[pl.ds(2 * k, 2), at] if self.a1 == "z" else self.v.at[at, pl.ds(2 * k, 2)]

    def copy(self, k):
        src, dst, to = self.plan[k]
        return send(src, dst, self.send_sem.at[k], self.recv_sem.at[k], to)

    def start(self, *ks):
        for k in ks:
            self.copy(k).start()

    def arrive(self, *ks):
        for k in ks:
            self.copy(k).wait_recv()

    def step(self, n):
        v, r1, r2, h, q1, q2, p, q, yh = self.v, self.r1, self.r2, self.h, self.q1, self.q2, self.p, self.q, self.yh
        if n == 0:
            self.start(0, 1, 2, 3)
        elif n == 1:
            for side, d in ((0, 1), (1, -1)):
                self.arrive(side)
                at = m4(p + d)

                def add(j, _, side=side, at=at):
                    e, y = j // 2, j % 2
                    ix = (2 * side + e, at, y) if self.a1 == "z" else (at, 2 * side + e, y)
                    v[ix] = (v[ix].astype(F32) + r1[side, e, y].astype(F32)).astype(BF)
                    return 0

                lax.fori_loop(0, 4, add, 0)
                self.start(4 + side)
        elif n == 2:
            self.arrive(2, 3, 4, 5)

            def add(j, _):
                e, y = j // 2, j % 2
                own = v[e, p, y] if self.a1 == "z" else v[p, e, y]
                h[e, y] = (own.astype(F32) + r2[0, e, y].astype(F32) + r2[1, e, y].astype(F32)).astype(BF)
                return 0

            lax.fori_loop(0, 8, add, 0)
            self.start(6, 7, 8, 9)
        elif n == 3:
            for side, d in ((0, 1), (1, -1)):
                self.arrive(6 + side)
                at = m4(q + d)
                h[at, side] = (h[at, side].astype(F32) + q1[side].astype(F32)).astype(BF)
                self.start(10 + side)
        elif n == 4:
            self.arrive(8, 9, 10, 11)
            self.kk[...] = (h[q, 1 - yh].astype(F32) + q2[0, 1 - yh].astype(F32) + q2[1, 1 - yh].astype(F32)).astype(BF)
            self.start(12)
        else:
            self.arrive(12)
            self.out[...] = h[q, yh].astype(F32) + q2[0, yh].astype(F32) + q2[1, yh].astype(F32) + self.yy[...].astype(F32)

    def finish(self):
        for k in range(self.N):
            self.copy(k).wait_send()


class TokenScatter:
    def __init__(self, v, from_core, from_chip, out, send_sem, recv_sem):
        t = place()[3]
        tp, slots = tensor_peers()
        self.t, self.v, self.from_core, self.from_chip, self.out = t, v, from_core, from_chip, out
        rows = lambda s: pl.ds(pl.multiple_of(s * 256, 256), 256)
        self.pass_on, self.mine = slots[1], rows(t)
        self.copies = lambda k: (
            lambda: send(v.at[rows(slots[2])], from_core.at[0], send_sem.at[0], recv_sem.at[0], tp[0]),
            lambda: send(v.at[rows(slots[0])], from_core.at[1], send_sem.at[1], recv_sem.at[1], tp[0]),
            lambda: send(v.at[rows(slots[1])], from_chip, send_sem.at[2], recv_sem.at[2], tp[1]),
        )[k]()

    def step(self, n):
        if n == 0:
            self.copies(0).start()
            self.copies(1).start()
        elif n == 1:
            self.copies(0).wait_recv()

            def add(j, _):
                rows = pl.ds(pl.multiple_of(j * 32, 32), 32)
                own = pl.ds(pl.multiple_of(self.pass_on * 256 + j * 32, 32), 32)
                self.v[own] = (self.v[own].astype(F32) + self.from_core[0, rows].astype(F32)).astype(BF)
                return 0

            lax.fori_loop(0, 8, add, 0)
            self.copies(2).start()
        else:
            self.copies(1).wait_recv()
            self.copies(2).wait_recv()

            def add(j, _):
                rows = pl.ds(pl.multiple_of(j * 32, 32), 32)
                own = self.v[pl.ds(pl.multiple_of(self.t * 256 + j * 32, 32), 32)]
                self.out[rows] = own.astype(F32) + self.from_core[1, rows].astype(F32) + self.from_chip[rows].astype(F32)
                return 0

            lax.fori_loop(0, 8, add, 0)

    def finish(self):
        for k in range(3):
            self.copies(k).wait_send()


def backward_kernel(
    names, nv,
    h_w0, h_w1, h_w2, h_w3, h_nrm, h_cot, h_vals, h_states, h_no, h_lg, h_dy, pgain, segc, segr, cx, cbc, hp, gg,
    o_gate, o_out, o_x0, o_x1, o_bc, o_own, o_grad, o_small,
    w0, w1, w23, nrm, cot, vals, states, nody, lg, low, po, t_gate, t_out, t_x0, t_x1,
    own_v, sx, sz, sy, st, sacc, bct, fc0, ch0, fc1, ch1, gx, gbc, gh, pre,
    wsend, wrecv, tsend, trecv, ssend, srecv, bsend, brecv, lsem, *rest,
):
    bufs, s = [rest[6 * k : 6 * k + 6] for k in range(4)], dict(zip(names, rest[24:]))
    x, z, yh, t = place()
    tp, slots = tensor_peers()
    loads = [
        pltpu.make_async_copy(a, b, lsem.at[k])
        for k, (a, b) in enumerate(((h_no, nody), (h_w3, w23), (h_cot, cot), (h_nrm, nrm), (h_lg, lg), (h_vals, vals), (h_states, states), (h_w0, w0), (h_w1, w1)))
    ]
    for c in loads:
        c.start()
    load_dy, load_w2 = pltpu.make_async_copy(h_dy, nody, lsem.at[9]), pltpu.make_async_copy(h_w2, w23, lsem.at[10])
    greet([dev(x, z, 1 - yh, t)] + [neighbour(a, d) for a in "xz" for d in (1, 2, 3)] + tp)
    scat = [
        Scatter(v, bufs[k], o, a1, wsend.at[k], wrecv.at[k])
        for k, (v, o, a1) in enumerate(((t_out, o_out, "x"), (t_gate, o_gate, "z"), (t_x0, o_x0, "x"), (t_x1, o_x1, "z")))
    ]
    s_out, s_gate, s_x0, s_x1 = scat
    k_out = TokenScatter(po, fc0, ch0, o_own, tsend.at[0], trecv.at[0])
    k_nrm = TokenScatter(cot, fc1, ch1, o_grad, tsend.at[1], trecv.at[1])

    def by_rows(fn):
        def body(i, _):
            fn(pl.ds(pl.multiple_of(i * 256, 256), 256))
            return 0

        lax.fori_loop(0, 4, body, 0)

    def outer_product(dst, left, right):
        def body(i, _):
            cols = pl.ds(pl.multiple_of(i * 384, 384), 384)
            r = lax.dot_general(left[:, cols], right[...], (((0,), (0,)), ((), ())), preferred_element_type=F32)
            dst[i] = r.astype(BF).reshape(dst.shape[1:])
            return 0

        lax.fori_loop(0, 4, body, 0)

    for k in (0, 1):
        loads[k].wait()

    def out_rows(rows):
        left = nody[rows]
        for k in range(0, po.shape[1], 512):
            po[rows, k : k + 512] = dnt(left, w23[k : k + 512]).astype(BF)

    by_rows(out_rows)
    load_w2.start()
    k_out.step(0)
    loads[2].wait()
    outer_product(t_out, cot, nody)
    load_dy.start()
    s_out.step(0)
    k_out.step(1)
    loads[3].wait()
    loads[4].wait()
    outer_product(t_gate, nrm, lg)
    s_gate.step(0)
    for k in (5, 6, 7, 8):
        loads[k].wait()
    load_dy.wait()
    both = lambda n: lambda: (s_out.step(n), s_gate.step(n))
    events = [(6, both(1)), (12, both(2)), (16, both(3)), (18, both(4)), (20, both(5)), (22, lambda: k_out.step(2))]
    ssd_backward(nv, vals, segc, segr, cx, cbc, hp, nody, states, low, gx, gbc, gh, s, lambda at: at_step(at, events))
    load_w2.wait()
    pre[...] = jnp.zeros_like(pre)
    c0 = w0.shape[1]

    def grad_rows(rows):
        for k in range(0, cot.shape[1], 512):
            cols = slice(k, k + 512)
            g = dnt(lg[rows], w23[cols]) + dnt(low[rows, :c0], w0[cols]) + dnt(low[rows, c0:], w1[cols])
            pre[0:1, cols] += jnp.sum(g * nrm[rows, cols].astype(F32), axis=0, keepdims=True)
            cot[rows, cols] = g.astype(BF)

    by_rows(grad_rows)
    k_nrm.step(0)
    outer_product(t_x0, nrm, low.at[:, :c0])
    s_x0.step(0)
    k_nrm.step(1)
    own_v[...] = jnp.zeros_like(own_v)
    own_v[0:6] = gx[0:6]
    own_v[6:7] = gg[0:1]
    pv = pre[0:1] / pgain[0:1]
    own_v[7:8], own_v[8:9] = pv[:, :nv], pv[:, nv:]
    for k in range(3):
        own_v[9:10, k * 256 : k * 256 + 256] = gbc[k : k + 1]
    for k in range(2):
        own_v[10:11, k * 256 : k * 256 + 256] = gbc[3 + k : 4 + k]
        own_v[11:12, k * 128 : k * 128 + 128] = gh[k : k + 1]
    small = [send(own_v, sx.at[d - 1], ssend.at[d - 1], srecv.at[d - 1], neighbour("x", d)) for d in (1, 2, 3)]
    for c in small:
        c.start()
    outer_product(t_x1, nrm, low.at[:, c0:])
    s_x1.step(0)
    last = lambda n: (s_x0.step(n), s_x1.step(n))

    def next_small(have, total, copies):
        for c in have:
            c.wait_recv()
        total()
        for c in copies:
            c.start()
        return copies

    def total_x():
        sacc[0] = own_v[...] + sx[0] + sx[1] + sx[2]

    def total_z():
        sacc[1] = sacc[0] + sz[0] + sz[1] + sz[2]

    def total_y():
        sacc[2] = sacc[1] + sy[...]

    small_z = next_small(small, total_x, [send(sacc.at[0], sz.at[d - 1], ssend.at[2 + d], srecv.at[2 + d], neighbour("z", d)) for d in (1, 2, 3)])
    last(1)
    small_y = next_small(small_z, total_z, [send(sacc.at[1], sy, ssend.at[6], srecv.at[6], dev(x, z, 1 - yh, t))])
    last(2)
    small_t = next_small(small_y, total_y, [send(sacc.at[2], st.at[k], ssend.at[7 + k], srecv.at[7 + k], p) for k, p in enumerate(tp)])
    k_nrm.step(2)
    last(3)
    last(4)
    s_x1.step(5)
    bc0 = o_x1.shape[1] - 384
    bct[3] = o_x1[:, bc0 : bc0 + 256]
    bcs = [send(bct.at[3], bct.at[k], bsend.at[k], brecv.at[k], p) for k, p in enumerate(tp)]
    for c in bcs:
        c.start()
    s_x0.step(5)
    for c in small_t:
        c.wait_recv()
    o_small[t] = sacc[2]
    for k in range(3):
        o_small[slots[k]] = st[k]
    for c in bcs:
        c.wait_recv()
    o_bc[...] = bct[3] + bct[0] + bct[1] + bct[2]
    for c in small + small_z + small_y + small_t + bcs:
        c.wait_send()
    for g in scat + [k_out, k_nrm]:
        g.finish()


def run_k2(ws, nrm, cot, vals, states, no, lg, dy, pgain, segc, segr, cx, cbc, hp, gg):
    anys, vm = pl.BlockSpec(memory_space=pl.ANY), pl.BlockSpec(memory_space=pltpu.VMEM)
    nv = cx.shape[1]
    rows, d = nrm.shape
    sh = lambda *s: jax.ShapeDtypeStruct(s, F32)
    cols = [w.shape[1] for w in ws]
    n = d // 32
    V = lambda *s, dt=BF: pltpu.VMEM(s, dt)
    D = pltpu.SemaphoreType.DMA
    outs = [sh(n, cols[2]), sh(n, cols[3]), sh(n, cols[0]), sh(n, cols[1]), sh(n, 256), sh(256, d), sh(256, d), sh(4, 16, nv)]
    term = lambda c: V(4, 4, 2, n, c)
    scratch = [V(d, cols[0]), V(d, cols[1]), V(d, cols[2]), V(rows, d), V(rows, d), V(*vals.shape, dt=F32), V(*states.shape), V(rows, nv), V(rows, nv), V(*vals.shape), V(rows, d)]
    scratch += [term(cols[2]), term(cols[3]), term(cols[0]), term(cols[1])]
    sv = (16, nv)
    scratch += [V(*sv, dt=F32), V(3, *sv, dt=F32), V(3, *sv, dt=F32), V(*sv, dt=F32), V(3, *sv, dt=F32), V(3, *sv, dt=F32), V(4, n, 256, dt=F32)]
    scratch += [V(2, 256, d), V(256, d)] * 2
    scratch += [V(8, nv, dt=F32), V(8, 256, dt=F32), V(8, 128, dt=F32), V(8, d, dt=F32)]
    scratch += [D((4, Scatter.N))] * 2 + [D((2, 3))] * 2 + [D((10,))] * 2 + [D((3,))] * 2 + [D((11,))]
    for c in (cols[3], cols[2], cols[0], cols[1]):
        scratch += [V(2, 2, 2, n, c), V(2, 4, 2, n, c), V(2, n, c), V(2, 2, n, c), V(n, c), V(n, c)]
    scan = bwd_scratch(nv)
    scratch += list(scan.values())
    return pl.pallas_call(
        functools.partial(backward_kernel, list(scan), nv), out_shape=outs, in_specs=[anys] * 11 + [vm] * 7, out_specs=[vm] * 8, scratch_shapes=scratch,
        compiler_params=pltpu.CompilerParams(collective_id=1, has_side_effects=True, vmem_limit_bytes=64 * 2**20), name="backward_all",
    )(*ws, nrm, cot, vals, states, no, lg, dy, pgain, segc, segr, cx, cbc, hp, gg)


def finish_kernel(
    heads, hid, cot, pgain, own_out, grad_own, smalls, r_gate, r_out, r_x0, r_x1, r_bc,
    out, d_hid, d_pre, d_gate, d_x, d_bc, d_dt, d_conv_x, d_bias_x, d_conv_bc, d_bias_bc, d_dt_bias, d_a_log, d_skip, d_gain, d_out, square,
):
    def rows(i, _):
        at = pl.ds(pl.multiple_of(i * 64, 64), 64)
        h = hid[at].astype(F32)
        g = grad_own[at]
        inv = lax.rsqrt(jnp.mean(h * h, axis=1, keepdims=True) + EPS)
        scaled = g * pgain[...]
        back = jnp.mean(scaled * h, axis=1, keepdims=True)
        out[at] = (h + own_out[at]).astype(BF)
        d_hid[at] = cot[at].astype(F32) + scaled * inv - h * (inv * inv * inv * back)
        return 0

    lax.fori_loop(0, hid.shape[0] // 64, rows, 0)
    nv = smalls.shape[2]
    square[...] = jnp.zeros_like(square)
    d_gate[...] = r_gate[...]
    d_out[...] = r_out[...]
    cut = r_x0.shape[1]
    d_x[:, :cut] = r_x0[...]
    d_x[:, cut:] = r_x1[:, : nv - cut]
    d_bc[...] = r_bc[...]
    square[: r_x1.shape[0]] = r_x1[:, nv - cut + 256 :]
    d_dt[...] = square[...].T[:heads, : r_x1.shape[0]]
    parts = [smalls[k] for k in range(4)]
    both = parts[0] + parts[1] + parts[2] + parts[3]
    d_pre[:, :nv] = both[7:8]
    d_pre[:, nv:] = both[8:9]
    for k in range(3):
        d_conv_bc[k : k + 1] = both[9:10, k * 256 : k * 256 + 256]
    d_conv_bc[3:4] = both[10:11, :256]
    d_bias_bc[...] = both[10:11, 256:512]
    per_head = [jnp.zeros((8, 128), F32)] * 3
    for k in range(4):
        lanes = slice(k * nv, k * nv + nv)
        d_conv_x[:, lanes] = parts[k][0:4]
        d_bias_x[:, lanes] = parts[k][4:5]
        d_gain[:, lanes] = parts[k][6:7]
        row = parts[k][8:16]
        i, j = ii((128, 128), 0), ii((128, 128), 1)
        pick = ((i + k * heads == j) & (i < heads)).astype(BF)
        for n in range(2):
            per_head[n] = per_head[n] + sum(dnn(p, pick) for p in split3(row[:, n * 128 : n * 128 + 128]))
        i, j = ii((nv, 128), 0), ii((nv, 128), 1)
        group = (i // 64 + k * heads == j).astype(BF)
        per_head[2] = per_head[2] + sum(dnn(p, group) for p in split3(parts[k][0:8]))
    d_dt_bias[...] = per_head[0][3:4, : 4 * heads]
    d_a_log[...] = per_head[1][3:4, : 4 * heads]
    d_skip[...] = per_head[2][5:6, : 4 * heads]


def run_k3(heads, *args):
    vm = pl.BlockSpec(memory_space=pltpu.VMEM)
    smalls, r_gate = args[5], args[6]
    n, nv = r_gate.shape
    d = args[0].shape[1]
    sh = lambda *s: jax.ShapeDtypeStruct(s, F32)
    outs = [jax.ShapeDtypeStruct(args[0].shape, BF), sh(*args[0].shape), sh(1, d), sh(n, nv), sh(n, nv), sh(n, 256), sh(heads, n), sh(4, 4 * nv), sh(1, 4 * nv), sh(4, 256), sh(1, 256)]
    outs += [sh(1, 4 * heads)] * 3 + [sh(1, 4 * nv), sh(n, nv)]
    return pl.pallas_call(
        functools.partial(finish_kernel, heads), out_shape=outs, in_specs=[vm] * len(args), out_specs=[vm] * len(outs), scratch_shapes=[pltpu.VMEM((128, 128), F32)],
        compiler_params=pltpu.CompilerParams(vmem_limit_bytes=62 * 2**20), name="finish",
    )(*args)


def per_device(
    hidden_in, seg_ids, pre_gain, proj_gate, proj_x, proj_bc, proj_dt, conv_x, conv_bias_x, conv_bc, conv_bias_bc,
    dt_bias, a_log, skip_d, gate_gain, proj_out, cotangent,
):
    row = lambda v: v.reshape(1, -1)
    pgain = row(pre_gain)
    params = (conv_x, row(conv_bias_x), conv_bc, row(conv_bias_bc), row(dt_bias), row(a_log), row(skip_d), row(gate_gain))
    w0, w1, w2, w3, normed, cot, vals, states, normed_out, low_gate, dy, gg, cx, cbc, hp, segc, segr = run_k1(
        hidden_in, cotangent, (proj_x, proj_bc, proj_dt.T, proj_gate, proj_out.T), pgain, seg_ids.reshape(-1, 128), params
    )
    r_gate, r_out, r_x0, r_x1, r_bc, own_out, grad_own, smalls = run_k2(
        (w0, w1, w2, w3), normed, cot, vals, states, normed_out, low_gate, dy, pgain, segc, segr, cx, cbc, hp, gg
    )
    outs = run_k3(proj_dt.shape[1], hidden_in, cotangent, pgain, own_out, grad_own, smalls, r_gate, r_out, r_x0, r_x1, r_bc)
    flat = (2, 8, 10, 11, 12, 13, 14)
    turned = (6, 15)
    return tuple(o.reshape(-1) if k in flat else o.T if k in turned else o for k, o in enumerate(outs))


def solution(mesh):
    tok = P(("dp", "tensor"), None)
    mat = P("dp", "tensor")
    in_specs = (tok, P("dp"), P(), mat, mat, P("dp", None), mat) + (P(),) * 8 + (P("tensor", "dp"), tok)
    out_specs = (tok, tok, P(), mat, mat, P("dp", None), mat) + (P(),) * 8 + (P("tensor", "dp"),)
    return jax.shard_map(per_device, mesh=mesh, in_specs=in_specs, out_specs=out_specs, check_vma=False)
```

```python
import functools

import jax
import jax.numpy as jnp
from jax import lax
from jax.experimental import pallas as pl
from jax.experimental.pallas import tpu as pltpu
from jax.sharding import PartitionSpec as P

MESH = pl.DeviceIdType.MESH
F32 = jnp.float32
BF = jnp.bfloat16


def place():
    dp = lax.axis_index("dp")
    t = lax.axis_index("tensor")
    return dp // 8, (dp // 2) % 4, dp % 2, t


def dev(x, z, yh, t):
    return ((x * 4 + z) * 2 + yh, t)


def m4(v):
    return (v + 8) % 4


def neighbour(axis, d):
    x, z, yh, t = place()
    return dev(m4(x + d), z, yh, t) if axis == "x" else dev(x, m4(z + d), yh, t)


def tensor_peers():
    x, z, yh, t = place()
    yl, co = t // 2, t % 2
    slots = (yl * 2 + 1 - co, (1 - yl) * 2 + co, (1 - yl) * 2 + 1 - co)
    return [dev(x, z, yh, s) for s in slots], slots


def greet(peers):
    bar = pltpu.get_barrier_semaphore()
    for p in peers:
        pl.semaphore_signal(bar, inc=1, device_id=p, device_id_type=MESH)
    pl.semaphore_wait(bar, len(peers))


def send(src, dst, send_sem, recv_sem, to):
    return pltpu.make_async_remote_copy(
        src_ref=src, dst_ref=dst, send_sem=send_sem, recv_sem=recv_sem, device_id=to, device_id_type=MESH
    )


class Gather:
    N = 25

    def __init__(self, own, dst, r1, send_sem, recv_sem):
        x, z, yh, _ = place()
        r2 = "z" if r1 == "x" else "x"
        n = own.shape[0]

        def rows(d1, d2, y=None):
            ix, iz = (m4(x + d1), m4(z + d2)) if r1 == "x" else (m4(x + d2), m4(z + d1))
            first = (ix * 4 + iz) * 2
            if y is None:
                return dst.at[pl.ds(pl.multiple_of(first * n, n), 2 * n)]
            return dst.at[pl.ds(pl.multiple_of((first + y) * n, n), n)]

        self.mine = rows(0, 0, yh)
        self.own = own
        near1, near2 = [neighbour(r1, 1), neighbour(r1, -1)], [neighbour(r2, 1), neighbour(r2, -1)]
        other = rows(0, 0, 1 - yh)
        plan = [(own, self.mine, dev(x, z, 1 - yh, place()[3]))]
        plan += [(own, self.mine, p) for p in near1 + near2]
        plan += [(other, other, p) for p in near1 + near2]
        plan += [(rows(-1, 0, 0),) * 2 + (near1[0],), (rows(1, 0, 1),) * 2 + (near1[1],)]
        for d1 in (-1, 1, 2):
            plan += [(rows(d1, 0),) * 2 + (p,) for p in near2]
        for d1 in (0, -1, 1, 2):
            plan += [(rows(d1, -1, 0),) * 2 + (near2[0],), (rows(d1, 1, 1),) * 2 + (near2[1],)]
        self.plan, self.send_sem, self.recv_sem = plan, send_sem, recv_sem

    def copy(self, k):
        src, dst, to = self.plan[k]
        return send(src, dst, self.send_sem.at[k], self.recv_sem.at[k], to)

    STEPS = (
        ((), (1, 2, 3, 4)),
        ((0,), (5, 6, 7, 8)),
        ((1, 2, 5, 6), (9, 10, 11, 12, 13, 14)),
        ((9, 10), (15, 16)),
        ((3, 4, 7, 8), (17, 18)),
        ((11, 12, 13, 14), (19, 20, 21, 22)),
        ((15, 16), (23, 24)),
        ((17, 18, 19, 20, 21, 22, 23, 24), ()),
    )

    def begin(self):
        self.copy(0).start()

    def step(self, k):
        arrive, go = self.STEPS[k]
        for i in arrive:
            self.copy(i).wait_recv()
        for i in go:
            self.copy(i).start()

    def finish(self):
        for k in range(self.N):
            self.copy(k).wait_send()


Q = 256
LOG2E = 1.4426950408889634
NEG = -1e30


def dnn(a, b):
    return jnp.dot(a, b, preferred_element_type=F32)


def dnt(a, b):
    return lax.dot_general(a, b, (((1,), (1,)), ((), ())), preferred_element_type=F32)


def split3(v):
    hi = v.astype(BF)
    r = v - hi.astype(F32)
    mid = r.astype(BF)
    lo = (r - mid.astype(F32)).astype(BF)
    return hi, mid, lo


def spread3(v, mat):
    hi, mid, lo = split3(v)
    return dnn(jnp.concatenate([hi, mid, lo], axis=1), jnp.concatenate([mat, mat, mat], axis=0))


def tri_times(mat, v):
    hi, mid, lo = split3(v)
    out = dnn(mat, jnp.concatenate([hi, mid, lo], axis=1))
    w = v.shape[1]
    return out[:, :w] + out[:, w : 2 * w] + out[:, 2 * w :]


def ii(shape, dim):
    return lax.broadcasted_iota(jnp.int32, shape, dim)


def sigmoid(v):
    return 1.0 / (1.0 + jnp.exp2(v * -LOG2E))


def softplus(v):
    e = jnp.exp2(jnp.abs(v) * -LOG2E)
    u = 1.0 + e
    log1p = jnp.where(u == 1.0, e, jnp.log(u) * (e / jnp.where(u == 1.0, 1.0, u - 1.0)))
    return jnp.maximum(v, 0.0) + log1p


def conv_terms(ext, match, taps):
    n = ext.shape[0] - 8
    shifted = [ext[8:]] + [jnp.where(match[k], ext[8 - k : 8 + n - k], 0.0) for k in (1, 2, 3)]
    pre = taps[4:5] + sum(taps[3 - k : 4 - k] * shifted[k] for k in range(4))
    return pre, shifted


def with_earlier(ref, r0, lanes):
    prev = ref[pl.ds(pl.multiple_of(jnp.maximum(r0 - 8, 0), 8), 8), lanes]
    return jnp.concatenate([prev, ref[pl.ds(r0, Q), lanes]], axis=0)


def match_rows(segc, r0):
    prev = segc[pl.ds(pl.multiple_of(jnp.maximum(r0 - 8, 0), 8), 8), :]
    prev = jnp.where(r0 > 0, prev, -1.0)
    cur = segc[pl.ds(r0, Q), :]
    ext = jnp.concatenate([prev, cur], axis=0)
    return [None] + [ext[8 - k : 8 + Q - k] == cur for k in (1, 2, 3)]


def block_setup(c, nv, vals, segc, segr, cbc, hp, bt_ref, b_ref, c_ref, ct_ref, qk_ref, bias_ref, cum_ref, cumt_ref, step_ref, tail_ref, keep_ref, ex_ref, keep_out):
    r0 = pl.multiple_of(c * Q, Q)
    match = match_rows(segc, r0)
    m2 = [None] + [jnp.concatenate([m, m], axis=1) for m in match[1:]]
    ext = with_earlier(vals, r0, pl.ds(nv, 256))
    pre, shifted = conv_terms(ext, m2, cbc[...])
    bc = pre * sigmoid(pre)
    bb = bc[:, :128].astype(BF)
    cc = bc[:, 128:].astype(BF)
    b_ref[...] = bb
    c_ref[...] = cc
    bt_ref[...] = bc[:, :128].T.astype(BF)
    if ct_ref is not None:
        ct_ref[...] = bc[:, 128:].T.astype(BF)
    qk_ref[...] = dnt(cc, bb)
    seg = segc[pl.ds(r0, Q), :]
    segs = segr[0:1, pl.ds(r0, Q)]
    tt, ss = ii((Q, Q), 0), ii((Q, Q), 1)
    allowed = (tt >= ss) & (jnp.concatenate([seg, seg], axis=1) == segs)
    bias_ref[...] = jnp.where(allowed, 0.0, NEG)
    raw = vals[pl.ds(r0, Q), pl.ds(nv + 256, 128)] + hp[0:1]
    step = softplus(raw)
    tri = (tt >= ss).astype(BF)
    cum = tri_times(tri, step * (hp[1:2] * LOG2E))
    cumt = cum.T
    for h in range(nv // 64):
        cumt_ref[h] = jnp.broadcast_to(cumt[h : h + 1], (8, Q))
    exm = ex_ref[...]
    cum_ref[...] = spread3(cum, exm)
    e64 = (ii((128, nv), 0) == ii((128, nv), 1) // 64).astype(BF)
    step_ref[...] = spread3(step, e64)
    prev_seg = jnp.where(c > 0, segc[pl.ds(pl.multiple_of(jnp.maximum(r0 - 8, 0), 8), 8), :][7:8], -1.0)
    last_seg = seg[Q - 1 :]
    cum_last = cum[Q - 1 :]
    carry = (seg == prev_seg).astype(F32)
    tailm = (seg == last_seg).astype(F32)
    tail = jnp.exp2(cum_last - cum) * tailm
    tail_ref[...] = spread3(tail, e64)
    keep = jnp.exp2(cum_last) * (last_seg == prev_seg).astype(F32)
    keep_ref[...] = spread3(jnp.broadcast_to(keep, (8, 128)), e64)
    keep_out[...] = spread3(jnp.exp2(cum) * carry, e64)
    return match, pre, shifted, raw, step


def decay(cum_ref, cumt_ref, bias_ref, h, rows, cols):
    col = cum_ref[rows, pl.ds(pl.multiple_of(h * 128, 128), 128)]
    row = cumt_ref[h, 0:1, cols]
    return jnp.exp2(col - row + bias_ref[rows, cols])


def fwd_scratch(nv):
    V = lambda s, d=F32: pltpu.VMEM(s, d)
    nh = nv // 64
    return dict(
        bt=V((128, Q), BF), b=V((Q, 128), BF), c=V((Q, 128), BF), qk=V((Q, Q)), bias=V((Q, Q)), cum=V((Q, nh * 128)), cumt=V((nh, 8, Q)),
        step=V((Q, nv)), tail=V((Q, nv)), keep=V((8, nv)), ecum=V((Q, nv)), ex=V((128, nh * 128), BF), state=V((128, nv)), m=V((4, Q, Q), BF),
    )


def ssd_forward(nv, vals, segc, segr, cx, cbc, hp, ssd, states, s, hook=lambda at: None):
    nh = nv // 64
    s["ex"][...] = (ii((128, nh * 128), 0) == ii((128, nh * 128), 1) // 128).astype(BF)
    s["state"][...] = jnp.zeros_like(s["state"])
    s["m"][...] = jnp.zeros_like(s["m"])

    def block(c, _):
        r0 = pl.multiple_of(c * Q, Q)
        match, *_r = block_setup(c, nv, vals, segc, segr, cbc, hp, s["bt"], s["b"], s["c"], None, s["qk"], s["bias"], s["cum"], s["cumt"], s["step"], s["tail"], s["keep"], s["ex"], s["ecum"])
        states[c] = s["state"][...].astype(BF)

        def pairs(jj, _):
            hook(c * (nv // 256) + jj)
            done = []
            for p in range(2):
                j = 2 * jj + p
                lanes = pl.ds(pl.multiple_of(j * 128, 128), 128)
                pre, _sh = conv_terms(with_earlier(vals, r0, lanes), match, cx[:, lanes])
                x = pre * sigmoid(pre)
                u = x * s["step"][:, lanes]
                st = s["state"][:, lanes]
                y = dnn(s["c"][...], st.astype(BF)) * s["ecum"][:, lanes] + cx[5:6, lanes] * x
                new = st * s["keep"][0:1, lanes] + dnn(s["bt"][...], (u * s["tail"][:, lanes]).astype(BF))
                done.append((j, lanes, u.astype(BF), y, new))
            for r in range(4):
                rows = slice(r * 64, r * 64 + 64)
                for k in range(1 if r < 2 else 2):
                    cols = slice(k * 128, k * 128 + 128)
                    qk, bias = s["qk"][rows, cols], s["bias"][rows, cols]
                    for p in range(2):
                        for e in range(2):
                            h = 2 * done[p][0] + e
                            col = s["cum"][rows, pl.ds(pl.multiple_of(h * 128, 128), 128)]
                            s["m"][2 * p + e, rows, cols] = (jnp.exp2(col - s["cumt"][h, 0:1, cols] + bias) * qk).astype(BF)
            outs = []
            for p in range(2):
                _j, lanes, ub, y, new = done[p]
                y0, y1 = dnn(s["m"][2 * p], ub), dnn(s["m"][2 * p + 1], ub)
                outs.append(y + jnp.where(ii((Q, 128), 1) < 64, y0, y1))
            for p in range(2):
                ssd[pl.ds(r0, Q), done[p][1]] = outs[p]
                s["state"][:, done[p][1]] = done[p][4]
            return 0

        lax.fori_loop(0, nv // 256, pairs, 0)
        return 0

    lax.fori_loop(0, vals.shape[0] // Q, block, 0)


def later_sum(dpre, halo, match_ext, taps):
    ext = jnp.concatenate([dpre, halo], axis=0)
    n = dpre.shape[0]
    out = taps[3:4] * dpre
    for k in (1, 2, 3):
        out = out + taps[3 - k : 4 - k] * jnp.where(match_ext[k], ext[k : n + k], 0.0)
    return out


def run_forward(nv, vals, segc, segr, cx, cbc, hp):
    sc = fwd_scratch(nv)
    names = list(sc)
    rows = vals.shape[0]

    def kernel(vals, segc, segr, cx, cbc, hp, ssd, states, *scr):
        ssd_forward(nv, vals, segc, segr, cx, cbc, hp, ssd, states, dict(zip(names, scr)))

    vm = pl.BlockSpec(memory_space=pltpu.VMEM)
    return pl.pallas_call(
        kernel, out_shape=(jax.ShapeDtypeStruct((rows, nv), F32), jax.ShapeDtypeStruct((rows // Q, 128, nv), F32)),
        in_specs=[vm] * 6, out_specs=[vm] * 2, scratch_shapes=[sc[n] for n in names],
        compiler_params=pltpu.CompilerParams(vmem_limit_bytes=60 * 2**20), name="scan_forward",
    )(vals, segc, segr, cx, cbc, hp)


def pack_heads(nh, cum, step, tail, ecum):
    parts = list(split3(cum))
    for v in (step, tail, ecum):
        hi = v.astype(BF)
        parts += [hi, (v - hi.astype(F32)).astype(BF)]
    out = parts[0].astype(F32)
    for k, p in enumerate(parts[1:]):
        out = out + pltpu.roll(p.astype(F32), (k + 1) * nh, 1)
    return out.astype(BF)


def unpack_matrix(nh, j):
    k, col = ii((128, 640), 0), ii((128, 640), 1)
    kind = jnp.where(k < 3 * nh, 0, jnp.where(k < 5 * nh, 1, jnp.where(k < 7 * nh, 2, jnp.where(k < 9 * nh, 3, 9))))
    want = jnp.maximum(col // 128 - 1, 0)
    sub = jnp.where(col < 256, col // 128, (col % 128) // 64)
    return ((kind == want) & (k % nh == 2 * j + sub)).astype(BF)


def back_scratch(nv, rows):
    V = lambda s, d=F32: pltpu.VMEM(s, d)
    nb, nh = rows // Q, nv // 64
    return dict(
        b=V((rows, 128), BF), c=V((rows, 128), BF), bt=V((nb, 128, Q), BF), ct=V((nb, 128, Q), BF), qk=V((nb, Q, Q)), bias=V((nb, Q, Q)), pack=V((rows, 128), BF),
        cumt=V((nb, nh, 8, Q)), un=V((2, 128, 640), BF), ex=V((2, Q, 640)), dqk=V((nb, Q, Q)), dcs=V((rows, 128)), dbs=V((rows, 128)), hsum=V((rows, 128)),
        colg=V((nb, nh, 8, Q)), krow=V((nb, 8, nv)), dstate=V((2, 128, 128)), halo=V((2, 8, 128)), halobc=V((8, 256)), m=V((4, Q, Q), BF), dm=V((4, Q, Q)),
    )


def block_rows(c):
    return pl.ds(pl.multiple_of(c * Q, Q), Q)


def wide(match):
    return [None] + [jnp.concatenate([m, m], axis=1) for m in match[1:]]


def back_setup(nv, vals, segc, segr, cbc, hp, s):
    nh = nv // 64
    for n in ("dqk", "dcs", "dbs", "hsum", "m"):
        s[n][...] = jnp.zeros_like(s[n])

    def block(c, _):
        r0 = pl.multiple_of(c * Q, Q)
        rows = block_rows(c)
        pre, _sh = conv_terms(with_earlier(vals, r0, pl.ds(nv, 256)), wide(match_rows(segc, r0)), cbc[...])
        bc = pre * sigmoid(pre)
        bb, cc = bc[:, :128].astype(BF), bc[:, 128:].astype(BF)
        s["b"][rows], s["c"][rows] = bb, cc
        s["bt"][c], s["ct"][c] = bc[:, :128].T.astype(BF), bc[:, 128:].T.astype(BF)
        s["qk"][c] = dnt(cc, bb)
        seg = segc[rows]
        tt, ss = ii((Q, Q), 0), ii((Q, Q), 1)
        allowed = (tt >= ss) & (jnp.concatenate([seg, seg], axis=1) == segr[0:1, rows])
        s["bias"][c] = jnp.where(allowed, 0.0, NEG)
        mine = ii((Q, 128), 1) < nh
        step = jnp.where(mine, softplus(vals[rows, pl.ds(nv + 256, 128)] + hp[0:1]), 0.0)
        cum = tri_times((tt >= ss).astype(BF), step * (hp[1:2] * LOG2E))
        cumt = cum.T
        for h in range(nh):
            s["cumt"][c, h] = jnp.broadcast_to(cumt[h : h + 1], (8, Q))
        before = segc[pl.ds(pl.multiple_of(jnp.maximum(r0 - 8, 0), 8), 8)][7:8]
        before = jnp.where(c > 0, before, -1.0)
        zero = lambda v: jnp.where(mine, v, 0.0)
        tail = zero(jnp.exp2(cum[Q - 1 :] - cum) * (seg == seg[Q - 1 :]).astype(F32))
        ecum = zero(jnp.exp2(cum) * (seg == before).astype(F32))
        s["pack"][rows] = pack_heads(nh, cum, step, tail, ecum)
        return 0

    lax.fori_loop(0, vals.shape[0] // Q, block, 0)


def back_pairs(at, nv, vals, segc, cx, dy_ref, states, low, gx, s):
    nb, nh = vals.shape[0] // Q, nv // 64
    jj, i = at // nb, at % nb
    c = nb - 1 - i
    r0 = pl.multiple_of(c * Q, Q)
    rows_c = block_rows(c)

    @pl.when(i == 0)
    def _():
        s["dstate"][...] = jnp.zeros_like(s["dstate"])
        s["halo"][...] = jnp.zeros_like(s["halo"])
        for p in range(2):
            s["un"][p] = unpack_matrix(nh, 2 * jj + p)

    match, after = match_rows(segc, r0), match_after(segc, r0)
    lane = ii((Q, 128), 1)
    one = []
    dcs = dbs = 0.0
    for p in range(2):
        j = 2 * jj + p
        lanes = pl.ds(pl.multiple_of(j * 128, 128), 128)
        s["ex"][p] = dnn(s["pack"][rows_c], s["un"][p])
        stepe, taile, ecume = s["ex"][p, :, 256:384], s["ex"][p, :, 384:512], s["ex"][p, :, 512:640]
        keep = s["ex"][p, Q - 1 : Q, 512:640]
        taps = cx[:, lanes]
        pre, shifted = conv_terms(with_earlier(vals, r0, lanes), match, taps)
        sig = sigmoid(pre)
        x = pre * sig
        u = x * stepe
        dy = dy_ref[rows_c, lanes].astype(F32)
        stb = states[c, :, lanes]
        dst = s["dstate"][p]
        dstb = dst.astype(BF)
        edy = ecume * dy
        edyb = edy.astype(BF)
        rs = edy * dnn(s["c"][rows_c], stb)
        dcs = dcs + dnt(edyb, stb)
        tu = taile * u
        v = dnn(s["b"][rows_c], dstb)
        dbs = dbs + dnt(tu.astype(BF), dstb)
        krow = keep * jnp.sum(stb.astype(F32) * dst, axis=0, keepdims=True)
        s["dstate"][p] = keep * dst + dnn(s["ct"][c], edyb)
        ub = u.astype(BF)
        for e in range(2):
            mine = (lane < 64) if e == 0 else (lane >= 64)
            s["dm"][2 * p + e] = dnt(jnp.where(mine, dy, 0.0).astype(BF), ub)
        one.append((j, lanes, stepe, taile, taps, shifted, sig, x, dy, dy.T.astype(BF), rs, tu, v, krow))
    s["dcs"][rows_c] += dcs
    s["dbs"][rows_c] += dbs
    colsum = [[jnp.zeros((8, 128), F32) for _ in range(2)] for _ in range(4)]
    rowg = []
    for r in range(4):
        rows = slice(r * 64, r * 64 + 64)
        rowsum = [None] * 4
        for k in range(1 if r < 2 else 2):
            cols = slice(k * 128, k * 128 + 128)
            qk, bias = s["qk"][c, rows, cols], s["bias"][c, rows, cols]
            total = None
            for n in range(4):
                p, e = n // 2, n % 2
                dec = jnp.exp2(s["ex"][p, rows, e * 128 : e * 128 + 128] - s["cumt"][c, 4 * jj + n, 0:1, cols] + bias)
                s["m"][n, rows, cols] = (dec * qk).astype(BF)
                g = s["dm"][n, rows, cols] * dec
                total = g if n == 0 else total + g
                g = g * qk
                rowsum[n] = g if k == 0 else rowsum[n] + g
                colsum[n][k] = colsum[n][k] + jnp.sum(g.reshape(8, 8, 128), axis=0)
            s["dqk"][c, rows, cols] += total
        at_lane = ii((64, 128), 1)
        row = jnp.zeros((64, 128), F32)
        for n in range(4):
            row = jnp.where(at_lane == 48 + 4 * jj + n, jnp.sum(rowsum[n], axis=1, keepdims=True), row)
        rowg.append(row)
    heads = jnp.concatenate(rowg, axis=0)
    ends = []
    for p in range(2):
        j, lanes, stepe, taile, taps, shifted, sig, x, dy, dyt, rs, tu, v, krow = one[p]
        parts = [dnn(dyt[e * 64 : e * 64 + 64], s["m"][2 * p + e]) for e in range(2)]
        du = jnp.concatenate(parts, axis=0).T + taile * v
        k, col = ii((384, 128), 0), ii((384, 128), 1)
        red = (col == 16 * (k // 128) + 2 * j + (k % 128) // 64).astype(BF)
        heads = heads + dnn(jnp.concatenate([rs.astype(BF), (tu * v).astype(BF), (du * x).astype(BF)], axis=1), red)
        dx = du * stepe + taps[5:6] * dy
        dpre = dx * (sig + x * (1.0 - sig))
        grow = jnp.concatenate(
            [jnp.sum(dpre * shifted[3 - k], axis=0, keepdims=True) for k in range(4)]
            + [jnp.sum(dpre, axis=0, keepdims=True), jnp.sum(dy * x, axis=0, keepdims=True), jnp.zeros((2, 128), F32)], axis=0)
        ends.append((later_sum(dpre, s["halo"][p], after, taps).astype(BF), dpre[:8], grow))
    s["hsum"][rows_c] += heads
    for n in range(4):
        s["colg"][c, 4 * jj + n] = jnp.broadcast_to(jnp.concatenate([jnp.sum(q, axis=0, keepdims=True) for q in colsum[n]], axis=1), (8, Q))
    for p in range(2):
        lanes = one[p][1]
        low[rows_c, lanes], s["halo"][p] = ends[p][0], ends[p][1]
        gx[:, lanes] += ends[p][2]
        s["krow"][c, :, lanes] = jnp.broadcast_to(one[p][13], (8, 128))


def match_after(segc, r0):
    nxt = segc[pl.ds(pl.multiple_of(jnp.minimum(r0 + Q, segc.shape[0] - 8), 8), 8)]
    seg = segc[pl.ds(r0, Q)]
    ext = jnp.concatenate([seg, nxt], axis=0)
    return [None] + [ext[k : Q + k] == seg for k in (1, 2, 3)]


def back_finish(nv, vals, segc, cbc, hp, low, gbc, gh, s):
    nb, nh = vals.shape[0] // Q, nv // 64
    s["halobc"][...] = jnp.zeros_like(s["halobc"])
    gbc[...] = jnp.zeros_like(gbc)
    gh[...] = jnp.zeros_like(gh)

    def block(i, _):
        c = nb - 1 - i
        r0 = pl.multiple_of(c * Q, Q)
        rows = block_rows(c)
        tt, ss = ii((Q, Q), 0), ii((Q, Q), 1)
        e64t = (ii((nv, 128), 0) // 64 == ii((nv, 128), 1)).astype(BF)
        kterm = sum(dnn(p, e64t) for p in split3(s["krow"][c]))
        colg = jnp.concatenate([s["colg"][c, h, 0:1] for h in range(nh)] + [jnp.zeros((128 - nh, Q), F32)], axis=0)
        hs = s["hsum"][rows]
        mine = ii((Q, 128), 1) < nh
        part = lambda k: jnp.where(mine, hs if k == 0 else pltpu.roll(hs, 128 - 16 * k, 1), 0.0)
        dcum = part(3) - colg.T + part(0)
        da = tri_times((ss >= tt).astype(BF), dcum) + tri_times((ss < tt).astype(BF), part(1)) + kterm[0:1]
        rate = hp[1:2]
        raw = vals[rows, pl.ds(nv + 256, 128)] + hp[0:1]
        draw = jnp.where(mine, (part(2) + rate * da) * sigmoid(raw), 0.0)
        low[rows, pl.ds(nv + 256, 128)] = draw.astype(BF)
        gh[...] += jnp.concatenate(
            [jnp.sum(draw, axis=0, keepdims=True), jnp.sum(da * softplus(raw), axis=0, keepdims=True) * rate, jnp.zeros((6, 128), F32)], axis=0)
        dqk = s["dqk"][c]
        dc = dnn(dqk.astype(BF), s["b"][rows]) + s["dcs"][rows]
        db = dnn(dqk.T.astype(BF), s["c"][rows]) + s["dbs"][rows]
        pre, shifted = conv_terms(with_earlier(vals, r0, pl.ds(nv, 256)), wide(match_rows(segc, r0)), cbc[...])
        sig = sigmoid(pre)
        dpre = jnp.concatenate([db, dc], axis=1) * (sig + pre * sig * (1.0 - sig))
        low[rows, pl.ds(nv, 256)] = later_sum(dpre, s["halobc"][...], wide(match_after(segc, r0)), cbc[...]).astype(BF)
        s["halobc"][...] = dpre[:8]
        gbc[...] += jnp.concatenate(
            [jnp.sum(dpre * shifted[3 - k], axis=0, keepdims=True) for k in range(4)] + [jnp.sum(dpre, axis=0, keepdims=True), jnp.zeros((3, 256), F32)], axis=0)
        return 0

    lax.fori_loop(0, nb, block, 0)


def run_backward2(nv, vals, segc, segr, cx, cbc, hp, dy, states):
    rows = vals.shape[0]
    sc = back_scratch(nv, rows)
    names = list(sc)

    def kernel(vals, segc, segr, cx, cbc, hp, dy, states, low, gx, gbc, gh, *scr):
        s = dict(zip(names, scr))
        gx[...] = jnp.zeros_like(gx)
        back_setup(nv, vals, segc, segr, cbc, hp, s)

        def body(at, _):
            back_pairs(at, nv, vals, segc, cx, dy, states, low, gx, s)
            return 0

        lax.fori_loop(0, nv // 256 * (rows // Q), body, 0)
        back_finish(nv, vals, segc, cbc, hp, low, gbc, gh, s)

    vm = pl.BlockSpec(memory_space=pltpu.VMEM)
    outs = (jax.ShapeDtypeStruct((rows, nv + 384), BF), jax.ShapeDtypeStruct((8, nv), F32), jax.ShapeDtypeStruct((8, 256), F32), jax.ShapeDtypeStruct((8, 128), F32))
    return pl.pallas_call(
        kernel, out_shape=outs, in_specs=[vm] * 8, out_specs=[vm] * 4, scratch_shapes=[sc[n] for n in names],
        compiler_params=pltpu.CompilerParams(vmem_limit_bytes=60 * 2**20), name="scan_backward",
    )(vals, segc, segr, cx, cbc, hp, dy, states)


INNER = 3072
EPS = 1e-05


def at_step(step, events):
    for k, fn in events:

        @pl.when(step == k)
        def _(fn=fn):
            fn()


def forward_kernel(
    names, nv,
    hid, cot_own, p_x, p_bc, p_dt, p_gate, p_out, pgain, seg, conv_x, bias_x, conv_bc, bias_bc, dt_bias, a_log, skip_d, gate_gain,
    o_w0, o_w1, o_w2, o_w3, o_nrm, o_cot, o_vals, o_states, o_no, o_lg, o_dy, o_gg, cx, cbc, hp, segc, segr,
    square, w_own1, w0, w1, w2, w3, nrm, cot, vals, states, ssd, gate, gno, no, lg, dy, sums_own, sums_in,
    wsend, wrecv, tsend, trecv, ssend, srecv, lsem, *scan_scratch,
):
    s = dict(zip(names, scan_scratch))
    x, z, yh, t = place()
    yl, co = t // 2, t % 2
    tp, slots = tensor_peers()
    width = hid.shape[1]
    cut = w0.shape[1]
    w_own0, w_own2, w_own3 = p_x.at[:, :cut], p_gate, p_out
    w_own1[...] = jnp.zeros_like(w_own1)
    w_own1[:, : nv - cut] = p_x[:, cut:]
    w_own1[:, nv - cut : nv - cut + 256] = p_bc[...]
    square[...] = jnp.zeros_like(square)
    square[: p_dt.shape[0], : p_dt.shape[1]] = p_dt[...].astype(F32)
    w_own1[:, nv - cut + 256 :] = square[...].T[: p_dt.shape[1]].astype(BF)
    greet([dev(x, z, 1 - yh, t)] + [neighbour(a, d) for a in "xz" for d in (1, -1)] + tp)
    owns, dsts, outs = (w_own0, w_own1, w_own2, w_own3), (w0, w1, w2, w3), (o_w0, o_w1, o_w2, o_w3)
    groups = lambda ks: [Gather(owns[k], dsts[k], "xz"[k % 2], wsend.at[k], wrecv.at[k]) for k in ks]
    first, second = (0, 1), (2, 3)

    def step(ks, n):
        for g in groups(ks):
            g.step(n)

    def saved(i, src, dst):
        return pltpu.make_async_copy(src, dst, lsem.at[i])

    mine = pl.ds(pl.multiple_of(t * 256, 256), 256)
    theirs = pl.ds(pl.multiple_of(slots[1] * 256, 256), 256)

    def tensor_copies(i, own, dst):
        return (
            send(own, dst.at[mine], tsend.at[i, 0], trecv.at[i, 0], tp[1]),
            send(own, dst.at[mine], tsend.at[i, 1], trecv.at[i, 1], tp[0]),
            send(dst.at[theirs], dst.at[theirs], tsend.at[i, 2], trecv.at[i, 2], tp[0]),
        )

    for g in groups((0, 1, 2, 3)):
        g.begin()
    step(first, 0)

    def norm_rows(i, _):
        rows = pl.ds(pl.multiple_of(i * 64, 64), 64)
        h = hid[rows].astype(F32)
        inv = lax.rsqrt(jnp.mean(h * h, axis=1, keepdims=True) + EPS)
        nrm[pl.ds(pl.multiple_of(t * 256 + i * 64, 64), 64)] = (h * inv * pgain[0:1]).astype(BF)
        return 0

    lax.fori_loop(0, 4, norm_rows, 0)
    own_lanes = pl.ds(pl.multiple_of(t * nv, 128), nv)
    heads = p_dt.shape[0]

    def own_heads(v, lanes, per):
        i, j = ii((v.shape[1], lanes), 0), ii((v.shape[1], lanes), 1)
        pick = ((i == t * heads + j // per) & (j < heads * per)).astype(BF)
        return sum(dnn(part, pick) for part in split3(jnp.broadcast_to(v[...], (8, v.shape[1]))))

    cx[0:4] = conv_x[:, own_lanes]
    cx[4:5] = bias_x[:, own_lanes]
    cx[5:8] = own_heads(skip_d, nv, 64)[5:8]
    cbc[0:4] = conv_bc[...]
    cbc[4:8] = jnp.broadcast_to(bias_bc[...], (4, 256))
    hp[0:1] = own_heads(dt_bias, 128, 1)[0:1]
    hp[1:2] = jnp.where(ii((1, 128), 1) < heads, -jnp.exp(own_heads(a_log, 128, 1)[0:1]), 0.0)
    hp[2:8] = jnp.zeros((6, 128), F32)
    gains = gate_gain[:, own_lanes]
    sf = seg[...].astype(F32)
    for k in range(seg.shape[0]):
        segr[:, k * 128 : k * 128 + 128] = jnp.broadcast_to(sf[k : k + 1], (8, 128))
        segc[k * 128 : k * 128 + 128] = jnp.broadcast_to(sf[k : k + 1], (128, 128)).T
    for k in range(4):
        g = groups((k,))[0]
        g.mine[...] = g.own[...]
    cot[mine] = cot_own[...]
    nrm_copies = tensor_copies(0, nrm.at[mine], nrm)
    cot_copies = tensor_copies(1, cot_own, cot)
    nrm_copies[0].start()
    nrm_copies[1].start()
    for n in (1, 4, 2, 3):
        step(first, n)
    cot_copies[0].start()
    cot_copies[1].start()
    step(second, 0)
    step(second, 1)
    step(first, 5)
    step(first, 6)
    nrm_copies[0].wait_recv()
    nrm_copies[2].start()
    step(second, 4)
    step(first, 7)
    nrm_copies[1].wait_recv()
    nrm_copies[2].wait_recv()

    def project(i, _):
        pl.when(i == 2)(lambda: step(second, 2))
        rows = pl.ds(pl.multiple_of(i * 256, 256), 256)
        n = nrm[rows]
        at = 0
        for w in (w0, w1):
            c = w.shape[1]
            vals[rows, at : at + c] = jnp.dot(n, w[...], preferred_element_type=F32)
            at += c
        return 0

    lax.fori_loop(0, 4, project, 0)
    early = [(0, w0, o_w0), (1, w1, o_w1), (2, nrm, o_nrm), (3, vals, o_vals)]
    for e in early:
        saved(*e).start()

    def cot_forward():
        cot_copies[0].wait_recv()
        cot_copies[2].start()

    events = [(1, lambda: step(second, 3)), (3, lambda: step(second, 5)), (5, lambda: step(second, 6)), (7, cot_forward)]
    ssd_forward(nv, vals, segc, segr, cx, cbc, hp, ssd, states, s, lambda at: at_step(at, events))
    step(second, 7)
    cot_copies[1].wait_recv()
    cot_copies[2].wait_recv()
    late = [(4, w2, o_w2), (5, w3, o_w3), (6, cot, o_cot), (7, states, o_states)]
    for e in late:
        saved(*e).start()

    def inner(i, _):
        rows = pl.ds(pl.multiple_of(i * 256, 256), 256)
        g = jnp.dot(nrm[rows], w2[...], preferred_element_type=F32)
        gate[rows] = g
        o = jnp.dot(cot[rows], w3[...], preferred_element_type=F32)
        gno[rows] = o
        gated = ssd[rows] * (g * sigmoid(g))
        sq = jnp.sum(gated * gated, axis=1, keepdims=True)
        cr = jnp.sum(o * gains * gated, axis=1, keepdims=True)
        lane = ii((256, 128), 1)
        both = jnp.where(lane == 0, sq, jnp.where(lane == 1, cr, 0.0))
        sums_own[:, rows] = both.T[:8]
        return 0

    lax.fori_loop(0, 4, inner, 0)
    small = [send(sums_own, sums_in.at[k], ssend.at[k], srecv.at[k], p) for k, p in enumerate(tp)]
    for c in small:
        c.start()
    for c in small:
        c.wait_recv()
    o_gg[...] = jnp.zeros_like(o_gg)

    def outer(i, _):
        rows = pl.ds(pl.multiple_of(i * 256, 256), 256)
        tot = sums_own[:, rows] + sums_in[0, :, rows] + sums_in[1, :, rows] + sums_in[2, :, rows]
        cols = jnp.concatenate([tot, jnp.zeros((120, 256), F32)], axis=0).T
        inv = lax.rsqrt(cols[:, 0:1] / INNER + EPS)
        cross = inv * inv * inv * cols[:, 1:2] / INNER
        for k in range(nv // 128):
            lanes = pl.ds(k * 128, 128)
            g, y, o, gain = gate[rows, lanes], ssd[rows, lanes], gno[rows, lanes], gains[:, k * 128 : k * 128 + 128]
            sig = sigmoid(g)
            silu = g * sig
            gated = y * silu
            scaled = gated * inv
            no[rows, lanes] = (scaled * gain).astype(BF)
            o_gg[0:1, lanes] += jnp.sum(o * scaled, axis=0, keepdims=True)
            grad = o * gain * inv - gated * cross
            dy[rows, lanes] = (grad * silu).astype(BF)
            lg[rows, lanes] = (grad * y * (sig + silu * (1.0 - sig))).astype(BF)
        return 0

    lax.fori_loop(0, 4, outer, 0)
    last = [(8, no, o_no), (9, lg, o_lg), (10, dy, o_dy)]
    for e in last:
        saved(*e).start()
    for g in groups((0, 1, 2, 3)):
        g.finish()
    for c in nrm_copies + cot_copies + tuple(small):
        c.wait_send()
    for e in early + late + last:
        saved(*e).wait()


def run_k1(hid, cot_own, projs, pgain, seg, params):
    anys, vm = pl.BlockSpec(memory_space=pl.ANY), pl.BlockSpec(memory_space=pltpu.VMEM)
    nv = projs[0].shape[1]
    rows = seg.shape[0] * seg.shape[1]
    n, d = projs[0].shape[0], hid.shape[1]
    sh = jax.ShapeDtypeStruct
    cols = [nv - 128, 512, nv, nv]
    nvals = cols[0] + cols[1]
    outs = [sh((d, c), BF) for c in cols] + [sh((rows, d), BF)] * 2 + [sh((rows, nvals), F32), sh((rows // Q, 128, nv), BF)] + [sh((rows, nv), BF)] * 3
    outs += [sh((8, nv), F32), sh((8, nv), F32), sh((8, 256), F32), sh((8, 128), F32), sh((rows, 128), F32), sh((8, rows), F32)]
    V = lambda shape, dt: pltpu.VMEM(shape, dt)
    D = pltpu.SemaphoreType.DMA
    scan = fwd_scratch(nv)
    scratch = [V((128, 128), F32), V((n, cols[1]), BF)] + [V((d, c), BF) for c in cols] + [V((rows, d), BF)] * 2
    scratch += [V((rows, nvals), F32), V((rows // Q, 128, nv), BF)] + [V((rows, nv), F32)] * 3 + [V((rows, nv), BF)] * 3
    scratch += [V((8, rows), F32), V((3, 8, rows), F32), D((4, Gather.N)), D((4, Gather.N)), D((2, 3)), D((2, 3)), D((3,)), D((3,)), D((11,))]
    scratch += list(scan.values())
    return pl.pallas_call(
        functools.partial(forward_kernel, list(scan), nv), out_shape=outs, in_specs=[vm] * 17, out_specs=[anys] * 11 + [vm] * 6, scratch_shapes=scratch,
        compiler_params=pltpu.CompilerParams(collective_id=0, has_side_effects=True, vmem_limit_bytes=62 * 2**20), name="forward_all",
    )(hid, cot_own, *projs, pgain, seg, *params)


class Scatter:
    N = 13

    def __init__(self, v, bufs, out, a1, send_sem, recv_sem):
        x, z, yh, t = place()
        self.v, self.out, self.a1, self.yh = v, out, a1, yh
        self.r1, self.r2, self.q1, self.q2, self.kk, self.yy = bufs
        self.h = self.r2.at[0]
        a2 = "z" if a1 == "x" else "x"
        self.p, self.q = (x, z) if a1 == "x" else (z, x)
        self.send_sem, self.recv_sem = send_sem, recv_sem
        right1, left1, right2, left2 = neighbour(a1, 1), neighbour(a1, -1), neighbour(a2, 1), neighbour(a2, -1)
        r1, r2, h, q1, q2, q = self.r1, self.r2, self.h, self.q1, self.q2, self.q
        self.plan = [
            (self.half(2, 0), r1.at[0], right1), (self.half(2, 1), r1.at[1], left1),
            (self.half(1, 1), r2.at[0, pl.ds(2, 2)], right1), (self.half(-1, 0), r2.at[1, pl.ds(0, 2)], left1),
            (self.half(1, 0), r2.at[0, pl.ds(0, 2)], right1), (self.half(-1, 1), r2.at[1, pl.ds(2, 2)], left1),
            (h.at[m4(q + 2), 0], q1.at[0], right2), (h.at[m4(q + 2), 1], q1.at[1], left2),
            (h.at[m4(q + 1), 1], q2.at[0, 1], right2), (h.at[m4(q - 1), 0], q2.at[1, 0], left2),
            (h.at[m4(q + 1), 0], q2.at[0, 0], right2), (h.at[m4(q - 1), 1], q2.at[1, 1], left2),
            (self.kk, self.yy, dev(x, z, 1 - yh, t)),
        ]

    def half(self, d, k):
        at = m4(self.p + d)
        return self.v.at[pl.ds(2 * k, 2), at] if self.a1 == "z" else self.v.at[at, pl.ds(2 * k, 2)]

    def copy(self, k):
        src, dst, to = self.plan[k]
        return send(src, dst, self.send_sem.at[k], self.recv_sem.at[k], to)

    def start(self, *ks):
        for k in ks:
            self.copy(k).start()

    def arrive(self, *ks):
        for k in ks:
            self.copy(k).wait_recv()

    def step(self, n):
        v, r1, r2, h, q1, q2, p, q, yh = self.v, self.r1, self.r2, self.h, self.q1, self.q2, self.p, self.q, self.yh
        if n == 0:
            self.start(0, 1, 2, 3)
        elif n == 1:
            for side, d in ((0, 1), (1, -1)):
                self.arrive(side)
                at = m4(p + d)

                def add(j, _, side=side, at=at):
                    e, y = j // 2, j % 2
                    ix = (2 * side + e, at, y) if self.a1 == "z" else (at, 2 * side + e, y)
                    v[ix] = v[ix] + r1[side, e, y]
                    return 0

                lax.fori_loop(0, 4, add, 0)
                self.start(4 + side)
        elif n == 2:
            self.arrive(2, 3, 4, 5)

            def add(j, _):
                e, y = j // 2, j % 2
                own = v[e, p, y] if self.a1 == "z" else v[p, e, y]
                h[e, y] = own + (r2[0, e, y] + r2[1, e, y])
                return 0

            lax.fori_loop(0, 8, add, 0)
            self.start(6, 7, 8, 9)
        elif n == 3:
            for side, d in ((0, 1), (1, -1)):
                self.arrive(6 + side)
                at = m4(q + d)
                h[at, side] = h[at, side] + q1[side]
                self.start(10 + side)
        elif n == 4:
            self.arrive(8, 9, 10, 11)
            self.kk[...] = (h[q, 1 - yh].astype(F32) + q2[0, 1 - yh].astype(F32) + q2[1, 1 - yh].astype(F32)).astype(BF)
            self.start(12)
        else:
            self.arrive(12)
            self.out[...] = h[q, yh].astype(F32) + q2[0, yh].astype(F32) + q2[1, yh].astype(F32) + self.yy[...].astype(F32)

    def finish(self):
        for k in range(self.N):
            self.copy(k).wait_send()


class TokenScatter:
    def __init__(self, v, from_core, from_chip, out, send_sem, recv_sem):
        t = place()[3]
        tp, slots = tensor_peers()
        self.t, self.v, self.from_core, self.from_chip, self.out = t, v, from_core, from_chip, out
        rows = lambda s: pl.ds(pl.multiple_of(s * 256, 256), 256)
        self.pass_on, self.mine = slots[1], rows(t)
        self.copies = lambda k: (
            lambda: send(v.at[rows(slots[2])], from_core.at[0], send_sem.at[0], recv_sem.at[0], tp[0]),
            lambda: send(v.at[rows(slots[0])], from_core.at[1], send_sem.at[1], recv_sem.at[1], tp[0]),
            lambda: send(v.at[rows(slots[1])], from_chip, send_sem.at[2], recv_sem.at[2], tp[1]),
        )[k]()

    def step(self, n):
        if n == 0:
            self.copies(0).start()
            self.copies(1).start()
        elif n == 1:
            self.copies(0).wait_recv()

            def add(j, _):
                rows = pl.ds(pl.multiple_of(j * 32, 32), 32)
                own = pl.ds(pl.multiple_of(self.pass_on * 256 + j * 32, 32), 32)
                self.v[own] = self.v[own] + self.from_core[0, rows]
                return 0

            lax.fori_loop(0, 8, add, 0)
            self.copies(2).start()
        else:
            self.copies(1).wait_recv()
            self.copies(2).wait_recv()

            def add(j, _):
                rows = pl.ds(pl.multiple_of(j * 32, 32), 32)
                own = self.v[pl.ds(pl.multiple_of(self.t * 256 + j * 32, 32), 32)]
                self.out[rows] = own.astype(F32) + self.from_core[1, rows].astype(F32) + self.from_chip[rows].astype(F32)
                return 0

            lax.fori_loop(0, 8, add, 0)

    def finish(self):
        for k in range(3):
            self.copies(k).wait_send()


def backward_kernel(
    names, nv,
    h_w0, h_w1, h_w2, h_w3, h_nrm, h_cot, h_vals, h_states, h_no, h_lg, h_dy, pgain, segc, segr, cx, cbc, hp, gg,
    o_gate, o_out, o_x, o_dt, o_bc, o_own, o_grad, o_small,
    w0, w1, w23, nrm, cot, vals, states, nody, lg, low, po, t_out, t_gate, t_0, t_1, t_2, t_bc, t_dt,
    bc_sum, own_v, sx, sz, sy, st, sacc, bct, fc0, ch0, fc1, ch1, gx, gbc, gh, pre,
    wsend, wrecv, tsend, trecv, ssend, srecv, bsend, brecv, lsem, *rest,
):
    bufs, s = [rest[6 * k : 6 * k + 6] for k in range(7)], dict(zip(names, rest[42:]))
    x, z, yh, t = place()
    tp, slots = tensor_peers()
    loads = [
        pltpu.make_async_copy(a, b, lsem.at[k])
        for k, (a, b) in enumerate(((h_no, nody), (h_w3, w23), (h_cot, cot), (h_nrm, nrm), (h_lg, lg), (h_vals, vals), (h_states, states), (h_w0, w0), (h_w1, w1)))
    ]
    for c in loads:
        c.start()
    load_dy, load_w2 = pltpu.make_async_copy(h_dy, nody, lsem.at[9]), pltpu.make_async_copy(h_w2, w23, lsem.at[10])
    greet([dev(x, z, 1 - yh, t)] + [neighbour(a, d) for a in "xz" for d in (1, 2, 3)] + tp)
    wide_x = o_x.shape[1] // 3
    x_part = lambda k: o_x.at[:, k * wide_x : k * wide_x + wide_x]
    scat = [
        Scatter(v, bufs[k], o, "xzxzxzx"[k], wsend.at[k], wrecv.at[k])
        for k, (v, o) in enumerate(((t_out, o_out), (t_gate, o_gate), (t_0, x_part(0)), (t_1, x_part(1)), (t_2, x_part(2)), (t_bc, bc_sum), (t_dt, o_dt)))
    ]
    s_out, s_gate, s_0, s_1, s_2, s_bc, s_dt = scat
    k_out = TokenScatter(po, fc0, ch0, o_own, tsend.at[0], trecv.at[0])
    k_nrm = TokenScatter(cot, fc1, ch1, o_grad, tsend.at[1], trecv.at[1])

    def by_rows(fn):
        def body(i, _):
            fn(pl.ds(pl.multiple_of(i * 256, 256), 256))
            return 0

        lax.fori_loop(0, 4, body, 0)

    def outer_product(dst, left, right):
        def body(i, _):
            cols = pl.ds(pl.multiple_of(i * 384, 384), 384)
            r = lax.dot_general(left[:, cols], right[...], (((0,), (0,)), ((), ())), preferred_element_type=F32)
            dst[i] = r.astype(BF).reshape(dst.shape[1:])
            return 0

        lax.fori_loop(0, 4, body, 0)

    loads[0].wait()
    loads[2].wait()
    outer_product(t_out, cot, nody)
    s_out.step(0)
    loads[3].wait()
    loads[4].wait()
    outer_product(t_gate, nrm, lg)
    s_gate.step(0)

    def out_rows(rows):
        left = nody[rows]
        for k in range(0, po.shape[1], 512):
            po[rows, k : k + 512] = dnt(left, w23[k : k + 512]).astype(BF)

    loads[1].wait()
    by_rows(out_rows)
    load_w2.start()
    load_dy.start()
    k_out.step(0)
    for k in (5, 6, 7, 8):
        loads[k].wait()
    back_setup(nv, vals, segc, segr, cbc, hp, s)
    load_dy.wait()
    both = lambda n: lambda: (s_out.step(n), s_gate.step(n))

    def chunk(n):
        def go():
            outer_product((t_0, t_1, t_2)[n], nrm, low.at[:, n * wide_x : n * wide_x + wide_x])
            scat[2 + n].step(0)

        return go

    gx[...] = jnp.zeros_like(gx)
    events = [
        (1, lambda: k_out.step(1)),
        (4, both(1)),
        (6, chunk(0)),
        (8, both(2)),
        (9, chunk(1)),
        (10, lambda: k_out.step(2)),
        (11, both(3)),
    ]

    def scan_step(at, _):
        at_step(at, events)
        back_pairs(at, nv, vals, segc, cx, nody, states, low, gx, s)
        return 0

    lax.fori_loop(0, nv // 256 * (vals.shape[0] // Q), scan_step, 0)
    chunk(2)()
    back_finish(nv, vals, segc, cbc, hp, low, gbc, gh, s)
    outer_product(t_bc, nrm, low.at[:, nv : nv + 256])
    s_bc.step(0)
    outer_product(t_dt, nrm, low.at[:, nv + 256 :])
    s_dt.step(0)
    s_out.step(4)
    s_gate.step(4)
    s_0.step(1)
    s_1.step(1)
    load_w2.wait()
    pre[...] = jnp.zeros_like(pre)
    c0 = w0.shape[1]

    def grad_rows(rows):
        for k in range(0, cot.shape[1], 512):
            cols = slice(k, k + 512)
            g = dnt(lg[rows], w23[cols]) + dnt(low[rows, :c0], w0[cols]) + dnt(low[rows, c0:], w1[cols])
            pre[0:1, cols] += jnp.sum(g * nrm[rows, cols].astype(F32), axis=0, keepdims=True)
            cot[rows, cols] = g.astype(BF)

    def grad_slot(i, _):
        slot = ((t // 2 + 1 - i // 2) % 2) * 2 + (t + 1 - i % 2) % 2
        grad_rows(pl.ds(pl.multiple_of(slot * 256, 256), 256))
        at_step(i, [(0, lambda: k_nrm.copies(0).start()), (1, lambda: k_nrm.step(1)), (2, lambda: k_nrm.copies(1).start())])
        return 0

    lax.fori_loop(0, 4, grad_slot, 0)
    own_v[...] = jnp.zeros_like(own_v)
    own_v[0:6] = gx[0:6]
    own_v[6:7] = gg[0:1]
    pv = pre[0:1] / pgain[0:1]
    own_v[7:8], own_v[8:9] = pv[:, :nv], pv[:, nv:]
    for k in range(3):
        own_v[9:10, k * 256 : k * 256 + 256] = gbc[k : k + 1]
    for k in range(2):
        own_v[10:11, k * 256 : k * 256 + 256] = gbc[3 + k : 4 + k]
        own_v[11:12, k * 128 : k * 128 + 128] = gh[k : k + 1]
    small = [send(own_v, sx.at[d - 1], ssend.at[d - 1], srecv.at[d - 1], neighbour("x", d)) for d in (1, 2, 3)]
    for c in small:
        c.start()
    s_2.step(1)
    s_bc.step(1)
    s_dt.step(1)
    s_out.step(5)
    s_gate.step(5)
    s_0.step(2)
    s_1.step(2)

    def next_small(have, total, copies):
        for c in have:
            c.wait_recv()
        total()
        for c in copies:
            c.start()
        return copies

    def total_x():
        sacc[0] = own_v[...] + sx[0] + sx[1] + sx[2]

    def total_z():
        sacc[1] = sacc[0] + sz[0] + sz[1] + sz[2]

    def total_y():
        sacc[2] = sacc[1] + sy[...]

    small_z = next_small(small, total_x, [send(sacc.at[0], sz.at[d - 1], ssend.at[2 + d], srecv.at[2 + d], neighbour("z", d)) for d in (1, 2, 3)])
    s_2.step(2)
    s_bc.step(2)
    s_dt.step(2)
    small_y = next_small(small_z, total_z, [send(sacc.at[1], sy, ssend.at[6], srecv.at[6], dev(x, z, 1 - yh, t))])
    s_0.step(3)
    s_1.step(3)
    s_2.step(3)
    s_bc.step(3)
    s_dt.step(3)
    small_t = next_small(small_y, total_y, [send(sacc.at[2], st.at[k], ssend.at[7 + k], srecv.at[7 + k], p) for k, p in enumerate(tp)])
    s_2.step(4)
    s_bc.step(4)
    s_dt.step(4)
    s_0.step(4)
    s_1.step(4)
    s_2.step(5)
    s_bc.step(5)
    s_dt.step(5)
    s_0.step(5)
    s_1.step(5)
    bct[3] = bc_sum[...]
    bcs = [send(bct.at[3], bct.at[k], bsend.at[k], brecv.at[k], p) for k, p in enumerate(tp)]
    for c in bcs:
        c.start()
    k_nrm.step(2)
    for c in small_t:
        c.wait_recv()
    o_small[t] = sacc[2]
    for k in range(3):
        o_small[slots[k]] = st[k]
    for c in bcs:
        c.wait_recv()
    o_bc[...] = bct[3] + bct[0] + bct[1] + bct[2]
    for c in small + small_z + small_y + small_t + bcs:
        c.wait_send()
    for g in scat + [k_out, k_nrm]:
        g.finish()


def run_k2(ws, nrm, cot, vals, states, no, lg, dy, pgain, segc, segr, cx, cbc, hp, gg):
    anys, vm = pl.BlockSpec(memory_space=pl.ANY), pl.BlockSpec(memory_space=pltpu.VMEM)
    nv = cx.shape[1]
    rows, d = nrm.shape
    sh = lambda *s: jax.ShapeDtypeStruct(s, F32)
    cols = [w.shape[1] for w in ws]
    n = d // 32
    V = lambda *s, dt=BF: pltpu.VMEM(s, dt)
    D = pltpu.SemaphoreType.DMA
    parts = (nv, nv, nv // 3, nv // 3, nv // 3, 256, 128)
    outs = [sh(n, nv), sh(n, nv), sh(n, nv), sh(n, 128), sh(n, 256), sh(256, d), sh(256, d), sh(4, 16, nv)]
    term = lambda c: V(4, 4, 2, n, c)
    scratch = [V(d, cols[0]), V(d, cols[1]), V(d, cols[2]), V(rows, d), V(rows, d), V(*vals.shape, dt=F32), V(*states.shape), V(rows, nv), V(rows, nv), V(*vals.shape), V(rows, d)]
    scratch += [term(c) for c in parts]
    sv = (16, nv)
    scratch += [V(n, 256, dt=F32)]
    scratch += [V(*sv, dt=F32), V(3, *sv, dt=F32), V(3, *sv, dt=F32), V(*sv, dt=F32), V(3, *sv, dt=F32), V(3, *sv, dt=F32), V(4, n, 256, dt=F32)]
    scratch += [V(2, 256, d), V(256, d)] * 2
    scratch += [V(8, nv, dt=F32), V(8, 256, dt=F32), V(8, 128, dt=F32), V(8, d, dt=F32)]
    scratch += [D((7, Scatter.N))] * 2 + [D((2, 3))] * 2 + [D((10,))] * 2 + [D((3,))] * 2 + [D((11,))]
    for c in parts:
        scratch += [V(2, 2, 2, n, c), V(2, 4, 2, n, c), V(2, n, c), V(2, 2, n, c), V(n, c), V(n, c)]
    scan = back_scratch(nv, rows)
    scratch += list(scan.values())
    return pl.pallas_call(
        functools.partial(backward_kernel, list(scan), nv), out_shape=outs, in_specs=[anys] * 11 + [vm] * 7, out_specs=[vm] * 8, scratch_shapes=scratch,
        compiler_params=pltpu.CompilerParams(collective_id=1, has_side_effects=True, vmem_limit_bytes=64 * 2**20), name="backward_all",
    )(*ws, nrm, cot, vals, states, no, lg, dy, pgain, segc, segr, cx, cbc, hp, gg)


def finish_kernel(
    heads, hid, cot, pgain, own_out, grad_own, smalls, r_gate, r_out, r_x, r_last, r_bc,
    out, d_hid, d_pre, d_gate, d_x, d_bc, d_dt, d_conv_x, d_bias_x, d_conv_bc, d_bias_bc, d_dt_bias, d_a_log, d_skip, d_gain, d_out, square,
):
    def rows(i, _):
        at = pl.ds(pl.multiple_of(i * 64, 64), 64)
        h = hid[at].astype(F32)
        g = grad_own[at]
        inv = lax.rsqrt(jnp.mean(h * h, axis=1, keepdims=True) + EPS)
        scaled = g * pgain[...]
        back = jnp.mean(scaled * h, axis=1, keepdims=True)
        out[at] = (h + own_out[at]).astype(BF)
        d_hid[at] = cot[at].astype(F32) + scaled * inv - h * (inv * inv * inv * back)
        return 0

    lax.fori_loop(0, hid.shape[0] // 64, rows, 0)
    nv = smalls.shape[2]
    square[...] = jnp.zeros_like(square)
    d_gate[...] = r_gate[...]
    d_out[...] = r_out[...]
    d_x[...] = r_x[...]
    d_bc[...] = r_bc[...]
    square[: r_last.shape[0]] = r_last[...]
    d_dt[...] = square[...].T[:heads, : r_last.shape[0]]
    parts = [smalls[k] for k in range(4)]
    both = parts[0] + parts[1] + parts[2] + parts[3]
    d_pre[:, :nv] = both[7:8]
    d_pre[:, nv:] = both[8:9]
    for k in range(3):
        d_conv_bc[k : k + 1] = both[9:10, k * 256 : k * 256 + 256]
    d_conv_bc[3:4] = both[10:11, :256]
    d_bias_bc[...] = both[10:11, 256:512]
    per_head = [jnp.zeros((8, 128), F32)] * 3
    for k in range(4):
        lanes = slice(k * nv, k * nv + nv)
        d_conv_x[:, lanes] = parts[k][0:4]
        d_bias_x[:, lanes] = parts[k][4:5]
        d_gain[:, lanes] = parts[k][6:7]
        row = parts[k][8:16]
        i, j = ii((128, 128), 0), ii((128, 128), 1)
        pick = ((i + k * heads == j) & (i < heads)).astype(BF)
        for n in range(2):
            per_head[n] = per_head[n] + sum(dnn(p, pick) for p in split3(row[:, n * 128 : n * 128 + 128]))
        i, j = ii((nv, 128), 0), ii((nv, 128), 1)
        group = (i // 64 + k * heads == j).astype(BF)
        per_head[2] = per_head[2] + sum(dnn(p, group) for p in split3(parts[k][0:8]))
    d_dt_bias[...] = per_head[0][3:4, : 4 * heads]
    d_a_log[...] = per_head[1][3:4, : 4 * heads]
    d_skip[...] = per_head[2][5:6, : 4 * heads]


def run_k3(heads, *args):
    vm = pl.BlockSpec(memory_space=pltpu.VMEM)
    smalls, r_gate = args[5], args[6]
    n, nv = r_gate.shape
    d = args[0].shape[1]
    sh = lambda *s: jax.ShapeDtypeStruct(s, F32)
    outs = [jax.ShapeDtypeStruct(args[0].shape, BF), sh(*args[0].shape), sh(1, d), sh(n, nv), sh(n, nv), sh(n, 256), sh(heads, n), sh(4, 4 * nv), sh(1, 4 * nv), sh(4, 256), sh(1, 256)]
    outs += [sh(1, 4 * heads)] * 3 + [sh(1, 4 * nv), sh(n, nv)]
    return pl.pallas_call(
        functools.partial(finish_kernel, heads), out_shape=outs, in_specs=[vm] * len(args), out_specs=[vm] * len(outs), scratch_shapes=[pltpu.VMEM((128, 128), F32)],
        compiler_params=pltpu.CompilerParams(vmem_limit_bytes=62 * 2**20), name="finish",
    )(*args)


def per_device(
    hidden_in, seg_ids, pre_gain, proj_gate, proj_x, proj_bc, proj_dt, conv_x, conv_bias_x, conv_bc, conv_bias_bc,
    dt_bias, a_log, skip_d, gate_gain, proj_out, cotangent,
):
    row = lambda v: v.reshape(1, -1)
    pgain = row(pre_gain)
    params = (conv_x, row(conv_bias_x), conv_bc, row(conv_bias_bc), row(dt_bias), row(a_log), row(skip_d), row(gate_gain))
    w0, w1, w2, w3, normed, cot, vals, states, normed_out, low_gate, dy, gg, cx, cbc, hp, segc, segr = run_k1(
        hidden_in, cotangent, (proj_x, proj_bc, proj_dt.T, proj_gate, proj_out.T), pgain, seg_ids.reshape(-1, 128), params
    )
    r_gate, r_out, r_x, r_last, r_bc, own_out, grad_own, smalls = run_k2(
        (w0, w1, w2, w3), normed, cot, vals, states, normed_out, low_gate, dy, pgain, segc, segr, cx, cbc, hp, gg
    )
    outs = run_k3(proj_dt.shape[1], hidden_in, cotangent, pgain, own_out, grad_own, smalls, r_gate, r_out, r_x, r_last, r_bc)
    flat = (2, 8, 10, 11, 12, 13, 14)
    turned = (6, 15)
    return tuple(o.reshape(-1) if k in flat else o.T if k in turned else o for k, o in enumerate(outs))


def solution(mesh):
    tok = P(("dp", "tensor"), None)
    mat = P("dp", "tensor")
    in_specs = (tok, P("dp"), P(), mat, mat, P("dp", None), mat) + (P(),) * 8 + (P("tensor", "dp"), tok)
    out_specs = (tok, tok, P(), mat, mat, P("dp", None), mat) + (P(),) * 8 + (P("tensor", "dp"),)
    return jax.shard_map(per_device, mesh=mesh, in_specs=in_specs, out_specs=out_specs, check_vma=False)
```

```python
import functools

import jax
import jax.numpy as jnp
from jax import lax
from jax.experimental import pallas as pl
from jax.experimental.pallas import tpu as pltpu
from jax.sharding import PartitionSpec as P

MESH = pl.DeviceIdType.MESH
F32 = jnp.float32
BF = jnp.bfloat16


def place():
    dp = lax.axis_index("dp")
    t = lax.axis_index("tensor")
    return dp // 8, (dp // 2) % 4, dp % 2, t


def dev(x, z, yh, t):
    return ((x * 4 + z) * 2 + yh, t)


def m4(v):
    return (v + 8) % 4


def neighbour(axis, d):
    x, z, yh, t = place()
    return dev(m4(x + d), z, yh, t) if axis == "x" else dev(x, m4(z + d), yh, t)


def tensor_peers():
    x, z, yh, t = place()
    yl, co = t // 2, t % 2
    slots = (yl * 2 + 1 - co, (1 - yl) * 2 + co, (1 - yl) * 2 + 1 - co)
    return [dev(x, z, yh, s) for s in slots], slots


def greet(peers):
    bar = pltpu.get_barrier_semaphore()
    for p in peers:
        pl.semaphore_signal(bar, inc=1, device_id=p, device_id_type=MESH)
    pl.semaphore_wait(bar, len(peers))


def send(src, dst, send_sem, recv_sem, to):
    return pltpu.make_async_remote_copy(
        src_ref=src, dst_ref=dst, send_sem=send_sem, recv_sem=recv_sem, device_id=to, device_id_type=MESH
    )


class Gather:
    N = 25

    def __init__(self, own, dst, r1, send_sem, recv_sem):
        x, z, yh, _ = place()
        r2 = "z" if r1 == "x" else "x"
        n = own.shape[0]

        def rows(d1, d2, y=None):
            ix, iz = (m4(x + d1), m4(z + d2)) if r1 == "x" else (m4(x + d2), m4(z + d1))
            first = (ix * 4 + iz) * 2
            if y is None:
                return dst.at[pl.ds(pl.multiple_of(first * n, n), 2 * n)]
            return dst.at[pl.ds(pl.multiple_of((first + y) * n, n), n)]

        self.mine = rows(0, 0, yh)
        self.own = own
        near1, near2 = [neighbour(r1, 1), neighbour(r1, -1)], [neighbour(r2, 1), neighbour(r2, -1)]
        other = rows(0, 0, 1 - yh)
        plan = [(own, self.mine, dev(x, z, 1 - yh, place()[3]))]
        plan += [(own, self.mine, p) for p in near1 + near2]
        plan += [(other, other, p) for p in near1 + near2]
        plan += [(rows(-1, 0, 0),) * 2 + (near1[0],), (rows(1, 0, 1),) * 2 + (near1[1],)]
        for d1 in (-1, 1, 2):
            plan += [(rows(d1, 0),) * 2 + (p,) for p in near2]
        for d1 in (0, -1, 1, 2):
            plan += [(rows(d1, -1, 0),) * 2 + (near2[0],), (rows(d1, 1, 1),) * 2 + (near2[1],)]
        self.plan, self.send_sem, self.recv_sem = plan, send_sem, recv_sem

    def copy(self, k):
        src, dst, to = self.plan[k]
        return send(src, dst, self.send_sem.at[k], self.recv_sem.at[k], to)

    STEPS = (
        ((), (1, 2, 3, 4)),
        ((0,), (5, 6, 7, 8)),
        ((1, 2, 5, 6), (9, 10, 11, 12, 13, 14)),
        ((9, 10), (15, 16)),
        ((3, 4, 7, 8), (17, 18)),
        ((11, 12, 13, 14), (19, 20, 21, 22)),
        ((15, 16), (23, 24)),
        ((17, 18, 19, 20, 21, 22, 23, 24), ()),
    )

    def begin(self):
        self.copy(0).start()

    def step(self, k):
        arrive, go = self.STEPS[k]
        for i in arrive:
            self.copy(i).wait_recv()
        for i in go:
            self.copy(i).start()

    def finish(self):
        for k in range(self.N):
            self.copy(k).wait_send()


Q = 256
LOG2E = 1.4426950408889634
NEG = -1e30


def dnn(a, b):
    return jnp.dot(a, b, preferred_element_type=F32)


def dnt(a, b):
    return lax.dot_general(a, b, (((1,), (1,)), ((), ())), preferred_element_type=F32)


def split3(v):
    hi = v.astype(BF)
    r = v - hi.astype(F32)
    mid = r.astype(BF)
    lo = (r - mid.astype(F32)).astype(BF)
    return hi, mid, lo


def tri_times(mat, v):
    hi, mid, lo = split3(v)
    out = dnn(mat, jnp.concatenate([hi, mid, lo], axis=1))
    w = v.shape[1]
    return out[:, :w] + out[:, w : 2 * w] + out[:, 2 * w :]


def ii(shape, dim):
    return lax.broadcasted_iota(jnp.int32, shape, dim)


def sigmoid(v):
    return 1.0 / (1.0 + jnp.exp2(v * -LOG2E))


def softplus(v):
    e = jnp.exp2(jnp.abs(v) * -LOG2E)
    u = 1.0 + e
    log1p = jnp.where(u == 1.0, e, jnp.log(u) * (e / jnp.where(u == 1.0, 1.0, u - 1.0)))
    return jnp.maximum(v, 0.0) + log1p


def conv_terms(ext, match, taps):
    n = ext.shape[0] - 8
    shifted = [ext[8:]] + [jnp.where(match[k], ext[8 - k : 8 + n - k], 0.0) for k in (1, 2, 3)]
    pre = taps[4:5] + sum(taps[3 - k : 4 - k] * shifted[k] for k in range(4))
    return pre, shifted


def with_earlier(ref, r0, lanes):
    prev = ref[pl.ds(pl.multiple_of(jnp.maximum(r0 - 8, 0), 8), 8), lanes]
    return jnp.concatenate([prev, ref[pl.ds(r0, Q), lanes]], axis=0)


def match_rows(segc, r0):
    prev = segc[pl.ds(pl.multiple_of(jnp.maximum(r0 - 8, 0), 8), 8), :]
    prev = jnp.where(r0 > 0, prev, -1.0)
    cur = segc[pl.ds(r0, Q), :]
    ext = jnp.concatenate([prev, cur], axis=0)
    return [None] + [ext[8 - k : 8 + Q - k] == cur for k in (1, 2, 3)]


def pack_heads(nh, cum, step, tail, ecum):
    parts = list(split3(cum))
    for v in (step, tail, ecum):
        hi = v.astype(BF)
        parts += [hi, (v - hi.astype(F32)).astype(BF)]
    out = parts[0].astype(F32)
    for k, p in enumerate(parts[1:]):
        out = out + pltpu.roll(p.astype(F32), (k + 1) * nh, 1)
    return out.astype(BF)


def unpack_matrix(nh, jj):
    k, col = ii((128, 1280), 0), ii((128, 1280), 1)
    kind = jnp.where(k < 3 * nh, 0, jnp.where(k < 5 * nh, 1, jnp.where(k < 7 * nh, 2, jnp.where(k < 9 * nh, 3, 9))))
    want = jnp.where(col < 512, 0, (col - 256) // 256)
    sub = jnp.where(col < 512, col // 128, (col % 256) // 64)
    return ((kind == want) & (k % nh == 4 * jj + sub)).astype(BF)


def block_rows(c):
    return pl.ds(pl.multiple_of(c * Q, Q), Q)


def wide(match):
    return [None] + [jnp.concatenate([m, m], axis=1) for m in match[1:]]


def prepare_block(c, nv, vals, segc, segr, cbc, hp):
    nh = nv // 64
    r0 = pl.multiple_of(c * Q, Q)
    rows = block_rows(c)
    pre, _sh = conv_terms(with_earlier(vals, r0, pl.ds(nv, 256)), wide(match_rows(segc, r0)), cbc[...])
    bc = pre * sigmoid(pre)
    bb, cc = bc[:, :128].astype(BF), bc[:, 128:].astype(BF)
    seg = segc[rows]
    tt, ss = ii((Q, Q), 0), ii((Q, Q), 1)
    allowed = (tt >= ss) & (jnp.concatenate([seg, seg], axis=1) == segr[0:1, rows])
    bias = jnp.where(allowed, 0.0, NEG)
    mine = ii((Q, 128), 1) < nh
    zero = lambda v: jnp.where(mine, v, 0.0)
    step = zero(softplus(vals[rows, pl.ds(nv + 256, 128)] + hp[0:1]))
    cum = tri_times((tt >= ss).astype(BF), step * (hp[1:2] * LOG2E))
    before = segc[pl.ds(pl.multiple_of(jnp.maximum(r0 - 8, 0), 8), 8)][7:8]
    before = jnp.where(c > 0, before, -1.0)
    tail = zero(jnp.exp2(cum[Q - 1 :] - cum) * (seg == seg[Q - 1 :]).astype(F32))
    ecum = zero(jnp.exp2(cum) * (seg == before).astype(F32))
    return bb, cc, bc[:, :128].T.astype(BF), bc[:, 128:].T.astype(BF), dnt(cc, bb), bias, cum.T, pack_heads(nh, cum, step, tail, ecum)


def fwd_scratch(nv):
    V = lambda s, d=F32: pltpu.VMEM(s, d)
    nh = nv // 64
    return dict(
        bt=V((128, Q), BF), c=V((Q, 128), BF), qk=V((Q, Q)), bias=V((Q, Q)), cumt=V((nh, 8, Q)), pack=V((Q, 128), BF),
        un=V((nh // 4, 128, 1280), BF), ex=V((Q, 1280)), state=V((128, nv)), m=V((4, Q, Q), BF),
    )


def ssd_forward(nv, vals, segc, segr, cx, cbc, hp, ssd, states, s, hook=lambda at: None):
    nh = nv // 64
    for jj in range(nh // 4):
        s["un"][jj] = unpack_matrix(nh, jj)
    s["state"][...] = jnp.zeros_like(s["state"])
    s["m"][...] = jnp.zeros_like(s["m"])

    def block(c, _):
        r0 = pl.multiple_of(c * Q, Q)
        _bb, s["c"][...], s["bt"][...], _ct, s["qk"][...], s["bias"][...], cumt, s["pack"][...] = prepare_block(c, nv, vals, segc, segr, cbc, hp)
        for h in range(nh):
            s["cumt"][h] = jnp.broadcast_to(cumt[h : h + 1], (8, Q))
        states[c] = s["state"][...].astype(BF)
        match = wide(match_rows(segc, r0))

        def quad(jj, _):
            hook(c * (nv // 256) + jj)
            lanes = pl.ds(pl.multiple_of(jj * 256, 256), 256)
            s["ex"][...] = dnn(s["pack"][...], s["un"][jj])
            pre, _sh = conv_terms(with_earlier(vals, r0, lanes), match, cx[:, lanes])
            x = pre * sigmoid(pre)
            u = x * s["ex"][:, 512:768]
            ub = u.astype(BF)
            st = s["state"][:, lanes]
            y = dnn(s["c"][...], st.astype(BF)) * s["ex"][:, 1024:1280] + cx[5:6, lanes] * x
            s["state"][:, lanes] = st * s["ex"][Q - 1 : Q, 1024:1280] + dnn(s["bt"][...], (u * s["ex"][:, 768:1024]).astype(BF))
            for r in range(4):
                rows = slice(r * 64, r * 64 + 64)
                for k in range(1 if r < 2 else 2):
                    cols = slice(k * 128, k * 128 + 128)
                    qk, bias = s["qk"][rows, cols], s["bias"][rows, cols]
                    for n in range(4):
                        dec = jnp.exp2(s["ex"][rows, n * 128 : n * 128 + 128] - s["cumt"][4 * jj + n, 0:1, cols] + bias)
                        s["m"][n, rows, cols] = (dec * qk).astype(BF)
            low_half = ii((Q, 128), 1) < 64
            outs = []
            for p in range(2):
                right = ub[:, p * 128 : p * 128 + 128]
                outs.append(jnp.where(low_half, dnn(s["m"][2 * p], right), dnn(s["m"][2 * p + 1], right)))
            ssd[pl.ds(r0, Q), lanes] = y + jnp.concatenate(outs, axis=1)
            return 0

        lax.fori_loop(0, nv // 256, quad, 0)
        return 0

    lax.fori_loop(0, vals.shape[0] // Q, block, 0)


def later_sum(dpre, halo, match_ext, taps):
    ext = jnp.concatenate([dpre, halo], axis=0)
    n = dpre.shape[0]
    out = taps[3:4] * dpre
    for k in (1, 2, 3):
        out = out + taps[3 - k : 4 - k] * jnp.where(match_ext[k], ext[k : n + k], 0.0)
    return out


def run_forward(nv, vals, segc, segr, cx, cbc, hp):
    sc = fwd_scratch(nv)
    names = list(sc)
    rows = vals.shape[0]

    def kernel(vals, segc, segr, cx, cbc, hp, ssd, states, *scr):
        ssd_forward(nv, vals, segc, segr, cx, cbc, hp, ssd, states, dict(zip(names, scr)))

    vm = pl.BlockSpec(memory_space=pltpu.VMEM)
    return pl.pallas_call(
        kernel, out_shape=(jax.ShapeDtypeStruct((rows, nv), F32), jax.ShapeDtypeStruct((rows // Q, 128, nv), F32)),
        in_specs=[vm] * 6, out_specs=[vm] * 2, scratch_shapes=[sc[n] for n in names],
        compiler_params=pltpu.CompilerParams(vmem_limit_bytes=60 * 2**20), name="scan_forward",
    )(vals, segc, segr, cx, cbc, hp)


def back_scratch(nv, rows):
    V = lambda s, d=F32: pltpu.VMEM(s, d)
    nb, nh = rows // Q, nv // 64
    return dict(
        b=V((rows, 128), BF), c=V((rows, 128), BF), bt=V((nb, 128, Q), BF), ct=V((nb, 128, Q), BF), qk=V((nb, Q, Q)), bias=V((nb, Q, Q)), pack=V((rows, 128), BF),
        cumt=V((nb, nh, 8, Q)), un=V((128, 1280), BF), ex=V((Q, 1280)), dqk=V((nb, Q, Q)), dcs=V((rows, 128)), dbs=V((rows, 128)), hsum=V((rows, 128)),
        colg=V((nb, nh, 8, Q)), krow=V((nb, 8, nv)), dstate=V((128, 256)), halo=V((8, 256)), halobc=V((8, 256)), m=V((4, Q, Q), BF), dm=V((4, Q, Q)),
    )


def back_setup(nv, vals, segc, segr, cbc, hp, s):
    nh = nv // 64
    for n in ("dqk", "dcs", "dbs", "hsum", "m"):
        s[n][...] = jnp.zeros_like(s[n])

    def block(c, _):
        rows = block_rows(c)
        s["b"][rows], s["c"][rows], s["bt"][c], s["ct"][c], s["qk"][c], s["bias"][c], cumt, s["pack"][rows] = prepare_block(c, nv, vals, segc, segr, cbc, hp)
        for h in range(nh):
            s["cumt"][c, h] = jnp.broadcast_to(cumt[h : h + 1], (8, Q))
        return 0

    lax.fori_loop(0, vals.shape[0] // Q, block, 0)


def back_pairs(at, nv, vals, segc, cx, dy_ref, states, low, gx, s):
    nb, nh = vals.shape[0] // Q, nv // 64
    jj, i = at // nb, at % nb
    c = nb - 1 - i
    r0 = pl.multiple_of(c * Q, Q)
    rows_c = block_rows(c)
    lanes = pl.ds(pl.multiple_of(jj * 256, 256), 256)

    @pl.when(i == 0)
    def _():
        s["dstate"][...] = jnp.zeros_like(s["dstate"])
        s["halo"][...] = jnp.zeros_like(s["halo"])
        s["un"][...] = unpack_matrix(nh, jj)

    match, after = wide(match_rows(segc, r0)), wide(match_after(segc, r0))
    s["ex"][...] = dnn(s["pack"][rows_c], s["un"][...])
    stepe, taile, ecume = s["ex"][:, 512:768], s["ex"][:, 768:1024], s["ex"][:, 1024:1280]
    keep = s["ex"][Q - 1 : Q, 1024:1280]
    taps = cx[:, lanes]
    pre, shifted = conv_terms(with_earlier(vals, r0, lanes), match, taps)
    sig = sigmoid(pre)
    x = pre * sig
    u = x * stepe
    ub = u.astype(BF)
    dy = dy_ref[rows_c, lanes].astype(F32)
    dyt = dy.T.astype(BF)
    stb = states[c, :, lanes]
    dst = s["dstate"][...]
    dstb = dst.astype(BF)
    edy = ecume * dy
    edyb = edy.astype(BF)
    rs = edy * dnn(s["c"][rows_c], stb)
    tu = taile * u
    v = dnn(s["b"][rows_c], dstb)
    s["dcs"][rows_c] += dnt(edyb, stb)
    s["dbs"][rows_c] += dnt(tu.astype(BF), dstb)
    krow = keep * jnp.sum(stb.astype(F32) * dst, axis=0, keepdims=True)
    s["dstate"][...] = keep * dst + dnn(s["ct"][c], edyb)
    lane = ii((Q, 128), 1)
    for n in range(4):
        half = slice(n // 2 * 128, n // 2 * 128 + 128)
        mine = (lane < 64) if n % 2 == 0 else (lane >= 64)
        s["dm"][n] = dnt(jnp.where(mine, dy[:, half], 0.0).astype(BF), ub[:, half])
    colsum = [[jnp.zeros((8, 128), F32) for _ in range(2)] for _ in range(4)]
    rowg = []
    for r in range(4):
        rows = slice(r * 64, r * 64 + 64)
        rowsum = [None] * 4
        for k in range(1 if r < 2 else 2):
            cols = slice(k * 128, k * 128 + 128)
            qk, bias = s["qk"][c, rows, cols], s["bias"][c, rows, cols]
            total = None
            for n in range(4):
                dec = jnp.exp2(s["ex"][rows, n * 128 : n * 128 + 128] - s["cumt"][c, 4 * jj + n, 0:1, cols] + bias)
                s["m"][n, rows, cols] = (dec * qk).astype(BF)
                g = s["dm"][n, rows, cols] * dec
                total = g if n == 0 else total + g
                g = g * qk
                rowsum[n] = g if k == 0 else rowsum[n] + g
                colsum[n][k] = colsum[n][k] + jnp.sum(g.reshape(8, 8, 128), axis=0)
            s["dqk"][c, rows, cols] += total
        at_lane = ii((64, 128), 1)
        row = jnp.zeros((64, 128), F32)
        for n in range(4):
            row = jnp.where(at_lane == 48 + 4 * jj + n, jnp.sum(rowsum[n], axis=1, keepdims=True), row)
        rowg.append(row)
    parts = [dnn(dyt[n * 64 : n * 64 + 64], s["m"][n]) for n in range(4)]
    du = jnp.concatenate(parts, axis=0).T + taile * v
    k, col = ii((768, 128), 0), ii((768, 128), 1)
    red = (col == 16 * (k // 256) + 4 * jj + (k % 256) // 64).astype(BF)
    sums = jnp.concatenate([rs.astype(BF), (tu * v).astype(BF), (du * x).astype(BF)], axis=1)
    s["hsum"][rows_c] += dnn(sums, red) + jnp.concatenate(rowg, axis=0)
    dx = du * stepe + taps[5:6] * dy
    dpre = dx * (sig + x * (1.0 - sig))
    low[rows_c, lanes] = later_sum(dpre, s["halo"][...], after, taps).astype(BF)
    s["halo"][...] = dpre[:8]
    gx[:, lanes] += jnp.concatenate(
        [jnp.sum(dpre * shifted[3 - k], axis=0, keepdims=True) for k in range(4)]
        + [jnp.sum(dpre, axis=0, keepdims=True), jnp.sum(dy * x, axis=0, keepdims=True), jnp.zeros((2, 256), F32)], axis=0)
    for n in range(4):
        s["colg"][c, 4 * jj + n] = jnp.broadcast_to(jnp.concatenate([jnp.sum(q, axis=0, keepdims=True) for q in colsum[n]], axis=1), (8, Q))
    s["krow"][c, :, lanes] = jnp.broadcast_to(krow, (8, 256))


def match_after(segc, r0):
    nxt = segc[pl.ds(pl.multiple_of(jnp.minimum(r0 + Q, segc.shape[0] - 8), 8), 8)]
    seg = segc[pl.ds(r0, Q)]
    ext = jnp.concatenate([seg, nxt], axis=0)
    return [None] + [ext[k : Q + k] == seg for k in (1, 2, 3)]


def back_finish(nv, vals, segc, cbc, hp, low, gbc, gh, s):
    nb, nh = vals.shape[0] // Q, nv // 64
    s["halobc"][...] = jnp.zeros_like(s["halobc"])
    gbc[...] = jnp.zeros_like(gbc)
    gh[...] = jnp.zeros_like(gh)

    def block(i, _):
        c = nb - 1 - i
        r0 = pl.multiple_of(c * Q, Q)
        rows = block_rows(c)
        tt, ss = ii((Q, Q), 0), ii((Q, Q), 1)
        e64t = (ii((nv, 128), 0) // 64 == ii((nv, 128), 1)).astype(BF)
        kterm = sum(dnn(p, e64t) for p in split3(s["krow"][c]))
        colg = jnp.concatenate([s["colg"][c, h, 0:1] for h in range(nh)] + [jnp.zeros((128 - nh, Q), F32)], axis=0)
        hs = s["hsum"][rows]
        mine = ii((Q, 128), 1) < nh
        part = lambda k: jnp.where(mine, hs if k == 0 else pltpu.roll(hs, 128 - 16 * k, 1), 0.0)
        dcum = part(3) - colg.T + part(0)
        da = tri_times((ss >= tt).astype(BF), dcum) + tri_times((ss < tt).astype(BF), part(1)) + kterm[0:1]
        rate = hp[1:2]
        raw = vals[rows, pl.ds(nv + 256, 128)] + hp[0:1]
        draw = jnp.where(mine, (part(2) + rate * da) * sigmoid(raw), 0.0)
        low[rows, pl.ds(nv + 256, 128)] = draw.astype(BF)
        gh[...] += jnp.concatenate(
            [jnp.sum(draw, axis=0, keepdims=True), jnp.sum(da * softplus(raw), axis=0, keepdims=True) * rate, jnp.zeros((6, 128), F32)], axis=0)
        dqk = s["dqk"][c]
        dc = dnn(dqk.astype(BF), s["b"][rows]) + s["dcs"][rows]
        db = dnn(dqk.T.astype(BF), s["c"][rows]) + s["dbs"][rows]
        pre, shifted = conv_terms(with_earlier(vals, r0, pl.ds(nv, 256)), wide(match_rows(segc, r0)), cbc[...])
        sig = sigmoid(pre)
        dpre = jnp.concatenate([db, dc], axis=1) * (sig + pre * sig * (1.0 - sig))
        low[rows, pl.ds(nv, 256)] = later_sum(dpre, s["halobc"][...], wide(match_after(segc, r0)), cbc[...]).astype(BF)
        s["halobc"][...] = dpre[:8]
        gbc[...] += jnp.concatenate(
            [jnp.sum(dpre * shifted[3 - k], axis=0, keepdims=True) for k in range(4)] + [jnp.sum(dpre, axis=0, keepdims=True), jnp.zeros((3, 256), F32)], axis=0)
        return 0

    lax.fori_loop(0, nb, block, 0)


def run_backward2(nv, vals, segc, segr, cx, cbc, hp, dy, states):
    rows = vals.shape[0]
    sc = back_scratch(nv, rows)
    names = list(sc)

    def kernel(vals, segc, segr, cx, cbc, hp, dy, states, low, gx, gbc, gh, *scr):
        s = dict(zip(names, scr))
        gx[...] = jnp.zeros_like(gx)
        back_setup(nv, vals, segc, segr, cbc, hp, s)

        def body(at, _):
            back_pairs(at, nv, vals, segc, cx, dy, states, low, gx, s)
            return 0

        lax.fori_loop(0, nv // 256 * (rows // Q), body, 0)
        back_finish(nv, vals, segc, cbc, hp, low, gbc, gh, s)

    vm = pl.BlockSpec(memory_space=pltpu.VMEM)
    outs = (jax.ShapeDtypeStruct((rows, nv + 384), BF), jax.ShapeDtypeStruct((8, nv), F32), jax.ShapeDtypeStruct((8, 256), F32), jax.ShapeDtypeStruct((8, 128), F32))
    return pl.pallas_call(
        kernel, out_shape=outs, in_specs=[vm] * 8, out_specs=[vm] * 4, scratch_shapes=[sc[n] for n in names],
        compiler_params=pltpu.CompilerParams(vmem_limit_bytes=60 * 2**20), name="scan_backward",
    )(vals, segc, segr, cx, cbc, hp, dy, states)


INNER = 3072
EPS = 1e-05


def at_step(step, events):
    for k, fn in events:

        @pl.when(step == k)
        def _(fn=fn):
            fn()


def forward_kernel(
    names, nv,
    hid, cot_own, p_x, p_bc, p_dt, p_gate, p_out, pgain, seg, conv_x, bias_x, conv_bc, bias_bc, dt_bias, a_log, skip_d, gate_gain,
    o_w0, o_w1, o_w2, o_w3, o_nrm, o_cot, o_vals, o_states, o_no, o_lg, o_dy, o_gg, cx, cbc, hp, segc, segr,
    square, w_own1, w0, w1, w2, w3, nrm, cot, vals, states, ssd, gate, gno, no, lg, dy, sums_own, sums_in,
    wsend, wrecv, tsend, trecv, ssend, srecv, lsem, *scan_scratch,
):
    s = dict(zip(names, scan_scratch))
    x, z, yh, t = place()
    yl, co = t // 2, t % 2
    tp, slots = tensor_peers()
    width = hid.shape[1]
    cut = w0.shape[1]
    w_own0, w_own2, w_own3 = p_x.at[:, :cut], p_gate, p_out
    w_own1[...] = jnp.zeros_like(w_own1)
    w_own1[:, : nv - cut] = p_x[:, cut:]
    w_own1[:, nv - cut : nv - cut + 256] = p_bc[...]
    square[...] = jnp.zeros_like(square)
    square[: p_dt.shape[0], : p_dt.shape[1]] = p_dt[...].astype(F32)
    w_own1[:, nv - cut + 256 :] = square[...].T[: p_dt.shape[1]].astype(BF)
    greet([dev(x, z, 1 - yh, t)] + [neighbour(a, d) for a in "xz" for d in (1, -1)] + tp)
    owns, dsts, outs = (w_own0, w_own1, w_own2, w_own3), (w0, w1, w2, w3), (o_w0, o_w1, o_w2, o_w3)
    groups = lambda ks: [Gather(owns[k], dsts[k], "xz"[k % 2], wsend.at[k], wrecv.at[k]) for k in ks]
    first, second = (0, 1), (2, 3)

    def step(ks, n):
        for g in groups(ks):
            g.step(n)

    def saved(i, src, dst):
        return pltpu.make_async_copy(src, dst, lsem.at[i])

    mine = pl.ds(pl.multiple_of(t * 256, 256), 256)
    theirs = pl.ds(pl.multiple_of(slots[1] * 256, 256), 256)

    def tensor_copies(i, own, dst):
        return (
            send(own, dst.at[mine], tsend.at[i, 0], trecv.at[i, 0], tp[1]),
            send(own, dst.at[mine], tsend.at[i, 1], trecv.at[i, 1], tp[0]),
            send(dst.at[theirs], dst.at[theirs], tsend.at[i, 2], trecv.at[i, 2], tp[0]),
        )

    for g in groups((0, 1, 2, 3)):
        g.begin()
    step(first, 0)

    def norm_rows(i, _):
        rows = pl.ds(pl.multiple_of(i * 64, 64), 64)
        h = hid[rows].astype(F32)
        inv = lax.rsqrt(jnp.mean(h * h, axis=1, keepdims=True) + EPS)
        nrm[pl.ds(pl.multiple_of(t * 256 + i * 64, 64), 64)] = (h * inv * pgain[0:1]).astype(BF)
        return 0

    lax.fori_loop(0, 4, norm_rows, 0)
    own_lanes = pl.ds(pl.multiple_of(t * nv, 128), nv)
    heads = p_dt.shape[0]

    def own_heads(v, lanes, per):
        i, j = ii((v.shape[1], lanes), 0), ii((v.shape[1], lanes), 1)
        pick = ((i == t * heads + j // per) & (j < heads * per)).astype(BF)
        return sum(dnn(part, pick) for part in split3(jnp.broadcast_to(v[...], (8, v.shape[1]))))

    cx[0:4] = conv_x[:, own_lanes]
    cx[4:5] = bias_x[:, own_lanes]
    cx[5:8] = own_heads(skip_d, nv, 64)[5:8]
    cbc[0:4] = conv_bc[...]
    cbc[4:8] = jnp.broadcast_to(bias_bc[...], (4, 256))
    hp[0:1] = own_heads(dt_bias, 128, 1)[0:1]
    hp[1:2] = jnp.where(ii((1, 128), 1) < heads, -jnp.exp(own_heads(a_log, 128, 1)[0:1]), 0.0)
    hp[2:8] = jnp.zeros((6, 128), F32)
    gains = gate_gain[:, own_lanes]
    sf = seg[...].astype(F32)
    for k in range(seg.shape[0]):
        segr[:, k * 128 : k * 128 + 128] = jnp.broadcast_to(sf[k : k + 1], (8, 128))
        segc[k * 128 : k * 128 + 128] = jnp.broadcast_to(sf[k : k + 1], (128, 128)).T
    for k in range(4):
        g = groups((k,))[0]
        g.mine[...] = g.own[...]
    cot[mine] = cot_own[...]
    nrm_copies = tensor_copies(0, nrm.at[mine], nrm)
    cot_copies = tensor_copies(1, cot_own, cot)
    nrm_copies[0].start()
    nrm_copies[1].start()
    for n in (1, 4, 2, 3):
        step(first, n)
    cot_copies[0].start()
    cot_copies[1].start()
    step(second, 0)
    step(second, 1)
    step(first, 5)
    step(first, 6)
    nrm_copies[0].wait_recv()
    nrm_copies[2].start()
    step(second, 4)
    step(first, 7)
    nrm_copies[1].wait_recv()
    nrm_copies[2].wait_recv()

    def project(i, _):
        pl.when(i == 2)(lambda: step(second, 2))
        rows = pl.ds(pl.multiple_of(i * 256, 256), 256)
        n = nrm[rows]
        at = 0
        for w in (w0, w1):
            c = w.shape[1]
            vals[rows, at : at + c] = jnp.dot(n, w[...], preferred_element_type=F32)
            at += c
        return 0

    lax.fori_loop(0, 4, project, 0)
    early = [(0, w0, o_w0), (1, w1, o_w1), (2, nrm, o_nrm), (3, vals, o_vals)]
    for e in early:
        saved(*e).start()

    def cot_forward():
        cot_copies[0].wait_recv()
        cot_copies[2].start()

    events = [(1, lambda: step(second, 3)), (3, lambda: step(second, 5)), (5, lambda: step(second, 6)), (7, cot_forward)]
    ssd_forward(nv, vals, segc, segr, cx, cbc, hp, ssd, states, s, lambda at: at_step(at, events))
    step(second, 7)
    cot_copies[1].wait_recv()
    cot_copies[2].wait_recv()
    late = [(4, w2, o_w2), (5, w3, o_w3), (6, cot, o_cot), (7, states, o_states)]
    for e in late:
        saved(*e).start()

    def inner(i, _):
        rows = pl.ds(pl.multiple_of(i * 256, 256), 256)
        g = jnp.dot(nrm[rows], w2[...], preferred_element_type=F32)
        gate[rows] = g
        o = jnp.dot(cot[rows], w3[...], preferred_element_type=F32)
        gno[rows] = o
        gated = ssd[rows] * (g * sigmoid(g))
        sq = jnp.sum(gated * gated, axis=1, keepdims=True)
        cr = jnp.sum(o * gains * gated, axis=1, keepdims=True)
        lane = ii((256, 128), 1)
        both = jnp.where(lane == 0, sq, jnp.where(lane == 1, cr, 0.0))
        sums_own[:, rows] = both.T[:8]
        return 0

    lax.fori_loop(0, 4, inner, 0)
    small = [send(sums_own, sums_in.at[k], ssend.at[k], srecv.at[k], p) for k, p in enumerate(tp)]
    for c in small:
        c.start()
    for c in small:
        c.wait_recv()
    o_gg[...] = jnp.zeros_like(o_gg)

    def outer(i, _):
        rows = pl.ds(pl.multiple_of(i * 256, 256), 256)
        tot = sums_own[:, rows] + sums_in[0, :, rows] + sums_in[1, :, rows] + sums_in[2, :, rows]
        cols = jnp.concatenate([tot, jnp.zeros((120, 256), F32)], axis=0).T
        inv = lax.rsqrt(cols[:, 0:1] / INNER + EPS)
        cross = inv * inv * inv * cols[:, 1:2] / INNER
        for k in range(nv // 128):
            lanes = pl.ds(k * 128, 128)
            g, y, o, gain = gate[rows, lanes], ssd[rows, lanes], gno[rows, lanes], gains[:, k * 128 : k * 128 + 128]
            sig = sigmoid(g)
            silu = g * sig
            gated = y * silu
            scaled = gated * inv
            no[rows, lanes] = (scaled * gain).astype(BF)
            o_gg[0:1, lanes] += jnp.sum(o * scaled, axis=0, keepdims=True)
            grad = o * gain * inv - gated * cross
            dy[rows, lanes] = (grad * silu).astype(BF)
            lg[rows, lanes] = (grad * y * (sig + silu * (1.0 - sig))).astype(BF)
        return 0

    lax.fori_loop(0, 4, outer, 0)
    last = [(8, no, o_no), (9, lg, o_lg), (10, dy, o_dy)]
    for e in last:
        saved(*e).start()
    for g in groups((0, 1, 2, 3)):
        g.finish()
    for c in nrm_copies + cot_copies + tuple(small):
        c.wait_send()
    for e in early + late + last:
        saved(*e).wait()


def run_k1(hid, cot_own, projs, pgain, seg, params):
    anys, vm = pl.BlockSpec(memory_space=pl.ANY), pl.BlockSpec(memory_space=pltpu.VMEM)
    nv = projs[0].shape[1]
    rows = seg.shape[0] * seg.shape[1]
    n, d = projs[0].shape[0], hid.shape[1]
    sh = jax.ShapeDtypeStruct
    cols = [nv - 128, 512, nv, nv]
    nvals = cols[0] + cols[1]
    outs = [sh((d, c), BF) for c in cols] + [sh((rows, d), BF)] * 2 + [sh((rows, nvals), F32), sh((rows // Q, 128, nv), BF)] + [sh((rows, nv), BF)] * 3
    outs += [sh((8, nv), F32), sh((8, nv), F32), sh((8, 256), F32), sh((8, 128), F32), sh((rows, 128), F32), sh((8, rows), F32)]
    V = lambda shape, dt: pltpu.VMEM(shape, dt)
    D = pltpu.SemaphoreType.DMA
    scan = fwd_scratch(nv)
    scratch = [V((128, 128), F32), V((n, cols[1]), BF)] + [V((d, c), BF) for c in cols] + [V((rows, d), BF)] * 2
    scratch += [V((rows, nvals), F32), V((rows // Q, 128, nv), BF)] + [V((rows, nv), F32)] * 3 + [V((rows, nv), BF)] * 3
    scratch += [V((8, rows), F32), V((3, 8, rows), F32), D((4, Gather.N)), D((4, Gather.N)), D((2, 3)), D((2, 3)), D((3,)), D((3,)), D((11,))]
    scratch += list(scan.values())
    return pl.pallas_call(
        functools.partial(forward_kernel, list(scan), nv), out_shape=outs, in_specs=[vm] * 17, out_specs=[anys] * 11 + [vm] * 6, scratch_shapes=scratch,
        compiler_params=pltpu.CompilerParams(collective_id=0, has_side_effects=True, vmem_limit_bytes=62 * 2**20), name="forward_all",
    )(hid, cot_own, *projs, pgain, seg, *params)


class Scatter:
    N = 13

    def __init__(self, v, bufs, out, a1, send_sem, recv_sem):
        x, z, yh, t = place()
        self.v, self.out, self.a1, self.yh = v, out, a1, yh
        self.r1, self.r2, self.q1, self.q2, self.kk, self.yy = bufs
        self.h = self.r2.at[0]
        a2 = "z" if a1 == "x" else "x"
        self.p, self.q = (x, z) if a1 == "x" else (z, x)
        self.send_sem, self.recv_sem = send_sem, recv_sem
        right1, left1, right2, left2 = neighbour(a1, 1), neighbour(a1, -1), neighbour(a2, 1), neighbour(a2, -1)
        r1, r2, h, q1, q2, q = self.r1, self.r2, self.h, self.q1, self.q2, self.q
        self.plan = [
            (self.half(2, 0), r1.at[0], right1), (self.half(2, 1), r1.at[1], left1),
            (self.half(1, 1), r2.at[0, pl.ds(2, 2)], right1), (self.half(-1, 0), r2.at[1, pl.ds(0, 2)], left1),
            (self.half(1, 0), r2.at[0, pl.ds(0, 2)], right1), (self.half(-1, 1), r2.at[1, pl.ds(2, 2)], left1),
            (h.at[m4(q + 2), 0], q1.at[0], right2), (h.at[m4(q + 2), 1], q1.at[1], left2),
            (h.at[m4(q + 1), 1], q2.at[0, 1], right2), (h.at[m4(q - 1), 0], q2.at[1, 0], left2),
            (h.at[m4(q + 1), 0], q2.at[0, 0], right2), (h.at[m4(q - 1), 1], q2.at[1, 1], left2),
            (self.kk, self.yy, dev(x, z, 1 - yh, t)),
        ]

    def half(self, d, k):
        at = m4(self.p + d)
        return self.v.at[pl.ds(2 * k, 2), at] if self.a1 == "z" else self.v.at[at, pl.ds(2 * k, 2)]

    def copy(self, k):
        src, dst, to = self.plan[k]
        return send(src, dst, self.send_sem.at[k], self.recv_sem.at[k], to)

    def start(self, *ks):
        for k in ks:
            self.copy(k).start()

    def arrive(self, *ks):
        for k in ks:
            self.copy(k).wait_recv()

    def step(self, n):
        v, r1, r2, h, q1, q2, p, q, yh = self.v, self.r1, self.r2, self.h, self.q1, self.q2, self.p, self.q, self.yh
        if n == 0:
            self.start(0, 1, 2, 3)
        elif n == 1:
            for side, d in ((0, 1), (1, -1)):
                self.arrive(side)
                at = m4(p + d)

                def add(j, _, side=side, at=at):
                    e, y = j // 2, j % 2
                    ix = (2 * side + e, at, y) if self.a1 == "z" else (at, 2 * side + e, y)
                    v[ix] = v[ix] + r1[side, e, y]
                    return 0

                lax.fori_loop(0, 4, add, 0)
                self.start(4 + side)
        elif n == 2:
            self.arrive(2, 3, 4, 5)

            def add(j, _):
                e, y = j // 2, j % 2
                own = v[e, p, y] if self.a1 == "z" else v[p, e, y]
                h[e, y] = own + (r2[0, e, y] + r2[1, e, y])
                return 0

            lax.fori_loop(0, 8, add, 0)
            self.start(6, 7, 8, 9)
        elif n == 3:
            for side, d in ((0, 1), (1, -1)):
                self.arrive(6 + side)
                at = m4(q + d)
                h[at, side] = h[at, side] + q1[side]
                self.start(10 + side)
        elif n == 4:
            self.arrive(8, 9, 10, 11)
            self.kk[...] = (h[q, 1 - yh].astype(F32) + q2[0, 1 - yh].astype(F32) + q2[1, 1 - yh].astype(F32)).astype(BF)
            self.start(12)
        else:
            self.arrive(12)
            self.out[...] = h[q, yh].astype(F32) + q2[0, yh].astype(F32) + q2[1, yh].astype(F32) + self.yy[...].astype(F32)

    def finish(self):
        for k in range(self.N):
            self.copy(k).wait_send()


class TokenScatter:
    def __init__(self, v, from_core, from_chip, out, send_sem, recv_sem):
        t = place()[3]
        tp, slots = tensor_peers()
        self.t, self.v, self.from_core, self.from_chip, self.out = t, v, from_core, from_chip, out
        rows = lambda s: pl.ds(pl.multiple_of(s * 256, 256), 256)
        self.pass_on, self.mine = slots[1], rows(t)
        self.copies = lambda k: (
            lambda: send(v.at[rows(slots[2])], from_core.at[0], send_sem.at[0], recv_sem.at[0], tp[0]),
            lambda: send(v.at[rows(slots[0])], from_core.at[1], send_sem.at[1], recv_sem.at[1], tp[0]),
            lambda: send(v.at[rows(slots[1])], from_chip, send_sem.at[2], recv_sem.at[2], tp[1]),
        )[k]()

    def step(self, n):
        if n == 0:
            self.copies(0).start()
            self.copies(1).start()
        elif n == 1:
            self.copies(0).wait_recv()

            def add(j, _):
                rows = pl.ds(pl.multiple_of(j * 32, 32), 32)
                own = pl.ds(pl.multiple_of(self.pass_on * 256 + j * 32, 32), 32)
                self.v[own] = self.v[own] + self.from_core[0, rows]
                return 0

            lax.fori_loop(0, 8, add, 0)
            self.copies(2).start()
        else:
            self.copies(1).wait_recv()
            self.copies(2).wait_recv()

            def add(j, _):
                rows = pl.ds(pl.multiple_of(j * 32, 32), 32)
                own = self.v[pl.ds(pl.multiple_of(self.t * 256 + j * 32, 32), 32)]
                self.out[rows] = own.astype(F32) + self.from_core[1, rows].astype(F32) + self.from_chip[rows].astype(F32)
                return 0

            lax.fori_loop(0, 8, add, 0)

    def finish(self):
        for k in range(3):
            self.copies(k).wait_send()


def backward_kernel(
    names, nv,
    h_w0, h_w1, h_w2, h_w3, h_nrm, h_cot, h_vals, h_states, h_no, h_lg, h_dy, pgain, segc, segr, cx, cbc, hp, gg,
    o_gate, o_out, o_x, o_dt, o_bc, o_own, o_grad, o_small,
    w0, w1, w23, nrm, cot, vals, states, nody, lg, low, po, t_out, t_gate, t_0, t_1, t_2, t_bc, t_dt,
    bc_sum, own_v, sx, sz, sy, st, sacc, bct, fc0, ch0, fc1, ch1, gx, gbc, gh, pre,
    wsend, wrecv, tsend, trecv, ssend, srecv, bsend, brecv, lsem, *rest,
):
    bufs, s = [rest[6 * k : 6 * k + 6] for k in range(7)], dict(zip(names, rest[42:]))
    x, z, yh, t = place()
    tp, slots = tensor_peers()
    loads = [
        pltpu.make_async_copy(a, b, lsem.at[k])
        for k, (a, b) in enumerate(((h_no, nody), (h_w3, w23), (h_cot, cot), (h_nrm, nrm), (h_lg, lg), (h_vals, vals), (h_states, states), (h_w0, w0), (h_w1, w1)))
    ]
    for c in loads:
        c.start()
    load_dy, load_w2 = pltpu.make_async_copy(h_dy, nody, lsem.at[9]), pltpu.make_async_copy(h_w2, w23, lsem.at[10])
    greet([dev(x, z, 1 - yh, t)] + [neighbour(a, d) for a in "xz" for d in (1, 2, 3)] + tp)
    wide_x = o_x.shape[1] // 3
    x_part = lambda k: o_x.at[:, k * wide_x : k * wide_x + wide_x]
    scat = [
        Scatter(v, bufs[k], o, "xzxzxzx"[k], wsend.at[k], wrecv.at[k])
        for k, (v, o) in enumerate(((t_out, o_out), (t_gate, o_gate), (t_0, x_part(0)), (t_1, x_part(1)), (t_2, x_part(2)), (t_bc, bc_sum), (t_dt, o_dt)))
    ]
    s_out, s_gate, s_0, s_1, s_2, s_bc, s_dt = scat
    k_out = TokenScatter(po, fc0, ch0, o_own, tsend.at[0], trecv.at[0])
    k_nrm = TokenScatter(cot, fc1, ch1, o_grad, tsend.at[1], trecv.at[1])

    def by_rows(fn):
        def body(i, _):
            fn(pl.ds(pl.multiple_of(i * 256, 256), 256))
            return 0

        lax.fori_loop(0, 4, body, 0)

    def outer_product(dst, left, right):
        def body(i, _):
            cols = pl.ds(pl.multiple_of(i * 384, 384), 384)
            r = lax.dot_general(left[:, cols], right[...], (((0,), (0,)), ((), ())), preferred_element_type=F32)
            first = 0
            for d in dst:
                d[i] = r[:, first : first + d.shape[-1]].astype(BF).reshape(d.shape[1:])
                first += d.shape[-1]
            return 0

        lax.fori_loop(0, 4, body, 0)

    loads[0].wait()
    loads[2].wait()
    outer_product((t_out,), cot, nody)
    s_out.step(0)
    loads[3].wait()
    loads[4].wait()
    outer_product((t_gate,), nrm, lg)
    s_gate.step(0)

    def out_rows(rows):
        left = nody[rows]
        for k in range(0, po.shape[1], 512):
            po[rows, k : k + 512] = dnt(left, w23[k : k + 512]).astype(BF)

    loads[1].wait()
    by_rows(out_rows)
    load_w2.start()
    load_dy.start()
    k_out.step(0)
    for k in (5, 6, 7, 8):
        loads[k].wait()
    back_setup(nv, vals, segc, segr, cbc, hp, s)
    load_dy.wait()
    both = lambda n: lambda: (s_out.step(n), s_gate.step(n))

    def chunk(n):
        def go():
            outer_product(((t_0, t_1, t_2)[n],), nrm, low.at[:, n * wide_x : n * wide_x + wide_x])
            scat[2 + n].step(0)

        return go

    gx[...] = jnp.zeros_like(gx)
    events = [
        (1, lambda: k_out.step(1)),
        (4, both(1)),
        (6, chunk(0)),
        (8, both(2)),
        (9, chunk(1)),
        (10, lambda: k_out.step(2)),
        (11, both(3)),
    ]

    def scan_step(at, _):
        at_step(at, events)
        back_pairs(at, nv, vals, segc, cx, nody, states, low, gx, s)
        return 0

    lax.fori_loop(0, nv // 256 * (vals.shape[0] // Q), scan_step, 0)
    chunk(2)()
    back_finish(nv, vals, segc, cbc, hp, low, gbc, gh, s)
    outer_product((t_bc, t_dt), nrm, low.at[:, nv:])
    s_bc.step(0)
    s_dt.step(0)
    s_out.step(4)
    s_gate.step(4)
    s_0.step(1)
    s_1.step(1)
    load_w2.wait()
    pre[...] = jnp.zeros_like(pre)
    c0 = w0.shape[1]

    def grad_rows(rows):
        for k in range(0, cot.shape[1], 512):
            cols = slice(k, k + 512)
            g = dnt(lg[rows], w23[cols]) + dnt(low[rows, :c0], w0[cols]) + dnt(low[rows, c0:], w1[cols])
            pre[0:1, cols] += jnp.sum(g * nrm[rows, cols].astype(F32), axis=0, keepdims=True)
            cot[rows, cols] = g.astype(BF)

    def grad_slot(i, _):
        slot = ((t // 2 + 1 - i // 2) % 2) * 2 + (t + 1 - i % 2) % 2
        grad_rows(pl.ds(pl.multiple_of(slot * 256, 256), 256))
        at_step(i, [(0, lambda: k_nrm.copies(0).start()), (1, lambda: k_nrm.step(1)), (2, lambda: k_nrm.copies(1).start())])
        return 0

    lax.fori_loop(0, 4, grad_slot, 0)
    own_v[...] = jnp.zeros_like(own_v)
    own_v[0:6] = gx[0:6]
    own_v[6:7] = gg[0:1]
    pv = pre[0:1] / pgain[0:1]
    own_v[7:8], own_v[8:9] = pv[:, :nv], pv[:, nv:]
    for k in range(3):
        own_v[9:10, k * 256 : k * 256 + 256] = gbc[k : k + 1]
    for k in range(2):
        own_v[10:11, k * 256 : k * 256 + 256] = gbc[3 + k : 4 + k]
        own_v[11:12, k * 128 : k * 128 + 128] = gh[k : k + 1]
    small = [send(own_v, sx.at[d - 1], ssend.at[d - 1], srecv.at[d - 1], neighbour("x", d)) for d in (1, 2, 3)]
    for c in small:
        c.start()
    s_2.step(1)
    s_bc.step(1)
    s_dt.step(1)
    s_out.step(5)
    s_gate.step(5)
    s_0.step(2)
    s_1.step(2)

    def next_small(have, total, copies):
        for c in have:
            c.wait_recv()
        total()
        for c in copies:
            c.start()
        return copies

    def total_x():
        sacc[0] = own_v[...] + sx[0] + sx[1] + sx[2]

    def total_z():
        sacc[1] = sacc[0] + sz[0] + sz[1] + sz[2]

    def total_y():
        sacc[2] = sacc[1] + sy[...]

    small_z = next_small(small, total_x, [send(sacc.at[0], sz.at[d - 1], ssend.at[2 + d], srecv.at[2 + d], neighbour("z", d)) for d in (1, 2, 3)])
    s_2.step(2)
    s_bc.step(2)
    s_dt.step(2)
    small_y = next_small(small_z, total_z, [send(sacc.at[1], sy, ssend.at[6], srecv.at[6], dev(x, z, 1 - yh, t))])
    s_0.step(3)
    s_1.step(3)
    s_2.step(3)
    s_bc.step(3)
    s_dt.step(3)
    small_t = next_small(small_y, total_y, [send(sacc.at[2], st.at[k], ssend.at[7 + k], srecv.at[7 + k], p) for k, p in enumerate(tp)])
    s_2.step(4)
    s_bc.step(4)
    s_dt.step(4)
    s_0.step(4)
    s_1.step(4)
    s_2.step(5)
    s_bc.step(5)
    s_dt.step(5)
    s_0.step(5)
    s_1.step(5)
    bct[3] = bc_sum[...]
    bcs = [send(bct.at[3], bct.at[k], bsend.at[k], brecv.at[k], p) for k, p in enumerate(tp)]
    for c in bcs:
        c.start()
    k_nrm.step(2)
    for c in small_t:
        c.wait_recv()
    o_small[t] = sacc[2]
    for k in range(3):
        o_small[slots[k]] = st[k]
    for c in bcs:
        c.wait_recv()
    o_bc[...] = bct[3] + bct[0] + bct[1] + bct[2]
    for c in small + small_z + small_y + small_t + bcs:
        c.wait_send()
    for g in scat + [k_out, k_nrm]:
        g.finish()


def run_k2(ws, nrm, cot, vals, states, no, lg, dy, pgain, segc, segr, cx, cbc, hp, gg):
    anys, vm = pl.BlockSpec(memory_space=pl.ANY), pl.BlockSpec(memory_space=pltpu.VMEM)
    nv = cx.shape[1]
    rows, d = nrm.shape
    sh = lambda *s: jax.ShapeDtypeStruct(s, F32)
    cols = [w.shape[1] for w in ws]
    n = d // 32
    V = lambda *s, dt=BF: pltpu.VMEM(s, dt)
    D = pltpu.SemaphoreType.DMA
    parts = (nv, nv, nv // 3, nv // 3, nv // 3, 256, 128)
    outs = [sh(n, nv), sh(n, nv), sh(n, nv), sh(n, 128), sh(n, 256), sh(256, d), sh(256, d), sh(4, 16, nv)]
    term = lambda c: V(4, 4, 2, n, c)
    scratch = [V(d, cols[0]), V(d, cols[1]), V(d, cols[2]), V(rows, d), V(rows, d), V(*vals.shape, dt=F32), V(*states.shape), V(rows, nv), V(rows, nv), V(*vals.shape), V(rows, d)]
    scratch += [term(c) for c in parts]
    sv = (16, nv)
    scratch += [V(n, 256, dt=F32)]
    scratch += [V(*sv, dt=F32), V(3, *sv, dt=F32), V(3, *sv, dt=F32), V(*sv, dt=F32), V(3, *sv, dt=F32), V(3, *sv, dt=F32), V(4, n, 256, dt=F32)]
    scratch += [V(2, 256, d), V(256, d)] * 2
    scratch += [V(8, nv, dt=F32), V(8, 256, dt=F32), V(8, 128, dt=F32), V(8, d, dt=F32)]
    scratch += [D((7, Scatter.N))] * 2 + [D((2, 3))] * 2 + [D((10,))] * 2 + [D((3,))] * 2 + [D((11,))]
    for c in parts:
        scratch += [V(2, 2, 2, n, c), V(2, 4, 2, n, c), V(2, n, c), V(2, 2, n, c), V(n, c), V(n, c)]
    scan = back_scratch(nv, rows)
    scratch += list(scan.values())
    return pl.pallas_call(
        functools.partial(backward_kernel, list(scan), nv), out_shape=outs, in_specs=[anys] * 11 + [vm] * 7, out_specs=[vm] * 8, scratch_shapes=scratch,
        compiler_params=pltpu.CompilerParams(collective_id=1, has_side_effects=True, vmem_limit_bytes=64 * 2**20), name="backward_all",
    )(*ws, nrm, cot, vals, states, no, lg, dy, pgain, segc, segr, cx, cbc, hp, gg)


def finish_kernel(
    heads, hid, cot, pgain, own_out, grad_own, smalls, r_gate, r_out, r_x, r_last, r_bc,
    out, d_hid, d_pre, d_gate, d_x, d_bc, d_dt, d_conv_x, d_bias_x, d_conv_bc, d_bias_bc, d_dt_bias, d_a_log, d_skip, d_gain, d_out, square,
):
    def rows(i, _):
        at = pl.ds(pl.multiple_of(i * 64, 64), 64)
        h = hid[at].astype(F32)
        g = grad_own[at]
        inv = lax.rsqrt(jnp.mean(h * h, axis=1, keepdims=True) + EPS)
        scaled = g * pgain[...]
        back = jnp.mean(scaled * h, axis=1, keepdims=True)
        out[at] = (h + own_out[at]).astype(BF)
        d_hid[at] = cot[at].astype(F32) + scaled * inv - h * (inv * inv * inv * back)
        return 0

    lax.fori_loop(0, hid.shape[0] // 64, rows, 0)
    nv = smalls.shape[2]
    square[...] = jnp.zeros_like(square)
    d_gate[...] = r_gate[...]
    d_out[...] = r_out[...]
    d_x[...] = r_x[...]
    d_bc[...] = r_bc[...]
    square[: r_last.shape[0]] = r_last[...]
    d_dt[...] = square[...].T[:heads, : r_last.shape[0]]
    parts = [smalls[k] for k in range(4)]
    both = parts[0] + parts[1] + parts[2] + parts[3]
    d_pre[:, :nv] = both[7:8]
    d_pre[:, nv:] = both[8:9]
    for k in range(3):
        d_conv_bc[k : k + 1] = both[9:10, k * 256 : k * 256 + 256]
    d_conv_bc[3:4] = both[10:11, :256]
    d_bias_bc[...] = both[10:11, 256:512]
    per_head = [jnp.zeros((8, 128), F32)] * 3
    for k in range(4):
        lanes = slice(k * nv, k * nv + nv)
        d_conv_x[:, lanes] = parts[k][0:4]
        d_bias_x[:, lanes] = parts[k][4:5]
        d_gain[:, lanes] = parts[k][6:7]
        row = parts[k][8:16]
        i, j = ii((128, 128), 0), ii((128, 128), 1)
        pick = ((i + k * heads == j) & (i < heads)).astype(BF)
        for n in range(2):
            per_head[n] = per_head[n] + sum(dnn(p, pick) for p in split3(row[:, n * 128 : n * 128 + 128]))
        i, j = ii((nv, 128), 0), ii((nv, 128), 1)
        group = (i // 64 + k * heads == j).astype(BF)
        per_head[2] = per_head[2] + sum(dnn(p, group) for p in split3(parts[k][0:8]))
    d_dt_bias[...] = per_head[0][3:4, : 4 * heads]
    d_a_log[...] = per_head[1][3:4, : 4 * heads]
    d_skip[...] = per_head[2][5:6, : 4 * heads]


def run_k3(heads, *args):
    vm = pl.BlockSpec(memory_space=pltpu.VMEM)
    smalls, r_gate = args[5], args[6]
    n, nv = r_gate.shape
    d = args[0].shape[1]
    sh = lambda *s: jax.ShapeDtypeStruct(s, F32)
    outs = [jax.ShapeDtypeStruct(args[0].shape, BF), sh(*args[0].shape), sh(1, d), sh(n, nv), sh(n, nv), sh(n, 256), sh(heads, n), sh(4, 4 * nv), sh(1, 4 * nv), sh(4, 256), sh(1, 256)]
    outs += [sh(1, 4 * heads)] * 3 + [sh(1, 4 * nv), sh(n, nv)]
    return pl.pallas_call(
        functools.partial(finish_kernel, heads), out_shape=outs, in_specs=[vm] * len(args), out_specs=[vm] * len(outs), scratch_shapes=[pltpu.VMEM((128, 128), F32)],
        compiler_params=pltpu.CompilerParams(vmem_limit_bytes=62 * 2**20), name="finish",
    )(*args)


def per_device(
    hidden_in, seg_ids, pre_gain, proj_gate, proj_x, proj_bc, proj_dt, conv_x, conv_bias_x, conv_bc, conv_bias_bc,
    dt_bias, a_log, skip_d, gate_gain, proj_out, cotangent,
):
    row = lambda v: v.reshape(1, -1)
    pgain = row(pre_gain)
    params = (conv_x, row(conv_bias_x), conv_bc, row(conv_bias_bc), row(dt_bias), row(a_log), row(skip_d), row(gate_gain))
    w0, w1, w2, w3, normed, cot, vals, states, normed_out, low_gate, dy, gg, cx, cbc, hp, segc, segr = run_k1(
        hidden_in, cotangent, (proj_x, proj_bc, proj_dt.T, proj_gate, proj_out.T), pgain, seg_ids.reshape(-1, 128), params
    )
    r_gate, r_out, r_x, r_last, r_bc, own_out, grad_own, smalls = run_k2(
        (w0, w1, w2, w3), normed, cot, vals, states, normed_out, low_gate, dy, pgain, segc, segr, cx, cbc, hp, gg
    )
    outs = run_k3(proj_dt.shape[1], hidden_in, cotangent, pgain, own_out, grad_own, smalls, r_gate, r_out, r_x, r_last, r_bc)
    flat = (2, 8, 10, 11, 12, 13, 14)
    turned = (6, 15)
    return tuple(o.reshape(-1) if k in flat else o.T if k in turned else o for k, o in enumerate(outs))


def solution(mesh):
    tok = P(("dp", "tensor"), None)
    mat = P("dp", "tensor")
    in_specs = (tok, P("dp"), P(), mat, mat, P("dp", None), mat) + (P(),) * 8 + (P("tensor", "dp"), tok)
    out_specs = (tok, tok, P(), mat, mat, P("dp", None), mat) + (P(),) * 8 + (P("tensor", "dp"),)
    return jax.shard_map(per_device, mesh=mesh, in_specs=in_specs, out_specs=out_specs, check_vma=False)
```

```python
import functools

import jax
import jax.numpy as jnp
from jax import lax
from jax.experimental import pallas as pl
from jax.experimental.pallas import tpu as pltpu
from jax.sharding import PartitionSpec as P

MESH = pl.DeviceIdType.MESH
F32 = jnp.float32
BF = jnp.bfloat16


def place():
    dp = lax.axis_index("dp")
    t = lax.axis_index("tensor")
    return dp // 8, (dp // 2) % 4, dp % 2, t


def dev(x, z, yh, t):
    return ((x * 4 + z) * 2 + yh, t)


def m4(v):
    return (v + 8) % 4


def neighbour(axis, d):
    x, z, yh, t = place()
    return dev(m4(x + d), z, yh, t) if axis == "x" else dev(x, m4(z + d), yh, t)


def tensor_peers():
    x, z, yh, t = place()
    yl, co = t // 2, t % 2
    slots = (yl * 2 + 1 - co, (1 - yl) * 2 + co, (1 - yl) * 2 + 1 - co)
    return [dev(x, z, yh, s) for s in slots], slots


def greet(peers):
    bar = pltpu.get_barrier_semaphore()
    for p in peers:
        pl.semaphore_signal(bar, inc=1, device_id=p, device_id_type=MESH)
    pl.semaphore_wait(bar, len(peers))


def send(src, dst, send_sem, recv_sem, to):
    return pltpu.make_async_remote_copy(
        src_ref=src, dst_ref=dst, send_sem=send_sem, recv_sem=recv_sem, device_id=to, device_id_type=MESH
    )


class Gather:
    N = 25

    def __init__(self, own, dst, r1, send_sem, recv_sem):
        x, z, yh, _ = place()
        r2 = "z" if r1 == "x" else "x"
        n = own.shape[0]

        def rows(d1, d2, y=None):
            ix, iz = (m4(x + d1), m4(z + d2)) if r1 == "x" else (m4(x + d2), m4(z + d1))
            first = (ix * 4 + iz) * 2
            if y is None:
                return dst.at[pl.ds(pl.multiple_of(first * n, n), 2 * n)]
            return dst.at[pl.ds(pl.multiple_of((first + y) * n, n), n)]

        self.mine = rows(0, 0, yh)
        self.own = own
        near1, near2 = [neighbour(r1, 1), neighbour(r1, -1)], [neighbour(r2, 1), neighbour(r2, -1)]
        other = rows(0, 0, 1 - yh)
        plan = [(own, self.mine, dev(x, z, 1 - yh, place()[3]))]
        plan += [(own, self.mine, p) for p in near1 + near2]
        plan += [(other, other, p) for p in near1 + near2]
        plan += [(rows(-1, 0, 0),) * 2 + (near1[0],), (rows(1, 0, 1),) * 2 + (near1[1],)]
        for d1 in (-1, 1, 2):
            plan += [(rows(d1, 0),) * 2 + (p,) for p in near2]
        for d1 in (0, -1, 1, 2):
            plan += [(rows(d1, -1, 0),) * 2 + (near2[0],), (rows(d1, 1, 1),) * 2 + (near2[1],)]
        self.plan, self.send_sem, self.recv_sem = plan, send_sem, recv_sem

    def copy(self, k):
        src, dst, to = self.plan[k]
        return send(src, dst, self.send_sem.at[k], self.recv_sem.at[k], to)

    STEPS = (
        ((), (1, 2, 3, 4)),
        ((0,), (5, 6, 7, 8)),
        ((1, 2, 5, 6), (9, 10, 11, 12, 13, 14)),
        ((9, 10), (15, 16)),
        ((3, 4, 7, 8), (17, 18)),
        ((11, 12, 13, 14), (19, 20, 21, 22)),
        ((15, 16), (23, 24)),
        ((17, 18, 19, 20, 21, 22, 23, 24), ()),
    )

    def begin(self):
        self.copy(0).start()

    def step(self, k):
        arrive, go = self.STEPS[k]
        for i in arrive:
            self.copy(i).wait_recv()
        for i in go:
            self.copy(i).start()

    def finish(self):
        for k in range(self.N):
            self.copy(k).wait_send()


Q = 256
LOG2E = 1.4426950408889634
NEG = -1e30


def dnn(a, b):
    return jnp.dot(a, b, preferred_element_type=F32)


def dnt(a, b):
    return lax.dot_general(a, b, (((1,), (1,)), ((), ())), preferred_element_type=F32)


def split3(v):
    hi = v.astype(BF)
    r = v - hi.astype(F32)
    mid = r.astype(BF)
    lo = (r - mid.astype(F32)).astype(BF)
    return hi, mid, lo


def tri_times(mat, v):
    hi, mid, lo = split3(v)
    out = dnn(mat, jnp.concatenate([hi, mid, lo], axis=1))
    w = v.shape[1]
    return out[:, :w] + out[:, w : 2 * w] + out[:, 2 * w :]


def ii(shape, dim):
    return lax.broadcasted_iota(jnp.int32, shape, dim)


def sigmoid(v):
    return 1.0 / (1.0 + jnp.exp2(v * -LOG2E))


def softplus(v):
    e = jnp.exp2(jnp.abs(v) * -LOG2E)
    u = 1.0 + e
    log1p = jnp.where(u == 1.0, e, jnp.log(u) * (e / jnp.where(u == 1.0, 1.0, u - 1.0)))
    return jnp.maximum(v, 0.0) + log1p


def conv_terms(ext, match, taps):
    n = ext.shape[0] - 8
    shifted = [ext[8:]] + [jnp.where(match[k], ext[8 - k : 8 + n - k], 0.0) for k in (1, 2, 3)]
    pre = taps[4:5] + sum(taps[3 - k : 4 - k] * shifted[k] for k in range(4))
    return pre, shifted


def with_earlier(ref, r0, lanes):
    prev = ref[pl.ds(pl.multiple_of(jnp.maximum(r0 - 8, 0), 8), 8), lanes]
    return jnp.concatenate([prev, ref[pl.ds(r0, Q), lanes]], axis=0)


def match_rows(segc, r0):
    prev = segc[pl.ds(pl.multiple_of(jnp.maximum(r0 - 8, 0), 8), 8), :]
    prev = jnp.where(r0 > 0, prev, -1.0)
    cur = segc[pl.ds(r0, Q), :]
    ext = jnp.concatenate([prev, cur], axis=0)
    return [None] + [ext[8 - k : 8 + Q - k] == cur for k in (1, 2, 3)]


def pack_heads(nh, cum, step, tail, ecum):
    parts = list(split3(cum))
    for v in (step, tail, ecum):
        hi = v.astype(BF)
        parts += [hi, (v - hi.astype(F32)).astype(BF)]
    out = parts[0].astype(F32)
    for k, p in enumerate(parts[1:]):
        out = out + pltpu.roll(p.astype(F32), (k + 1) * nh, 1)
    return out.astype(BF)


def unpack_matrix(nh, jj):
    k, col = ii((128, 1280), 0), ii((128, 1280), 1)
    kind = jnp.where(k < 3 * nh, 0, jnp.where(k < 5 * nh, 1, jnp.where(k < 7 * nh, 2, jnp.where(k < 9 * nh, 3, 9))))
    want = jnp.where(col < 512, 0, (col - 256) // 256)
    sub = jnp.where(col < 512, col // 128, (col % 256) // 64)
    return ((kind == want) & (k % nh == 4 * jj + sub)).astype(BF)


def block_rows(c):
    return pl.ds(pl.multiple_of(c * Q, Q), Q)


def wide(match):
    return [None] + [jnp.concatenate([m, m], axis=1) for m in match[1:]]


def prepare_block(c, nv, vals, segc, segr, cbc, hp):
    nh = nv // 64
    r0 = pl.multiple_of(c * Q, Q)
    rows = block_rows(c)
    pre, _sh = conv_terms(with_earlier(vals, r0, pl.ds(nv, 256)), wide(match_rows(segc, r0)), cbc[...])
    bc = pre * sigmoid(pre)
    bb, cc = bc[:, :128].astype(BF), bc[:, 128:].astype(BF)
    seg = segc[rows]
    tt, ss = ii((Q, Q), 0), ii((Q, Q), 1)
    allowed = (tt >= ss) & (jnp.concatenate([seg, seg], axis=1) == segr[0:1, rows])
    bias = jnp.where(allowed, 0.0, NEG)
    mine = ii((Q, 128), 1) < nh
    zero = lambda v: jnp.where(mine, v, 0.0)
    step = zero(softplus(vals[rows, pl.ds(nv + 256, 128)] + hp[0:1]))
    cum = tri_times((tt >= ss).astype(BF), step * (hp[1:2] * LOG2E))
    before = segc[pl.ds(pl.multiple_of(jnp.maximum(r0 - 8, 0), 8), 8)][7:8]
    before = jnp.where(c > 0, before, -1.0)
    tail = zero(jnp.exp2(cum[Q - 1 :] - cum) * (seg == seg[Q - 1 :]).astype(F32))
    ecum = zero(jnp.exp2(cum) * (seg == before).astype(F32))
    return bb, cc, bc[:, :128].T.astype(BF), bc[:, 128:].T.astype(BF), dnt(cc, bb), bias, cum.T, pack_heads(nh, cum, step, tail, ecum)


def fwd_scratch(nv):
    V = lambda s, d=F32: pltpu.VMEM(s, d)
    nh = nv // 64
    return dict(
        bt=V((128, Q), BF), c=V((Q, 128), BF), qk=V((Q, Q)), bias=V((Q, Q)), cumt=V((nh, 8, Q)), pack=V((Q, 128), BF),
        un=V((nh // 4, 128, 1280), BF), ex=V((Q, 1280)), state=V((128, nv)), m=V((4, Q, Q), BF),
    )


def ssd_forward(nv, vals, segc, segr, cx, cbc, hp, ssd, states, s, hook=lambda at: None):
    nh = nv // 64
    for jj in range(nh // 4):
        s["un"][jj] = unpack_matrix(nh, jj)
    s["state"][...] = jnp.zeros_like(s["state"])
    s["m"][...] = jnp.zeros_like(s["m"])

    def block(c, _):
        r0 = pl.multiple_of(c * Q, Q)
        _bb, s["c"][...], s["bt"][...], _ct, s["qk"][...], s["bias"][...], cumt, s["pack"][...] = prepare_block(c, nv, vals, segc, segr, cbc, hp)
        for h in range(nh):
            s["cumt"][h] = jnp.broadcast_to(cumt[h : h + 1], (8, Q))
        states[c] = s["state"][...].astype(BF)
        match = wide(match_rows(segc, r0))

        def quad(jj, _):
            hook(c * (nv // 256) + jj)
            lanes = pl.ds(pl.multiple_of(jj * 256, 256), 256)
            s["ex"][...] = dnn(s["pack"][...], s["un"][jj])
            pre, _sh = conv_terms(with_earlier(vals, r0, lanes), match, cx[:, lanes])
            x = pre * sigmoid(pre)
            u = x * s["ex"][:, 512:768]
            ub = u.astype(BF)
            st = s["state"][:, lanes]
            y = dnn(s["c"][...], st.astype(BF)) * s["ex"][:, 1024:1280] + cx[5:6, lanes] * x
            s["state"][:, lanes] = st * s["ex"][Q - 1 : Q, 1024:1280] + dnn(s["bt"][...], (u * s["ex"][:, 768:1024]).astype(BF))
            for r in range(4):
                rows = slice(r * 64, r * 64 + 64)
                for k in range(1 if r < 2 else 2):
                    cols = slice(k * 128, k * 128 + 128)
                    qk, bias = s["qk"][rows, cols], s["bias"][rows, cols]
                    for n in range(4):
                        dec = jnp.exp2(s["ex"][rows, n * 128 : n * 128 + 128] - s["cumt"][4 * jj + n, 0:1, cols] + bias)
                        s["m"][n, rows, cols] = (dec * qk).astype(BF)
            low_half = ii((Q, 128), 1) < 64
            outs = []
            for p in range(2):
                right = ub[:, p * 128 : p * 128 + 128]
                outs.append(jnp.where(low_half, dnn(s["m"][2 * p], right), dnn(s["m"][2 * p + 1], right)))
            ssd[pl.ds(r0, Q), lanes] = y + jnp.concatenate(outs, axis=1)
            return 0

        lax.fori_loop(0, nv // 256, quad, 0)
        return 0

    lax.fori_loop(0, vals.shape[0] // Q, block, 0)


def later_sum(dpre, halo, match_ext, taps):
    ext = jnp.concatenate([dpre, halo], axis=0)
    n = dpre.shape[0]
    out = taps[3:4] * dpre
    for k in (1, 2, 3):
        out = out + taps[3 - k : 4 - k] * jnp.where(match_ext[k], ext[k : n + k], 0.0)
    return out


def run_forward(nv, vals, segc, segr, cx, cbc, hp):
    sc = fwd_scratch(nv)
    names = list(sc)
    rows = vals.shape[0]

    def kernel(vals, segc, segr, cx, cbc, hp, ssd, states, *scr):
        ssd_forward(nv, vals, segc, segr, cx, cbc, hp, ssd, states, dict(zip(names, scr)))

    vm = pl.BlockSpec(memory_space=pltpu.VMEM)
    return pl.pallas_call(
        kernel, out_shape=(jax.ShapeDtypeStruct((rows, nv), F32), jax.ShapeDtypeStruct((rows // Q, 128, nv), F32)),
        in_specs=[vm] * 6, out_specs=[vm] * 2, scratch_shapes=[sc[n] for n in names],
        compiler_params=pltpu.CompilerParams(vmem_limit_bytes=60 * 2**20), name="scan_forward",
    )(vals, segc, segr, cx, cbc, hp)


def back_scratch(nv, rows):
    V = lambda s, d=F32: pltpu.VMEM(s, d)
    nb, nh = rows // Q, nv // 64
    return dict(
        b=V((rows, 128), BF), c=V((rows, 128), BF), bt=V((nb, 128, Q), BF), ct=V((nb, 128, Q), BF), qk=V((nb, Q, Q)), bias=V((nb, Q, Q)), pack=V((rows, 128), BF),
        cumt=V((nb, nh, 8, Q)), un=V((128, 1280), BF), ex=V((Q, 1280)), dqk=V((nb, Q, Q)), dcs=V((rows, 128)), dbs=V((rows, 128)), hsum=V((rows, 128)),
        colg=V((nb, nh, 8, Q)), krow=V((nb, 8, nv)), dstate=V((128, 256)), halo=V((8, 256)), halobc=V((8, 256)), m=V((4, Q, Q), BF), dm=V((4, Q, Q)),
    )


def back_setup(nv, vals, segc, segr, cbc, hp, s):
    nh = nv // 64
    for n in ("dqk", "dcs", "dbs", "hsum", "m"):
        s[n][...] = jnp.zeros_like(s[n])

    def block(c, _):
        rows = block_rows(c)
        s["b"][rows], s["c"][rows], s["bt"][c], s["ct"][c], s["qk"][c], s["bias"][c], cumt, s["pack"][rows] = prepare_block(c, nv, vals, segc, segr, cbc, hp)
        for h in range(nh):
            s["cumt"][c, h] = jnp.broadcast_to(cumt[h : h + 1], (8, Q))
        return 0

    lax.fori_loop(0, vals.shape[0] // Q, block, 0)


def back_pairs(at, nv, vals, segc, cx, dy_ref, states, low, gx, s):
    nb, nh = vals.shape[0] // Q, nv // 64
    jj, i = at // nb, at % nb
    c = nb - 1 - i
    r0 = pl.multiple_of(c * Q, Q)
    rows_c = block_rows(c)
    lanes = pl.ds(pl.multiple_of(jj * 256, 256), 256)

    @pl.when(i == 0)
    def _():
        s["dstate"][...] = jnp.zeros_like(s["dstate"])
        s["halo"][...] = jnp.zeros_like(s["halo"])
        s["un"][...] = unpack_matrix(nh, jj)

    match, after = wide(match_rows(segc, r0)), wide(match_after(segc, r0))
    s["ex"][...] = dnn(s["pack"][rows_c], s["un"][...])
    stepe, taile, ecume = s["ex"][:, 512:768], s["ex"][:, 768:1024], s["ex"][:, 1024:1280]
    keep = s["ex"][Q - 1 : Q, 1024:1280]
    taps = cx[:, lanes]
    pre, shifted = conv_terms(with_earlier(vals, r0, lanes), match, taps)
    sig = sigmoid(pre)
    x = pre * sig
    u = x * stepe
    ub = u.astype(BF)
    dy = dy_ref[rows_c, lanes].astype(F32)
    dyt = dy.T.astype(BF)
    stb = states[c, :, lanes]
    dst = s["dstate"][...]
    dstb = dst.astype(BF)
    edy = ecume * dy
    edyb = edy.astype(BF)
    rs = edy * dnn(s["c"][rows_c], stb)
    tu = taile * u
    v = dnn(s["b"][rows_c], dstb)
    s["dcs"][rows_c] += dnt(edyb, stb)
    s["dbs"][rows_c] += dnt(tu.astype(BF), dstb)
    krow = keep * jnp.sum(stb.astype(F32) * dst, axis=0, keepdims=True)
    s["dstate"][...] = keep * dst + dnn(s["ct"][c], edyb)
    lane = ii((Q, 128), 1)
    for n in range(4):
        half = slice(n // 2 * 128, n // 2 * 128 + 128)
        mine = (lane < 64) if n % 2 == 0 else (lane >= 64)
        s["dm"][n] = dnt(jnp.where(mine, dy[:, half], 0.0).astype(BF), ub[:, half])
    colsum = [[jnp.zeros((8, 128), F32) for _ in range(2)] for _ in range(4)]
    rowg = []
    for r in range(4):
        rows = slice(r * 64, r * 64 + 64)
        rowsum = [None] * 4
        for k in range(1 if r < 2 else 2):
            cols = slice(k * 128, k * 128 + 128)
            qk, bias = s["qk"][c, rows, cols], s["bias"][c, rows, cols]
            total = None
            for n in range(4):
                dec = jnp.exp2(s["ex"][rows, n * 128 : n * 128 + 128] - s["cumt"][c, 4 * jj + n, 0:1, cols] + bias)
                s["m"][n, rows, cols] = (dec * qk).astype(BF)
                g = s["dm"][n, rows, cols] * dec
                total = g if n == 0 else total + g
                g = g * qk
                rowsum[n] = g if k == 0 else rowsum[n] + g
                colsum[n][k] = colsum[n][k] + jnp.sum(g.reshape(8, 8, 128), axis=0)
            s["dqk"][c, rows, cols] += total
        at_lane = ii((64, 128), 1)
        row = jnp.zeros((64, 128), F32)
        for n in range(4):
            row = jnp.where(at_lane == 48 + 4 * jj + n, jnp.sum(rowsum[n], axis=1, keepdims=True), row)
        rowg.append(row)
    parts = [dnn(dyt[n * 64 : n * 64 + 64], s["m"][n]) for n in range(4)]
    du = jnp.concatenate(parts, axis=0).T + taile * v
    k, col = ii((768, 128), 0), ii((768, 128), 1)
    red = (col == 16 * (k // 256) + 4 * jj + (k % 256) // 64).astype(BF)
    sums = jnp.concatenate([rs.astype(BF), (tu * v).astype(BF), (du * x).astype(BF)], axis=1)
    s["hsum"][rows_c] += dnn(sums, red) + jnp.concatenate(rowg, axis=0)
    dx = du * stepe + taps[5:6] * dy
    dpre = dx * (sig + x * (1.0 - sig))
    low[rows_c, lanes] = later_sum(dpre, s["halo"][...], after, taps).astype(BF)
    s["halo"][...] = dpre[:8]
    gx[:, lanes] += jnp.concatenate(
        [jnp.sum(dpre * shifted[3 - k], axis=0, keepdims=True) for k in range(4)]
        + [jnp.sum(dpre, axis=0, keepdims=True), jnp.sum(dy * x, axis=0, keepdims=True), jnp.zeros((2, 256), F32)], axis=0)
    for n in range(4):
        s["colg"][c, 4 * jj + n] = jnp.broadcast_to(jnp.concatenate([jnp.sum(q, axis=0, keepdims=True) for q in colsum[n]], axis=1), (8, Q))
    s["krow"][c, :, lanes] = jnp.broadcast_to(krow, (8, 256))


def match_after(segc, r0):
    nxt = segc[pl.ds(pl.multiple_of(jnp.minimum(r0 + Q, segc.shape[0] - 8), 8), 8)]
    seg = segc[pl.ds(r0, Q)]
    ext = jnp.concatenate([seg, nxt], axis=0)
    return [None] + [ext[k : Q + k] == seg for k in (1, 2, 3)]


def back_finish(nv, vals, segc, cbc, hp, low, gbc, gh, s):
    nb, nh = vals.shape[0] // Q, nv // 64
    s["halobc"][...] = jnp.zeros_like(s["halobc"])
    gbc[...] = jnp.zeros_like(gbc)
    gh[...] = jnp.zeros_like(gh)

    def block(i, _):
        c = nb - 1 - i
        r0 = pl.multiple_of(c * Q, Q)
        rows = block_rows(c)
        tt, ss = ii((Q, Q), 0), ii((Q, Q), 1)
        e64t = (ii((nv, 128), 0) // 64 == ii((nv, 128), 1)).astype(BF)
        kterm = sum(dnn(p, e64t) for p in split3(s["krow"][c]))
        colg = jnp.concatenate([s["colg"][c, h, 0:1] for h in range(nh)] + [jnp.zeros((128 - nh, Q), F32)], axis=0)
        hs = s["hsum"][rows]
        mine = ii((Q, 128), 1) < nh
        part = lambda k: jnp.where(mine, hs if k == 0 else pltpu.roll(hs, 128 - 16 * k, 1), 0.0)
        dcum = part(3) - colg.T + part(0)
        da = tri_times((ss >= tt).astype(BF), dcum) + tri_times((ss < tt).astype(BF), part(1)) + kterm[0:1]
        rate = hp[1:2]
        raw = vals[rows, pl.ds(nv + 256, 128)] + hp[0:1]
        draw = jnp.where(mine, (part(2) + rate * da) * sigmoid(raw), 0.0)
        low[rows, pl.ds(nv + 256, 128)] = draw.astype(BF)
        gh[...] += jnp.concatenate(
            [jnp.sum(draw, axis=0, keepdims=True), jnp.sum(da * softplus(raw), axis=0, keepdims=True) * rate, jnp.zeros((6, 128), F32)], axis=0)
        dqk = s["dqk"][c]
        dc = dnn(dqk.astype(BF), s["b"][rows]) + s["dcs"][rows]
        db = dnn(dqk.T.astype(BF), s["c"][rows]) + s["dbs"][rows]
        pre, shifted = conv_terms(with_earlier(vals, r0, pl.ds(nv, 256)), wide(match_rows(segc, r0)), cbc[...])
        sig = sigmoid(pre)
        dpre = jnp.concatenate([db, dc], axis=1) * (sig + pre * sig * (1.0 - sig))
        low[rows, pl.ds(nv, 256)] = later_sum(dpre, s["halobc"][...], wide(match_after(segc, r0)), cbc[...]).astype(BF)
        s["halobc"][...] = dpre[:8]
        gbc[...] += jnp.concatenate(
            [jnp.sum(dpre * shifted[3 - k], axis=0, keepdims=True) for k in range(4)] + [jnp.sum(dpre, axis=0, keepdims=True), jnp.zeros((3, 256), F32)], axis=0)
        return 0

    lax.fori_loop(0, nb, block, 0)


def run_backward2(nv, vals, segc, segr, cx, cbc, hp, dy, states):
    rows = vals.shape[0]
    sc = back_scratch(nv, rows)
    names = list(sc)

    def kernel(vals, segc, segr, cx, cbc, hp, dy, states, low, gx, gbc, gh, *scr):
        s = dict(zip(names, scr))
        gx[...] = jnp.zeros_like(gx)
        back_setup(nv, vals, segc, segr, cbc, hp, s)

        def body(at, _):
            back_pairs(at, nv, vals, segc, cx, dy, states, low, gx, s)
            return 0

        lax.fori_loop(0, nv // 256 * (rows // Q), body, 0)
        back_finish(nv, vals, segc, cbc, hp, low, gbc, gh, s)

    vm = pl.BlockSpec(memory_space=pltpu.VMEM)
    outs = (jax.ShapeDtypeStruct((rows, nv + 384), BF), jax.ShapeDtypeStruct((8, nv), F32), jax.ShapeDtypeStruct((8, 256), F32), jax.ShapeDtypeStruct((8, 128), F32))
    return pl.pallas_call(
        kernel, out_shape=outs, in_specs=[vm] * 8, out_specs=[vm] * 4, scratch_shapes=[sc[n] for n in names],
        compiler_params=pltpu.CompilerParams(vmem_limit_bytes=60 * 2**20), name="scan_backward",
    )(vals, segc, segr, cx, cbc, hp, dy, states)


INNER = 3072
EPS = 1e-05


def at_step(step, events):
    for k, fn in events:

        @pl.when(step == k)
        def _(fn=fn):
            fn()


def forward_kernel(
    names, nv,
    hid, cot_own, p_x, p_bc, p_dt, p_gate, p_out, pgain, seg, conv_x, bias_x, conv_bc, bias_bc, dt_bias, a_log, skip_d, gate_gain,
    o_w0, o_w1, o_w2, o_w3, o_nrm, o_cot, o_vals, o_states, o_no, o_lg, o_dy, o_gg, cx, cbc, hp, segc, segr,
    square, w_own1, w0, w1, w2, w3, nrm, cot, vals, states, ssd, gate, gno, no, lg, dy, sums_own, sums_in,
    wsend, wrecv, tsend, trecv, ssend, srecv, lsem, *scan_scratch,
):
    s = dict(zip(names, scan_scratch))
    x, z, yh, t = place()
    yl, co = t // 2, t % 2
    tp, slots = tensor_peers()
    width = hid.shape[1]
    cut = w0.shape[1]
    w_own0, w_own2, w_own3 = p_x.at[:, :cut], p_gate, p_out
    w_own1[...] = jnp.zeros_like(w_own1)
    w_own1[:, : nv - cut] = p_x[:, cut:]
    w_own1[:, nv - cut : nv - cut + 256] = p_bc[...]
    square[...] = jnp.zeros_like(square)
    square[: p_dt.shape[0], : p_dt.shape[1]] = p_dt[...].astype(F32)
    w_own1[:, nv - cut + 256 :] = square[...].T[: p_dt.shape[1]].astype(BF)
    greet([dev(x, z, 1 - yh, t)] + [neighbour(a, d) for a in "xz" for d in (1, -1)] + tp)
    owns, dsts, outs = (w_own0, w_own1, w_own2, w_own3), (w0, w1, w2, w3), (o_w0, o_w1, o_w2, o_w3)
    groups = lambda ks: [Gather(owns[k], dsts[k], "xz"[k % 2], wsend.at[k], wrecv.at[k]) for k in ks]
    first, second = (0, 1), (2, 3)

    def step(ks, n):
        for g in groups(ks):
            g.step(n)

    def saved(i, src, dst):
        return pltpu.make_async_copy(src, dst, lsem.at[i])

    mine = pl.ds(pl.multiple_of(t * 256, 256), 256)
    theirs = pl.ds(pl.multiple_of(slots[1] * 256, 256), 256)

    def tensor_copies(i, own, dst):
        return (
            send(own, dst.at[mine], tsend.at[i, 0], trecv.at[i, 0], tp[1]),
            send(own, dst.at[mine], tsend.at[i, 1], trecv.at[i, 1], tp[0]),
            send(dst.at[theirs], dst.at[theirs], tsend.at[i, 2], trecv.at[i, 2], tp[0]),
        )

    for g in groups((0, 1, 2, 3)):
        g.begin()
    step(first, 0)

    def norm_rows(i, _):
        rows = pl.ds(pl.multiple_of(i * 64, 64), 64)
        h = hid[rows].astype(F32)
        inv = lax.rsqrt(jnp.mean(h * h, axis=1, keepdims=True) + EPS)
        nrm[pl.ds(pl.multiple_of(t * 256 + i * 64, 64), 64)] = (h * inv * pgain[0:1]).astype(BF)
        return 0

    lax.fori_loop(0, 4, norm_rows, 0)
    nrm_copies = tensor_copies(0, nrm.at[mine], nrm)
    cot_copies = tensor_copies(1, cot_own, cot)
    nrm_copies[0].start()
    nrm_copies[1].start()
    step(first, 1)
    own_lanes = pl.ds(pl.multiple_of(t * nv, 128), nv)
    heads = p_dt.shape[0]

    def own_heads(v, lanes, per):
        i, j = ii((v.shape[1], lanes), 0), ii((v.shape[1], lanes), 1)
        pick = ((i == t * heads + j // per) & (j < heads * per)).astype(BF)
        return sum(dnn(part, pick) for part in split3(jnp.broadcast_to(v[...], (8, v.shape[1]))))

    cx[0:4] = conv_x[:, own_lanes]
    cx[4:5] = bias_x[:, own_lanes]
    cx[5:8] = own_heads(skip_d, nv, 64)[5:8]
    cbc[0:4] = conv_bc[...]
    cbc[4:8] = jnp.broadcast_to(bias_bc[...], (4, 256))
    hp[0:1] = own_heads(dt_bias, 128, 1)[0:1]
    hp[1:2] = jnp.where(ii((1, 128), 1) < heads, -jnp.exp(own_heads(a_log, 128, 1)[0:1]), 0.0)
    hp[2:8] = jnp.zeros((6, 128), F32)
    gains = gate_gain[:, own_lanes]
    sf = seg[...].astype(F32)
    for k in range(seg.shape[0]):
        segr[:, k * 128 : k * 128 + 128] = jnp.broadcast_to(sf[k : k + 1], (8, 128))
        segc[k * 128 : k * 128 + 128] = jnp.broadcast_to(sf[k : k + 1], (128, 128)).T
    for k in range(4):
        g = groups((k,))[0]
        g.mine[...] = g.own[...]
    cot[mine] = cot_own[...]
    for n in (4, 2, 3):
        step(first, n)
    cot_copies[0].start()
    cot_copies[1].start()
    step(second, 0)
    step(second, 1)
    step(first, 5)
    step(first, 6)
    nrm_copies[0].wait_recv()
    nrm_copies[2].start()
    step(second, 4)
    step(first, 7)
    nrm_copies[1].wait_recv()
    nrm_copies[2].wait_recv()

    def project(i, _):
        pl.when(i == 2)(lambda: step(second, 2))
        rows = pl.ds(pl.multiple_of(i * 256, 256), 256)
        n = nrm[rows]
        at = 0
        for w in (w0, w1):
            c = w.shape[1]
            vals[rows, at : at + c] = jnp.dot(n, w[...], preferred_element_type=F32)
            at += c
        return 0

    lax.fori_loop(0, 4, project, 0)
    early = [(0, w0, o_w0), (1, w1, o_w1), (2, nrm, o_nrm), (3, vals, o_vals)]
    for e in early:
        saved(*e).start()

    def cot_forward():
        cot_copies[0].wait_recv()
        cot_copies[2].start()

    events = [(1, lambda: step(second, 3)), (3, lambda: step(second, 5)), (5, lambda: step(second, 6)), (7, cot_forward)]
    ssd_forward(nv, vals, segc, segr, cx, cbc, hp, ssd, states, s, lambda at: at_step(at, events))
    step(second, 7)
    cot_copies[1].wait_recv()
    cot_copies[2].wait_recv()
    late = [(4, w2, o_w2), (5, w3, o_w3), (6, cot, o_cot), (7, states, o_states)]
    for e in late:
        saved(*e).start()

    def inner(i, _):
        rows = pl.ds(pl.multiple_of(i * 256, 256), 256)
        g = jnp.dot(nrm[rows], w2[...], preferred_element_type=F32)
        gate[rows] = g
        o = jnp.dot(cot[rows], w3[...], preferred_element_type=F32)
        gno[rows] = o
        gated = ssd[rows] * (g * sigmoid(g))
        sq = jnp.sum(gated * gated, axis=1, keepdims=True)
        cr = jnp.sum(o * gains * gated, axis=1, keepdims=True)
        lane = ii((256, 128), 1)
        both = jnp.where(lane == 0, sq, jnp.where(lane == 1, cr, 0.0))
        sums_own[:, rows] = both.T[:8]
        return 0

    lax.fori_loop(0, 4, inner, 0)
    small = [send(sums_own, sums_in.at[k], ssend.at[k], srecv.at[k], p) for k, p in enumerate(tp)]
    for c in small:
        c.start()
    for c in small:
        c.wait_recv()
    o_gg[...] = jnp.zeros_like(o_gg)

    def outer(i, _):
        rows = pl.ds(pl.multiple_of(i * 256, 256), 256)
        tot = sums_own[:, rows] + sums_in[0, :, rows] + sums_in[1, :, rows] + sums_in[2, :, rows]
        cols = jnp.concatenate([tot, jnp.zeros((120, 256), F32)], axis=0).T
        inv = lax.rsqrt(cols[:, 0:1] / INNER + EPS)
        cross = inv * inv * inv * cols[:, 1:2] / INNER
        for k in range(nv // 128):
            lanes = pl.ds(k * 128, 128)
            g, y, o, gain = gate[rows, lanes], ssd[rows, lanes], gno[rows, lanes], gains[:, k * 128 : k * 128 + 128]
            sig = sigmoid(g)
            silu = g * sig
            gated = y * silu
            scaled = gated * inv
            no[rows, lanes] = (scaled * gain).astype(BF)
            o_gg[0:1, lanes] += jnp.sum(o * scaled, axis=0, keepdims=True)
            grad = o * gain * inv - gated * cross
            dy[rows, lanes] = (grad * silu).astype(BF)
            lg[rows, lanes] = (grad * y * (sig + silu * (1.0 - sig))).astype(BF)
        return 0

    lax.fori_loop(0, 4, outer, 0)
    last = [(8, no, o_no), (9, lg, o_lg), (10, dy, o_dy)]
    for e in last:
        saved(*e).start()
    for g in groups((0, 1, 2, 3)):
        g.finish()
    for c in nrm_copies + cot_copies + tuple(small):
        c.wait_send()
    for e in early + late + last:
        saved(*e).wait()


def run_k1(hid, cot_own, projs, pgain, seg, params):
    anys, vm = pl.BlockSpec(memory_space=pl.ANY), pl.BlockSpec(memory_space=pltpu.VMEM)
    nv = projs[0].shape[1]
    rows = seg.shape[0] * seg.shape[1]
    n, d = projs[0].shape[0], hid.shape[1]
    sh = jax.ShapeDtypeStruct
    cols = [nv - 128, 512, nv, nv]
    nvals = cols[0] + cols[1]
    outs = [sh((d, c), BF) for c in cols] + [sh((rows, d), BF)] * 2 + [sh((rows, nvals), F32), sh((rows // Q, 128, nv), BF)] + [sh((rows, nv), BF)] * 3
    outs += [sh((8, nv), F32), sh((8, nv), F32), sh((8, 256), F32), sh((8, 128), F32), sh((rows, 128), F32), sh((8, rows), F32)]
    V = lambda shape, dt: pltpu.VMEM(shape, dt)
    D = pltpu.SemaphoreType.DMA
    scan = fwd_scratch(nv)
    scratch = [V((128, 128), F32), V((n, cols[1]), BF)] + [V((d, c), BF) for c in cols] + [V((rows, d), BF)] * 2
    scratch += [V((rows, nvals), F32), V((rows // Q, 128, nv), BF)] + [V((rows, nv), F32)] * 3 + [V((rows, nv), BF)] * 3
    scratch += [V((8, rows), F32), V((3, 8, rows), F32), D((4, Gather.N)), D((4, Gather.N)), D((2, 3)), D((2, 3)), D((3,)), D((3,)), D((11,))]
    scratch += list(scan.values())
    return pl.pallas_call(
        functools.partial(forward_kernel, list(scan), nv), out_shape=outs, in_specs=[vm] * 17, out_specs=[anys] * 11 + [vm] * 6, scratch_shapes=scratch,
        compiler_params=pltpu.CompilerParams(collective_id=0, has_side_effects=True, vmem_limit_bytes=62 * 2**20), name="forward_all",
    )(hid, cot_own, *projs, pgain, seg, *params)


class Scatter:
    N = 13

    def __init__(self, v, bufs, out, a1, send_sem, recv_sem):
        x, z, yh, t = place()
        self.v, self.out, self.a1, self.yh = v, out, a1, yh
        self.r1, self.r2, self.q1, self.q2, self.kk, self.yy = bufs
        self.h = self.r2.at[0]
        a2 = "z" if a1 == "x" else "x"
        self.p, self.q = (x, z) if a1 == "x" else (z, x)
        self.send_sem, self.recv_sem = send_sem, recv_sem
        right1, left1, right2, left2 = neighbour(a1, 1), neighbour(a1, -1), neighbour(a2, 1), neighbour(a2, -1)
        r1, r2, h, q1, q2, q = self.r1, self.r2, self.h, self.q1, self.q2, self.q
        self.plan = [
            (self.half(2, 0), r1.at[0], right1), (self.half(2, 1), r1.at[1], left1),
            (self.half(1, 1), r2.at[0, pl.ds(2, 2)], right1), (self.half(-1, 0), r2.at[1, pl.ds(0, 2)], left1),
            (self.half(1, 0), r2.at[0, pl.ds(0, 2)], right1), (self.half(-1, 1), r2.at[1, pl.ds(2, 2)], left1),
            (h.at[m4(q + 2), 0], q1.at[0], right2), (h.at[m4(q + 2), 1], q1.at[1], left2),
            (h.at[m4(q + 1), 1], q2.at[0, 1], right2), (h.at[m4(q - 1), 0], q2.at[1, 0], left2),
            (h.at[m4(q + 1), 0], q2.at[0, 0], right2), (h.at[m4(q - 1), 1], q2.at[1, 1], left2),
            (self.kk, self.yy, dev(x, z, 1 - yh, t)),
        ]

    def half(self, d, k):
        at = m4(self.p + d)
        return self.v.at[pl.ds(2 * k, 2), at] if self.a1 == "z" else self.v.at[at, pl.ds(2 * k, 2)]

    def copy(self, k):
        src, dst, to = self.plan[k]
        return send(src, dst, self.send_sem.at[k], self.recv_sem.at[k], to)

    def start(self, *ks):
        for k in ks:
            self.copy(k).start()

    def arrive(self, *ks):
        for k in ks:
            self.copy(k).wait_recv()

    def step(self, n):
        v, r1, r2, h, q1, q2, p, q, yh = self.v, self.r1, self.r2, self.h, self.q1, self.q2, self.p, self.q, self.yh
        if n == 0:
            self.start(0, 1, 2, 3)
        elif n == 1:
            for side, d in ((0, 1), (1, -1)):
                self.arrive(side)
                at = m4(p + d)

                def add(j, _, side=side, at=at):
                    e, y = j // 2, j % 2
                    ix = (2 * side + e, at, y) if self.a1 == "z" else (at, 2 * side + e, y)
                    v[ix] = v[ix] + r1[side, e, y]
                    return 0

                lax.fori_loop(0, 4, add, 0)
                self.start(4 + side)
        elif n == 2:
            self.arrive(2, 3, 4, 5)

            def add(j, _):
                e, y = j // 2, j % 2
                own = v[e, p, y] if self.a1 == "z" else v[p, e, y]
                h[e, y] = own + (r2[0, e, y] + r2[1, e, y])
                return 0

            lax.fori_loop(0, 8, add, 0)
            self.start(6, 7, 8, 9)
        elif n == 3:
            for side, d in ((0, 1), (1, -1)):
                self.arrive(6 + side)
                at = m4(q + d)
                h[at, side] = h[at, side] + q1[side]
                self.start(10 + side)
        elif n == 4:
            self.arrive(8, 9, 10, 11)
            self.kk[...] = (h[q, 1 - yh].astype(F32) + q2[0, 1 - yh].astype(F32) + q2[1, 1 - yh].astype(F32)).astype(BF)
            self.start(12)
        else:
            self.arrive(12)
            self.out[...] = h[q, yh].astype(F32) + q2[0, yh].astype(F32) + q2[1, yh].astype(F32) + self.yy[...].astype(F32)

    def finish(self):
        for k in range(self.N):
            self.copy(k).wait_send()


class TokenScatter:
    def __init__(self, v, from_core, from_chip, out, send_sem, recv_sem):
        t = place()[3]
        tp, slots = tensor_peers()
        self.t, self.v, self.from_core, self.from_chip, self.out = t, v, from_core, from_chip, out
        rows = lambda s: pl.ds(pl.multiple_of(s * 256, 256), 256)
        self.pass_on, self.mine = slots[1], rows(t)
        self.copies = lambda k: (
            lambda: send(v.at[rows(slots[2])], from_core.at[0], send_sem.at[0], recv_sem.at[0], tp[0]),
            lambda: send(v.at[rows(slots[0])], from_core.at[1], send_sem.at[1], recv_sem.at[1], tp[0]),
            lambda: send(v.at[rows(slots[1])], from_chip, send_sem.at[2], recv_sem.at[2], tp[1]),
        )[k]()

    def step(self, n):
        if n == 0:
            self.copies(0).start()
            self.copies(1).start()
        elif n == 1:
            self.copies(0).wait_recv()

            def add(j, _):
                rows = pl.ds(pl.multiple_of(j * 32, 32), 32)
                own = pl.ds(pl.multiple_of(self.pass_on * 256 + j * 32, 32), 32)
                self.v[own] = self.v[own] + self.from_core[0, rows]
                return 0

            lax.fori_loop(0, 8, add, 0)
            self.copies(2).start()
        else:
            self.copies(1).wait_recv()
            self.copies(2).wait_recv()

            def add(j, _):
                rows = pl.ds(pl.multiple_of(j * 32, 32), 32)
                own = self.v[pl.ds(pl.multiple_of(self.t * 256 + j * 32, 32), 32)]
                self.out[rows] = own.astype(F32) + self.from_core[1, rows].astype(F32) + self.from_chip[rows].astype(F32)
                return 0

            lax.fori_loop(0, 8, add, 0)

    def finish(self):
        for k in range(3):
            self.copies(k).wait_send()


def backward_kernel(
    names, nv,
    h_w0, h_w1, h_w2, h_w3, h_nrm, h_cot, h_vals, h_states, h_no, h_lg, h_dy, pgain, segc, segr, cx, cbc, hp, gg,
    o_gate, o_out, o_x, o_dt, o_bc, o_own, o_grad, o_small,
    w0, w1, w23, nrm, cot, vals, states, nody, lg, low, po, t_out, t_gate, t_0, t_1, t_2, t_bc, t_dt,
    bc_sum, own_v, sx, sz, sy, st, sacc, bct, fc0, ch0, fc1, ch1, gx, gbc, gh, pre,
    wsend, wrecv, tsend, trecv, ssend, srecv, bsend, brecv, lsem, *rest,
):
    bufs, s = [rest[6 * k : 6 * k + 6] for k in range(7)], dict(zip(names, rest[42:]))
    x, z, yh, t = place()
    tp, slots = tensor_peers()
    loads = [
        pltpu.make_async_copy(a, b, lsem.at[k])
        for k, (a, b) in enumerate(((h_no, nody), (h_w3, w23), (h_cot, cot), (h_nrm, nrm), (h_lg, lg), (h_vals, vals), (h_states, states), (h_w0, w0), (h_w1, w1)))
    ]
    for k in (0, 2, 3, 4, 1, 5, 6, 7, 8):
        loads[k].start()
    load_dy, load_w2 = pltpu.make_async_copy(h_dy, nody, lsem.at[9]), pltpu.make_async_copy(h_w2, w23, lsem.at[10])
    greet([dev(x, z, 1 - yh, t)] + [neighbour(a, d) for a in "xz" for d in (1, 2, 3)] + tp)
    wide_x = o_x.shape[1] // 3
    x_part = lambda k: o_x.at[:, k * wide_x : k * wide_x + wide_x]
    scat = [
        Scatter(v, bufs[k], o, "xzxzxzx"[k], wsend.at[k], wrecv.at[k])
        for k, (v, o) in enumerate(((t_out, o_out), (t_gate, o_gate), (t_0, x_part(0)), (t_1, x_part(1)), (t_2, x_part(2)), (t_bc, bc_sum), (t_dt, o_dt)))
    ]
    s_out, s_gate, s_0, s_1, s_2, s_bc, s_dt = scat
    k_out = TokenScatter(po, fc0, ch0, o_own, tsend.at[0], trecv.at[0])
    k_nrm = TokenScatter(cot, fc1, ch1, o_grad, tsend.at[1], trecv.at[1])

    def by_rows(fn):
        def body(i, _):
            fn(pl.ds(pl.multiple_of(i * 256, 256), 256))
            return 0

        lax.fori_loop(0, 4, body, 0)

    def outer_product(dst, left, right):
        def body(i, _):
            cols = pl.ds(pl.multiple_of(i * 384, 384), 384)
            r = lax.dot_general(left[:, cols], right[...], (((0,), (0,)), ((), ())), preferred_element_type=F32)
            first = 0
            for d in dst:
                d[i] = r[:, first : first + d.shape[-1]].astype(BF).reshape(d.shape[1:])
                first += d.shape[-1]
            return 0

        lax.fori_loop(0, 4, body, 0)

    loads[0].wait()
    loads[2].wait()
    outer_product((t_out,), cot, nody)
    s_out.step(0)
    loads[3].wait()
    loads[4].wait()
    outer_product((t_gate,), nrm, lg)
    s_gate.step(0)

    def out_rows(rows):
        left = nody[rows]
        for k in range(0, po.shape[1], 512):
            po[rows, k : k + 512] = dnt(left, w23[k : k + 512]).astype(BF)

    loads[1].wait()
    by_rows(out_rows)
    load_w2.start()
    load_dy.start()
    k_out.step(0)
    for k in (5, 6, 7, 8):
        loads[k].wait()
    back_setup(nv, vals, segc, segr, cbc, hp, s)
    load_dy.wait()
    both = lambda n: lambda: (s_out.step(n), s_gate.step(n))

    def chunk(n):
        def go():
            outer_product(((t_0, t_1, t_2)[n],), nrm, low.at[:, n * wide_x : n * wide_x + wide_x])
            scat[2 + n].step(0)

        return go

    gx[...] = jnp.zeros_like(gx)
    events = [
        (1, lambda: k_out.step(1)),
        (4, both(1)),
        (6, chunk(0)),
        (8, both(2)),
        (9, chunk(1)),
        (10, lambda: k_out.step(2)),
        (11, both(3)),
    ]

    def scan_step(at, _):
        at_step(at, events)
        back_pairs(at, nv, vals, segc, cx, nody, states, low, gx, s)
        return 0

    lax.fori_loop(0, nv // 256 * (vals.shape[0] // Q), scan_step, 0)
    chunk(2)()
    back_finish(nv, vals, segc, cbc, hp, low, gbc, gh, s)
    outer_product((t_bc, t_dt), nrm, low.at[:, nv:])
    s_bc.step(0)
    s_dt.step(0)
    s_out.step(4)
    s_gate.step(4)
    s_0.step(1)
    s_1.step(1)
    load_w2.wait()
    pre[...] = jnp.zeros_like(pre)
    c0 = w0.shape[1]

    def grad_rows(rows):
        for k in range(0, cot.shape[1], 512):
            cols = slice(k, k + 512)
            g = dnt(lg[rows], w23[cols]) + dnt(low[rows, :c0], w0[cols]) + dnt(low[rows, c0:], w1[cols])
            pre[0:1, cols] += jnp.sum(g * nrm[rows, cols].astype(F32), axis=0, keepdims=True)
            cot[rows, cols] = g.astype(BF)

    def grad_slot(i, _):
        slot = ((t // 2 + 1 - i // 2) % 2) * 2 + (t + 1 - i % 2) % 2
        grad_rows(pl.ds(pl.multiple_of(slot * 256, 256), 256))
        at_step(i, [(0, lambda: k_nrm.copies(0).start()), (1, lambda: k_nrm.step(1)), (2, lambda: k_nrm.copies(1).start())])
        return 0

    lax.fori_loop(0, 4, grad_slot, 0)
    own_v[...] = jnp.zeros_like(own_v)
    own_v[0:6] = gx[0:6]
    own_v[6:7] = gg[0:1]
    pv = pre[0:1] / pgain[0:1]
    own_v[7:8], own_v[8:9] = pv[:, :nv], pv[:, nv:]
    for k in range(3):
        own_v[9:10, k * 256 : k * 256 + 256] = gbc[k : k + 1]
    for k in range(2):
        own_v[10:11, k * 256 : k * 256 + 256] = gbc[3 + k : 4 + k]
        own_v[11:12, k * 128 : k * 128 + 128] = gh[k : k + 1]
    small = [send(own_v, sx.at[d - 1], ssend.at[d - 1], srecv.at[d - 1], neighbour("x", d)) for d in (1, 2, 3)]
    for c in small:
        c.start()
    s_0.step(2)
    s_1.step(2)
    s_out.step(5)
    s_gate.step(5)
    s_2.step(1)
    s_bc.step(1)
    s_dt.step(1)

    def next_small(have, total, copies):
        for c in have:
            c.wait_recv()
        total()
        for c in copies:
            c.start()
        return copies

    def total_x():
        sacc[0] = own_v[...] + sx[0] + sx[1] + sx[2]

    def total_z():
        sacc[1] = sacc[0] + sz[0] + sz[1] + sz[2]

    def total_y():
        sacc[2] = sacc[1] + sy[...]

    small_z = next_small(small, total_x, [send(sacc.at[0], sz.at[d - 1], ssend.at[2 + d], srecv.at[2 + d], neighbour("z", d)) for d in (1, 2, 3)])
    s_0.step(3)
    s_1.step(3)
    s_2.step(2)
    s_bc.step(2)
    s_dt.step(2)
    small_y = next_small(small_z, total_z, [send(sacc.at[1], sy, ssend.at[6], srecv.at[6], dev(x, z, 1 - yh, t))])
    s_0.step(4)
    s_1.step(4)
    s_2.step(3)
    s_bc.step(3)
    s_dt.step(3)
    small_t = next_small(small_y, total_y, [send(sacc.at[2], st.at[k], ssend.at[7 + k], srecv.at[7 + k], p) for k, p in enumerate(tp)])
    s_0.step(5)
    s_1.step(5)
    s_2.step(4)
    s_bc.step(4)
    s_dt.step(4)
    s_2.step(5)
    s_bc.step(5)
    bct[3] = bc_sum[...]
    bcs = [send(bct.at[3], bct.at[k], bsend.at[k], brecv.at[k], p) for k, p in enumerate(tp)]
    for c in bcs:
        c.start()
    s_dt.step(5)
    k_nrm.step(2)
    for c in small_t:
        c.wait_recv()
    o_small[t] = sacc[2]
    for k in range(3):
        o_small[slots[k]] = st[k]
    for c in bcs:
        c.wait_recv()
    o_bc[...] = bct[3] + bct[0] + bct[1] + bct[2]
    for c in small + small_z + small_y + small_t + bcs:
        c.wait_send()
    for g in scat + [k_out, k_nrm]:
        g.finish()


def run_k2(ws, nrm, cot, vals, states, no, lg, dy, pgain, segc, segr, cx, cbc, hp, gg):
    anys, vm = pl.BlockSpec(memory_space=pl.ANY), pl.BlockSpec(memory_space=pltpu.VMEM)
    nv = cx.shape[1]
    rows, d = nrm.shape
    sh = lambda *s: jax.ShapeDtypeStruct(s, F32)
    cols = [w.shape[1] for w in ws]
    n = d // 32
    V = lambda *s, dt=BF: pltpu.VMEM(s, dt)
    D = pltpu.SemaphoreType.DMA
    parts = (nv, nv, nv // 3, nv // 3, nv // 3, 256, 128)
    outs = [sh(n, nv), sh(n, nv), sh(n, nv), sh(n, 128), sh(n, 256), sh(256, d), sh(256, d), sh(4, 16, nv)]
    term = lambda c: V(4, 4, 2, n, c)
    scratch = [V(d, cols[0]), V(d, cols[1]), V(d, cols[2]), V(rows, d), V(rows, d), V(*vals.shape, dt=F32), V(*states.shape), V(rows, nv), V(rows, nv), V(*vals.shape), V(rows, d)]
    scratch += [term(c) for c in parts]
    sv = (16, nv)
    scratch += [V(n, 256, dt=F32)]
    scratch += [V(*sv, dt=F32), V(3, *sv, dt=F32), V(3, *sv, dt=F32), V(*sv, dt=F32), V(3, *sv, dt=F32), V(3, *sv, dt=F32), V(4, n, 256, dt=F32)]
    scratch += [V(2, 256, d), V(256, d)] * 2
    scratch += [V(8, nv, dt=F32), V(8, 256, dt=F32), V(8, 128, dt=F32), V(8, d, dt=F32)]
    scratch += [D((7, Scatter.N))] * 2 + [D((2, 3))] * 2 + [D((10,))] * 2 + [D((3,))] * 2 + [D((11,))]
    for c in parts:
        scratch += [V(2, 2, 2, n, c), V(2, 4, 2, n, c), V(2, n, c), V(2, 2, n, c), V(n, c), V(n, c)]
    scan = back_scratch(nv, rows)
    scratch += list(scan.values())
    return pl.pallas_call(
        functools.partial(backward_kernel, list(scan), nv), out_shape=outs, in_specs=[anys] * 11 + [vm] * 7, out_specs=[vm] * 8, scratch_shapes=scratch,
        compiler_params=pltpu.CompilerParams(collective_id=1, has_side_effects=True, vmem_limit_bytes=64 * 2**20), name="backward_all",
    )(*ws, nrm, cot, vals, states, no, lg, dy, pgain, segc, segr, cx, cbc, hp, gg)


def finish_kernel(
    heads, hid, cot, pgain, own_out, grad_own, smalls, r_gate, r_out, r_x, r_last, r_bc,
    out, d_hid, d_pre, d_gate, d_x, d_bc, d_dt, d_conv_x, d_bias_x, d_conv_bc, d_bias_bc, d_dt_bias, d_a_log, d_skip, d_gain, d_out, square,
):
    def rows(i, _):
        at = pl.ds(pl.multiple_of(i * 64, 64), 64)
        h = hid[at].astype(F32)
        g = grad_own[at]
        inv = lax.rsqrt(jnp.mean(h * h, axis=1, keepdims=True) + EPS)
        scaled = g * pgain[...]
        back = jnp.mean(scaled * h, axis=1, keepdims=True)
        out[at] = (h + own_out[at]).astype(BF)
        d_hid[at] = cot[at].astype(F32) + scaled * inv - h * (inv * inv * inv * back)
        return 0

    lax.fori_loop(0, hid.shape[0] // 64, rows, 0)
    nv = smalls.shape[2]
    square[...] = jnp.zeros_like(square)
    d_gate[...] = r_gate[...]
    d_out[...] = r_out[...]
    d_x[...] = r_x[...]
    d_bc[...] = r_bc[...]
    square[: r_last.shape[0]] = r_last[...]
    d_dt[...] = square[...].T[:heads, : r_last.shape[0]]
    parts = [smalls[k] for k in range(4)]
    both = parts[0] + parts[1] + parts[2] + parts[3]
    d_pre[:, :nv] = both[7:8]
    d_pre[:, nv:] = both[8:9]
    for k in range(3):
        d_conv_bc[k : k + 1] = both[9:10, k * 256 : k * 256 + 256]
    d_conv_bc[3:4] = both[10:11, :256]
    d_bias_bc[...] = both[10:11, 256:512]
    per_head = [jnp.zeros((8, 128), F32)] * 3
    for k in range(4):
        lanes = slice(k * nv, k * nv + nv)
        d_conv_x[:, lanes] = parts[k][0:4]
        d_bias_x[:, lanes] = parts[k][4:5]
        d_gain[:, lanes] = parts[k][6:7]
        row = parts[k][8:16]
        i, j = ii((128, 128), 0), ii((128, 128), 1)
        pick = ((i + k * heads == j) & (i < heads)).astype(BF)
        for n in range(2):
            per_head[n] = per_head[n] + sum(dnn(p, pick) for p in split3(row[:, n * 128 : n * 128 + 128]))
        i, j = ii((nv, 128), 0), ii((nv, 128), 1)
        group = (i // 64 + k * heads == j).astype(BF)
        per_head[2] = per_head[2] + sum(dnn(p, group) for p in split3(parts[k][0:8]))
    d_dt_bias[...] = per_head[0][3:4, : 4 * heads]
    d_a_log[...] = per_head[1][3:4, : 4 * heads]
    d_skip[...] = per_head[2][5:6, : 4 * heads]


def run_k3(heads, *args):
    vm = pl.BlockSpec(memory_space=pltpu.VMEM)
    smalls, r_gate = args[5], args[6]
    n, nv = r_gate.shape
    d = args[0].shape[1]
    sh = lambda *s: jax.ShapeDtypeStruct(s, F32)
    outs = [jax.ShapeDtypeStruct(args[0].shape, BF), sh(*args[0].shape), sh(1, d), sh(n, nv), sh(n, nv), sh(n, 256), sh(heads, n), sh(4, 4 * nv), sh(1, 4 * nv), sh(4, 256), sh(1, 256)]
    outs += [sh(1, 4 * heads)] * 3 + [sh(1, 4 * nv), sh(n, nv)]
    return pl.pallas_call(
        functools.partial(finish_kernel, heads), out_shape=outs, in_specs=[vm] * len(args), out_specs=[vm] * len(outs), scratch_shapes=[pltpu.VMEM((128, 128), F32)],
        compiler_params=pltpu.CompilerParams(vmem_limit_bytes=62 * 2**20), name="finish",
    )(*args)


def per_device(
    hidden_in, seg_ids, pre_gain, proj_gate, proj_x, proj_bc, proj_dt, conv_x, conv_bias_x, conv_bc, conv_bias_bc,
    dt_bias, a_log, skip_d, gate_gain, proj_out, cotangent,
):
    row = lambda v: v.reshape(1, -1)
    pgain = row(pre_gain)
    params = (conv_x, row(conv_bias_x), conv_bc, row(conv_bias_bc), row(dt_bias), row(a_log), row(skip_d), row(gate_gain))
    w0, w1, w2, w3, normed, cot, vals, states, normed_out, low_gate, dy, gg, cx, cbc, hp, segc, segr = run_k1(
        hidden_in, cotangent, (proj_x, proj_bc, proj_dt.T, proj_gate, proj_out.T), pgain, seg_ids.reshape(-1, 128), params
    )
    r_gate, r_out, r_x, r_last, r_bc, own_out, grad_own, smalls = run_k2(
        (w0, w1, w2, w3), normed, cot, vals, states, normed_out, low_gate, dy, pgain, segc, segr, cx, cbc, hp, gg
    )
    outs = run_k3(proj_dt.shape[1], hidden_in, cotangent, pgain, own_out, grad_own, smalls, r_gate, r_out, r_x, r_last, r_bc)
    flat = (2, 8, 10, 11, 12, 13, 14)
    turned = (6, 15)
    return tuple(o.reshape(-1) if k in flat else o.T if k in turned else o for k, o in enumerate(outs))


def solution(mesh):
    tok = P(("dp", "tensor"), None)
    mat = P("dp", "tensor")
    in_specs = (tok, P("dp"), P(), mat, mat, P("dp", None), mat) + (P(),) * 8 + (P("tensor", "dp"), tok)
    out_specs = (tok, tok, P(), mat, mat, P("dp", None), mat) + (P(),) * 8 + (P("tensor", "dp"),)
    return jax.shard_map(per_device, mesh=mesh, in_specs=in_specs, out_specs=out_specs, check_vma=False)
```
